32 devices in a mesh: tower: 2 (over x), dp: 16 (over z, y, core).
Axes of the slice: x: 2, y: 2, z: 4, core: 2. Of those that a mesh axis runs over, the one named last changes fastest.
Arguments:
- tokens: bfloat16 [2, 3072, 768], P('tower', 'dp'), may hold values from -21 to 21
- cotangent: bfloat16 [2, 3072, 768], P('tower', 'dp'), may hold values from -6 to 6
- kept_counts: int32 [16, 3], P('dp'), may hold values from 1 to 144, 192 in all within a row
- caption_lengths: int32 [48], P('dp'), may hold values from 16 to 64
- attn_gain: bfloat16 [2, 768], P('tower', 'dp'), may hold values from 0.5 to 1.5
- qkv_weight: bfloat16 [2, 768, 2304], P('tower', 'dp'), may hold values from -0.21875 to 0.21875
- attn_out: bfloat16 [2, 768, 768], P('tower', 'dp'), may hold values from -0.875 to 0.875
- mlp_gain: bfloat16 [2, 768], P('tower', 'dp'), may hold values from 0.5 to 1.5
- mlp_up: bfloat16 [2, 768, 3072], P('tower', 'dp'), may hold values from -0.21875 to 0.21875
- mlp_down: bfloat16 [2, 3072, 768], P('tower', 'dp'), may hold values from -0.109375 to 0.109375
- query_gain: bfloat16 [768], P(('tower', 'dp')), may hold values from 0.5 to 1.5
- image_gain: bfloat16 [768], P(('tower', 'dp')), may hold values from 0.5 to 1.5
- cross_gain: bfloat16 [768], P(('tower', 'dp')), may hold values from 0.5 to 1.5
- cross_query: bfloat16 [768, 768], P(('tower', 'dp')), may hold values from -0.21875 to 0.21875
- cross_keyval: bfloat16 [768, 1536], P(('tower', 'dp')), may hold values from -0.21875 to 0.21875
- cross_out: bfloat16 [768, 768], P(('tower', 'dp')), may hold values from -0.875 to 0.875
- cross_up: bfloat16 [768, 3072], P(('tower', 'dp')), may hold values from -0.21875 to 0.21875
- cross_down: bfloat16 [3072, 768], P(('tower', 'dp')), may hold values from -0.109375 to 0.109375
Outputs:
- layer_out: bfloat16 [2, 3072, 768], P('tower', 'dp')
- input_grad: float32 [2, 3072, 768], P('tower', 'dp')
- attn_gain_grad: float32 [2, 768], P('tower', 'dp')
- qkv_weight_grad: float32 [2, 768, 2304], P('tower', 'dp')
- attn_out_grad: float32 [2, 768, 768], P('tower', 'dp')
- mlp_gain_grad: float32 [2, 768], P('tower', 'dp')
- mlp_up_grad: float32 [2, 768, 3072], P('tower', 'dp')
- mlp_down_grad: float32 [2, 3072, 768], P('tower', 'dp')
- query_gain_grad: float32 [768], P(('tower', 'dp'))
- image_gain_grad: float32 [768], P(('tower', 'dp'))
- cross_gain_grad: float32 [768], P(('tower', 'dp'))
- cross_query_grad: float32 [768, 768], P(('tower', 'dp'))
- cross_keyval_grad: float32 [768, 1536], P(('tower', 'dp'))
- cross_out_grad: float32 [768, 768], P(('tower', 'dp'))
- cross_up_grad: float32 [768, 3072], P(('tower', 'dp'))
- cross_down_grad: float32 [3072, 768], P(('tower', 'dp'))
- rms_values: float32 [10], replicated
The draws below stay inside these ranges and needn't reach their ends.
Inputs may be any that keep to these rules, and one draw needn't show every extreme that they name: `kept_counts`: the 3 images of one device keep 192 patches together, one image after another.
All inputs are finite; a program needn't handle non-finite values.
Results may differ from the reference program's by a relative error of at most 0.019.
Values may be sent and summed in bfloat16 or wider, within the bound.
A program may use at most 256 MiB of HBM per device.

```python
import math
import jax
import jax.numpy as jnp
import numpy as np
from jax import lax

D = 768
HD = 64
FF = 3072
CAP_LEN = 64
MOST_KEPT = 144
CAPS_DEV = 3
ROWS = 192
CAPTIONS = 48
ROWS_ALL = 3072
N_DP = 16


def draw_tokens(key, part):
    key = jax.random.fold_in(key, 7)
    first_key = jax.random.fold_in(key, 0)
    rising = 3.0 ** (jnp.arange(ROWS_ALL, dtype=jnp.float32) / ROWS_ALL)
    base_draw = jnp.clip(jax.random.normal(first_key, (2, ROWS_ALL, D), jnp.float32), -5.0, 5.0)
    return (base_draw * rising[None, :, None]).astype(jnp.bfloat16)


def touch_ends(drawn, rng, low, largest):
    spot = [jax.random.randint(jax.random.fold_in(rng, axis), (), 0, length) for axis, length in enumerate(drawn.shape)]
    widest = drawn.shape.index(max(drawn.shape))
    next_to = spot[:widest] + [(spot[widest] + 1) % drawn.shape[widest]] + spot[widest + 1:]
    return drawn.at[tuple(spot)].set(low).at[tuple(next_to)].set(largest)


def block_scale(own_key, dims, shards, low, largest):
    def one(position, blocks):
        heights = jax.random.uniform(jax.random.fold_in(jax.random.fold_in(own_key, 6), position), (blocks,), jnp.float32, low / len(shards), largest / len(shards))
        return jnp.repeat(jnp.exp(heights), dims[position] // blocks).reshape((-1,) + (1,) * (len(dims) - position - 1))

    gain = one(*shards[0])
    for cut in shards[1:]:
        gain = gain * one(*cut)
    return gain


def split_up(number_of, total, bound, slope):
    portions = [(1 << 20) // math.isqrt(rank ** slope) + 1 for rank in range(2, number_of + 1)]
    surplus, holding = total - bound - (number_of - 1), [1] * (number_of - 1)
    while surplus > 0:
        candidates = [i for i in range(number_of - 1) if holding[i] < bound]
        mass, remaining = sum([portions[i] for i in candidates]), surplus
        for i in candidates:
            more = min(bound - holding[i], max(1, remaining * portions[i] // mass), surplus)
            holding[i] = holding[i] + more
            surplus = surplus - more
    return np.array([bound] + holding)


def ragged(stream_key, amount, total, most, lean):
    if amount == 2:
        one = jax.random.randint(stream_key, (), max(1, total - most), min(most, total - 1) + 1)
        return jnp.stack([one, total - one])
    tallies = jnp.asarray(split_up(amount, total, most, lean), jnp.int32)
    twos = (amount - 1) // 2
    source_of, taker = tallies[1:1 + 2 * twos:2], tallies[2:2 + 2 * twos:2]
    slack = jnp.minimum(source_of - 1, most - taker)
    moved = jax.random.randint(jax.random.fold_in(stream_key, 1), (twos,), 0, 1 << 20) % (slack + 1)
    tallies = tallies.at[1:1 + 2 * twos:2].set(source_of - moved).at[2:2 + 2 * twos:2].set(taker + moved)
    return tallies[jax.random.permutation(jax.random.fold_in(stream_key, 2), amount)]


def centred(rng, shape, width, bound, cuts=(), kind=jnp.bfloat16):
    loudness = block_scale(rng, shape, cuts, -0.22, 0.18) if cuts else 1.0
    result = jax.random.normal(rng, shape, jnp.float32) * width * loudness
    return jnp.minimum(jnp.maximum(result, -bound), bound).astype(kind)


def setup_inputs(seed: int = 0) -> dict:
    key_list = jax.random.split(jax.random.key(seed), 19)
    return {
        "tokens": draw_tokens(jax.random.fold_in(key_list[18], 71), 0),
        "cotangent": centred(key_list[1], (2, ROWS_ALL, D), 1.0, 6.0, ((0, 2), (1, 16))),
        "kept_counts": jax.vmap(lambda own: ragged(own, CAPS_DEV, ROWS, MOST_KEPT, 1))(jax.random.split(key_list[2], N_DP)).reshape((N_DP, CAPS_DEV)).astype(jnp.int32),
        "caption_lengths": touch_ends(jax.random.randint(key_list[3], (CAPTIONS,), CAP_LEN // 4, CAP_LEN + 1), jax.random.fold_in(key_list[3], 1), CAP_LEN // 4, CAP_LEN).astype(jnp.int32),
        "attn_gain": jnp.clip(1.0 + 0.1 * jax.random.normal(key_list[4], (2, D), jnp.float32), 0.5, 1.5).astype(jnp.bfloat16),
        "qkv_weight": centred(key_list[5], (2, D, 3 * D), D ** -0.5, 0.21875, ((0, 2), (1, 16))),
        "attn_out": centred(key_list[6], (2, D, D), (D // 16) ** -0.5, 0.875, ((0, 2), (1, 16))),
        "mlp_gain": jnp.clip(1.0 + 0.1 * jax.random.normal(key_list[7], (2, D), jnp.float32), 0.5, 1.5).astype(jnp.bfloat16),
        "mlp_up": centred(key_list[8], (2, D, FF), D ** -0.5, 0.21875, ((0, 2), (1, 16))),
        "mlp_down": centred(key_list[9], (2, FF, D), FF ** -0.5, 0.109375, ((0, 2), (1, 16))),
        "query_gain": jnp.clip(1.0 + 0.1 * jax.random.normal(key_list[10], (D,), jnp.float32), 0.5, 1.5).astype(jnp.bfloat16),
        "image_gain": jnp.clip(1.0 + 0.1 * jax.random.normal(key_list[11], (D,), jnp.float32), 0.5, 1.5).astype(jnp.bfloat16),
        "cross_gain": jnp.clip(1.0 + 0.1 * jax.random.normal(key_list[12], (D,), jnp.float32), 0.5, 1.5).astype(jnp.bfloat16),
        "cross_query": centred(key_list[13], (D, D), D ** -0.5, 0.21875, ((0, 32),)),
        "cross_keyval": centred(key_list[14], (D, 2 * D), D ** -0.5, 0.21875, ((0, 32),)),
        "cross_out": centred(key_list[15], (D, D), (D // 16) ** -0.5, 0.875, ((0, 32),)),
        "cross_up": centred(key_list[16], (D, FF), D ** -0.5, 0.21875, ((0, 32),)),
        "cross_down": centred(key_list[17], (FF, D), FF ** -0.5, 0.109375, ((0, 32),)),
    }


EPSILON = 1e-06
NEGATIVE = -1000000000.0
HIGHEST = lax.Precision.HIGHEST

@jax.custom_vjp
def low(v):
    return lax.optimization_barrier(v.astype(jnp.bfloat16)).astype(jnp.float32)

@jax.custom_vjp
def low_back(v):
    return v

def low_keep(v):
    return (low(v), None)

def low_pass(kept, grad):
    return (grad,)

def back_keep(v):
    return (v, None)

def back_low(kept, grad):
    return (low(grad),)
low.defvjp(low_keep, low_pass)
low_back.defvjp(back_keep, back_low)

def layer_norm(value_matrix, norm_gain):
    center = value_matrix - lax.optimization_barrier(jnp.mean(value_matrix, axis=-1, keepdims=True))
    spread = lax.optimization_barrier(jnp.mean(center * center, axis=-1, keepdims=True))
    return center * lax.rsqrt(spread + EPSILON) * norm_gain

def matmul(left_side, right_side):
    return jnp.dot(left_side, right_side, precision=HIGHEST)

def positions(counts, lengths, row_count):
    row_index = jnp.arange(row_count, dtype=jnp.int32)
    bounds = jnp.cumsum(counts).astype(jnp.int32)
    image_of = lax.optimization_barrier(jnp.sum((row_index[:, None] >= bounds[None, :]).astype(jnp.int32), axis=1)).astype(jnp.int32)
    caption_of = row_index // CAP_LEN
    in_place = row_index - caption_of * CAP_LEN
    caption_slots = jnp.arange(lengths.shape[0], dtype=jnp.int32)
    length_rows = lax.optimization_barrier(jnp.sum(jnp.where(caption_of[:, None] == caption_slots[None, :], lengths[None, :], 0), axis=1)).astype(jnp.int32)
    valid_rows = in_place < length_rows
    encoder_mask = image_of[:, None] == image_of[None, :]
    text_mask = (caption_of[:, None] == caption_of[None, :]) & (in_place[None, :] <= in_place[:, None]) & valid_rows[None, :]
    cross_mask = caption_of[:, None] == image_of[None, :]
    return (encoder_mask, text_mask, cross_mask, valid_rows)

def attention(query_rows, key_rows, value_rows, allowed):
    row_count = query_rows.shape[0]
    query_heads = query_rows.reshape(row_count, -1, HD)
    key_heads = key_rows.reshape(key_rows.shape[0], -1, HD)
    value_heads = value_rows.reshape(value_rows.shape[0], -1, HD)
    scores = low_back(jnp.einsum('qhd,khd->hqk', query_heads, key_heads, precision=HIGHEST) * HD ** (-0.5))
    scores = jnp.where(allowed[None], scores, NEGATIVE)
    attention_weight = jax.nn.softmax(scores, axis=-1)
    mixture = jnp.einsum('hqk,khd->qhd', low(attention_weight), value_heads, precision=HIGHEST)
    return low_back(low(mixture.reshape(row_count, -1)))

def feed_forward(stream, norm_gain, up_weight, down_weight):
    hidden_in = low(layer_norm(stream, norm_gain))
    up_value = low_back(matmul(hidden_in, up_weight))
    return low_back(matmul(low(jax.nn.gelu(up_value)), down_weight))

def self_layer(stream, attention_weight, allowed):
    attn_gain, qkv_weight, attn_out, mlp_gain, mlp_up, mlp_down = attention_weight
    joined = low_back(low(matmul(low(layer_norm(stream, attn_gain)), qkv_weight)))
    query_rows, key_rows, value_rows = jnp.split(joined, 3, axis=1)
    attn_branch = low_back(matmul(attention(query_rows, key_rows, value_rows, allowed), attn_out))
    middle = stream + attn_branch
    mlp_branch = feed_forward(middle, mlp_gain, mlp_up, mlp_down)
    return (middle + mlp_branch, attn_branch, mlp_branch)

def cross_layer(stream, image_rows, attention_weight, allowed):
    query_gain, image_gain, cross_gain, cross_query, cross_keyval, cross_out, cross_up, cross_down = attention_weight
    query_rows = low_back(low(matmul(low(layer_norm(stream, query_gain)), cross_query)))
    keyval = low_back(low(matmul(low(layer_norm(image_rows, image_gain)), cross_keyval)))
    key_rows, value_rows = jnp.split(keyval, 2, axis=1)
    attn_branch = low_back(matmul(attention(query_rows, key_rows, value_rows, allowed), cross_out))
    middle = stream + attn_branch
    mlp_branch = feed_forward(middle, cross_gain, cross_up, cross_down)
    return (middle + mlp_branch, attn_branch, mlp_branch)

def squares(value_matrix, row_weight):
    return jnp.sum(row_weight[:, None] * value_matrix * value_matrix)

def reference(tokens, cotangent, kept_counts, caption_lengths, attn_gain, qkv_weight, attn_out, mlp_gain, mlp_up, mlp_down, query_gain, image_gain, cross_gain, cross_query, cross_keyval, cross_out, cross_up, cross_down):
    params = tuple((member.astype(jnp.float32) for member in (attn_gain, qkv_weight, attn_out, mlp_gain, mlp_up, mlp_down, query_gain, image_gain, cross_gain, cross_query, cross_keyval, cross_out, cross_up, cross_down)))
    length_blocks = caption_lengths.reshape(N_DP, CAPS_DEV)

    def forward(stream_all, attention_weight):
        encoder_weights = tuple((member[0] for member in attention_weight[:6]))
        text_weights = tuple((member[1] for member in attention_weight[:6]))
        cross_weights = attention_weight[6:]

        def one_block(block_data):
            encoder_in, text_in, counts, lengths = block_data
            encoder_mask, text_mask, cross_mask, valid_rows = positions(counts, lengths, ROWS)
            encoder_y, encoder_attn, encoder_mlp = self_layer(encoder_in, encoder_weights, encoder_mask)
            image_rows = low(encoder_y)
            text_y, text_attn, text_mlp = self_layer(text_in, text_weights, text_mask)
            final_y, cross_attn, cross_mlp = cross_layer(text_y, image_rows, cross_weights, cross_mask)
            row_weight = valid_rows.astype(jnp.float32)
            all_rows = jnp.ones_like(row_weight)
            row_sums = jnp.stack([squares(encoder_in, all_rows), squares(encoder_attn, all_rows), squares(encoder_mlp, all_rows), squares(encoder_y, all_rows), squares(text_in, row_weight), squares(text_attn, row_weight), squares(text_mlp, row_weight), squares(cross_attn, row_weight), squares(cross_mlp, row_weight), squares(final_y, row_weight)])
            return (image_rows, low(final_y), row_sums)
        blocks = (stream_all[0].reshape(N_DP, ROWS, D), stream_all[1].reshape(N_DP, ROWS, D), kept_counts, length_blocks)
        image_rows, final_rows, row_sums = lax.map(jax.checkpoint(one_block), blocks)
        stacked = jnp.stack([image_rows.reshape(ROWS_ALL, D), final_rows.reshape(ROWS_ALL, D)])
        return (stacked, lax.optimization_barrier(jnp.sum(row_sums, axis=0)))
    (outputs, row_sums), puller = jax.vjp(forward, tokens.astype(jnp.float32), params)
    grad_stream, gradients = puller((cotangent.astype(jnp.float32), jnp.zeros_like(row_sums)))
    counted = jnp.sum(caption_lengths).astype(jnp.float32)
    divisor = jnp.concatenate([jnp.full((4,), ROWS_ALL, jnp.float32), jnp.full((6,), 1.0, jnp.float32) * counted]) * D
    rms_values = jnp.sqrt(row_sums / divisor)
    return (outputs.astype(jnp.bfloat16), grad_stream, gradients[0], gradients[1], gradients[2], gradients[3], gradients[4], gradients[5], gradients[6], gradients[7], gradients[8], gradients[9], gradients[10], gradients[11], gradients[12], gradients[13], rms_values)
```

```python
import functools

import jax
import jax.numpy as jnp
from jax import lax
from jax.experimental import pallas as pl
from jax.experimental.pallas import tpu as pltpu
from jax.sharding import PartitionSpec as P

HD = 64
CAP_LEN = 64
EPSILON = 1e-06
NEGATIVE = -1000000000.0

MESH_ID = pl.DeviceIdType.MESH
ANY = pl.BlockSpec(memory_space=pl.ANY)
VMEM = pl.BlockSpec(memory_space=pltpu.VMEM)


class Net:
    def __init__(self, lines):
        self.lines = lines
        self.tower = lax.axis_index("tower")
        self.dp = lax.axis_index("dp")
        self.core = self.dp % 2
        self.y = (self.dp // 2) % 2
        self.z = self.dp // 4
        self.chip = self.dp // 2
        self.text = self.tower == 1
        self.image = self.tower == 0
        self.low = self.z > 0
        self.high = self.z < lines - 1
        self.sends = []

    def target(self, way):
        if way == "core":
            return (self.tower, self.dp + 1 - 2 * self.core)
        if way == "y":
            return (self.tower, self.dp + 2 - 4 * self.y)
        if way == "x":
            return (1 - self.tower, self.dp)
        if way == "up":
            return (self.tower, jnp.minimum(self.dp + 4, 4 * self.lines - 1))
        return (self.tower, jnp.maximum(self.dp - 4, 0))

    def beyond(self, k):
        return (self.tower, 4 * lax.rem(self.z + k, self.lines) + self.dp % 4)

    def barrier(self):
        sem = pltpu.get_barrier_semaphore()
        partners = [self.target(way) for way in ("core", "y", "x")]
        partners += [self.beyond(k) for k in range(1, self.lines)]
        for partner in partners:
            pl.semaphore_signal(sem, inc=1, device_id=partner, device_id_type=MESH_ID)
        pl.semaphore_wait(sem, len(partners))

    def copy(self, way, src, dst, send_sem, recv_sem):
        return pltpu.make_async_remote_copy(
            src_ref=src,
            dst_ref=dst,
            send_sem=send_sem,
            recv_sem=recv_sem,
            device_id=self.target(way),
            device_id_type=MESH_ID,
        )

    def send(self, way, src, dst, send_sem, recv_sem, there=None):
        copy = self.copy(way, src, dst, send_sem, recv_sem)
        when(there, copy.start)
        self.sends.append((copy, there))

    def arrive(self, src, send_sem, recv_sem, there=None):
        copy = self.copy("core", src, src, send_sem, recv_sem)
        when(there, copy.wait_recv)

    def finish(self):
        for copy, there in self.sends:
            when(there, copy.wait_send)
        self.sends = []


def when(there, act):
    if there is None:
        act()
    else:
        pl.when(there)(act)


def both(*conditions):
    kept = [c for c in conditions if c is not None]
    if not kept:
        return None
    result = kept[0]
    for c in kept[1:]:
        result = jnp.logical_and(result, c)
    return result


class Gather:
    def __init__(self, net, own, place, crossing, send_sem, recv_sem, local_sem, everywhere=False):
        self.net, self.own, self.place, self.crossing = net, own, place, crossing
        self.send_sem, self.recv_sem, self.local_sem = send_sem, recv_sem, local_sem
        lines = net.lines
        self.at_z, self.at_y, self.at_x, self.at_core = 0, 2 * lines, 3 * lines, 5 * lines
        self.to_x = net.image if crossing else None
        self.to_core = net.text if crossing and not everywhere else None

    @staticmethod
    def sems(lines):
        return 9 * lines

    def piece(self, chip, tower=None, core=None):
        net = self.net
        return self.place(
            net.tower if tower is None else tower, chip, net.core if core is None else core
        )

    def pass_on(self, chip, src, there=None, tower=None):
        net = self.net
        dst = self.piece(chip, tower)
        plane = net.tower if tower is None else tower
        if self.crossing and tower is None:
            s = self.at_x + chip
            net.send("x", src, dst, self.send_sem.at[s], self.recv_sem.at[s], both(there, net.image))
        s = self.at_core + plane * 2 * net.lines + chip
        net.send("core", src, dst, self.send_sem.at[s], self.recv_sem.at[s], both(there, self.to_core))

    def start(self):
        net = self.net
        dst = self.piece(net.chip)
        self.local = pltpu.make_async_copy(self.own, dst, self.local_sem)
        self.local.start()
        for way, there, slot in (("up", net.high, 1), ("down", net.low, net.lines + 1)):
            s = self.at_z + slot
            net.send(way, self.own, dst, self.send_sem.at[s], self.recv_sem.at[s], there)
        s = self.at_y + net.z
        net.send("y", self.own, dst, self.send_sem.at[s], self.recv_sem.at[s])
        self.pass_on(net.chip, self.own)

    def hop(self, k):
        net = self.net
        for way, there, further, sign, base in (
            ("up", net.z >= k, net.high, -1, 0),
            ("down", net.z + k < net.lines, net.low, 1, net.lines),
        ):
            z = jnp.clip(net.z + sign * k, 0, net.lines - 1)
            chip = 2 * z + net.y
            src = self.piece(chip)
            s = self.at_z + base + k
            net.arrive(src, self.send_sem.at[s], self.recv_sem.at[s], there)
            if k + 1 < net.lines:
                s = s + 1
                net.send(way, src, src, self.send_sem.at[s], self.recv_sem.at[s], both(there, further))
            s = self.at_y + z
            net.send("y", src, src, self.send_sem.at[s], self.recv_sem.at[s], there)
            self.pass_on(chip, src, there)

    def beside(self, k):
        net = self.net
        ways = ((None, 0),) if k == 0 else ((net.z >= k, -k), (net.z + k < net.lines, k))
        for there, offset in ways:
            z = jnp.clip(net.z + offset, 0, net.lines - 1)
            chip = 2 * z + 1 - net.y
            src = self.piece(chip)
            s = self.at_y + z
            net.arrive(src, self.send_sem.at[s], self.recv_sem.at[s], there)
            self.pass_on(chip, src, there)

    def from_image(self, k):
        if not self.crossing:
            return
        net = self.net
        ways = ((None, 0),) if k == 0 else ((net.z >= k, -k), (net.z + k < net.lines, k))
        for there, offset in ways:
            z = jnp.clip(net.z + offset, 0, net.lines - 1)
            for y in (net.y, 1 - net.y):
                chip = 2 * z + y
                src = self.piece(chip, 0)
                s = self.at_x + chip
                net.arrive(src, self.send_sem.at[s], self.recv_sem.at[s], both(there, net.text))
                self.pass_on(chip, src, both(there, net.text), 0)

    def done(self):
        net = self.net
        self.local.wait()

        def all_of(tower, base):
            def one(chip, carry):
                s = self.at_core + base + chip
                src = self.piece(chip, tower, 1 - net.core)
                net.arrive(src, self.send_sem.at[s], self.recv_sem.at[s])
                return carry

            def run():
                lax.fori_loop(0, 2 * net.lines, one, 0)

            return run

        when(self.to_core, all_of(net.tower, net.tower * 2 * net.lines))
        if self.crossing:
            when(net.text, all_of(0, 0))


def gather_kernel(
    lines, wide, half, own_a, own_d, pack, own_cd, own_g, full_a, full_d, full_ca, full_cd, full_g,
    swap, block, send_sem, recv_sem, local_sem, swap_sem,
):
    net = Net(lines)
    net.barrier()
    rows, depth = own_a.shape[0], own_d.shape[0]
    few, part = pack.shape[1], own_cd.shape[0]
    swapped = net.copy("core", pack.at[1 - net.core], swap, swap_sem.at[0], swap_sem.at[1])
    swapped.start()

    def columns(first, last):
        return lambda tower, chip, core: full_a.at[
            pl.ds(pl.multiple_of((2 * chip + core) * rows, rows), rows), first:last
        ]

    def plan(index, own, place, crossing, everywhere=False):
        return Gather(
            net, own, place, crossing, send_sem.at[index], recv_sem.at[index], local_sem.at[index], everywhere
        )

    jobs = [
        plan(0, own_g, lambda tower, chip, core: full_g.at[tower, 2 * chip + core], True, True),
        plan(1, own_a.at[:, 0:wide], columns(0, wide), False),
        plan(2, own_a.at[:, wide:], columns(wide, own_a.shape[1]), False),
        plan(
            3,
            own_d,
            lambda tower, chip, core: full_d.at[
                pl.ds(pl.multiple_of((2 * chip + core) * depth, depth), depth), :
            ],
            False,
        ),
        plan(
            4,
            block,
            lambda tower, chip, core: full_ca.at[
                core, pl.ds(pl.multiple_of((tower * 2 * lines + chip) * 2 * few, 2 * few), 2 * few), :
            ],
            True,
        ),
        plan(
            5,
            own_cd,
            lambda tower, chip, core: full_cd.at[
                pl.ds(
                    pl.multiple_of((tower * 4 * lines + 2 * chip + core) * part, part), part
                ),
                :,
            ],
            True,
        ),
    ]
    for job in jobs[:4]:
        job.start()
    swapped.wait()
    first = net.core == 0
    mine = pack[net.core]
    theirs = swap[...]
    block[0:few] = jnp.where(first, mine, theirs).astype(jnp.bfloat16)
    block[few:] = jnp.where(first, theirs, mine).astype(jnp.bfloat16)
    for job in jobs[4:]:
        job.start()
    for job in jobs:
        job.beside(0)
        job.from_image(0)
    for k in range(1, lines):
        for job in jobs:
            job.hop(k)
        for job in jobs:
            job.beside(k)
            job.from_image(k)
    for job in jobs:
        job.done()
    net.finish()


def gather(lines, wide, own_a, own_d, pack, own_cd, own_g):
    count = 4 * lines
    half, few, width = pack.shape
    jobs = 6
    return pl.pallas_call(
        functools.partial(gather_kernel, lines, wide, width),
        out_shape=(
            jax.ShapeDtypeStruct((count * own_a.shape[0], own_a.shape[1]), jnp.bfloat16),
            jax.ShapeDtypeStruct((count * own_d.shape[0], own_d.shape[1]), jnp.bfloat16),
            jax.ShapeDtypeStruct((2, 2 * count * few, width), jnp.bfloat16),
            jax.ShapeDtypeStruct((2 * count * own_cd.shape[0], own_cd.shape[1]), jnp.bfloat16),
            jax.ShapeDtypeStruct((2, count) + own_g.shape, jnp.float32),
        ),
        in_specs=[ANY, ANY, VMEM, ANY, ANY],
        out_specs=[ANY] * 5,
        scratch_shapes=[
            pltpu.VMEM((few, width), jnp.float32),
            pltpu.VMEM((2 * few, width), jnp.bfloat16),
            pltpu.SemaphoreType.DMA((jobs, Gather.sems(lines))),
            pltpu.SemaphoreType.DMA((jobs, Gather.sems(lines))),
            pltpu.SemaphoreType.DMA((jobs,)),
            pltpu.SemaphoreType.DMA((2,)),
        ],
        compiler_params=pltpu.CompilerParams(
            collective_id=0, has_side_effects=True, vmem_limit_bytes=32 << 20
        ),
    )(own_a, own_d, pack, own_cd, own_g)


class Scatter:
    def __init__(self, net, crossing, grad, own, beside, near, far, sems):
        self.net, self.crossing, self.grad = net, crossing, grad
        self.own, self.rcv, self.near, self.far = own, beside, near, far
        self.send_sem, self.recv_sem, self.local_sem = sems

    def add(self, pairs, out):
        shape = out.shape
        step = 16

        def one(i, carry):
            rows = pl.ds(pl.multiple_of(i * step, step), step)
            total = pairs[0][rows, :].astype(jnp.float32)
            for other in pairs[1:]:
                total = total + other[rows, :].astype(jnp.float32)
            out[rows, :] = total.astype(out.dtype)
            return carry

        lax.fori_loop(0, shape[0] // step, one, 0)

    @staticmethod
    def sems(lines):
        return 1 + 5 * lines

    def plane(self):
        return self.own.at[self.net.tower] if self.crossing else self.own

    def start(self):
        net = self.net
        there = net.text if self.crossing else None
        self.load = pltpu.make_async_copy(self.grad(net.core), self.own, self.local_sem)
        when(there, self.load.start)
        net.send(
            "core", self.grad(1 - net.core), self.rcv, self.send_sem.at[0], self.recv_sem.at[0], there
        )

    def chips(self, k):
        net = self.net
        if k == 0:
            return ((None, net.z),)
        return (
            (net.z + k < net.lines, jnp.minimum(net.z + k, net.lines - 1)),
            (net.z >= k, jnp.maximum(net.z - k, 0)),
        )

    def cores(self):
        net = self.net
        lines = net.lines
        there = net.text if self.crossing else None

        def arrived():
            self.load.wait()

        when(there, arrived)
        net.arrive(self.rcv, self.send_sem.at[0], self.recv_sem.at[0], there)

        def sum_of(own, rcv):
            def one(i, carry):
                self.add([own.at[i], rcv.at[i]], own.at[i])
                return carry

            lax.fori_loop(0, 2 * lines, one, 0)

        if self.crossing:

            def text():
                sum_of(self.own.at[0], self.rcv.at[0])

            when(there, text)
            for k in range(lines - 1, -1, -1):
                for there_k, z in self.chips(k):
                    for y in (1 - net.y, net.y):
                        chip = 2 * z + y
                        s = 1 + chip
                        net.send(
                            "x",
                            self.own.at[0, chip],
                            self.own.at[0, chip],
                            self.send_sem.at[s],
                            self.recv_sem.at[s],
                            both(there_k, net.text),
                        )

            def text_too():
                sum_of(self.own.at[1], self.rcv.at[1])

            when(there, text_too)
        else:
            sum_of(self.own, self.rcv)

    def across(self):
        net = self.net
        lines = net.lines
        for k in range(lines - 1, -1, -1):
            for there, z in self.chips(k):
                chip = 2 * z + 1 - net.y
                if self.crossing:
                    s = 1 + chip
                    net.arrive(
                        self.own.at[0, chip],
                        self.send_sem.at[s],
                        self.recv_sem.at[s],
                        both(there, net.image),
                    )
                s = 1 + 2 * lines + z
                net.send(
                    "y", self.plane().at[chip], self.near.at[z], self.send_sem.at[s], self.recv_sem.at[s], there
                )

    def along(self):
        net = self.net
        lines = net.lines
        own = self.plane()
        for k in range(lines - 1, 0, -1):
            for way, (there, z) in zip(("up", "down"), self.chips(k)):
                chip = 2 * z + net.y
                up = way == "up"
                base = 1 + 3 * lines if up else 1 + 4 * lines
                if self.crossing:
                    s = 1 + chip
                    net.arrive(
                        self.own.at[0, chip],
                        self.send_sem.at[s],
                        self.recv_sem.at[s],
                        both(there, net.image),
                    )
                s = 1 + 2 * lines + z
                net.arrive(self.near.at[z], self.send_sem.at[s], self.recv_sem.at[s], there)
                more = net.low if up else net.high
                s = base + z
                net.arrive(self.far.at[z], self.send_sem.at[s], self.recv_sem.at[s], both(there, more))

                def with_far():
                    self.add([own.at[chip], self.near.at[z], self.far.at[z]], own.at[chip])

                def without():
                    self.add([own.at[chip], self.near.at[z]], own.at[chip])

                when(both(there, more), with_far)
                when(both(there, jnp.logical_not(more)), without)
                slot = z
                if up:
                    target = self.far.at[slot]
                else:
                    last = jnp.where(z == net.z - 1, lines, z)
                    target = self.far.at[last]
                net.send(way, own.at[chip], target, self.send_sem.at[s], self.recv_sem.at[s], there)

    def total(self, out):
        net = self.net
        lines = net.lines
        own = self.plane()
        chip = net.chip
        if self.crossing:
            s = 1 + chip
            net.arrive(
                self.own.at[0, chip], self.send_sem.at[s], self.recv_sem.at[s], net.image
            )
        s = 1 + 2 * lines + net.z
        net.arrive(self.near.at[net.z], self.send_sem.at[s], self.recv_sem.at[s])
        s = 1 + 3 * lines + net.z
        net.arrive(self.far.at[net.z], self.send_sem.at[s], self.recv_sem.at[s], net.low)
        s = 1 + 4 * lines + net.z
        net.arrive(self.far.at[lines], self.send_sem.at[s], self.recv_sem.at[s], net.high)
        here = [own.at[chip], self.near.at[net.z]]
        from_low, from_high = self.far.at[net.z], self.far.at[lines]
        when(both(net.low, net.high), lambda: self.add(here + [from_low, from_high], out))
        when(jnp.logical_not(net.low), lambda: self.add(here + [from_high], out))
        when(jnp.logical_not(net.high), lambda: self.add(here + [from_low], out))


class Small:
    def __init__(self, net, mine, arrived, sums, wide, send_sem, recv_sem):
        self.net, self.mine, self.arrived, self.sums, self.wide = net, mine, arrived, sums, wide
        self.send_sem, self.recv_sem = send_sem, recv_sem

    def exchange(self, step):
        src = self.mine if step == 0 else self.sums.at[step - 1]
        self.net.send(
            ("core", "y", "x")[step],
            src,
            self.arrived.at[step],
            self.send_sem.at[step],
            self.recv_sem.at[step],
        )

    def collect(self, step):
        self.net.arrive(self.arrived.at[step], self.send_sem.at[step], self.recv_sem.at[step])
        src = self.mine if step == 0 else self.sums.at[step - 1]
        self.sums[step] = src[...] + self.arrived[step]

    def spread(self):
        net = self.net
        for k in range(1, net.lines):
            s = 2 + k
            copy = pltpu.make_async_remote_copy(
                src_ref=self.sums.at[2],
                dst_ref=self.wide.at[k - 1],
                send_sem=self.send_sem.at[s],
                recv_sem=self.recv_sem.at[s],
                device_id=net.beyond(k),
                device_id_type=MESH_ID,
            )
            copy.start()
            net.sends.append((copy, None))

    def total(self, out):
        total = self.sums[2]
        for k in range(1, self.net.lines):
            s = 2 + k
            self.net.arrive(self.wide.at[k - 1], self.send_sem.at[s], self.recv_sem.at[s])
            total = total + self.wide[k - 1]
        out[...] = total


def scatter_kernel(
    lines, wide, cuts, g_a, g_d, g_ca, g_cd, vec,
    o_qkv, o_out, o_up, o_d, o_cq, o_ckv, o_co, o_cu, o_cd, o_vec,
    *scratch,
):
    net = Net(lines)
    net.barrier()
    buffers = [scratch[4 * i : 4 * i + 4] for i in range(5)]
    send_sem, recv_sem, local_sem, fin, swap, swap_sem, arrived, sums, spread, s_send, s_recv = scratch[20:]
    small = Small(net, vec, arrived, sums, spread, s_send, s_recv)
    width = g_ca.shape[-1]
    few = g_ca.shape[-2]

    def job(index, crossing, grad):
        return Scatter(
            net,
            crossing,
            grad,
            *buffers[index],
            (send_sem.at[index], recv_sem.at[index], local_sem.at[index]),
        )

    s_d = job(0, False, lambda core: g_d.at[:, core])
    c_d = job(1, True, lambda core: g_cd.at[:, :, core])
    s_up = job(2, False, lambda core: g_a.at[:, core, :, pl.ds(wide, g_a.shape[-1] - wide)])
    c_a = job(3, True, lambda core: g_ca.at[core])
    s_qkv = job(4, False, lambda core: g_a.at[:, core, :, pl.ds(0, wide)])

    small.exchange(0)
    s_d.start()
    c_d.start()
    s_d.cores()
    s_d.across()
    s_up.start()
    small.collect(0)
    small.exchange(1)
    c_d.cores()
    c_a.start()
    s_d.along()
    s_up.cores()
    s_qkv.start()
    c_d.across()
    s_up.across()
    small.collect(1)
    small.exchange(2)
    c_a.cores()
    c_d.along()
    s_qkv.cores()
    s_d.total(o_d)
    c_a.across()
    s_qkv.across()
    small.collect(2)
    small.spread()
    s_up.along()
    c_d.total(o_cd)
    c_a.along()
    s_up.total(fin.at[0:few, 0 : g_a.shape[-1] - wide])
    o_out[...] = fin[0:few, 0 : o_out.shape[1]]
    o_up[...] = fin[0:few, o_out.shape[1] : g_a.shape[-1] - wide]
    s_qkv.along()
    c_a.total(fin.at[0:few, 0:width])
    share = few // 2
    other = 1 - net.core
    swapped = net.copy(
        "core",
        fin.at[pl.ds(pl.multiple_of(other * share, share), share), 0:width],
        swap,
        swap_sem.at[0],
        swap_sem.at[1],
    )
    swapped.start()
    s_qkv.total(o_qkv)
    small.total(o_vec)
    swapped.wait()
    mine = fin[pl.ds(pl.multiple_of(net.core * share, share), share), 0:width]
    theirs = swap[...]
    first = net.core == 0
    left = jnp.where(first, mine, theirs)
    right = jnp.where(first, theirs, mine)
    at = 0
    for out, n in zip((o_cq, o_ckv, o_co, o_cu), cuts):
        out[:, 0:n] = left[:, at : at + n]
        out[:, n:] = right[:, at : at + n]
        at += n
    net.finish()


def scatter(lines, g_a, g_d, g_ca, g_cd, vec, parts, cuts):
    chips = 2 * lines
    wide = parts[0]
    rows = g_a.shape[2]
    few = g_ca.shape[3]
    bf16, f32 = jnp.bfloat16, jnp.float32

    def buffers(crossing, rows, n):
        whole = ((2, chips, rows, n) if crossing else (chips, rows, n))
        return [
            pltpu.VMEM(whole, bf16),
            pltpu.VMEM(whole, bf16),
            pltpu.VMEM((lines, rows, n), bf16),
            pltpu.VMEM((lines + 1, rows, n), bf16),
        ]

    scratch = (
        buffers(False, g_d.shape[2], g_d.shape[3])
        + buffers(True, g_cd.shape[3], g_cd.shape[4])
        + buffers(False, rows, g_a.shape[3] - wide)
        + buffers(True, few, g_ca.shape[4])
        + buffers(False, rows, wide)
        + [
            pltpu.SemaphoreType.DMA((5, Scatter.sems(lines))),
            pltpu.SemaphoreType.DMA((5, Scatter.sems(lines))),
            pltpu.SemaphoreType.DMA((5,)),
            pltpu.VMEM((rows, max(g_a.shape[3] - wide, g_ca.shape[4])), f32),
            pltpu.VMEM((few // 2, g_ca.shape[4]), f32),
            pltpu.SemaphoreType.DMA((2,)),
            pltpu.VMEM((3,) + vec.shape, f32),
            pltpu.VMEM((3,) + vec.shape, f32),
            pltpu.VMEM((lines - 1,) + vec.shape, f32),
            pltpu.SemaphoreType.DMA((2 + lines,)),
            pltpu.SemaphoreType.DMA((2 + lines,)),
        ]
    )
    share = few // 2
    outs = [
        (rows, parts[0]),
        (rows, parts[1]),
        (rows, parts[2]),
        (g_d.shape[2], g_d.shape[3]),
        (share, 2 * cuts[0]),
        (share, 2 * cuts[1]),
        (share, 2 * cuts[2]),
        (share, 2 * cuts[3]),
        (g_cd.shape[3], g_cd.shape[4]),
        vec.shape,
    ]
    return pl.pallas_call(
        functools.partial(scatter_kernel, lines, wide, cuts),
        out_shape=tuple(jax.ShapeDtypeStruct(s, f32) for s in outs),
        in_specs=[ANY, ANY, ANY, ANY, VMEM],
        out_specs=[VMEM] * len(outs),
        scratch_shapes=scratch,
        compiler_params=pltpu.CompilerParams(
            collective_id=1, has_side_effects=True, vmem_limit_bytes=62 << 20
        ),
    )(g_a, g_d, g_ca, g_cd, vec)


def plain_gather(own_a, own_d, pack, own_cd, own_g):
    axes = ("tower", "dp")
    tiles = lax.all_gather(own_g, axes, axis=0)
    return (
        lax.all_gather(own_a, "dp", axis=0, tiled=True),
        lax.all_gather(own_d, "dp", axis=0, tiled=True),
        lax.all_gather(pack.astype(jnp.bfloat16), axes, axis=1, tiled=True),
        lax.all_gather(own_cd, axes, axis=0, tiled=True),
        tiles.reshape((2, -1) + own_g.shape),
    )


def plain_scatter(g_a, g_d, g_ca, g_cd, vec, parts, cuts):
    axes = ("tower", "dp")

    def added(grad, over, axis):
        return lax.psum_scatter(
            grad.astype(jnp.float32), over, scatter_dimension=axis, tiled=True
        )

    a = added(g_a.reshape(-1, g_a.shape[-1]), "dp", 0)
    d = added(g_d.reshape(-1, g_d.shape[-1]), "dp", 0)
    ca = added(g_ca.reshape(2, -1, g_ca.shape[-1]), axes, 1)
    cd = added(g_cd.reshape(-1, g_cd.shape[-1]), axes, 0)
    at = [sum(cuts[:i]) for i in range(len(cuts) + 1)]
    cross = [
        jnp.concatenate([ca[0][:, i:j], ca[1][:, i:j]], axis=1) for i, j in zip(at[:-1], at[1:])
    ]
    first, second = parts[0], parts[0] + parts[1]
    self_parts = [a[:, :first], a[:, first:second], a[:, second:]]
    return (*self_parts, d, *cross, cd, lax.psum(vec, axes))


def layer_norm(value_matrix, norm_gain):
    center = value_matrix - jnp.mean(value_matrix, axis=-1, keepdims=True)
    spread = jnp.mean(center * center, axis=-1, keepdims=True)
    return center * lax.rsqrt(spread + EPSILON) * norm_gain


def norm_back(value_matrix, norm_gain, grad_out):
    result, puller = jax.vjp(layer_norm, value_matrix, norm_gain)
    return puller(grad_out)


def dot(a, b):
    return jnp.dot(a, b, preferred_element_type=jnp.float32)


def dot_tn(a, b):
    return jnp.einsum("rd,re->de", a, b, preferred_element_type=jnp.float32)


def dot_nt(a, b):
    return jnp.einsum("re,de->rd", a, b, preferred_element_type=jnp.float32)


def low(value_matrix):
    return value_matrix.astype(jnp.bfloat16)


def masks(counts, lengths, row_count, decoder):
    row_index = jnp.arange(row_count, dtype=jnp.int32)
    bounds = jnp.cumsum(counts)
    image_of = jnp.sum((row_index[:, None] >= bounds[None, :]).astype(jnp.int32), axis=1)
    caption_of = row_index // CAP_LEN
    in_place = row_index - caption_of * CAP_LEN
    caption_slots = jnp.arange(lengths.shape[0], dtype=jnp.int32)
    length_rows = jnp.sum(
        jnp.where(caption_of[:, None] == caption_slots[None, :], lengths[None, :], 0), axis=1
    )
    valid_rows = in_place < length_rows
    image_mask = image_of[:, None] == image_of[None, :]
    text_mask = (
        (caption_of[:, None] == caption_of[None, :])
        & (in_place[None, :] <= in_place[:, None])
        & valid_rows[None, :]
    )
    cross_mask = caption_of[:, None] == image_of[None, :]
    return jnp.where(decoder, text_mask, image_mask), cross_mask, valid_rows


def heads(value_matrix):
    return value_matrix.reshape(value_matrix.shape[0], -1, HD)


def attend(query, key, value, allowed):
    scores = jnp.einsum(
        "qhd,khd->hqk", heads(query), heads(key), preferred_element_type=jnp.float32
    ) * HD ** (-0.5)
    weight = jax.nn.softmax(jnp.where(allowed[None], scores, NEGATIVE), axis=-1)
    mixed = jnp.einsum("hqk,khd->qhd", low(weight), heads(value), preferred_element_type=jnp.float32)
    return low(mixed.reshape(query.shape)), weight


def attend_back(query, key, value, weight, grad_mixed):
    grad_mixed = heads(grad_mixed)
    grad_value = jnp.einsum("hqk,qhd->khd", low(weight), grad_mixed, preferred_element_type=jnp.float32)
    grad_weight = jnp.einsum("qhd,khd->hqk", grad_mixed, heads(value), preferred_element_type=jnp.float32)
    grad_score = low(
        weight * (grad_weight - jnp.sum(grad_weight * weight, axis=-1, keepdims=True))
    )
    grad_query = jnp.einsum(
        "hqk,khd->qhd", grad_score, heads(key), preferred_element_type=jnp.float32
    ) * HD ** (-0.5)
    grad_key = jnp.einsum(
        "hqk,qhd->khd", grad_score, heads(query), preferred_element_type=jnp.float32
    ) * HD ** (-0.5)
    return tuple(low(g.reshape(query.shape)) for g in (grad_query, grad_key, grad_value))


def mlp_forward(stream, gain, up, down):
    hidden = low(layer_norm(stream, gain))
    wide = dot(hidden, up)
    active = low(jax.nn.gelu(wide))
    return dot(active, down), (hidden, wide, active)


def mlp_back(stream, gain, up, down, stored, grad):
    hidden, wide, active = stored
    branch = low(grad)
    grad_down = dot_tn(active, branch)
    result, puller = jax.vjp(jax.nn.gelu, wide)
    grad_wide = low(puller(dot_nt(branch, down))[0])
    grad_up = dot_tn(hidden, grad_wide)
    grad_stream, grad_gain = norm_back(stream, gain, dot_nt(grad_wide, up))
    return grad + grad_stream, grad_gain, grad_up, grad_down


def squares(value_matrix, row_weight):
    return jnp.sum(row_weight[:, None] * value_matrix * value_matrix)


def shards(
    tokens, cotangent, kept_counts, caption_lengths, attn_gain, qkv_weight, attn_out, mlp_gain,
    mlp_up, mlp_down, query_gain, image_gain, cross_gain, cross_query, cross_keyval, cross_out,
    cross_up, cross_down,
):
    f32 = jnp.float32
    dp_count = lax.axis_size("dp")
    lines = dp_count // 4
    tower, dp = lax.axis_index("tower"), lax.axis_index("dp")
    decoder = tower == 1
    row_count, width = tokens.shape[1:]
    rows = attn_gain.shape[1]
    few = query_gain.shape[0]

    def tile_row(value):
        return jnp.pad(value.astype(f32), (0, 128 - value.shape[0]))

    gain_tile = jnp.stack(
        [tile_row(attn_gain[0]), tile_row(mlp_gain[0])]
        + [tile_row(g) for g in (query_gain, image_gain, cross_gain)]
        + [jnp.zeros((128,), f32)] * 3
    )
    cross_shards = (cross_query, cross_keyval, cross_out, cross_up)
    cuts = tuple(w.shape[1] // 2 for w in cross_shards)
    pack = jnp.stack(
        [
            jnp.concatenate([w[:, h * n : (h + 1) * n] for w, n in zip(cross_shards, cuts)], axis=1)
            for h in range(2)
        ]
    ).astype(f32)
    self_parts = (qkv_weight.shape[2], attn_out.shape[2], mlp_up.shape[2])
    own_a = jnp.concatenate([qkv_weight[0], attn_out[0], mlp_up[0]], axis=1)
    fills = dp_count % 4 == 0 and dp_count > 4 and rows % 16 == 0 and few % 8 == 0
    fills = fills and cross_down.shape[0] % 16 == 0
    own = (own_a, mlp_down[0], pack, cross_down, gain_tile)
    full = gather(lines, self_parts[0], *own) if fills else plain_gather(*own)
    full_a, full_d, full_ca, full_cd, full_g = full
    qkv = full_a[:, : self_parts[0]]
    out = full_a[:, self_parts[0] : self_parts[0] + self_parts[1]]
    up = full_a[:, self_parts[0] + self_parts[1] :]
    down = full_d
    plane_gains = lax.dynamic_index_in_dim(full_g, tower, 0, keepdims=False)
    gain_1 = plane_gains[:, 0, :rows].reshape(-1)
    gain_2 = plane_gains[:, 1, :rows].reshape(-1)
    gain_q, gain_i, gain_c = (full_g[:, :, 2 + i, :few].reshape(-1) for i in range(3))

    stream = tokens[0].astype(f32)
    upstream = cotangent[0].astype(f32)
    allowed, cross_allowed, valid_rows = masks(kept_counts[0], caption_lengths, row_count, decoder)
    row_weight = jnp.where(decoder, valid_rows, True).astype(f32)

    normed = low(layer_norm(stream, gain_1))
    joined = low(dot(normed, qkv))
    query, key, value = jnp.split(joined, 3, axis=1)
    mixed, weight = attend(query, key, value, allowed)
    attn_branch = dot(mixed, out)
    middle = stream + attn_branch
    mlp_branch, mlp_stored = mlp_forward(middle, gain_2, up, down)
    layer_y = middle + mlp_branch
    image_rows = low(layer_y)
    arrived = lax.ppermute(image_rows, "tower", [(0, 1)])

    def run_cross(operands):
        text_y, image_in = operands
        at = [0]
        for n in cuts:
            at.append(at[-1] + n)
        cq, ckv, co, cu = (
            jnp.concatenate([full_ca[0][:, a:b], full_ca[1][:, a:b]], axis=1)
            for a, b in zip(at[:-1], at[1:])
        )
        image_in = image_in.astype(f32)
        image_normed = low(layer_norm(image_in, gain_i))
        keyval = low(dot(image_normed, ckv))
        c_key, c_value = jnp.split(keyval, 2, axis=1)
        c_normed = low(layer_norm(text_y, gain_q))
        c_query = low(dot(c_normed, cq))
        c_mixed, c_weight = attend(c_query, c_key, c_value, cross_allowed)
        c_branch = dot(c_mixed, co)
        c_middle = text_y + c_branch
        c_mlp, c_stored = mlp_forward(c_middle, gain_c, cu, full_cd)
        final_rows = c_middle + c_mlp
        grad_middle, grad_gain_c, grad_cu, grad_cd = mlp_back(
            c_middle, gain_c, cu, full_cd, c_stored, upstream
        )
        grad_branch = low(grad_middle)
        grad_co = dot_tn(c_mixed, grad_branch)
        grad_q, grad_k, grad_v = attend_back(
            c_query, c_key, c_value, c_weight, low(dot_nt(grad_branch, co))
        )
        grad_cq = dot_tn(c_normed, grad_q)
        grad_text, grad_gain_q = norm_back(text_y, gain_q, dot_nt(grad_q, cq))
        grad_keyval = jnp.concatenate([grad_k, grad_v], axis=1)
        grad_ckv = dot_tn(image_normed, grad_keyval)
        grad_image, grad_gain_i = norm_back(image_in, gain_i, dot_nt(grad_keyval, ckv))
        cross_sums = jnp.stack(
            [
                squares(c_branch, row_weight),
                squares(c_mlp, row_weight),
                squares(final_rows, row_weight),
            ]
        )
        grads = tuple(low(g) for g in (grad_cq, grad_ckv, grad_co, grad_cu))
        grad_ca = jnp.stack(
            [
                jnp.concatenate([g[:, h * n : (h + 1) * n] for g, n in zip(grads, cuts)], axis=1)
                for h in range(2)
            ]
        )
        return (
            low(final_rows),
            grad_middle + grad_text,
            low(grad_image),
            grad_ca,
            low(grad_cd),
            jnp.concatenate([grad_gain_q, grad_gain_i, grad_gain_c]),
            cross_sums,
        )

    def skip_cross(operands):
        shapes = jax.eval_shape(run_cross, operands)
        return tuple(jnp.zeros(s.shape, s.dtype) for s in shapes)

    final_rows, grad_text, grad_image, grad_ca, grad_cd, grad_cross_gains, cross_sums = lax.cond(
        decoder, run_cross, skip_cross, (layer_y, arrived)
    )
    returned = lax.ppermute(grad_image, "tower", [(1, 0)]).astype(f32)
    grad_top = jnp.where(decoder, grad_text, upstream + returned)

    grad_middle, grad_gain_2, grad_up, grad_down = mlp_back(
        middle, gain_2, up, down, mlp_stored, grad_top
    )
    grad_branch = low(grad_middle)
    grad_out = dot_tn(mixed, grad_branch)
    grad_joined = jnp.concatenate(
        attend_back(query, key, value, weight, low(dot_nt(grad_branch, out))), axis=1
    )
    grad_qkv = dot_tn(normed, grad_joined)
    grad_stream, grad_gain_1 = norm_back(stream, gain_1, dot_nt(grad_joined, qkv))
    grad_stream = grad_middle + grad_stream

    layer_sums = jnp.stack(
        [
            squares(stream, row_weight),
            squares(attn_branch, row_weight),
            squares(mlp_branch, row_weight),
            squares(layer_y, row_weight),
        ]
    )
    encoder_part = jnp.where(decoder, 0.0, layer_sums)
    decoder_part = jnp.where(decoder, jnp.concatenate([layer_sums[:3], cross_sums]), 0.0)
    counted = jnp.where(decoder, jnp.sum(valid_rows.astype(f32)), 0.0)
    line = tile_row(jnp.concatenate([encoder_part, decoder_part, counted[None]]))
    self_gains = jnp.concatenate([grad_gain_1, grad_gain_2])
    zero = jnp.zeros_like(self_gains)
    vec = jnp.concatenate(
        [
            jnp.where(decoder, zero, self_gains),
            jnp.where(decoder, self_gains, zero),
            grad_cross_gains,
            line,
        ]
    ).reshape(-1, 128)
    vec = jnp.pad(vec, ((0, -vec.shape[0] % 8), (0, 0)))
    grad_a = jnp.concatenate([low(grad_qkv), low(grad_out), low(grad_up)], axis=1)
    chips = 2 * lines
    partial_sums = (
        grad_a.reshape(chips, 2, rows, -1),
        low(grad_down).reshape(chips, 2, -1, width),
        grad_ca.reshape(2, 2, chips, 2 * few, -1),
        grad_cd.reshape(2, chips, 2, -1, width),
        vec,
    )
    if fills:
        results = scatter(lines, *partial_sums, self_parts, cuts)
    else:
        results = plain_scatter(*partial_sums, self_parts, cuts)
    o_qkv, o_out, o_up, o_d, o_cq, o_ckv, o_co, o_cu, o_cd, o_vec = results
    flat = o_vec.reshape(-1)
    own_gains = lax.dynamic_slice(flat, (tower * 2 * width,), (2 * width,))
    g_1, g_2 = (lax.dynamic_slice(own_gains, (i * width + dp * rows,), (rows,)) for i in range(2))
    g_q, g_i, g_c = (
        lax.dynamic_slice(
            flat, ((4 + i) * width + (tower * dp_count + dp) * few,), (few,)
        )
        for i in range(3)
    )
    sums = flat[7 * width : 7 * width + 11]
    encoder_count = jnp.full((4,), float(row_count * dp_count), f32)
    divisor = jnp.concatenate([encoder_count, jnp.full((6,), 1.0, f32) * sums[10]]) * width
    rms_values = jnp.sqrt(sums[:10] / divisor)
    layer_out = jnp.where(decoder, final_rows, image_rows)
    return (
        layer_out[None], grad_stream[None], g_1[None], o_qkv[None], o_out[None], g_2[None],
        o_up[None], o_d[None], g_q, g_i, g_c, o_cq, o_ckv, o_co, o_cu, o_cd, rms_values,
    )


def solution(mesh):
    rows = P("tower", "dp", None)
    gain = P("tower", "dp")
    cross_gain = P(("tower", "dp"))
    cross = P(("tower", "dp"), None)
    weights = (gain, rows, rows, gain, rows, rows) + (cross_gain,) * 3 + (cross,) * 5
    return jax.shard_map(
        shards,
        mesh=mesh,
        in_specs=(rows, rows, P("dp", None), P("dp")) + weights,
        out_specs=(rows, rows) + weights + (P(),),
        check_vma=False,
    )
```

```python
import functools

import jax
import jax.numpy as jnp
from jax import lax
from jax.experimental import pallas as pl
from jax.experimental.pallas import tpu as pltpu
from jax.sharding import PartitionSpec as P

HD = 64
CAP_LEN = 64
EPSILON = 1e-06
NEGATIVE = -1000000000.0

MESH_ID = pl.DeviceIdType.MESH
ANY = pl.BlockSpec(memory_space=pl.ANY)
VMEM = pl.BlockSpec(memory_space=pltpu.VMEM)


class Net:
    def __init__(self, lines):
        self.lines = lines
        self.tower = lax.axis_index("tower")
        self.dp = lax.axis_index("dp")
        self.core = self.dp % 2
        self.y = (self.dp // 2) % 2
        self.z = self.dp // 4
        self.chip = self.dp // 2
        self.text = self.tower == 1
        self.image = self.tower == 0
        self.low = self.z > 0
        self.high = self.z < lines - 1
        self.sends = []

    def target(self, way):
        if way == "core":
            return (self.tower, self.dp + 1 - 2 * self.core)
        if way == "y":
            return (self.tower, self.dp + 2 - 4 * self.y)
        if way == "x":
            return (1 - self.tower, self.dp)
        if way == "up":
            return (self.tower, jnp.minimum(self.dp + 4, 4 * self.lines - 1))
        return (self.tower, jnp.maximum(self.dp - 4, 0))

    def beyond(self, k):
        return (self.tower, 4 * lax.rem(self.z + k, self.lines) + self.dp % 4)

    def barrier(self):
        sem = pltpu.get_barrier_semaphore()
        partners = [self.target(way) for way in ("core", "y", "x")]
        partners += [self.beyond(k) for k in range(1, self.lines)]
        for partner in partners:
            pl.semaphore_signal(sem, inc=1, device_id=partner, device_id_type=MESH_ID)
        pl.semaphore_wait(sem, len(partners))

    def copy(self, way, src, dst, send_sem, recv_sem):
        return pltpu.make_async_remote_copy(
            src_ref=src,
            dst_ref=dst,
            send_sem=send_sem,
            recv_sem=recv_sem,
            device_id=self.target(way),
            device_id_type=MESH_ID,
        )

    def send(self, way, src, dst, send_sem, recv_sem, there=None):
        copy = self.copy(way, src, dst, send_sem, recv_sem)
        when(there, copy.start)
        self.sends.append((copy, there))

    def arrive(self, src, send_sem, recv_sem, there=None):
        copy = self.copy("core", src, src, send_sem, recv_sem)
        when(there, copy.wait_recv)

    def finish(self):
        for copy, there in self.sends:
            when(there, copy.wait_send)
        self.sends = []


def when(there, act):
    if there is None:
        act()
    else:
        pl.when(there)(act)


def both(*conditions):
    kept = [c for c in conditions if c is not None]
    if not kept:
        return None
    result = kept[0]
    for c in kept[1:]:
        result = jnp.logical_and(result, c)
    return result


class Gather:
    def __init__(self, net, own, place, crossing, send_sem, recv_sem, local_sem, everywhere=False):
        self.net, self.own, self.place, self.crossing = net, own, place, crossing
        self.send_sem, self.recv_sem, self.local_sem = send_sem, recv_sem, local_sem
        lines = net.lines
        self.at_z, self.at_y, self.at_x, self.at_core = 0, 2 * lines, 3 * lines, 5 * lines
        self.to_x = net.image if crossing else None
        self.to_core = net.text if crossing and not everywhere else None

    @staticmethod
    def sems(lines):
        return 9 * lines

    def piece(self, chip, tower=None, core=None):
        net = self.net
        return self.place(
            net.tower if tower is None else tower, chip, net.core if core is None else core
        )

    def pass_on(self, chip, src, there=None, tower=None):
        net = self.net
        dst = self.piece(chip, tower)
        plane = net.tower if tower is None else tower
        if self.crossing and tower is None:
            s = self.at_x + chip
            net.send("x", src, dst, self.send_sem.at[s], self.recv_sem.at[s], both(there, net.image))
        s = self.at_core + plane * 2 * net.lines + chip
        net.send("core", src, dst, self.send_sem.at[s], self.recv_sem.at[s], both(there, self.to_core))

    def start(self):
        net = self.net
        dst = self.piece(net.chip)
        self.local = pltpu.make_async_copy(self.own, dst, self.local_sem)
        self.local.start()
        for way, there, slot in (("up", net.high, 1), ("down", net.low, net.lines + 1)):
            s = self.at_z + slot
            net.send(way, self.own, dst, self.send_sem.at[s], self.recv_sem.at[s], there)
        s = self.at_y + net.z
        net.send("y", self.own, dst, self.send_sem.at[s], self.recv_sem.at[s])
        self.pass_on(net.chip, self.own)

    def hop(self, k):
        net = self.net
        for way, there, further, sign, base in (
            ("up", net.z >= k, net.high, -1, 0),
            ("down", net.z + k < net.lines, net.low, 1, net.lines),
        ):
            z = jnp.clip(net.z + sign * k, 0, net.lines - 1)
            chip = 2 * z + net.y
            src = self.piece(chip)
            s = self.at_z + base + k
            net.arrive(src, self.send_sem.at[s], self.recv_sem.at[s], there)
            if k + 1 < net.lines:
                s = s + 1
                net.send(way, src, src, self.send_sem.at[s], self.recv_sem.at[s], both(there, further))
            s = self.at_y + z
            net.send("y", src, src, self.send_sem.at[s], self.recv_sem.at[s], there)
            self.pass_on(chip, src, there)

    def beside(self, k):
        net = self.net
        ways = ((None, 0),) if k == 0 else ((net.z >= k, -k), (net.z + k < net.lines, k))
        for there, offset in ways:
            z = jnp.clip(net.z + offset, 0, net.lines - 1)
            chip = 2 * z + 1 - net.y
            src = self.piece(chip)
            s = self.at_y + z
            net.arrive(src, self.send_sem.at[s], self.recv_sem.at[s], there)
            self.pass_on(chip, src, there)

    def from_image(self, k):
        if not self.crossing:
            return
        net = self.net
        ways = ((None, 0),) if k == 0 else ((net.z >= k, -k), (net.z + k < net.lines, k))
        for there, offset in ways:
            z = jnp.clip(net.z + offset, 0, net.lines - 1)
            for y in (net.y, 1 - net.y):
                chip = 2 * z + y
                src = self.piece(chip, 0)
                s = self.at_x + chip
                net.arrive(src, self.send_sem.at[s], self.recv_sem.at[s], both(there, net.text))
                self.pass_on(chip, src, both(there, net.text), 0)

    def done(self):
        net = self.net
        self.local.wait()

        def all_of(tower, base):
            def one(chip, carry):
                s = self.at_core + base + chip
                src = self.piece(chip, tower, 1 - net.core)
                net.arrive(src, self.send_sem.at[s], self.recv_sem.at[s])
                return carry

            def run():
                lax.fori_loop(0, 2 * net.lines, one, 0)

            return run

        when(self.to_core, all_of(net.tower, net.tower * 2 * net.lines))
        if self.crossing:
            when(net.text, all_of(0, 0))


class Small:
    def __init__(self, net, mine, arrived, sums, wide, send_sem, recv_sem):
        self.net, self.mine, self.arrived, self.sums, self.wide = net, mine, arrived, sums, wide
        self.send_sem, self.recv_sem = send_sem, recv_sem

    def exchange(self, step):
        src = self.mine if step == 0 else self.sums.at[step - 1]
        self.net.send(
            ("core", "y", "x")[step],
            src,
            self.arrived.at[step],
            self.send_sem.at[step],
            self.recv_sem.at[step],
        )

    def collect(self, step):
        self.net.arrive(self.arrived.at[step], self.send_sem.at[step], self.recv_sem.at[step])
        src = self.mine if step == 0 else self.sums.at[step - 1]
        self.sums[step] = src[...] + self.arrived[step]

    def spread(self):
        net = self.net
        for k in range(1, net.lines):
            s = 2 + k
            copy = pltpu.make_async_remote_copy(
                src_ref=self.sums.at[2],
                dst_ref=self.wide.at[k - 1],
                send_sem=self.send_sem.at[s],
                recv_sem=self.recv_sem.at[s],
                device_id=net.beyond(k),
                device_id_type=MESH_ID,
            )
            copy.start()
            net.sends.append((copy, None))

    def total(self, out):
        total = self.sums[2]
        for k in range(1, self.net.lines):
            s = 2 + k
            self.net.arrive(self.wide.at[k - 1], self.send_sem.at[s], self.recv_sem.at[s])
            total = total + self.wide[k - 1]
        out[...] = total


def product(a, b, axis_a=1, axis_b=0):
    return lax.dot_general(
        a, b, (((axis_a,), (axis_b,)), ((), ())), preferred_element_type=jnp.float32
    )


def low(value):
    return value.astype(jnp.bfloat16)


def blocks(count, size, body):
    def one(i, carry):
        body(pl.ds(pl.multiple_of(i * size, size), size))
        return carry

    lax.fori_loop(0, count // size, one, 0)


def row_step(rows):
    return next(s for s in (96, 64, 48, 32, 16) if rows % s == 0)


def centred(value):
    center = value - jnp.mean(value, axis=-1, keepdims=True)
    spread = jnp.mean(center * center, axis=-1, keepdims=True)
    return center * lax.rsqrt(spread + EPSILON), lax.rsqrt(spread + EPSILON)


def norm_rows(src, gain, out, also=None):
    def body(rows):
        value = src[rows, :].astype(jnp.float32)
        if also is not None:
            also(rows, value)
        out[rows, :] = low(centred(value)[0] * gain)

    blocks(src.shape[0], row_step(src.shape[0]), body)


def norm_back_rows(src, gain, grad, done, gain_grad):
    gain_grad[...] = jnp.zeros_like(gain_grad)

    def body(rows):
        n, scale = centred(src[rows, :].astype(jnp.float32))
        out = grad[rows, :]
        dn = out * gain
        gain_grad[...] += jnp.sum(out * n, axis=0, keepdims=True)
        back = dn - jnp.mean(dn, axis=-1, keepdims=True)
        done(rows, (back - n * jnp.mean(dn * n, axis=-1, keepdims=True)) * scale)

    blocks(src.shape[0], row_step(src.shape[0]), body)


class Sums:
    def __init__(self, ref, weight):
        self.ref, self.weight = ref, weight
        ref[...] = jnp.zeros_like(ref)

    def add(self, slot, rows, value):
        kept = jnp.sum(value * value, axis=-1, keepdims=True) * self.weight[rows, :]
        total = jnp.sum(kept, axis=0, keepdims=True)
        at = pl.ds(slot, 1)
        self.ref[at, :] = self.ref[at, :] + jnp.broadcast_to(total, (1, self.ref.shape[1]))

    def line(self):
        shape = self.ref.shape
        row = lax.broadcasted_iota(jnp.int32, shape, 0)
        lane = lax.broadcasted_iota(jnp.int32, shape, 1)
        return jnp.sum(jnp.where(row == lane, self.ref[...], 0.0), axis=0, keepdims=True)


def pair_count(width):
    pairs = width // (2 * HD)
    return next(n for n in (3, 2, 1) if pairs % n == 0)


def attention(query, key, value, allowed, weight, mixed):
    count, width = mixed.shape
    group = pair_count(width)
    left = lax.broadcasted_iota(jnp.int32, (count, 2 * HD), 1) < HD

    def one(step, carry):
        kept, scores = [], []
        for i in range(group):
            pair = step * group + i
            q, k, v = query(pair), key(pair), value(pair)
            zero = jnp.zeros_like(q)
            kept.append((pair, v))
            for part in (jnp.where(left, q, zero), jnp.where(left, zero, q)):
                scores.append(product(part, k, 1, 1) * HD ** (-0.5))
        weights = []
        for s in scores:
            s = jnp.where(allowed[...] > 0, s, NEGATIVE)
            e = jnp.exp(s - jnp.max(s, axis=-1, keepdims=True))
            weights.append(low(e / jnp.sum(e, axis=-1, keepdims=True)))
        for i, (pair, v) in enumerate(kept):
            first, second = weights[2 * i : 2 * i + 2]
            weight[2 * pair] = first
            weight[2 * pair + 1] = second
            both_heads = jnp.where(left, product(first, v), product(second, v))
            mixed[:, pl.ds(pl.multiple_of(pair * 2 * HD, 2 * HD), 2 * HD)] = low(both_heads)
        return carry

    lax.fori_loop(0, width // (2 * HD) // group, one, 0)


def attention_back(query, key, value, grad_mixed, weight, width, done):
    count = weight.shape[1]
    group = pair_count(width)
    left = lax.broadcasted_iota(jnp.int32, (count, 2 * HD), 1) < HD

    def one(step, carry):
        kept, raw = [], []
        for i in range(group):
            pair = step * group + i
            q, k, v, d = query(pair), key(pair), value(pair), grad_mixed(pair)
            zero = jnp.zeros_like(q)
            kept.append((pair, q, k))
            for h, part in enumerate((jnp.where(left, d, zero), jnp.where(left, zero, d))):
                raw.append((part, product(part, v, 1, 1), weight[2 * pair + h]))
        grads = []
        for part, dp, p in raw:
            p32 = p.astype(jnp.float32)
            grads.append(low(p32 * (dp - jnp.sum(dp * p32, axis=-1, keepdims=True))))
        for i, (pair, q, k) in enumerate(kept):
            (d0, _, p0), (d1, _, p1) = raw[2 * i : 2 * i + 2]
            s0, s1 = grads[2 * i : 2 * i + 2]
            zero = jnp.zeros_like(q)
            dv = product(p0, d0, 0, 0) + product(p1, d1, 0, 0)
            dk = product(s0, jnp.where(left, q, zero), 0, 0)
            dk = dk + product(s1, jnp.where(left, zero, q), 0, 0)
            dq = jnp.where(left, product(s0, k), product(s1, k))
            done(pair, low(dq * HD ** (-0.5)), low(dk * HD ** (-0.5)), low(dv))
        return carry

    lax.fori_loop(0, width // (2 * HD) // group, one, 0)


def pairs_of(ref, base=0):
    return lambda pair: ref[:, pl.ds(pl.multiple_of(base + pair * 2 * HD, 2 * HD), 2 * HD)]


def gelu_both(value):
    scale = 0.7978845608028654
    cube = 0.044715
    square = value * value
    bend = jnp.tanh(scale * value * (1.0 + cube * square))
    half = 0.5 * (1.0 + bend)
    slope = half + 0.5 * value * (1.0 - bend * bend) * scale * (1.0 + 3.0 * cube * square)
    return value * half, slope


def activate(wide, active, slope, columns):
    def body(rows):
        a, s = gelu_both(wide[rows, :])
        active[rows, columns] = low(a)
        slope[rows, columns] = s.astype(slope.dtype)

    blocks(wide.shape[0], 16, body)


def forward_kernel(
    lines, cuts, parts,
    tok, cot, allowed, cross_allowed, row_weight, gvec, own_a, own_d, pack, own_cd,
    full_a, full_d, sum_ca, sum_cd, o_h1, o_qkv, o_mixed, o_weight, o_middle, o_h2, o_active, o_slope,
    gains, layer_out, top, vec,
    w_a, w_d, w_ca, w_cd, h1, qkv, mixed, weight, middle, h2, active, slope, out_y, wide, branch,
    passed, image_out, n_q, n_i, query, keyval, c_mixed, c_weight, c_middle, h3, grad_wide, g_small,
    swap, block, rcv_a, rcv_d, arrived, totals, spread, sums_ref, gain_rows,
    send_sem, recv_sem, local_sem, swap_sem, s_send, s_recv, pass_sem, out_sem, d_send, d_recv, d_local,
):
    net = Net(lines)
    net.barrier()
    text, image = net.text, net.image
    rows, depth = own_a.shape[0], own_d.shape[0]
    few, part = pack.shape[1], own_cd.shape[0]
    width = tok.shape[1]
    half = pack.shape[2]
    a_qkv, a_out = parts[0], parts[0] + parts[1]
    q_end, kv_end, o_end = cuts[0], cuts[0] + cuts[1], cuts[0] + cuts[1] + cuts[2]
    tile = width

    def columns(first, last):
        return lambda tower, chip, core: w_a.at[
            pl.ds(pl.multiple_of((2 * chip + core) * rows, rows), rows), first:last
        ]

    def crossed(first, last):
        return lambda tower, chip, core: w_ca.at[
            core,
            pl.ds(pl.multiple_of((tower * 2 * lines + chip) * 2 * few, 2 * few), 2 * few),
            first:last,
        ]

    def plan(index, own, place, crossing):
        return Gather(
            net, own, place, crossing, send_sem.at[index], recv_sem.at[index], local_sem.at[index]
        )

    j_qkv = plan(0, own_a.at[:, 0:a_qkv], columns(0, a_qkv), False)
    j_out = plan(1, own_a.at[:, a_qkv:a_out], columns(a_qkv, a_out), False)
    j_up = plan(2, own_a.at[:, a_out:], columns(a_out, own_a.shape[1]), False)
    j_down = plan(
        3,
        own_d,
        lambda tower, chip, core: w_d.at[
            pl.ds(pl.multiple_of((2 * chip + core) * depth, depth), depth), :
        ],
        False,
    )
    j_att = plan(4, block.at[:, 0:o_end], crossed(0, o_end), True)
    j_cup = plan(5, block.at[:, o_end:], crossed(o_end, half), True)
    j_cdown = plan(
        6,
        own_cd,
        lambda tower, chip, core: w_cd.at[
            pl.ds(pl.multiple_of((tower * 4 * lines + 2 * chip + core) * part, part), part), :
        ],
        True,
    )
    kept = []

    def keep(src, dst):
        copy = pltpu.make_async_copy(src, dst, out_sem.at[len(kept)])
        copy.start()
        kept.append(copy)

    swapped = net.copy("core", pack.at[1 - net.core], swap, swap_sem.at[0], swap_sem.at[1])
    swapped.start()
    small = Small(net, gvec, arrived, totals, spread, s_send, s_recv)
    small.exchange(0)
    j_qkv.start()
    j_out.start()
    swapped.wait()
    first = net.core == 0
    mine = pack[net.core]
    theirs = swap[...]
    block[0:few] = low(jnp.where(first, mine, theirs))
    block[few:] = low(jnp.where(first, theirs, mine))
    small.collect(0)
    small.exchange(1)
    j_qkv.beside(0)
    small.collect(1)
    small.exchange(2)
    j_qkv.hop(1)
    j_qkv.beside(1)
    small.collect(2)
    small.spread()
    j_qkv.hop(2)
    j_qkv.beside(2)
    j_up.start()
    small.total(gains)
    sums = Sums(sums_ref, row_weight)
    gain_rows[...] = jnp.zeros_like(gain_rows)
    base = 4 * net.tower

    def gain(at):
        return jnp.where(text, gains[at + 2 : at + 3, :], gains[at : at + 1, :])

    norm_rows(tok, gain(0), h1, lambda r, v: sums.add(base, r, v))
    for k in range(3, lines):
        j_qkv.hop(k)
        j_qkv.beside(k)
    j_qkv.done()

    def qkv_tile(cols):
        qkv[:, cols] = low(product(h1[...], w_a[:, cols]))

    blocks(a_qkv, tile, qkv_tile)
    keep(h1, o_h1)

    def step(job, follow):
        job.beside(0)
        job.from_image(0)
        for k in range(1, lines):
            if k == lines - 1 and follow is not None:
                follow.start()
            job.hop(k)
            job.beside(k)
            job.from_image(k)
        job.done()

    step(j_out, None)
    attention(
        pairs_of(qkv), pairs_of(qkv, width), pairs_of(qkv, 2 * width), allowed, weight, mixed
    )
    keep(qkv, o_qkv)
    keep(weight, o_weight)
    keep(mixed, o_mixed)
    branch[...] = product(mixed[...], w_a[:, a_qkv:a_out])

    def add_branch(r):
        value = branch[r, :]
        sums.add(base + 1, r, value)
        middle[r, :] = tok[r, :].astype(jnp.float32) + value

    blocks(tok.shape[0], row_step(tok.shape[0]), add_branch)
    keep(middle, o_middle)
    norm_rows(middle, gain(1), h2)
    keep(h2, o_h2)
    step(j_up, j_down)

    def up_tile(i, carry):
        at = pl.multiple_of(i * tile, tile)
        wide[...] = product(h2[...], w_a[:, pl.ds(a_out + at, tile)])
        activate(wide, active, slope, pl.ds(at, tile))
        return carry

    lax.fori_loop(0, active.shape[1] // tile, up_tile, 0)
    keep(active, o_active)
    keep(slope, o_slope)
    keep(w_a, full_a)
    step(j_down, j_att)
    keep(w_d, full_d)
    branch[...] = product(active[...], w_d[...])

    def add_mlp(r):
        value = branch[r, :]
        sums.add(base + 2, r, value)
        y = middle[r, :] + value
        out_y[r, :] = y
        image_out[r, :] = low(y)

        @pl.when(image)
        def _():
            sums.add(3, r, y)

    blocks(tok.shape[0], row_step(tok.shape[0]), add_mlp)
    net.send("x", image_out, passed, pass_sem.at[0], pass_sem.at[1], image)
    step(j_att, j_cup)

    @pl.when(text)
    def _():
        norm_rows(out_y, gains[4:5, :], n_q)
        for h in range(2):
            at = h * cuts[0]
            query[:, at : at + cuts[0]] = low(product(n_q[...], w_ca[h, :, 0:q_end]))

    step(j_cup, j_cdown)
    net.arrive(passed, pass_sem.at[0], pass_sem.at[1], text)
    step(j_cdown, None)

    net.finish()
    for copy in kept:
        copy.wait()
    def hand(index, src, rcv, there=text):
        net.send("core", src, rcv, d_send.at[index], d_recv.at[index], there)

    def merge(index, own, rcv, out):
        net.arrive(rcv, d_send.at[index], d_recv.at[index], text)

        @pl.when(text)
        def _():
            def add(r):
                rcv[r, :] = low(own[r, :].astype(jnp.float32) + rcv[r, :].astype(jnp.float32))

            blocks(rcv.shape[0], 16, add)
            pltpu.make_async_copy(rcv, out, d_local.at[index]).start()

    @pl.when(text)
    def _():
        norm_rows(passed, gains[5:6, :], n_i)
        for h in range(2):
            at = h * width
            keyval[:, at : at + width] = low(product(n_i[...], w_ca[h, :, q_end:kv_end]))
        attention(
            pairs_of(query), pairs_of(keyval), pairs_of(keyval, width), cross_allowed, c_weight, c_mixed
        )
        for h in range(2):
            at = h * cuts[2]
            branch[:, at : at + cuts[2]] = product(c_mixed[...], w_ca[h, :, kv_end:o_end])

        def add_cross(r):
            value = branch[r, :]
            sums.add(7, r, value)
            c_middle[r, :] = out_y[r, :] + value

        blocks(tok.shape[0], row_step(tok.shape[0]), add_cross)
        norm_rows(c_middle, gains[6:7, :], h3)

        for h in range(2):

            def cross_up(i, carry):
                at = pl.multiple_of(i * tile, tile)
                wide[...] = product(h3[...], w_ca[h, :, pl.ds(o_end + at, tile)])
                activate(wide, active, slope, pl.ds(h * cuts[3] + at, tile))
                return carry

            lax.fori_loop(0, cuts[3] // tile, cross_up, 0)
        branch[...] = product(active[...], w_cd[...])

        def add_final(r):
            value = branch[r, :]
            sums.add(8, r, value)
            z = c_middle[r, :] + value
            sums.add(9, r, z)
            layer_out[r, :] = low(z)

        blocks(tok.shape[0], row_step(tok.shape[0]), add_final)

        def down_tile(i, carry):
            cols = pl.ds(pl.multiple_of(i * tile, tile), tile)
            found = low(product(active[:, cols], cot[...], 0, 0))
            for k in range(tile // part):
                at = (k % 2) * (w_d.shape[0] // 2) + (k // 2) * part + i * (tile // 2)
                w_d[pl.ds(pl.multiple_of(at, part), part), :] = found[k * part : (k + 1) * part]
            grad = product(cot[...], w_cd[cols, :], 1, 1)
            grad_wide[:, cols] = low(grad * slope[:, cols])
            return carry

        lax.fori_loop(0, active.shape[1] // tile, down_tile, 0)

    share = w_d.shape[0] // 2
    hand(0, w_d.at[pl.ds(pl.multiple_of((1 - net.core) * share, share), share), :], rcv_d)

    @pl.when(text)
    def _():
        for h in range(2):

            def up_grad(i, carry):
                at = pl.multiple_of(i * tile, tile)
                w_a[:, pl.ds(h * half + o_end + at, tile)] = low(
                    product(h3[...], grad_wide[:, pl.ds(h * cuts[3] + at, tile)], 0, 0)
                )
                return carry

            lax.fori_loop(0, cuts[3] // tile, up_grad, 0)

    theirs_at = pl.multiple_of((1 - net.core) * half, half)
    mine_at = pl.multiple_of(net.core * half, half)
    hand(1, w_a.at[:, pl.ds(theirs_at + o_end, half - o_end)], rcv_a.at[:, o_end:half])

    @pl.when(text)
    def _():
        branch[...] = product(grad_wide[:, 0 : cuts[3]], w_ca[0, :, o_end:half], 1, 1) + product(
            grad_wide[:, cuts[3] :], w_ca[1, :, o_end:half], 1, 1
        )

        def mid_done(r, back):
            total = cot[r, :].astype(jnp.float32) + back
            c_middle[r, :] = total
            h3[r, :] = low(total)

        norm_back_rows(c_middle, gains[6:7, :], branch, mid_done, g_small)
        gain_rows[6:7, :] = g_small[...]
        for h in range(2):
            at = h * cuts[2]
            w_a[:, h * half + kv_end : h * half + o_end] = low(
                product(c_mixed[...], h3[:, at : at + cuts[2]], 0, 0)
            )
        branch[...] = product(h3[:, 0 : cuts[2]], w_ca[0, :, kv_end:o_end], 1, 1) + product(
            h3[:, cuts[2] :], w_ca[1, :, kv_end:o_end], 1, 1
        )
        c_mixed[...] = low(branch[...])

        def att_done(pair, dq, dk, dv):
            at = pl.multiple_of(pair * 2 * HD, 2 * HD)
            query[:, pl.ds(at, 2 * HD)] = dq
            keyval[:, pl.ds(at, 2 * HD)] = dk
            keyval[:, pl.ds(width + at, 2 * HD)] = dv

        attention_back(
            pairs_of(query),
            pairs_of(keyval),
            pairs_of(keyval, width),
            pairs_of(c_mixed),
            c_weight,
            width,
            att_done,
        )
        branch[...] = product(keyval[:, 0:width], w_ca[0, :, q_end:kv_end], 1, 1) + product(
            keyval[:, width:], w_ca[1, :, q_end:kv_end], 1, 1
        )

        def image_done(r, back):
            image_out[r, :] = low(back)

        norm_back_rows(passed, gains[5:6, :], branch, image_done, g_small)
        gain_rows[5:6, :] = g_small[...]

    net.send("x", image_out, passed, pass_sem.at[0], pass_sem.at[1], text)

    @pl.when(text)
    def _():
        for h in range(2):
            at = h * width
            w_a[:, h * half + q_end : h * half + kv_end] = low(
                product(n_i[...], keyval[:, at : at + width], 0, 0)
            )
            at = h * cuts[0]
            w_a[:, h * half : h * half + q_end] = low(
                product(n_q[...], query[:, at : at + cuts[0]], 0, 0)
            )

    hand(2, w_a.at[:, pl.ds(theirs_at, o_end)], rcv_a.at[:, 0:o_end])
    mine_d = w_d.at[pl.ds(pl.multiple_of(net.core * share, share), share), :]
    merge(0, mine_d, rcv_d, sum_cd)
    merge(
        1,
        w_a.at[:, pl.ds(mine_at + o_end, half - o_end)],
        rcv_a.at[:, o_end:half],
        sum_ca.at[:, o_end:half],
    )

    @pl.when(text)
    def _():
        branch[...] = product(query[:, 0 : cuts[0]], w_ca[0, :, 0:q_end], 1, 1) + product(
            query[:, cuts[0] :], w_ca[1, :, 0:q_end], 1, 1
        )

        def text_done(r, back):
            top[r, :] = c_middle[r, :] + back

        norm_back_rows(out_y, gains[4:5, :], branch, text_done, g_small)
        gain_rows[4:5, :] = g_small[...]
        sums_ref[10:11, :] = jnp.broadcast_to(
            jnp.sum(row_weight[...], axis=0, keepdims=True), (1, sums_ref.shape[1])
        )
        vec[...] = gain_rows[...]

    merge(2, w_a.at[:, pl.ds(mine_at, o_end)], rcv_a.at[:, 0:o_end], sum_ca.at[:, 0:o_end])
    net.arrive(passed, pass_sem.at[0], pass_sem.at[1], image)

    @pl.when(image)
    def _():
        vec[...] = jnp.zeros_like(vec)

        def add_back(r):
            top[r, :] = cot[r, :].astype(jnp.float32) + passed[r, :].astype(jnp.float32)
            layer_out[r, :] = image_out[r, :]

        blocks(tok.shape[0], row_step(tok.shape[0]), add_back)

    vec[7:8, 0 : sums_ref.shape[1]] = sums.line()

    @pl.when(text)
    def _():
        for index, (src, out) in enumerate(
            (
                (rcv_d, sum_cd),
                (rcv_a.at[:, o_end:half], sum_ca.at[:, o_end:half]),
                (rcv_a.at[:, 0:o_end], sum_ca.at[:, 0:o_end]),
            )
        ):
            pltpu.make_async_copy(src, out, d_local.at[index]).wait()

    net.finish()


def forward(lines, cuts, parts, *operands):
    tok, cot, allowed, cross_allowed, row_weight, gvec, own_a, own_d, pack, own_cd = operands
    bf16, f32 = jnp.bfloat16, jnp.float32
    count = 4 * lines
    rows, width = tok.shape
    few, half = pack.shape[1:]
    hidden = count * own_d.shape[0]
    all_a = (count * own_a.shape[0], own_a.shape[1])
    heads_n = width // HD
    jobs = 7
    shape = jax.ShapeDtypeStruct
    wide_b, wide_f = (rows, width), (rows, hidden)
    stored = [
        (wide_b, bf16),
        ((rows, parts[0]), bf16),
        (wide_b, bf16),
        ((heads_n, rows, rows), bf16),
        (wide_b, f32),
        (wide_b, bf16),
        (wide_f, bf16),
        (wide_f, f32),
    ]
    outs = [
        (all_a, bf16),
        ((hidden, width), bf16),
        ((width, half), bf16),
        ((hidden // 2, width), bf16),
        *stored,
        (gvec.shape, f32),
        (wide_b, bf16),
        (wide_b, f32),
        (gvec.shape, f32),
    ]
    scratch = [
        (all_a, bf16),
        ((hidden, width), bf16),
        ((2, width, half), bf16),
        ((hidden, width), bf16),
        *stored,
        (wide_b, f32),
        (wide_b, f32),
        (wide_b, f32),
        (wide_b, bf16),
        (wide_b, bf16),
        (wide_b, bf16),
        (wide_b, bf16),
        (wide_b, bf16),
        ((rows, 2 * width), bf16),
        (wide_b, bf16),
        ((heads_n, rows, rows), bf16),
        (wide_b, f32),
        (wide_b, bf16),
        (wide_f, bf16),
        ((1, width), f32),
        ((few, half), f32),
        ((2 * few, half), bf16),
        ((width, half), bf16),
        ((hidden // 2, width), bf16),
        ((3,) + gvec.shape, f32),
        ((3,) + gvec.shape, f32),
        ((lines - 1,) + gvec.shape, f32),
        ((16, 128), f32),
        (gvec.shape, f32),
    ]
    dma = pltpu.SemaphoreType.DMA
    return pl.pallas_call(
        functools.partial(forward_kernel, lines, cuts, parts),
        out_shape=tuple(shape(*o) for o in outs),
        in_specs=[VMEM] * 6 + [ANY, ANY, VMEM, ANY],
        out_specs=[ANY] * 12 + [VMEM] * 4,
        scratch_shapes=[pltpu.VMEM(*s) for s in scratch]
        + [
            dma((jobs, Gather.sems(lines))),
            dma((jobs, Gather.sems(lines))),
            dma((jobs,)),
            dma((2,)),
            dma((2 + lines,)),
            dma((2 + lines,)),
            dma((2,)),
            dma((12,)),
            dma((3,)),
            dma((3,)),
            dma((3,)),
        ],
        compiler_params=pltpu.CompilerParams(
            collective_id=0, has_side_effects=True, vmem_limit_bytes=63 << 20
        ),
    )(*operands)


class Scatter:
    def __init__(self, net, own, near, far, rcv, sems):
        self.net, self.own, self.near, self.far, self.rcv = net, own, near, far, rcv
        self.send_sem, self.recv_sem = sems

    @staticmethod
    def sems(lines):
        return 1 + 5 * lines

    def sem(self, s):
        return self.send_sem.at[s], self.recv_sem.at[s]

    def add(self, pairs, out):
        def one(r):
            total = pairs[0][r, :].astype(jnp.float32)
            for other in pairs[1:]:
                total = total + other[r, :].astype(jnp.float32)
            out[r, :] = total.astype(out.dtype)

        blocks(out.shape[0], 16, one)

    def chips(self, k):
        net = self.net
        if k == 0:
            return ((None, net.z),)
        return (
            (net.z + k < net.lines, jnp.minimum(net.z + k, net.lines - 1)),
            (net.z >= k, jnp.maximum(net.z - k, 0)),
        )

    def order(self):
        return [pair for k in range(self.net.lines - 1, -1, -1) for pair in self.chips(k)]

    def swap(self, theirs, rcv):
        self.whole = rcv
        self.net.send("core", theirs, rcv, *self.sem(0))

    def swapped(self):
        self.net.arrive(self.whole, *self.sem(0))

    def over_x(self, part):
        net = self.net
        for there, z in self.order():
            for y in (1 - net.y, net.y):
                chip = 2 * z + y
                net.send("x", part(chip), self.own(chip), *self.sem(1 + chip), both(there, net.text))

    def from_x(self, chip, there):
        if self.rcv is None:
            net = self.net
            net.arrive(self.own(chip), *self.sem(1 + chip), both(there, net.image))

    def across(self, only=None):
        net = self.net
        for there, z in self.order():
            there = both(there, only)
            chip = 2 * z + 1 - net.y
            self.from_x(chip, there)
            own = self.own(chip)
            if self.rcv is not None:
                when(there, lambda: self.add([own, self.rcv(chip)], own))
            net.send("y", own, self.near(z), *self.sem(1 + 2 * net.lines + z), there)

    def here(self, chip, z):
        parts = [self.own(chip), self.near(z)]
        return parts if self.rcv is None else parts + [self.rcv(chip)]

    def along(self, k):
        net = self.net
        lines = net.lines
        for up, (there, z) in zip((True, False), self.chips(k)):
            chip = 2 * z + net.y
            base = (1 + 3 * lines) if up else (1 + 4 * lines)
            self.from_x(chip, there)
            net.arrive(self.near(z), *self.sem(1 + 2 * lines + z), there)
            more = net.low if up else net.high
            s = base + z
            net.arrive(self.far(z), *self.sem(s), both(there, more))
            own = self.own(chip)
            parts = self.here(chip, z)
            when(both(there, more), lambda: self.add(parts + [self.far(z)], own))
            when(both(there, jnp.logical_not(more)), lambda: self.add(parts, own))
            slot = z if up else jnp.where(z == net.z - 1, lines, z)
            net.send("up" if up else "down", own, self.far(slot), *self.sem(s), there)

    def total(self, out):
        net = self.net
        lines = net.lines
        self.from_x(net.chip, None)
        net.arrive(self.near(net.z), *self.sem(1 + 2 * lines + net.z))
        net.arrive(self.far(net.z), *self.sem(1 + 3 * lines + net.z), net.low)
        net.arrive(self.far(lines), *self.sem(1 + 4 * lines + net.z), net.high)
        parts = self.here(net.chip, net.z)
        low_part, high_part = self.far(net.z), self.far(lines)
        when(both(net.low, net.high), lambda: self.add(parts + [low_part, high_part], out))
        when(jnp.logical_not(net.low), lambda: self.add(parts + [high_part], out))
        when(jnp.logical_not(net.high), lambda: self.add(parts + [low_part], out))


def strip(ref, size, first, last):
    return lambda i: ref.at[pl.ds(pl.multiple_of(i * size, size), size), first:last]


def backward_kernel(
    lines, cuts, parts,
    tok, top_in, gains, vec_in, full_a, full_d, sum_ca, sum_cd,
    i_h1, i_qkv, i_mixed, i_weight, i_middle, i_h2, i_active, i_slope,
    o_qkv, o_out, o_up, o_d, o_cq, o_ckv, o_co, o_cu, o_cd, input_grad, o_vec,
    h1, qkv, mixed, weight, middle, h2, active, slope,
    g_a, g_d, rcv_a, rcv_d, near_a, near_d, far_a, far_d,
    own_ca, own_cd, near_ca, near_cd, far_ca, far_cd,
    w_d, w_up, top, branch, n_grad, g_small, vec, fin, swap, arrived, totals, spread,
    send_sem, recv_sem, load_sem, swap_sem, s_send, s_recv,
):
    net = Net(lines)
    net.barrier()
    text, image = net.text, net.image
    width = tok.shape[1]
    tile = width
    rows, depth = o_qkv.shape[0], o_d.shape[0]
    few, part = 2 * o_cq.shape[0], o_cd.shape[0]
    half = own_ca.shape[1]
    a_out = parts[0] + parts[1]
    all_a = g_a.shape[2]
    o_end = cuts[0] + cuts[1] + cuts[2]
    theirs = 1 - net.core

    def load(index, src, dst):
        copy = pltpu.make_async_copy(src, dst, load_sem.at[index])
        copy.start()
        return copy

    l_active = load(0, i_active, active)
    l_wd = load(1, full_d, w_d)
    l_slope = load(2, i_slope, slope)
    l_h2 = load(3, i_h2, h2)
    l_up = load(4, full_a.at[:, a_out:], w_up)
    l_middle = load(5, i_middle, middle)
    l_mixed = load(6, i_mixed, mixed)
    l_qkv = load(7, i_qkv, qkv)
    l_weight = load(8, i_weight, weight)
    l_h1 = load(9, i_h1, h1)

    def job(index, own, near, far, rcv):
        return Scatter(net, own, near, far, rcv, (send_sem.at[index], recv_sem.at[index]))

    def self_a(index, first, last):
        return job(
            index,
            strip(g_a.at[net.core], rows, first, last),
            strip(near_a, rows, first, last),
            strip(far_a, rows, first, last),
            strip(rcv_a, rows, first, last),
        )

    def cross_a(index, first, last):
        return job(
            index,
            strip(own_ca, few, first, last),
            strip(near_ca, few, first, last),
            strip(far_ca, few, first, last),
            None,
        )

    s_d = job(
        0,
        strip(g_d.at[net.core], depth, 0, width),
        strip(near_d, depth, 0, width),
        strip(far_d, depth, 0, width),
        strip(rcv_d, depth, 0, width),
    )
    s_up = self_a(1, a_out, all_a)
    s_att = self_a(2, 0, a_out)
    c_d = job(
        3,
        strip(own_cd, part, 0, width),
        strip(near_cd, part, 0, width),
        strip(far_cd, part, 0, width),
        None,
    )
    c_up = cross_a(4, o_end, half)
    c_att = cross_a(5, 0, o_end)

    plane_a, plane_d = own_ca.shape[0], own_cd.shape[0]
    c_loads = (
        pltpu.make_async_copy(sum_cd.at[plane_d : 2 * plane_d, :], own_cd, load_sem.at[10]),
        pltpu.make_async_copy(sum_ca.at[plane_a : 2 * plane_a, :], own_ca, load_sem.at[11]),
    )

    @pl.when(text)
    def _():
        for copy in c_loads:
            copy.start()

    c_d.over_x(strip(sum_cd, part, 0, width))
    c_up.over_x(strip(sum_ca, few, o_end, half))
    c_att.over_x(strip(sum_ca, few, 0, o_end))

    def copy_top(r):
        n_grad[r, :] = low(top_in[r, :])

    blocks(tok.shape[0], row_step(tok.shape[0]), copy_top)

    @pl.when(text)
    def _():
        for copy in c_loads:
            copy.wait()

    c_d.across(text)
    l_active.wait()
    l_wd.wait()
    l_slope.wait()

    def down_tile(i, carry):
        cols = pl.ds(pl.multiple_of(i * tile, tile), tile)
        found = low(product(active[:, cols], n_grad[...], 0, 0))
        each = tile // depth
        for k in range(each):
            at = pl.multiple_of(((i * each + k) // 2) * depth, depth)
            g_d[k % 2, pl.ds(at, depth), :] = found[k * depth : (k + 1) * depth]
        grad = product(n_grad[...], w_d[cols, :], 1, 1)
        active[:, cols] = low(grad * slope[:, cols])
        return carry

    lax.fori_loop(0, active.shape[1] // tile, down_tile, 0)
    s_d.swap(g_d.at[theirs], rcv_d)
    l_four = [
        load(12 + i, full_a.at[:, i * width : (i + 1) * width], w_d.at[i * width : (i + 1) * width, :])
        for i in range(4)
    ]
    l_h2.wait()

    def put_a(found, at):
        for k in range(width // rows):
            g_a[k % 2, (k // 2) * rows : (k // 2 + 1) * rows, pl.ds(at, found.shape[1])] = found[
                k * rows : (k + 1) * rows
            ]

    def up_tile(i, carry):
        at = pl.multiple_of(i * tile, tile)
        put_a(low(product(h2[...], active[:, pl.ds(at, tile)], 0, 0)), pl.multiple_of(a_out + at, tile))
        return carry

    lax.fori_loop(0, (all_a - a_out) // tile, up_tile, 0)
    s_up.swap(g_a.at[theirs, :, a_out:all_a], rcv_a.at[:, a_out:all_a])
    s_d.swapped()
    s_d.across()
    l_up.wait()
    branch[...] = product(active[...], w_up[...], 1, 1)
    l_middle.wait()

    def mid_done(r, back):
        total = top_in[r, :] + back
        top[r, :] = total
        n_grad[r, :] = low(total)

    def own_gain(at):
        return jnp.where(text, gains[at + 2 : at + 3, :], gains[at : at + 1, :])

    norm_back_rows(middle, own_gain(1), branch, mid_done, g_small)
    vec[...] = vec_in[...]
    at_vec = 2 * net.tower
    vec[pl.ds(at_vec + 1, 1), :] = g_small[...]
    s_up.swapped()
    s_up.across()
    l_mixed.wait()
    for copy in l_four:
        copy.wait()
    put_a(low(product(mixed[...], n_grad[...], 0, 0)), parts[0])
    mixed[...] = low(product(n_grad[...], w_d[3 * width : 4 * width, :], 1, 1))
    l_qkv.wait()
    l_weight.wait()

    def att_done(pair, dq, dk, dv):
        at = pl.multiple_of(pair * 2 * HD, 2 * HD)
        for k, grad in enumerate((dq, dk, dv)):
            qkv[:, pl.ds(pl.multiple_of(k * width + at, 2 * HD), 2 * HD)] = grad

    attention_back(
        pairs_of(qkv),
        pairs_of(qkv, width),
        pairs_of(qkv, 2 * width),
        pairs_of(mixed),
        weight,
        width,
        att_done,
    )
    l_h1.wait()

    def qkv_tile(i, carry):
        at = pl.multiple_of(i * tile, tile)
        put_a(low(product(h1[...], qkv[:, pl.ds(at, tile)], 0, 0)), at)
        return carry

    lax.fori_loop(0, parts[0] // tile, qkv_tile, 0)
    s_att.swap(g_a.at[theirs, :, 0:a_out], rcv_a.at[:, 0:a_out])
    branch[...] = (
        product(qkv[:, 0:width], w_d[0:width, :], 1, 1)
        + product(qkv[:, width : 2 * width], w_d[width : 2 * width, :], 1, 1)
        + product(qkv[:, 2 * width :], w_d[2 * width : 3 * width, :], 1, 1)
    )

    def first_done(r, back):
        input_grad[r, :] = top[r, :] + back

    norm_back_rows(tok, own_gain(0), branch, first_done, g_small)
    vec[pl.ds(at_vec, 1), :] = g_small[...]
    small = Small(net, vec, arrived, totals, spread, s_send, s_recv)
    small.exchange(0)
    s_att.swapped()
    s_att.across()
    small.collect(0)
    small.exchange(1)
    c_d.across(image)
    small.collect(1)
    small.exchange(2)
    far_first = range(lines - 1, 0, -1)
    for k in far_first:
        s_d.along(k)
    small.collect(2)
    small.spread()
    c_up.across()
    s_d.total(o_d)
    for k in far_first:
        s_up.along(k)
    small.total(o_vec)
    for k in far_first:
        c_d.along(k)
    s_up.total(o_up)
    c_att.across()
    c_d.total(o_cd)
    for k in far_first:
        s_att.along(k)
    for k in far_first:
        c_up.along(k)
    s_att.total(fin)
    o_qkv[...] = fin[:, 0 : parts[0]]
    o_out[...] = fin[:, parts[0] : a_out]
    for k in far_first:
        c_att.along(k)
    c_up.total(fin.at[:, o_end:half])
    c_att.total(fin.at[:, 0:o_end])
    share = few // 2
    swapped = net.copy(
        "core",
        fin.at[pl.ds(pl.multiple_of(theirs * share, share), share), :],
        swap,
        swap_sem.at[0],
        swap_sem.at[1],
    )
    swapped.start()
    swapped.wait()
    mine = fin[pl.ds(pl.multiple_of(net.core * share, share), share), :]
    other = swap[...]
    first = net.core == 0
    left = jnp.where(first, mine, other)
    right = jnp.where(first, other, mine)
    at = 0
    for out, n in zip((o_cq, o_ckv, o_co, o_cu), cuts):
        out[:, 0:n] = left[:, at : at + n]
        out[:, n:] = right[:, at : at + n]
        at += n
    net.finish()


def backward(lines, cuts, parts, own_shapes, *operands):
    bf16, f32 = jnp.bfloat16, jnp.float32
    tok, top, gains, vec, full_a, full_d, sum_ca, sum_cd = operands[:8]
    stored = [(o.shape, o.dtype) for o in operands[8:]]
    chips = 2 * lines
    row_count, width = tok.shape
    hidden, all_a = full_d.shape[0], full_a.shape[1]
    half = sum_ca.shape[1]
    rows, depth = width // (2 * chips), hidden // (2 * chips)
    few, part = width // (2 * chips), hidden // (4 * chips)
    outs = [*own_shapes, (row_count, width), vec.shape]
    rcv_a, rcv_d = (chips * rows, all_a), (chips * depth, width)
    own_ca, own_cd = (chips * few, half), (chips * part, width)

    def line(size, count):
        return (size * count, all_a), (depth * count, width)

    scratch = [
        *stored,
        ((2,) + rcv_a, bf16),
        ((2,) + rcv_d, bf16),
        (rcv_a, bf16),
        (rcv_d, bf16),
        ((lines * rows, all_a), bf16),
        ((lines * depth, width), bf16),
        (((lines + 1) * rows, all_a), bf16),
        (((lines + 1) * depth, width), bf16),
        (own_ca, bf16),
        (own_cd, bf16),
        ((lines * few, half), bf16),
        ((lines * part, width), bf16),
        (((lines + 1) * few, half), bf16),
        (((lines + 1) * part, width), bf16),
        ((hidden, width), bf16),
        ((width, hidden), bf16),
        ((row_count, width), f32),
        ((row_count, width), f32),
        ((row_count, width), bf16),
        ((1, width), f32),
        (vec.shape, f32),
        ((rows, half), f32),
        ((few // 2, half), f32),
        ((3,) + vec.shape, f32),
        ((3,) + vec.shape, f32),
        ((lines - 1,) + vec.shape, f32),
    ]
    dma = pltpu.SemaphoreType.DMA
    return pl.pallas_call(
        functools.partial(backward_kernel, lines, cuts, parts),
        out_shape=tuple(jax.ShapeDtypeStruct(s, f32) for s in outs),
        in_specs=[VMEM] * 4 + [ANY] * 12,
        out_specs=[VMEM] * len(outs),
        scratch_shapes=[pltpu.VMEM(*s) for s in scratch]
        + [
            dma((6, Scatter.sems(lines))),
            dma((6, Scatter.sems(lines))),
            dma((16,)),
            dma((2,)),
            dma((2 + lines,)),
            dma((2 + lines,)),
        ],
        compiler_params=pltpu.CompilerParams(
            collective_id=1, has_side_effects=True, vmem_limit_bytes=63 << 20
        ),
    )(*operands)


def plain_gather(own_a, own_d, pack, own_cd, own_g):
    axes = ("tower", "dp")
    tiles = lax.all_gather(own_g, axes, axis=0)
    return (
        lax.all_gather(own_a, "dp", axis=0, tiled=True),
        lax.all_gather(own_d, "dp", axis=0, tiled=True),
        lax.all_gather(pack.astype(jnp.bfloat16), axes, axis=1, tiled=True),
        lax.all_gather(own_cd, axes, axis=0, tiled=True),
        tiles.reshape((2, -1) + own_g.shape),
    )


def plain_scatter(g_a, g_d, g_ca, g_cd, vec, parts, cuts):
    axes = ("tower", "dp")

    def added(grad, over, axis):
        return lax.psum_scatter(
            grad.astype(jnp.float32), over, scatter_dimension=axis, tiled=True
        )

    a = added(g_a.reshape(-1, g_a.shape[-1]), "dp", 0)
    d = added(g_d.reshape(-1, g_d.shape[-1]), "dp", 0)
    ca = added(g_ca.reshape(2, -1, g_ca.shape[-1]), axes, 1)
    cd = added(g_cd.reshape(-1, g_cd.shape[-1]), axes, 0)
    at = [sum(cuts[:i]) for i in range(len(cuts) + 1)]
    cross = [
        jnp.concatenate([ca[0][:, i:j], ca[1][:, i:j]], axis=1) for i, j in zip(at[:-1], at[1:])
    ]
    first, second = parts[0], parts[0] + parts[1]
    self_parts = [a[:, :first], a[:, first:second], a[:, second:]]
    return (*self_parts, d, *cross, cd, lax.psum(vec, axes))


def layer_norm(value_matrix, norm_gain):
    center = value_matrix - jnp.mean(value_matrix, axis=-1, keepdims=True)
    spread = jnp.mean(center * center, axis=-1, keepdims=True)
    return center * lax.rsqrt(spread + EPSILON) * norm_gain


def norm_back(value_matrix, norm_gain, grad_out):
    result, puller = jax.vjp(layer_norm, value_matrix, norm_gain)
    return puller(grad_out)


def dot(a, b):
    return jnp.dot(a, b, preferred_element_type=jnp.float32)


def dot_tn(a, b):
    return jnp.einsum("rd,re->de", a, b, preferred_element_type=jnp.float32)


def dot_nt(a, b):
    return jnp.einsum("re,de->rd", a, b, preferred_element_type=jnp.float32)


def low(value_matrix):
    return value_matrix.astype(jnp.bfloat16)


def masks(counts, lengths, row_count, decoder):
    row_index = jnp.arange(row_count, dtype=jnp.int32)
    bounds = jnp.cumsum(counts)
    image_of = jnp.sum((row_index[:, None] >= bounds[None, :]).astype(jnp.int32), axis=1)
    caption_of = row_index // CAP_LEN
    in_place = row_index - caption_of * CAP_LEN
    caption_slots = jnp.arange(lengths.shape[0], dtype=jnp.int32)
    length_rows = jnp.sum(
        jnp.where(caption_of[:, None] == caption_slots[None, :], lengths[None, :], 0), axis=1
    )
    valid_rows = in_place < length_rows
    image_mask = image_of[:, None] == image_of[None, :]
    text_mask = (
        (caption_of[:, None] == caption_of[None, :])
        & (in_place[None, :] <= in_place[:, None])
        & valid_rows[None, :]
    )
    cross_mask = caption_of[:, None] == image_of[None, :]
    return jnp.where(decoder, text_mask, image_mask), cross_mask, valid_rows


def heads(value_matrix):
    return value_matrix.reshape(value_matrix.shape[0], -1, HD)


def attend(query, key, value, allowed):
    scores = jnp.einsum(
        "qhd,khd->hqk", heads(query), heads(key), preferred_element_type=jnp.float32
    ) * HD ** (-0.5)
    weight = jax.nn.softmax(jnp.where(allowed[None], scores, NEGATIVE), axis=-1)
    mixed = jnp.einsum("hqk,khd->qhd", low(weight), heads(value), preferred_element_type=jnp.float32)
    return low(mixed.reshape(query.shape)), weight


def attend_back(query, key, value, weight, grad_mixed):
    grad_mixed = heads(grad_mixed)
    grad_value = jnp.einsum("hqk,qhd->khd", low(weight), grad_mixed, preferred_element_type=jnp.float32)
    grad_weight = jnp.einsum("qhd,khd->hqk", grad_mixed, heads(value), preferred_element_type=jnp.float32)
    grad_score = low(
        weight * (grad_weight - jnp.sum(grad_weight * weight, axis=-1, keepdims=True))
    )
    grad_query = jnp.einsum(
        "hqk,khd->qhd", grad_score, heads(key), preferred_element_type=jnp.float32
    ) * HD ** (-0.5)
    grad_key = jnp.einsum(
        "hqk,qhd->khd", grad_score, heads(query), preferred_element_type=jnp.float32
    ) * HD ** (-0.5)
    return tuple(low(g.reshape(query.shape)) for g in (grad_query, grad_key, grad_value))


def mlp_forward(stream, gain, up, down):
    hidden = low(layer_norm(stream, gain))
    wide = dot(hidden, up)
    active = low(jax.nn.gelu(wide))
    return dot(active, down), (hidden, wide, active)


def mlp_back(stream, gain, up, down, stored, grad):
    hidden, wide, active = stored
    branch = low(grad)
    grad_down = dot_tn(active, branch)
    result, puller = jax.vjp(jax.nn.gelu, wide)
    grad_wide = low(puller(dot_nt(branch, down))[0])
    grad_up = dot_tn(hidden, grad_wide)
    grad_stream, grad_gain = norm_back(stream, gain, dot_nt(grad_wide, up))
    return grad + grad_stream, grad_gain, grad_up, grad_down


def squares(value_matrix, row_weight):
    return jnp.sum(row_weight[:, None] * value_matrix * value_matrix)


def plain_shards(
    tokens, cotangent, kept_counts, caption_lengths, attn_gain, qkv_weight, attn_out, mlp_gain,
    mlp_up, mlp_down, query_gain, image_gain, cross_gain, cross_query, cross_keyval, cross_out,
    cross_up, cross_down,
):
    f32 = jnp.float32
    dp_count = lax.axis_size("dp")
    lines = dp_count // 4
    tower, dp = lax.axis_index("tower"), lax.axis_index("dp")
    decoder = tower == 1
    row_count, width = tokens.shape[1:]
    rows = attn_gain.shape[1]
    few = query_gain.shape[0]

    def tile_row(value):
        return jnp.pad(value.astype(f32), (0, 128 - value.shape[0]))

    gain_tile = jnp.stack(
        [tile_row(attn_gain[0]), tile_row(mlp_gain[0])]
        + [tile_row(g) for g in (query_gain, image_gain, cross_gain)]
        + [jnp.zeros((128,), f32)] * 3
    )
    cross_shards = (cross_query, cross_keyval, cross_out, cross_up)
    cuts = tuple(w.shape[1] // 2 for w in cross_shards)
    pack = jnp.stack(
        [
            jnp.concatenate([w[:, h * n : (h + 1) * n] for w, n in zip(cross_shards, cuts)], axis=1)
            for h in range(2)
        ]
    ).astype(f32)
    self_parts = (qkv_weight.shape[2], attn_out.shape[2], mlp_up.shape[2])
    own_a = jnp.concatenate([qkv_weight[0], attn_out[0], mlp_up[0]], axis=1)
    full_a, full_d, full_ca, full_cd, full_g = plain_gather(
        own_a, mlp_down[0], pack, cross_down, gain_tile
    )
    qkv = full_a[:, : self_parts[0]]
    out = full_a[:, self_parts[0] : self_parts[0] + self_parts[1]]
    up = full_a[:, self_parts[0] + self_parts[1] :]
    down = full_d
    plane_gains = lax.dynamic_index_in_dim(full_g, tower, 0, keepdims=False)
    gain_1 = plane_gains[:, 0, :rows].reshape(-1)
    gain_2 = plane_gains[:, 1, :rows].reshape(-1)
    gain_q, gain_i, gain_c = (full_g[:, :, 2 + i, :few].reshape(-1) for i in range(3))

    stream = tokens[0].astype(f32)
    upstream = cotangent[0].astype(f32)
    allowed, cross_allowed, valid_rows = masks(kept_counts[0], caption_lengths, row_count, decoder)
    row_weight = jnp.where(decoder, valid_rows, True).astype(f32)

    normed = low(layer_norm(stream, gain_1))
    joined = low(dot(normed, qkv))
    query, key, value = jnp.split(joined, 3, axis=1)
    mixed, weight = attend(query, key, value, allowed)
    attn_branch = dot(mixed, out)
    middle = stream + attn_branch
    mlp_branch, mlp_stored = mlp_forward(middle, gain_2, up, down)
    layer_y = middle + mlp_branch
    image_rows = low(layer_y)
    arrived = lax.ppermute(image_rows, "tower", [(0, 1)])

    def run_cross(operands):
        text_y, image_in = operands
        at = [0]
        for n in cuts:
            at.append(at[-1] + n)
        cq, ckv, co, cu = (
            jnp.concatenate([full_ca[0][:, a:b], full_ca[1][:, a:b]], axis=1)
            for a, b in zip(at[:-1], at[1:])
        )
        image_in = image_in.astype(f32)
        image_normed = low(layer_norm(image_in, gain_i))
        keyval = low(dot(image_normed, ckv))
        c_key, c_value = jnp.split(keyval, 2, axis=1)
        c_normed = low(layer_norm(text_y, gain_q))
        c_query = low(dot(c_normed, cq))
        c_mixed, c_weight = attend(c_query, c_key, c_value, cross_allowed)
        c_branch = dot(c_mixed, co)
        c_middle = text_y + c_branch
        c_mlp, c_stored = mlp_forward(c_middle, gain_c, cu, full_cd)
        final_rows = c_middle + c_mlp
        grad_middle, grad_gain_c, grad_cu, grad_cd = mlp_back(
            c_middle, gain_c, cu, full_cd, c_stored, upstream
        )
        grad_branch = low(grad_middle)
        grad_co = dot_tn(c_mixed, grad_branch)
        grad_q, grad_k, grad_v = attend_back(
            c_query, c_key, c_value, c_weight, low(dot_nt(grad_branch, co))
        )
        grad_cq = dot_tn(c_normed, grad_q)
        grad_text, grad_gain_q = norm_back(text_y, gain_q, dot_nt(grad_q, cq))
        grad_keyval = jnp.concatenate([grad_k, grad_v], axis=1)
        grad_ckv = dot_tn(image_normed, grad_keyval)
        grad_image, grad_gain_i = norm_back(image_in, gain_i, dot_nt(grad_keyval, ckv))
        cross_sums = jnp.stack(
            [
                squares(c_branch, row_weight),
                squares(c_mlp, row_weight),
                squares(final_rows, row_weight),
            ]
        )
        grads = tuple(low(g) for g in (grad_cq, grad_ckv, grad_co, grad_cu))
        grad_ca = jnp.stack(
            [
                jnp.concatenate([g[:, h * n : (h + 1) * n] for g, n in zip(grads, cuts)], axis=1)
                for h in range(2)
            ]
        )
        return (
            low(final_rows),
            grad_middle + grad_text,
            low(grad_image),
            grad_ca,
            low(grad_cd),
            jnp.concatenate([grad_gain_q, grad_gain_i, grad_gain_c]),
            cross_sums,
        )

    def skip_cross(operands):
        shapes = jax.eval_shape(run_cross, operands)
        return tuple(jnp.zeros(s.shape, s.dtype) for s in shapes)

    final_rows, grad_text, grad_image, grad_ca, grad_cd, grad_cross_gains, cross_sums = lax.cond(
        decoder, run_cross, skip_cross, (layer_y, arrived)
    )
    returned = lax.ppermute(grad_image, "tower", [(1, 0)]).astype(f32)
    grad_top = jnp.where(decoder, grad_text, upstream + returned)

    grad_middle, grad_gain_2, grad_up, grad_down = mlp_back(
        middle, gain_2, up, down, mlp_stored, grad_top
    )
    grad_branch = low(grad_middle)
    grad_out = dot_tn(mixed, grad_branch)
    grad_joined = jnp.concatenate(
        attend_back(query, key, value, weight, low(dot_nt(grad_branch, out))), axis=1
    )
    grad_qkv = dot_tn(normed, grad_joined)
    grad_stream, grad_gain_1 = norm_back(stream, gain_1, dot_nt(grad_joined, qkv))
    grad_stream = grad_middle + grad_stream

    layer_sums = jnp.stack(
        [
            squares(stream, row_weight),
            squares(attn_branch, row_weight),
            squares(mlp_branch, row_weight),
            squares(layer_y, row_weight),
        ]
    )
    encoder_part = jnp.where(decoder, 0.0, layer_sums)
    decoder_part = jnp.where(decoder, jnp.concatenate([layer_sums[:3], cross_sums]), 0.0)
    counted = jnp.where(decoder, jnp.sum(valid_rows.astype(f32)), 0.0)
    line = tile_row(jnp.concatenate([encoder_part, decoder_part, counted[None]]))
    self_gains = jnp.concatenate([grad_gain_1, grad_gain_2])
    zero = jnp.zeros_like(self_gains)
    vec = jnp.concatenate(
        [
            jnp.where(decoder, zero, self_gains),
            jnp.where(decoder, self_gains, zero),
            grad_cross_gains,
            line,
        ]
    ).reshape(-1, 128)
    vec = jnp.pad(vec, ((0, -vec.shape[0] % 8), (0, 0)))
    grad_a = jnp.concatenate([low(grad_qkv), low(grad_out), low(grad_up)], axis=1)
    chips = 2 * lines
    results = plain_scatter(
        grad_a.reshape(chips, 2, rows, -1),
        low(grad_down).reshape(chips, 2, -1, width),
        grad_ca.reshape(2, 2, chips, 2 * few, -1),
        grad_cd.reshape(2, chips, 2, -1, width),
        vec,
        self_parts,
        cuts,
    )
    o_qkv, o_out, o_up, o_d, o_cq, o_ckv, o_co, o_cu, o_cd, o_vec = results
    flat = o_vec.reshape(-1)
    own_gains = lax.dynamic_slice(flat, (tower * 2 * width,), (2 * width,))
    g_1, g_2 = (lax.dynamic_slice(own_gains, (i * width + dp * rows,), (rows,)) for i in range(2))
    g_q, g_i, g_c = (
        lax.dynamic_slice(
            flat, ((4 + i) * width + (tower * dp_count + dp) * few,), (few,)
        )
        for i in range(3)
    )
    sums = flat[7 * width : 7 * width + 11]
    encoder_count = jnp.full((4,), float(row_count * dp_count), f32)
    divisor = jnp.concatenate([encoder_count, jnp.full((6,), 1.0, f32) * sums[10]]) * width
    rms_values = jnp.sqrt(sums[:10] / divisor)
    layer_out = jnp.where(decoder, final_rows, image_rows)
    return (
        layer_out[None], grad_stream[None], g_1[None], o_qkv[None], o_out[None], g_2[None],
        o_up[None], o_d[None], g_q, g_i, g_c, o_cq, o_ckv, o_co, o_cu, o_cd, rms_values,
    )


def fused_shards(
    tokens, cotangent, kept_counts, caption_lengths, attn_gain, qkv_weight, attn_out, mlp_gain,
    mlp_up, mlp_down, query_gain, image_gain, cross_gain, cross_query, cross_keyval, cross_out,
    cross_up, cross_down,
):
    f32 = jnp.float32
    dp_count = lax.axis_size("dp")
    lines = dp_count // 4
    tower, dp = lax.axis_index("tower"), lax.axis_index("dp")
    decoder = tower == 1
    row_count, width = tokens.shape[1:]
    rows = attn_gain.shape[1]
    few = query_gain.shape[0]
    lane = jnp.arange(width)

    def in_place(value, index):
        n = value.shape[0]
        return jnp.where(lane // n == index, jnp.tile(value.astype(f32), width // n), 0.0)

    first, second = in_place(attn_gain[0], dp), in_place(mlp_gain[0], dp)
    zero = jnp.zeros_like(first)
    gvec = jnp.stack(
        [
            jnp.where(decoder, zero, first),
            jnp.where(decoder, zero, second),
            jnp.where(decoder, first, zero),
            jnp.where(decoder, second, zero),
        ]
        + [in_place(g, tower * dp_count + dp) for g in (query_gain, image_gain, cross_gain)]
        + [zero]
    )
    cross_shards = (cross_query, cross_keyval, cross_out, cross_up)
    cuts = tuple(w.shape[1] // 2 for w in cross_shards)
    pack = jnp.stack(
        [
            jnp.concatenate([w[:, h * n : (h + 1) * n] for w, n in zip(cross_shards, cuts)], axis=1)
            for h in range(2)
        ]
    ).astype(f32)
    parts = (qkv_weight.shape[2], attn_out.shape[2], mlp_up.shape[2])
    own_a = jnp.concatenate([qkv_weight[0], attn_out[0], mlp_up[0]], axis=1)
    allowed, cross_allowed, valid_rows = masks(kept_counts[0], caption_lengths, row_count, decoder)
    row_weight = jnp.where(decoder, valid_rows, True).astype(f32)[:, None]
    (
        full_a, full_d, sum_ca, sum_cd, h1, qkv, mixed, weight, middle, h2, active, slope,
        gains, layer_out, top, vec,
    ) = forward(
        lines, cuts, parts, tokens[0], cotangent[0], allowed.astype(f32), cross_allowed.astype(f32),
        row_weight, gvec, own_a, mlp_down[0], pack, cross_down,
    )
    shard_shapes = [
        w.shape[-2:]
        for w in (
            qkv_weight, attn_out, mlp_up, mlp_down, cross_query, cross_keyval, cross_out, cross_up,
            cross_down,
        )
    ]
    o_qkv, o_out, o_up, o_d, o_cq, o_ckv, o_co, o_cu, o_cd, input_grad, o_vec = backward(
        lines, cuts, parts, shard_shapes, tokens[0], top, gains, vec, full_a, full_d, sum_ca,
        sum_cd, h1, qkv, mixed, weight, middle, h2, active, slope,
    )
    g_1, g_2 = (
        lax.dynamic_slice(o_vec, (2 * tower + i, dp * rows), (1, rows)) for i in range(2)
    )
    g_q, g_i, g_c = (
        lax.dynamic_slice(o_vec, (4 + i, (tower * dp_count + dp) * few), (1, few))[0]
        for i in range(3)
    )
    sums = o_vec[7]
    encoder_count = jnp.full((4,), float(row_count * dp_count), f32)
    divisor = jnp.concatenate([encoder_count, jnp.full((6,), 1.0, f32) * sums[10]]) * width
    rms_values = jnp.sqrt(sums[:10] / divisor)
    return (
        layer_out[None], input_grad[None], g_1, o_qkv[None], o_out[None], g_2, o_up[None],
        o_d[None], g_q, g_i, g_c, o_cq, o_ckv, o_co, o_cu, o_cd, rms_values,
    )


def shards(*arrays):
    dp_count = lax.axis_size("dp")
    cross_query, cross_down = arrays[13], arrays[17]
    fills = dp_count % 4 == 0 and dp_count > 4
    fills = fills and cross_query.shape[0] % 8 == 0 and cross_down.shape[0] % 16 == 0
    return fused_shards(*arrays) if fills else plain_shards(*arrays)


def solution(mesh):
    rows = P("tower", "dp", None)
    gain = P("tower", "dp")
    cross_gain = P(("tower", "dp"))
    cross = P(("tower", "dp"), None)
    weights = (gain, rows, rows, gain, rows, rows) + (cross_gain,) * 3 + (cross,) * 5
    return jax.shard_map(
        shards,
        mesh=mesh,
        in_specs=(rows, rows, P("dp", None), P("dp")) + weights,
        out_specs=(rows, rows) + weights + (P(),),
        check_vma=False,
    )
```

```python
import functools

import jax
import jax.numpy as jnp
from jax import lax
from jax.experimental import pallas as pl
from jax.experimental.pallas import tpu as pltpu
from jax.sharding import PartitionSpec as P

HD = 64
CAP_LEN = 64
EPSILON = 1e-06
NEGATIVE = -1000000000.0

MESH_ID = pl.DeviceIdType.MESH
ANY = pl.BlockSpec(memory_space=pl.ANY)
VMEM = pl.BlockSpec(memory_space=pltpu.VMEM)


class Net:
    def __init__(self, lines):
        self.lines = lines
        self.tower = lax.axis_index("tower")
        self.dp = lax.axis_index("dp")
        self.core = self.dp % 2
        self.y = (self.dp // 2) % 2
        self.z = self.dp // 4
        self.chip = self.dp // 2
        self.text = self.tower == 1
        self.image = self.tower == 0
        self.low = self.z > 0
        self.high = self.z < lines - 1
        self.sends = []

    def target(self, way):
        if way == "core":
            return (self.tower, self.dp + 1 - 2 * self.core)
        if way == "y":
            return (self.tower, self.dp + 2 - 4 * self.y)
        if way == "x":
            return (1 - self.tower, self.dp)
        if way == "up":
            return (self.tower, jnp.minimum(self.dp + 4, 4 * self.lines - 1))
        return (self.tower, jnp.maximum(self.dp - 4, 0))

    def beyond(self, k):
        return (self.tower, 4 * lax.rem(self.z + k, self.lines) + self.dp % 4)

    def barrier(self):
        sem = pltpu.get_barrier_semaphore()
        partners = [self.target(way) for way in ("core", "y", "x")]
        partners += [self.beyond(k) for k in range(1, self.lines)]
        for partner in partners:
            pl.semaphore_signal(sem, inc=1, device_id=partner, device_id_type=MESH_ID)
        pl.semaphore_wait(sem, len(partners))

    def copy(self, way, src, dst, send_sem, recv_sem):
        return pltpu.make_async_remote_copy(
            src_ref=src,
            dst_ref=dst,
            send_sem=send_sem,
            recv_sem=recv_sem,
            device_id=self.target(way),
            device_id_type=MESH_ID,
        )

    def send(self, way, src, dst, send_sem, recv_sem, there=None):
        copy = self.copy(way, src, dst, send_sem, recv_sem)
        when(there, copy.start)
        self.sends.append((copy, there))

    def arrive(self, src, send_sem, recv_sem, there=None):
        copy = self.copy("core", src, src, send_sem, recv_sem)
        when(there, copy.wait_recv)

    def finish(self):
        for copy, there in self.sends:
            when(there, copy.wait_send)
        self.sends = []


def when(there, act):
    if there is None:
        act()
    else:
        pl.when(there)(act)


def both(*conditions):
    kept = [c for c in conditions if c is not None]
    if not kept:
        return None
    result = kept[0]
    for c in kept[1:]:
        result = jnp.logical_and(result, c)
    return result


class Gather:
    def __init__(self, net, own, place, crossing, send_sem, recv_sem, local_sem, everywhere=False):
        self.net, self.own, self.place, self.crossing = net, own, place, crossing
        self.send_sem, self.recv_sem, self.local_sem = send_sem, recv_sem, local_sem
        lines = net.lines
        self.at_z, self.at_y, self.at_x, self.at_core = 0, 2 * lines, 3 * lines, 5 * lines
        self.to_x = net.image if crossing else None
        self.to_core = net.text if crossing and not everywhere else None

    @staticmethod
    def sems(lines):
        return 11 * lines

    def piece(self, chip, tower=None, core=None):
        net = self.net
        return self.place(
            net.tower if tower is None else tower, chip, net.core if core is None else core
        )

    def pass_on(self, chip, src, there=None, tower=None):
        net = self.net
        dst = self.piece(chip, tower)
        plane = net.tower if tower is None else tower
        if self.crossing and tower is None:
            s = self.at_x + chip
            net.send("x", src, dst, self.send_sem.at[s], self.recv_sem.at[s], both(there, net.image))
        s = self.at_core + plane * 2 * net.lines + chip
        net.send("core", src, dst, self.send_sem.at[s], self.recv_sem.at[s], both(there, self.to_core))

    def start(self):
        net = self.net
        dst = self.piece(net.chip)
        self.local = pltpu.make_async_copy(self.own, dst, self.local_sem)
        self.local.start()
        for way, there, slot in (("up", net.high, 1), ("down", net.low, net.lines + 1)):
            s = self.at_z + slot
            net.send(way, self.own, dst, self.send_sem.at[s], self.recv_sem.at[s], there)
        s = self.at_y + net.z
        net.send("y", self.own, dst, self.send_sem.at[s], self.recv_sem.at[s])
        self.pass_on(net.chip, self.own)

    def hop(self, k):
        net = self.net
        for way, there, further, sign, base in (
            ("up", net.z >= k, net.high, -1, 0),
            ("down", net.z + k < net.lines, net.low, 1, net.lines),
        ):
            z = jnp.clip(net.z + sign * k, 0, net.lines - 1)
            chip = 2 * z + net.y
            src = self.piece(chip)
            s = self.at_z + base + k
            net.arrive(src, self.send_sem.at[s], self.recv_sem.at[s], there)
            if k + 1 < net.lines:
                s = s + 1
                net.send(way, src, src, self.send_sem.at[s], self.recv_sem.at[s], both(there, further))
            s = self.at_y + z
            net.send("y", src, src, self.send_sem.at[s], self.recv_sem.at[s], there)
            self.pass_on(chip, src, there)

    def beside(self, k):
        net = self.net
        ways = ((None, 0),) if k == 0 else ((net.z >= k, -k), (net.z + k < net.lines, k))
        for there, offset in ways:
            z = jnp.clip(net.z + offset, 0, net.lines - 1)
            chip = 2 * z + 1 - net.y
            src = self.piece(chip)
            s = self.at_y + z
            net.arrive(src, self.send_sem.at[s], self.recv_sem.at[s], there)
            self.pass_on(chip, src, there)

    def from_image(self, k):
        if not self.crossing:
            return
        net = self.net
        ways = ((None, 0),) if k == 0 else ((net.z >= k, -k), (net.z + k < net.lines, k))
        for there, offset in ways:
            z = jnp.clip(net.z + offset, 0, net.lines - 1)
            for y in (net.y, 1 - net.y):
                chip = 2 * z + y
                src = self.piece(chip, 0)
                s = self.at_x + chip
                net.arrive(src, self.send_sem.at[s], self.recv_sem.at[s], both(there, net.text))
                self.pass_on(chip, src, both(there, net.text), 0)

    def done(self):
        net = self.net
        self.local.wait()

        def all_of(tower, base):
            def one(chip, carry):
                s = self.at_core + base + chip
                src = self.piece(chip, tower, 1 - net.core)
                net.arrive(src, self.send_sem.at[s], self.recv_sem.at[s])
                return carry

            def run():
                lax.fori_loop(0, 2 * net.lines, one, 0)

            return run

        when(self.to_core, all_of(net.tower, net.tower * 2 * net.lines))
        if self.crossing:
            when(net.text, all_of(0, 0))


class GatherBeside(Gather):
    def start(self):
        net = self.net
        dst = self.piece(net.chip)
        self.local = pltpu.make_async_copy(self.own, dst, self.local_sem)
        self.local.start()
        s = self.at_y
        net.send("y", self.own, dst, self.send_sem.at[s], self.recv_sem.at[s])
        self.set_off(self.own, net.chip, 0)
        self.pass_on(net.chip, self.own)

    def set_off(self, src, chip, second):
        net = self.net
        dst = self.piece(chip)
        for way, there, slot in (("up", net.high, 1), ("down", net.low, net.lines + 1)):
            s = self.z_sem(second) + slot
            net.send(way, src, dst, self.send_sem.at[s], self.recv_sem.at[s], there)

    def z_sem(self, second):
        return 9 * self.net.lines if second else self.at_z

    def hop(self, k):
        net = self.net
        for way, there, further, sign, base in (
            ("up", net.z >= k, net.high, -1, 0),
            ("down", net.z + k < net.lines, net.low, 1, net.lines),
        ):
            z = jnp.clip(net.z + sign * k, 0, net.lines - 1)
            for second, y in ((0, net.y), (1, 1 - net.y)):
                chip = 2 * z + y
                src = self.piece(chip)
                s = self.z_sem(second) + base + k
                net.arrive(src, self.send_sem.at[s], self.recv_sem.at[s], there)
                if k + 1 < net.lines:
                    s = s + 1
                    net.send(
                        way, src, src, self.send_sem.at[s], self.recv_sem.at[s], both(there, further)
                    )
                self.pass_on(chip, src, there)

    def beside(self, k):
        if k > 0:
            return
        net = self.net
        chip = 2 * net.z + 1 - net.y
        src = self.piece(chip)
        s = self.at_y
        net.arrive(src, self.send_sem.at[s], self.recv_sem.at[s])
        self.set_off(src, chip, 1)
        self.pass_on(chip, src)


class Small:
    def __init__(self, net, mine, arrived, sums, wide, send_sem, recv_sem):
        self.net, self.mine, self.arrived, self.sums, self.wide = net, mine, arrived, sums, wide
        self.send_sem, self.recv_sem = send_sem, recv_sem

    def exchange(self, step):
        src = self.mine if step == 0 else self.sums.at[step - 1]
        self.net.send(
            ("core", "y", "x")[step],
            src,
            self.arrived.at[step],
            self.send_sem.at[step],
            self.recv_sem.at[step],
        )

    def collect(self, step):
        self.net.arrive(self.arrived.at[step], self.send_sem.at[step], self.recv_sem.at[step])
        src = self.mine if step == 0 else self.sums.at[step - 1]
        self.sums[step] = src[...] + self.arrived[step]

    def spread(self):
        net = self.net
        for k in range(1, net.lines):
            s = 2 + k
            copy = pltpu.make_async_remote_copy(
                src_ref=self.sums.at[2],
                dst_ref=self.wide.at[k - 1],
                send_sem=self.send_sem.at[s],
                recv_sem=self.recv_sem.at[s],
                device_id=net.beyond(k),
                device_id_type=MESH_ID,
            )
            copy.start()
            net.sends.append((copy, None))

    def total(self, out):
        total = self.sums[2]
        for k in range(1, self.net.lines):
            s = 2 + k
            self.net.arrive(self.wide.at[k - 1], self.send_sem.at[s], self.recv_sem.at[s])
            total = total + self.wide[k - 1]
        out[...] = total


def product(a, b, axis_a=1, axis_b=0):
    return lax.dot_general(
        a, b, (((axis_a,), (axis_b,)), ((), ())), preferred_element_type=jnp.float32
    )


def low(value):
    return value.astype(jnp.bfloat16)


def blocks(count, size, body):
    def one(i, carry):
        body(pl.ds(pl.multiple_of(i * size, size), size))
        return carry

    lax.fori_loop(0, count // size, one, 0)


def row_step(rows):
    return next(s for s in (96, 64, 48, 32, 16) if rows % s == 0)


def centred(value):
    center = value - jnp.mean(value, axis=-1, keepdims=True)
    spread = jnp.mean(center * center, axis=-1, keepdims=True)
    return center * lax.rsqrt(spread + EPSILON), lax.rsqrt(spread + EPSILON)


def norm_rows(src, gain, out, also=None):
    def body(rows):
        value = src[rows, :].astype(jnp.float32)
        if also is not None:
            also(rows, value)
        out[rows, :] = low(centred(value)[0] * gain)

    blocks(src.shape[0], row_step(src.shape[0]), body)


def norm_back_rows(src, gain, grad, done, gain_grad):
    gain_grad[...] = jnp.zeros_like(gain_grad)

    def body(rows):
        n, scale = centred(src[rows, :].astype(jnp.float32))
        out = grad[rows, :]
        dn = out * gain
        gain_grad[...] += jnp.sum(out * n, axis=0, keepdims=True)
        back = dn - jnp.mean(dn, axis=-1, keepdims=True)
        done(rows, (back - n * jnp.mean(dn * n, axis=-1, keepdims=True)) * scale)

    blocks(src.shape[0], row_step(src.shape[0]), body)


class Sums:
    def __init__(self, ref, weight):
        self.ref, self.weight = ref, weight
        ref[...] = jnp.zeros_like(ref)

    def add(self, slot, rows, value):
        kept = jnp.sum(value * value, axis=-1, keepdims=True) * self.weight[rows, :]
        total = jnp.sum(kept, axis=0, keepdims=True)
        at = pl.ds(slot, 1)
        self.ref[at, :] = self.ref[at, :] + jnp.broadcast_to(total, (1, self.ref.shape[1]))

    def line(self):
        shape = self.ref.shape
        row = lax.broadcasted_iota(jnp.int32, shape, 0)
        lane = lax.broadcasted_iota(jnp.int32, shape, 1)
        return jnp.sum(jnp.where(row == lane, self.ref[...], 0.0), axis=0, keepdims=True)


def pair_count(width):
    pairs = width // (2 * HD)
    return next(n for n in (3, 2, 1) if pairs % n == 0)


def attention(query, key, value, allowed, weight, mixed):
    count, width = mixed.shape
    group = pair_count(width)
    left = lax.broadcasted_iota(jnp.int32, (count, 2 * HD), 1) < HD

    def one(step, carry):
        kept, scores = [], []
        for i in range(group):
            pair = step * group + i
            q, k, v = query(pair), key(pair), value(pair)
            zero = jnp.zeros_like(q)
            kept.append((pair, v))
            for part in (jnp.where(left, q, zero), jnp.where(left, zero, q)):
                scores.append(product(part, k, 1, 1) * HD ** (-0.5))
        weights = []
        for s in scores:
            s = jnp.where(allowed[...] > 0, s, NEGATIVE)
            e = jnp.exp(s - jnp.max(s, axis=-1, keepdims=True))
            weights.append(low(e / jnp.sum(e, axis=-1, keepdims=True)))
        for i, (pair, v) in enumerate(kept):
            first, second = weights[2 * i : 2 * i + 2]
            weight[2 * pair] = first
            weight[2 * pair + 1] = second
            both_heads = jnp.where(left, product(first, v), product(second, v))
            mixed[:, pl.ds(pl.multiple_of(pair * 2 * HD, 2 * HD), 2 * HD)] = low(both_heads)
        return carry

    lax.fori_loop(0, width // (2 * HD) // group, one, 0)


def attention_back(query, key, value, grad_mixed, weight, width, done):
    count = weight.shape[1]
    group = pair_count(width)
    left = lax.broadcasted_iota(jnp.int32, (count, 2 * HD), 1) < HD

    def one(step, carry):
        kept, raw = [], []
        for i in range(group):
            pair = step * group + i
            q, k, v, d = query(pair), key(pair), value(pair), grad_mixed(pair)
            zero = jnp.zeros_like(q)
            kept.append((pair, q, k))
            for h, part in enumerate((jnp.where(left, d, zero), jnp.where(left, zero, d))):
                raw.append((part, product(part, v, 1, 1), weight[2 * pair + h]))
        grads = []
        for part, dp, p in raw:
            p32 = p.astype(jnp.float32)
            grads.append(low(p32 * (dp - jnp.sum(dp * p32, axis=-1, keepdims=True))))
        for i, (pair, q, k) in enumerate(kept):
            (d0, _, p0), (d1, _, p1) = raw[2 * i : 2 * i + 2]
            s0, s1 = grads[2 * i : 2 * i + 2]
            zero = jnp.zeros_like(q)
            dv = product(p0, d0, 0, 0) + product(p1, d1, 0, 0)
            dk = product(s0, jnp.where(left, q, zero), 0, 0)
            dk = dk + product(s1, jnp.where(left, zero, q), 0, 0)
            dq = jnp.where(left, product(s0, k), product(s1, k))
            done(pair, low(dq * HD ** (-0.5)), low(dk * HD ** (-0.5)), low(dv))
        return carry

    lax.fori_loop(0, width // (2 * HD) // group, one, 0)


def pairs_of(ref, base=0):
    return lambda pair: ref[:, pl.ds(pl.multiple_of(base + pair * 2 * HD, 2 * HD), 2 * HD)]


def gelu_both(value):
    scale = 0.7978845608028654
    cube = 0.044715
    square = value * value
    bend = jnp.tanh(scale * value * (1.0 + cube * square))
    half = 0.5 * (1.0 + bend)
    slope = half + 0.5 * value * (1.0 - bend * bend) * scale * (1.0 + 3.0 * cube * square)
    return value * half, slope


def activate(wide, active, slope, columns):
    def body(rows):
        a, s = gelu_both(wide[rows, :])
        active[rows, columns] = low(a)
        slope[rows, columns] = s.astype(slope.dtype)

    blocks(wide.shape[0], 16, body)


GATHER = ("qk", "vo", "ca", "u0", "u1", "cu", "d0", "d1", "cd")
GATHER_NAMES = ("qk", "vo", "u0", "u1", "d0", "d1", "ca", "cu", "cd")
LEAD = 2
GATHER_BESIDE = ("cu",)
GATHER_FOUR = (
    "start d0", "start u0", "start vo", "do block", "start cd", "hop d0 1", "start ca", "start u1",
    "beside cd 0", "start cu", "hop ca 1", "hop vo 1", "start qk", "beside u0 0", "hop u0 1",
    "hop ca 2", "hop qk 1", "beside ca 0", "beside vo 0", "hop vo 2", "do gains0", "hop cd 1",
    "hop qk 2", "beside d0 0", "hop ca 3", "hop u0 2", "from_image cu 0", "hop vo 3",
    "from_image ca 0", "beside cu 0", "from_image ca 1", "hop u1 1", "beside d0 1", "beside ca 1",
    "beside vo 1", "start d1", "beside vo 2", "hop cu 1", "beside cd 1", "beside u0 1", "hop d0 2",
    "hop qk 3", "hop d1 1", "beside u1 0", "hop u1 2", "beside qk 0", "beside qk 1", "beside ca 2",
    "beside u0 2", "hop cu 2", "beside qk 2", "from_image cd 0", "do gains1", "from_image cd 1",
    "beside u1 1", "beside vo 3", "beside qk 3", "from_image ca 2", "beside ca 3", "hop u0 3",
    "do gains2", "hop d1 2", "done qk", "do norm", "do qk", "done vo", "do v", "do attend",
    "do out", "beside d0 2", "hop u1 3", "hop cu 3", "from_image cu 1", "hop d0 3", "hop cd 2",
    "from_image ca 3", "beside d1 0", "beside u0 3", "beside u1 2", "done ca", "hop d1 3",
    "done u0", "do up0", "from_image cu 2", "beside d1 1", "from_image cu 3", "beside d0 3",
    "hop cd 3", "beside d1 2", "beside u1 3", "done u1", "do up1", "do keep", "done cu",
    "from_image cd 2", "done d0", "do down0", "from_image cd 3", "beside cd 2", "beside d1 3",
    "beside cd 3", "done d1", "do down1", "do end", "done cd", "do query", "do rows",
)
AFTER = {
    "qk": ("norm", "qk"),
    "vo": ("v", "attend", "out"),
    "u0": ("up0",),
    "u1": ("up1", "keep"),
    "d0": ("down0",),
    "d1": ("down1", "end"),
}


def parsed(lines):
    events = []
    for line in lines:
        kind, name, *k = line.split()
        events.append((kind, name, int(k[0]) if k else 0))
    return events


def gather_order(lines):
    if lines == 4 and GATHER_FOUR:
        return parsed(GATHER_FOUR)
    slots = {}

    def put(slot, kind, name, k=0):
        slots.setdefault(max(slot, 0), []).append((kind, name, k))

    for index, name in enumerate(GATHER):
        late = 1 if name in GATHER_BESIDE else 0
        if name in ("ca", "cu"):
            put(index - LEAD + 1, "do", "block")
        put(index - LEAD + 1, "start", name)
        if late:
            put(index + 1, "beside", name)
        for k in range(1, lines):
            put(index + k + late, "hop", name, k)
        for k in range(late, lines):
            put(index + k + 1, "beside", name, k)
        for k in range(lines):
            put(index + k + 2 + late, "from_image", name, k)
        put(index + lines + 1 + late, "done", name)
        for step in AFTER.get(name, ()):
            put(index + lines + 1 + late, "do", step)
    for index in range(3):
        put(index + 1, "do", "gains%d" % index)
    rank = {"start": 0, "beside": 2, "hop": 1, "from_image": 3, "done": 4, "do": 5}
    events = []
    for slot in sorted(slots):

        def place(event):
            kind, name, k = event
            if kind == "beside" and name in GATHER_BESIDE:
                return 0.5
            if kind == "do" and name == "block":
                return -1
            if kind == "do" and name.startswith("gains"):
                return 0.2
            return rank[kind]

        events += [e for e in sorted(slots[slot], key=place) if e not in events]
    return events + [("do", "query", 0), ("do", "rows", 0)]


def forward_kernel(
    lines, cuts, parts,
    tok, cot, allowed, cross_allowed, row_weight, gvec, own_a, own_d, pack, own_cd,
    full_a, full_d, sum_ca, sum_cd, o_h1, o_qkv, o_mixed, o_weight, o_middle, o_h2, o_active, o_slope,
    gains, layer_out, top, vec,
    w_a, w_d, w_ca, w_cd, h1, qkv, mixed, weight, middle, h2, active, slope, out_y, wide, branch,
    passed, image_out, n_q, n_i, query, keyval, c_mixed, c_weight, c_middle, h3, grad_wide, g_small,
    swap, block, rcv_a, rcv_d, arrived, totals, spread, sums_ref, gain_rows,
    send_sem, recv_sem, local_sem, swap_sem, s_send, s_recv, pass_sem, out_sem, d_send, d_recv, d_local,
):
    net = Net(lines)
    net.barrier()
    text, image = net.text, net.image
    rows, depth = own_a.shape[0], own_d.shape[0]
    few, part = pack.shape[1], own_cd.shape[0]
    width = tok.shape[1]
    half = pack.shape[2]
    a_qkv, a_out = parts[0], parts[0] + parts[1]
    q_end, kv_end, o_end = cuts[0], cuts[0] + cuts[1], cuts[0] + cuts[1] + cuts[2]
    tile = width

    def columns(first, last):
        return lambda tower, chip, core: w_a.at[
            pl.ds(pl.multiple_of((2 * chip + core) * rows, rows), rows), first:last
        ]

    def crossed(first, last):
        return lambda tower, chip, core: w_ca.at[
            core,
            pl.ds(pl.multiple_of((tower * 2 * lines + chip) * 2 * few, 2 * few), 2 * few),
            first:last,
        ]

    def plan(index, own, place, crossing):
        beside = GATHER_NAMES[index] in GATHER_BESIDE
        kind = GatherBeside if beside else Gather
        return kind(
            net, own, place, crossing, send_sem.at[index], recv_sem.at[index], local_sem.at[index]
        )

    def self_part(index, first, last):
        return plan(index, own_a.at[:, first:last], columns(first, last), False)

    def down_part(index, first, last):
        return plan(
            index,
            own_d.at[:, first:last],
            lambda tower, chip, core: w_d.at[
                pl.ds(pl.multiple_of((2 * chip + core) * depth, depth), depth), first:last
            ],
            False,
        )

    def cross_part(index, first, last):
        return plan(index, block.at[:, first:last], crossed(first, last), True)

    mid = a_qkv - width
    jobs = {
        "qk": self_part(0, 0, mid),
        "vo": self_part(1, mid, a_out),
        "u0": self_part(2, a_out, a_out + 2 * width),
        "u1": self_part(3, a_out + 2 * width, own_a.shape[1]),
        "d0": down_part(4, 0, width // 2),
        "d1": down_part(5, width // 2, width),
        "ca": cross_part(6, 0, o_end),
        "cu": cross_part(7, o_end, half),
        "cd": plan(
            8,
            own_cd,
            lambda tower, chip, core: w_cd.at[
                pl.ds(pl.multiple_of((tower * 4 * lines + 2 * chip + core) * part, part), part), :
            ],
            True,
        ),
    }
    kept = []

    def keep(src, dst):
        copy = pltpu.make_async_copy(src, dst, out_sem.at[len(kept)])
        copy.start()
        kept.append(copy)

    swapped = net.copy("core", pack.at[1 - net.core], swap, swap_sem.at[0], swap_sem.at[1])
    swapped.start()
    small = Small(net, gvec, arrived, totals, spread, s_send, s_recv)
    sums = Sums(sums_ref, row_weight)
    base = 4 * net.tower
    gain_rows[...] = jnp.zeros_like(gain_rows)
    first = net.core == 0

    def gain(at):
        return jnp.where(text, gains[at + 2 : at + 3, :], gains[at : at + 1, :])

    def build_block():
        swapped.wait()
        mine = pack[net.core]
        theirs = swap[...]
        block[0:few] = low(jnp.where(first, mine, theirs))
        block[few:] = low(jnp.where(first, theirs, mine))

    def gains_over(index):
        def run():
            small.collect(index)
            if index < 2:
                small.exchange(index + 1)
            else:
                small.spread()

        return run

    def first_norm():
        small.total(gains)
        norm_rows(tok, gain(0), h1, lambda r, v: sums.add(base, r, v))
        keep(h1, o_h1)

    def project(first_column, last_column):
        def run():
            def qkv_tile(i, carry):
                cols = pl.ds(pl.multiple_of(first_column + i * tile, tile), tile)
                qkv[:, cols] = low(product(h1[...], w_a[:, cols]))
                return carry

            lax.fori_loop(0, (last_column - first_column) // tile, qkv_tile, 0)

        return run

    def attend():
        keep(qkv, o_qkv)
        attention(
            pairs_of(qkv), pairs_of(qkv, width), pairs_of(qkv, 2 * width), allowed, weight, mixed
        )
        keep(weight, o_weight)
        keep(mixed, o_mixed)

    def attn_out():
        branch[...] = product(mixed[...], w_a[:, a_qkv:a_out])

        def add_branch(r):
            value = branch[r, :]
            sums.add(base + 1, r, value)
            middle[r, :] = tok[r, :].astype(jnp.float32) + value

        blocks(tok.shape[0], row_step(tok.shape[0]), add_branch)
        keep(middle, o_middle)
        norm_rows(middle, gain(1), h2)
        keep(h2, o_h2)

    def go_up(first_tile, last_tile):
        def run():
            def up_tile(i, carry):
                at = pl.multiple_of((first_tile + i) * tile, tile)
                wide[...] = product(h2[...], w_a[:, pl.ds(a_out + at, tile)])
                activate(wide, active, slope, pl.ds(at, tile))
                return carry

            lax.fori_loop(0, last_tile - first_tile, up_tile, 0)

        return run

    def keep_up():
        keep(active, o_active)
        keep(slope, o_slope)
        keep(w_a, full_a)

    def go_down(first_column, last_column):
        def run():
            branch[:, first_column:last_column] = product(
                active[...], w_d[:, first_column:last_column]
            )

        return run

    def self_end():
        keep(w_d, full_d)

        def add_mlp(r):
            value = branch[r, :]
            sums.add(base + 2, r, value)
            y = middle[r, :] + value
            out_y[r, :] = y
            image_out[r, :] = low(y)

            @pl.when(image)
            def _():
                sums.add(3, r, y)

        blocks(tok.shape[0], row_step(tok.shape[0]), add_mlp)
        net.send("x", image_out, passed, pass_sem.at[0], pass_sem.at[1], image)

    def cross_queries():
        @pl.when(text)
        def _():
            norm_rows(out_y, gains[4:5, :], n_q)
            for h in range(2):
                at = h * cuts[0]
                query[:, at : at + cuts[0]] = low(product(n_q[...], w_ca[h, :, 0:q_end]))

    tiles = active.shape[1] // tile
    steps = {
        "block": build_block,
        "gains0": gains_over(0),
        "gains1": gains_over(1),
        "gains2": gains_over(2),
        "norm": first_norm,
        "qk": project(0, mid),
        "v": project(mid, a_qkv),
        "attend": attend,
        "out": attn_out,
        "up0": go_up(0, tiles // 2),
        "up1": go_up(tiles // 2, tiles),
        "keep": keep_up,
        "down0": go_down(0, width // 2),
        "down1": go_down(width // 2, width),
        "end": self_end,
        "query": cross_queries,
        "rows": lambda: net.arrive(passed, pass_sem.at[0], pass_sem.at[1], text),
    }
    small.exchange(0)
    for kind, name, k in gather_order(lines):
        if kind == "do":
            steps[name]()
        elif kind == "start":
            jobs[name].start()
        elif kind == "done":
            jobs[name].done()
        else:
            getattr(jobs[name], kind)(k)

    net.finish()
    for copy in kept:
        copy.wait()
    def hand(index, src, rcv, there=text):
        net.send("core", src, rcv, d_send.at[index], d_recv.at[index], there)

    def merge(index, own, rcv, out):
        net.arrive(rcv, d_send.at[index], d_recv.at[index], text)

        @pl.when(text)
        def _():
            def add(r):
                rcv[r, :] = low(own[r, :].astype(jnp.float32) + rcv[r, :].astype(jnp.float32))

            blocks(rcv.shape[0], 16, add)
            pltpu.make_async_copy(rcv, out, d_local.at[index]).start()

    @pl.when(text)
    def _():
        norm_rows(passed, gains[5:6, :], n_i)
        for h in range(2):
            at = h * width
            keyval[:, at : at + width] = low(product(n_i[...], w_ca[h, :, q_end:kv_end]))
        attention(
            pairs_of(query), pairs_of(keyval), pairs_of(keyval, width), cross_allowed, c_weight, c_mixed
        )
        for h in range(2):
            at = h * cuts[2]
            branch[:, at : at + cuts[2]] = product(c_mixed[...], w_ca[h, :, kv_end:o_end])

        def add_cross(r):
            value = branch[r, :]
            sums.add(7, r, value)
            c_middle[r, :] = out_y[r, :] + value

        blocks(tok.shape[0], row_step(tok.shape[0]), add_cross)
        norm_rows(c_middle, gains[6:7, :], h3)

        for h in range(2):

            def cross_up(i, carry):
                at = pl.multiple_of(i * tile, tile)
                wide[...] = product(h3[...], w_ca[h, :, pl.ds(o_end + at, tile)])
                activate(wide, active, slope, pl.ds(h * cuts[3] + at, tile))
                return carry

            lax.fori_loop(0, cuts[3] // tile, cross_up, 0)
        branch[...] = product(active[...], w_cd[...])

        def add_final(r):
            value = branch[r, :]
            sums.add(8, r, value)
            z = c_middle[r, :] + value
            sums.add(9, r, z)
            layer_out[r, :] = low(z)

        blocks(tok.shape[0], row_step(tok.shape[0]), add_final)

        def down_tile(i, carry):
            cols = pl.ds(pl.multiple_of(i * tile, tile), tile)
            found = low(product(active[:, cols], cot[...], 0, 0))
            for k in range(tile // part):
                at = (k % 2) * (w_d.shape[0] // 2) + (k // 2) * part + i * (tile // 2)
                w_d[pl.ds(pl.multiple_of(at, part), part), :] = found[k * part : (k + 1) * part]
            grad = product(cot[...], w_cd[cols, :], 1, 1)
            grad_wide[:, cols] = low(grad * slope[:, cols])
            return carry

        lax.fori_loop(0, active.shape[1] // tile, down_tile, 0)

    share = w_d.shape[0] // 2
    hand(0, w_d.at[pl.ds(pl.multiple_of((1 - net.core) * share, share), share), :], rcv_d)

    @pl.when(text)
    def _():
        for h in range(2):

            def up_grad(i, carry):
                at = pl.multiple_of(i * tile, tile)
                w_a[:, pl.ds(h * half + o_end + at, tile)] = low(
                    product(h3[...], grad_wide[:, pl.ds(h * cuts[3] + at, tile)], 0, 0)
                )
                return carry

            lax.fori_loop(0, cuts[3] // tile, up_grad, 0)

    theirs_at = pl.multiple_of((1 - net.core) * half, half)
    mine_at = pl.multiple_of(net.core * half, half)
    hand(1, w_a.at[:, pl.ds(theirs_at + o_end, half - o_end)], rcv_a.at[:, o_end:half])

    @pl.when(text)
    def _():
        branch[...] = product(grad_wide[:, 0 : cuts[3]], w_ca[0, :, o_end:half], 1, 1) + product(
            grad_wide[:, cuts[3] :], w_ca[1, :, o_end:half], 1, 1
        )

        def mid_done(r, back):
            total = cot[r, :].astype(jnp.float32) + back
            c_middle[r, :] = total
            h3[r, :] = low(total)

        norm_back_rows(c_middle, gains[6:7, :], branch, mid_done, g_small)
        gain_rows[6:7, :] = g_small[...]
        for h in range(2):
            at = h * cuts[2]
            w_a[:, h * half + kv_end : h * half + o_end] = low(
                product(c_mixed[...], h3[:, at : at + cuts[2]], 0, 0)
            )
        branch[...] = product(h3[:, 0 : cuts[2]], w_ca[0, :, kv_end:o_end], 1, 1) + product(
            h3[:, cuts[2] :], w_ca[1, :, kv_end:o_end], 1, 1
        )
        c_mixed[...] = low(branch[...])

        def att_done(pair, dq, dk, dv):
            at = pl.multiple_of(pair * 2 * HD, 2 * HD)
            query[:, pl.ds(at, 2 * HD)] = dq
            keyval[:, pl.ds(at, 2 * HD)] = dk
            keyval[:, pl.ds(width + at, 2 * HD)] = dv

        attention_back(
            pairs_of(query),
            pairs_of(keyval),
            pairs_of(keyval, width),
            pairs_of(c_mixed),
            c_weight,
            width,
            att_done,
        )
        branch[...] = product(keyval[:, 0:width], w_ca[0, :, q_end:kv_end], 1, 1) + product(
            keyval[:, width:], w_ca[1, :, q_end:kv_end], 1, 1
        )

        def image_done(r, back):
            image_out[r, :] = low(back)

        norm_back_rows(passed, gains[5:6, :], branch, image_done, g_small)
        gain_rows[5:6, :] = g_small[...]

    net.send("x", image_out, passed, pass_sem.at[0], pass_sem.at[1], text)

    @pl.when(text)
    def _():
        for h in range(2):
            at = h * width
            w_a[:, h * half + q_end : h * half + kv_end] = low(
                product(n_i[...], keyval[:, at : at + width], 0, 0)
            )
            at = h * cuts[0]
            w_a[:, h * half : h * half + q_end] = low(
                product(n_q[...], query[:, at : at + cuts[0]], 0, 0)
            )

    hand(2, w_a.at[:, pl.ds(theirs_at, o_end)], rcv_a.at[:, 0:o_end])
    mine_d = w_d.at[pl.ds(pl.multiple_of(net.core * share, share), share), :]
    merge(0, mine_d, rcv_d, sum_cd)
    merge(
        1,
        w_a.at[:, pl.ds(mine_at + o_end, half - o_end)],
        rcv_a.at[:, o_end:half],
        sum_ca.at[:, o_end:half],
    )

    @pl.when(text)
    def _():
        branch[...] = product(query[:, 0 : cuts[0]], w_ca[0, :, 0:q_end], 1, 1) + product(
            query[:, cuts[0] :], w_ca[1, :, 0:q_end], 1, 1
        )

        def text_done(r, back):
            top[r, :] = c_middle[r, :] + back

        norm_back_rows(out_y, gains[4:5, :], branch, text_done, g_small)
        gain_rows[4:5, :] = g_small[...]
        sums_ref[10:11, :] = jnp.broadcast_to(
            jnp.sum(row_weight[...], axis=0, keepdims=True), (1, sums_ref.shape[1])
        )
        vec[...] = gain_rows[...]

    merge(2, w_a.at[:, pl.ds(mine_at, o_end)], rcv_a.at[:, 0:o_end], sum_ca.at[:, 0:o_end])
    net.arrive(passed, pass_sem.at[0], pass_sem.at[1], image)

    @pl.when(image)
    def _():
        vec[...] = jnp.zeros_like(vec)

        def add_back(r):
            top[r, :] = cot[r, :].astype(jnp.float32) + passed[r, :].astype(jnp.float32)
            layer_out[r, :] = image_out[r, :]

        blocks(tok.shape[0], row_step(tok.shape[0]), add_back)

    vec[7:8, 0 : sums_ref.shape[1]] = sums.line()

    @pl.when(text)
    def _():
        for index, (src, out) in enumerate(
            (
                (rcv_d, sum_cd),
                (rcv_a.at[:, o_end:half], sum_ca.at[:, o_end:half]),
                (rcv_a.at[:, 0:o_end], sum_ca.at[:, 0:o_end]),
            )
        ):
            pltpu.make_async_copy(src, out, d_local.at[index]).wait()

    net.finish()


def forward(lines, cuts, parts, *operands):
    tok, cot, allowed, cross_allowed, row_weight, gvec, own_a, own_d, pack, own_cd = operands
    bf16, f32 = jnp.bfloat16, jnp.float32
    count = 4 * lines
    rows, width = tok.shape
    few, half = pack.shape[1:]
    hidden = count * own_d.shape[0]
    all_a = (count * own_a.shape[0], own_a.shape[1])
    heads_n = width // HD
    jobs = 9
    shape = jax.ShapeDtypeStruct
    wide_b, wide_f = (rows, width), (rows, hidden)
    stored = [
        (wide_b, bf16),
        ((rows, parts[0]), bf16),
        (wide_b, bf16),
        ((heads_n, rows, rows), bf16),
        (wide_b, f32),
        (wide_b, bf16),
        (wide_f, bf16),
        (wide_f, f32),
    ]
    outs = [
        (all_a, bf16),
        ((hidden, width), bf16),
        ((width, half), bf16),
        ((hidden // 2, width), bf16),
        *stored,
        (gvec.shape, f32),
        (wide_b, bf16),
        (wide_b, f32),
        (gvec.shape, f32),
    ]
    scratch = [
        (all_a, bf16),
        ((hidden, width), bf16),
        ((2, width, half), bf16),
        ((hidden, width), bf16),
        *stored,
        (wide_b, f32),
        (wide_b, f32),
        (wide_b, f32),
        (wide_b, bf16),
        (wide_b, bf16),
        (wide_b, bf16),
        (wide_b, bf16),
        (wide_b, bf16),
        ((rows, 2 * width), bf16),
        (wide_b, bf16),
        ((heads_n, rows, rows), bf16),
        (wide_b, f32),
        (wide_b, bf16),
        (wide_f, bf16),
        ((1, width), f32),
        ((few, half), f32),
        ((2 * few, half), bf16),
        ((width, half), bf16),
        ((hidden // 2, width), bf16),
        ((3,) + gvec.shape, f32),
        ((3,) + gvec.shape, f32),
        ((lines - 1,) + gvec.shape, f32),
        ((16, 128), f32),
        (gvec.shape, f32),
    ]
    dma = pltpu.SemaphoreType.DMA
    return pl.pallas_call(
        functools.partial(forward_kernel, lines, cuts, parts),
        out_shape=tuple(shape(*o) for o in outs),
        in_specs=[VMEM] * 6 + [ANY, ANY, VMEM, ANY],
        out_specs=[ANY] * 12 + [VMEM] * 4,
        scratch_shapes=[pltpu.VMEM(*s) for s in scratch]
        + [
            dma((jobs, Gather.sems(lines))),
            dma((jobs, Gather.sems(lines))),
            dma((jobs,)),
            dma((2,)),
            dma((2 + lines,)),
            dma((2 + lines,)),
            dma((2,)),
            dma((12,)),
            dma((3,)),
            dma((3,)),
            dma((3,)),
        ],
        compiler_params=pltpu.CompilerParams(
            collective_id=0, has_side_effects=True, vmem_limit_bytes=63 << 20
        ),
    )(*operands)


class Scatter:
    def __init__(self, net, own, near, far, rcv, sems):
        self.net, self.own, self.near, self.far, self.rcv = net, own, near, far, rcv
        self.send_sem, self.recv_sem = sems

    @staticmethod
    def sems(lines):
        return 1 + 7 * lines

    def sem(self, s):
        return self.send_sem.at[s], self.recv_sem.at[s]

    def add(self, pairs, out):
        def one(r):
            total = pairs[0][r, :].astype(jnp.float32)
            for other in pairs[1:]:
                total = total + other[r, :].astype(jnp.float32)
            out[r, :] = total.astype(out.dtype)

        blocks(out.shape[0], 16, one)

    def chips(self, k):
        net = self.net
        if k == 0:
            return ((None, net.z),)
        return (
            (net.z + k < net.lines, jnp.minimum(net.z + k, net.lines - 1)),
            (net.z >= k, jnp.maximum(net.z - k, 0)),
        )

    def order(self):
        return [pair for k in range(self.net.lines - 1, -1, -1) for pair in self.chips(k)]

    def swap(self, theirs, rcv):
        self.whole = rcv
        self.net.send("core", theirs, rcv, *self.sem(0))

    def swapped(self):
        self.net.arrive(self.whole, *self.sem(0))

    def over_x(self, part):
        net = self.net
        for there, z in self.order():
            for y in (1 - net.y, net.y):
                chip = 2 * z + y
                net.send("x", part(chip), self.own(chip), *self.sem(1 + chip), both(there, net.text))

    def from_x(self, chip, there):
        if self.rcv is None:
            net = self.net
            net.arrive(self.own(chip), *self.sem(1 + chip), both(there, net.image))

    def across(self, only=None):
        net = self.net
        for there, z in self.order():
            there = both(there, only)
            chip = 2 * z + 1 - net.y
            self.from_x(chip, there)
            own = self.own(chip)
            if self.rcv is not None:
                when(there, lambda: self.add([own, self.rcv(chip)], own))
            net.send("y", own, self.near(z), *self.sem(1 + 2 * net.lines + z), there)

    def here(self, chip, z):
        parts = [self.own(chip), self.near(z)]
        return parts if self.rcv is None else parts + [self.rcv(chip)]

    def along(self, k):
        net = self.net
        lines = net.lines
        for up, (there, z) in zip((True, False), self.chips(k)):
            chip = 2 * z + net.y
            base = (1 + 3 * lines) if up else (1 + 4 * lines)
            self.from_x(chip, there)
            net.arrive(self.near(z), *self.sem(1 + 2 * lines + z), there)
            more = net.low if up else net.high
            s = base + z
            net.arrive(self.far(z), *self.sem(s), both(there, more))
            own = self.own(chip)
            parts = self.here(chip, z)
            when(both(there, more), lambda: self.add(parts + [self.far(z)], own))
            when(both(there, jnp.logical_not(more)), lambda: self.add(parts, own))
            slot = z if up else jnp.where(z == net.z - 1, lines, z)
            net.send("up" if up else "down", own, self.far(slot), *self.sem(s), there)

    def turn(self):
        pass

    def total(self, out):
        net = self.net
        lines = net.lines
        self.from_x(net.chip, None)
        net.arrive(self.near(net.z), *self.sem(1 + 2 * lines + net.z))
        net.arrive(self.far(net.z), *self.sem(1 + 3 * lines + net.z), net.low)
        net.arrive(self.far(lines), *self.sem(1 + 4 * lines + net.z), net.high)
        parts = self.here(net.chip, net.z)
        low_part, high_part = self.far(net.z), self.far(lines)
        when(both(net.low, net.high), lambda: self.add(parts + [low_part, high_part], out))
        when(jnp.logical_not(net.low), lambda: self.add(parts + [high_part], out))
        when(jnp.logical_not(net.high), lambda: self.add(parts + [low_part], out))


class ScatterAlong(Scatter):
    def across(self, only=None):
        pass

    def spot(self, z, second):
        if not second:
            return self.far(z)
        if isinstance(z, int):
            return self.extra(0)
        return self.near(z)

    def line_sems(self, up, second):
        lines = self.net.lines
        return 1 + (3 + 2 * second + (0 if up else 1)) * lines

    def parts(self, chip):
        return [self.own(chip)] if self.rcv is None else [self.own(chip), self.rcv(chip)]

    def along(self, k):
        net = self.net
        for up, (there, z) in zip((True, False), self.chips(k)):
            for second, y in ((0, net.y), (1, 1 - net.y)):
                chip = 2 * z + y
                self.from_x(chip, there)
                more = net.low if up else net.high
                s = self.line_sems(up, second) + z
                net.arrive(self.spot(z, second), *self.sem(s), both(there, more))
                own = self.own(chip)
                parts = self.parts(chip)
                with_far = parts + [self.spot(z, second)]
                when(both(there, more), lambda: self.add(with_far, own))
                if len(parts) > 1:
                    when(both(there, jnp.logical_not(more)), lambda: self.add(parts, own))
                way = "up" if up else "down"
                if up:
                    net.send(way, own, self.spot(z, second), *self.sem(s), there)
                else:
                    last = z == net.z - 1
                    net.send(
                        way, own, self.spot(net.lines, second), *self.sem(s), both(there, last)
                    )
                    net.send(
                        way,
                        own,
                        self.spot(z, second),
                        *self.sem(s),
                        both(there, jnp.logical_not(last)),
                    )

    def gathered(self, second, more, out):
        net = self.net
        lines = net.lines
        chip = 2 * net.z + (1 - net.y if second else net.y)
        self.from_x(chip, None)
        s = self.line_sems(True, second) + net.z
        net.arrive(self.spot(net.z, second), *self.sem(s), net.low)
        s = self.line_sems(False, second) + net.z
        net.arrive(self.spot(lines, second), *self.sem(s), net.high)
        parts = self.parts(chip) + more
        low_part, high_part = self.spot(net.z, second), self.spot(lines, second)
        when(both(net.low, net.high), lambda: self.add(parts + [low_part, high_part], out))
        when(jnp.logical_not(net.low), lambda: self.add(parts + [high_part], out))
        when(jnp.logical_not(net.high), lambda: self.add(parts + [low_part], out))

    def turn(self):
        net = self.net
        own = self.own(2 * net.z + 1 - net.y)
        self.gathered(1, [], own)
        net.send("y", own, self.extra(1), *self.sem(1 + 2 * net.lines))

    def total(self, out):
        self.net.arrive(self.extra(1), *self.sem(1 + 2 * self.net.lines))
        self.gathered(0, [self.extra(1)], out)


def strip(ref, size, first, last):
    return lambda i: ref.at[pl.ds(pl.multiple_of(i * size, size), size), first:last]


def backward_kernel(
    lines, cuts, parts,
    tok, top_in, gains, vec_in, full_a, full_d, sum_ca, sum_cd,
    i_h1, i_qkv, i_mixed, i_weight, i_middle, i_h2, i_active, i_slope,
    o_qkv, o_out, o_up, o_d, o_cq, o_ckv, o_co, o_cu, o_cd, input_grad, o_vec,
    h1, qkv, mixed, weight, middle, h2, active, slope,
    g_a, g_d, rcv_a, rcv_d, near_a, near_d, far_a, far_d,
    own_ca, own_cd, near_ca, near_cd, far_ca, far_cd,
    w_d, w_up, top, branch, n_grad, g_small, vec, fin, fin_vo, extra_d, swap, arrived, totals, spread,
    send_sem, recv_sem, load_sem, swap_sem, s_send, s_recv,
):
    net = Net(lines)
    net.barrier()
    text, image = net.text, net.image
    width = tok.shape[1]
    tile = width
    rows, depth = o_qkv.shape[0], o_d.shape[0]
    few, part = 2 * o_cq.shape[0], o_cd.shape[0]
    half = own_ca.shape[1]
    a_out = parts[0] + parts[1]
    all_a = g_a.shape[2]
    o_end = cuts[0] + cuts[1] + cuts[2]
    theirs = 1 - net.core

    def load(index, src, dst):
        copy = pltpu.make_async_copy(src, dst, load_sem.at[index])
        copy.start()
        return copy

    l_active = load(0, i_active, active)
    l_wd = load(1, full_d, w_d)
    l_slope = load(2, i_slope, slope)
    l_h2 = load(3, i_h2, h2)
    l_up = load(4, full_a.at[:, a_out:], w_up)
    l_middle = load(5, i_middle, middle)
    l_mixed = load(6, i_mixed, mixed)
    l_qkv = load(7, i_qkv, qkv)
    l_weight = load(8, i_weight, weight)
    l_h1 = load(9, i_h1, h1)

    def job(index, own, near, far, rcv, extra=None):
        kind = ScatterAlong if SCATTER_NAMES[index] in SCATTER_ALONG else Scatter
        made = kind(net, own, near, far, rcv, (send_sem.at[index], recv_sem.at[index]))
        made.extra = extra
        return made

    def self_a(index, first, last):
        return job(
            index,
            strip(g_a.at[net.core], rows, first, last),
            strip(near_a, rows, first, last),
            strip(far_a, rows, first, last),
            strip(rcv_a, rows, first, last),
        )

    def cross_a(index, first, last):
        return job(
            index,
            strip(own_ca, few, first, last),
            strip(near_ca, few, first, last),
            strip(far_ca, few, first, last),
            None,
        )

    def self_d(index, first, last):
        return job(
            index,
            strip(g_d.at[net.core], depth, first, last),
            strip(near_d, depth, first, last),
            strip(far_d, depth, first, last),
            strip(rcv_d, depth, first, last),
            strip(extra_d, depth, first, last),
        )

    mid, middle_up, middle_d = parts[0] - width, a_out + 2 * width, width // 2
    jobs = {
        "d0": self_d(0, 0, middle_d),
        "d1": self_d(1, middle_d, width),
        "u0": self_a(2, a_out, middle_up),
        "u1": self_a(3, middle_up, all_a),
        "qk": self_a(4, 0, mid),
        "vo": self_a(5, mid, a_out),
        "cd": job(
            6,
            strip(own_cd, part, 0, width),
            strip(near_cd, part, 0, width),
            strip(far_cd, part, 0, width),
            None,
        ),
        "cu": cross_a(7, o_end, half),
        "ca": cross_a(8, 0, o_end),
    }

    def swap_a(name, first, last):
        jobs[name].swap(g_a.at[theirs, :, first:last], rcv_a.at[:, first:last])

    def swap_d(name, first, last):
        jobs[name].swap(g_d.at[theirs, :, first:last], rcv_d.at[:, first:last])

    def across(name, only=None):
        if jobs[name].rcv is not None:
            jobs[name].swapped()
        jobs[name].across(only)

    plane_a, plane_d = own_ca.shape[0], own_cd.shape[0]
    c_loads = (
        pltpu.make_async_copy(sum_cd.at[plane_d : 2 * plane_d, :], own_cd, load_sem.at[10]),
        pltpu.make_async_copy(sum_ca.at[plane_a : 2 * plane_a, :], own_ca, load_sem.at[11]),
    )

    @pl.when(text)
    def _():
        for copy in c_loads:
            copy.start()

    def start_x(name):
        at = {"cd": (sum_cd, part, 0, width), "cu": (sum_ca, few, o_end, half), "ca": (sum_ca, few, 0, o_end)}
        jobs[name].over_x(strip(*at[name]))

    def round_top():
        def body(r):
            n_grad[r, :] = low(top_in[r, :])

        blocks(tok.shape[0], row_step(tok.shape[0]), body)

        @pl.when(text)
        def _():
            for copy in c_loads:
                copy.wait()

    def down_grads():
        l_active.wait()
        l_wd.wait()
        l_slope.wait()

        def down_tile(i, carry):
            cols = pl.ds(pl.multiple_of(i * tile, tile), tile)
            found = low(product(active[:, cols], n_grad[...], 0, 0))
            each = tile // depth
            for k in range(each):
                at = pl.multiple_of(((i * each + k) // 2) * depth, depth)
                g_d[k % 2, pl.ds(at, depth), :] = found[k * depth : (k + 1) * depth]
            grad = product(n_grad[...], w_d[cols, :], 1, 1)
            active[:, cols] = low(grad * slope[:, cols])
            return carry

        lax.fori_loop(0, active.shape[1] // tile, down_tile, 0)
        for i in range(4):
            src = full_a.at[:, i * width : (i + 1) * width]
            l_four.append(load(12 + i, src, w_d.at[i * width : (i + 1) * width, :]))
        l_h2.wait()

    l_four = []

    def put_a(found, at):
        for k in range(width // rows):
            g_a[k % 2, (k // 2) * rows : (k // 2 + 1) * rows, pl.ds(at, found.shape[1])] = found[
                k * rows : (k + 1) * rows
            ]

    def up_grads(first_tile, last_tile):
        def run():
            def up_tile(i, carry):
                at = pl.multiple_of(i * tile, tile)
                found = low(product(h2[...], active[:, pl.ds(at, tile)], 0, 0))
                put_a(found, pl.multiple_of(a_out + at, tile))
                return carry

            lax.fori_loop(first_tile, last_tile, up_tile, 0)

        return run

    def own_gain(at):
        return jnp.where(text, gains[at + 2 : at + 3, :], gains[at : at + 1, :])

    at_vec = 2 * net.tower

    def mid_grads():
        l_up.wait()
        branch[...] = product(active[...], w_up[...], 1, 1)
        l_middle.wait()

        def mid_done(r, back):
            total = top_in[r, :] + back
            top[r, :] = total
            n_grad[r, :] = low(total)

        norm_back_rows(middle, own_gain(1), branch, mid_done, g_small)
        vec[...] = vec_in[...]
        vec[pl.ds(at_vec + 1, 1), :] = g_small[...]

    def out_grads():
        l_mixed.wait()
        for copy in l_four:
            copy.wait()
        put_a(low(product(mixed[...], n_grad[...], 0, 0)), parts[0])
        mixed[...] = low(product(n_grad[...], w_d[3 * width : 4 * width, :], 1, 1))

    def att_grads():
        l_qkv.wait()
        l_weight.wait()

        def att_done(pair, dq, dk, dv):
            at = pl.multiple_of(pair * 2 * HD, 2 * HD)
            for k, grad in enumerate((dq, dk, dv)):
                qkv[:, pl.ds(pl.multiple_of(k * width + at, 2 * HD), 2 * HD)] = grad

        attention_back(
            pairs_of(qkv),
            pairs_of(qkv, width),
            pairs_of(qkv, 2 * width),
            pairs_of(mixed),
            weight,
            width,
            att_done,
        )
        l_h1.wait()

    def qkv_grads(first_tile, last_tile):
        def run():
            def qkv_tile(i, carry):
                at = pl.multiple_of(i * tile, tile)
                put_a(low(product(h1[...], qkv[:, pl.ds(at, tile)], 0, 0)), at)
                return carry

            lax.fori_loop(first_tile, last_tile, qkv_tile, 0)

        return run

    small = Small(net, vec, arrived, totals, spread, s_send, s_recv)

    def first_grads():
        branch[...] = (
            product(qkv[:, 0:width], w_d[0:width, :], 1, 1)
            + product(qkv[:, width : 2 * width], w_d[width : 2 * width, :], 1, 1)
            + product(qkv[:, 2 * width :], w_d[2 * width : 3 * width, :], 1, 1)
        )

        def first_done(r, back):
            input_grad[r, :] = top[r, :] + back

        norm_back_rows(tok, own_gain(0), branch, first_done, g_small)
        vec[pl.ds(at_vec, 1), :] = g_small[...]
        small.exchange(0)

    def small_step(index):
        def run():
            small.collect(index)
            if index < 2:
                small.exchange(index + 1)
            else:
                small.spread()

        return run

    up_tiles = (all_a - a_out) // tile
    steps = {
        "top": round_top,
        "down": down_grads,
        "up0": up_grads(0, up_tiles // 2),
        "up1": up_grads(up_tiles // 2, up_tiles),
        "mid": mid_grads,
        "out": out_grads,
        "att": att_grads,
        "qk": qkv_grads(0, mid // tile),
        "v": qkv_grads(mid // tile, parts[0] // tile),
        "first": first_grads,
        "small0": small_step(0),
        "small1": small_step(1),
        "small2": small_step(2),
    }
    share = few // 2
    first = net.core == 0
    swaps = {}

    def start_swap(name, index, first_column, last_column):
        copy = net.copy(
            "core",
            fin.at[pl.ds(pl.multiple_of(theirs * share, share), share), first_column:last_column],
            swap.at[:, first_column:last_column],
            swap_sem.at[index, 0],
            swap_sem.at[index, 1],
        )
        copy.start()
        swaps[name] = copy

    def put_cross(out, at, n):
        mine = fin[pl.ds(pl.multiple_of(net.core * share, share), share), at : at + n]
        other = swap[:, at : at + n]
        out[:, 0:n] = jnp.where(first, mine, other)
        out[:, n:] = jnp.where(first, other, mine)

    def put_vo():
        o_qkv[:, mid:] = fin_vo[:, 0 : parts[0] - mid]
        o_out[...] = fin_vo[:, parts[0] - mid :]

    totals_to = {
        "d0": (o_d.at[:, 0:middle_d], None),
        "d1": (o_d.at[:, middle_d:], None),
        "u0": (o_up.at[:, 0 : middle_up - a_out], None),
        "u1": (o_up.at[:, middle_up - a_out :], None),
        "qk": (o_qkv.at[:, 0:mid], None),
        "vo": (fin_vo, put_vo),
        "cd": (o_cd, None),
        "cu": (fin.at[:, o_end:half], lambda: start_swap("cu", 0, o_end, half)),
        "ca": (fin.at[:, 0:o_end], lambda: start_swap("ca", 1, 0, o_end)),
    }
    spans = {
        "d0": (0, middle_d),
        "d1": (middle_d, width),
        "u0": (a_out, middle_up),
        "u1": (middle_up, all_a),
        "qk": (0, mid),
        "vo": (mid, a_out),
    }
    for kind, name, k in scatter_order(lines):
        if kind == "do":
            steps[name]()
        elif kind == "x":
            start_x(name)
        elif kind == "swap":
            (swap_d if name in ("d0", "d1") else swap_a)(name, *spans[name])
        elif kind == "across":
            across(name, (None, text, image)[k])
        elif kind == "along":
            jobs[name].along(k)
        elif kind == "turn":
            jobs[name].turn()
        else:
            out, then = totals_to[name]
            jobs[name].total(out)
            if then is not None:
                then()
    small.total(o_vec)
    swaps["cu"].wait()
    put_cross(o_cu, o_end, cuts[3])
    swaps["ca"].wait()
    at = 0
    for out, n in zip((o_cq, o_ckv, o_co), cuts):
        put_cross(out, at, n)
        at += n
    net.finish()


SCATTER = ("d0", "d1", "u0", "u1", "cd", "qk", "vo", "cu", "ca")
SCATTER_NAMES = ("d0", "d1", "u0", "u1", "qk", "vo", "cd", "cu", "ca")
SCATTER_ALONG = ("d0", "d1")
BEFORE = {0: ("qk", "vo", "cd"), 3: ("cu",), 5: ("ca",)}
SCATTER_HEAD = (
    "x cd", "x cu", "x ca", "do top", "across cd 1", "do down", "swap d0", "swap d1", "do up0", "swap u0",
    "across d0", "do up1", "swap u1", "across d1", "do mid", "across u0", "across u1", "do out", "do att",
    "do qk", "swap qk", "do v", "swap vo", "do first",
)


def scatter_order(lines):
    if lines == 4 and SCATTER_FOUR:
        return parsed(SCATTER_FOUR)
    events = parsed(SCATTER_HEAD)
    count = len(SCATTER)
    for slot in range(count + lines):
        for name in BEFORE.get(slot, ()):
            events.append(("across", name, 2 if name == "cd" else 0))
        if 1 <= slot <= 3:
            events.append(("do", "small%d" % (slot - 1), 0))
        for k in range(lines - 1, -2, -1):
            index = slot - (lines - 1 - k)
            if 0 <= index < count:
                kind = "along" if k > 0 else "turn" if k == 0 else "total"
                events.append((kind, SCATTER[index], k))
    return events


SCATTER_FOUR = (
    "do top", "do down", "swap d0", "swap d1", "do up0", "x cd", "x cu", "swap u0", "across d0",
    "along d0 3", "across d1", "do up1", "swap u1", "along d1 3", "across u0", "across cd 1",
    "do mid", "along u0 3", "across u1", "do out", "along d1 2", "do att", "x ca", "along d0 2",
    "across cd 2", "along u0 2", "do qk", "along d1 1", "along cd 3", "along u1 3", "swap qk",
    "along cd 2", "across cu", "along u0 1", "along cu 3", "do v", "along d0 1", "along cu 2",
    "along cd 1", "across qk", "along qk 3", "along cu 1", "swap vo", "do first", "along u1 2",
    "across ca", "across vo", "do small0", "along ca 3", "turn d0", "turn d1", "do small1",
    "along u1 1", "along qk 2", "along qk 1", "do small2", "along vo 3", "along ca 2", "along vo 2",
    "total u0", "along ca 1", "total u1", "along vo 1", "total d0", "total qk", "total cu",
    "total cd", "total d1", "total ca", "total vo",
)


def backward(lines, cuts, parts, own_shapes, *operands):
    bf16, f32 = jnp.bfloat16, jnp.float32
    tok, top, gains, vec, full_a, full_d, sum_ca, sum_cd = operands[:8]
    stored = [(o.shape, o.dtype) for o in operands[8:]]
    chips = 2 * lines
    row_count, width = tok.shape
    hidden, all_a = full_d.shape[0], full_a.shape[1]
    half = sum_ca.shape[1]
    rows, depth = width // (2 * chips), hidden // (2 * chips)
    few, part = width // (2 * chips), hidden // (4 * chips)
    outs = [*own_shapes, (row_count, width), vec.shape]
    rcv_a, rcv_d = (chips * rows, all_a), (chips * depth, width)
    own_ca, own_cd = (chips * few, half), (chips * part, width)

    def line(size, count):
        return (size * count, all_a), (depth * count, width)

    scratch = [
        *stored,
        ((2,) + rcv_a, bf16),
        ((2,) + rcv_d, bf16),
        (rcv_a, bf16),
        (rcv_d, bf16),
        ((lines * rows, all_a), bf16),
        ((lines * depth, width), bf16),
        (((lines + 1) * rows, all_a), bf16),
        (((lines + 1) * depth, width), bf16),
        (own_ca, bf16),
        (own_cd, bf16),
        ((lines * few, half), bf16),
        ((lines * part, width), bf16),
        (((lines + 1) * few, half), bf16),
        (((lines + 1) * part, width), bf16),
        ((hidden, width), bf16),
        ((width, hidden), bf16),
        ((row_count, width), f32),
        ((row_count, width), f32),
        ((row_count, width), bf16),
        ((1, width), f32),
        (vec.shape, f32),
        ((rows, half), f32),
        ((rows, 2 * width), f32),
        ((2 * depth, width), bf16),
        ((few // 2, half), f32),
        ((3,) + vec.shape, f32),
        ((3,) + vec.shape, f32),
        ((lines - 1,) + vec.shape, f32),
    ]
    dma = pltpu.SemaphoreType.DMA
    return pl.pallas_call(
        functools.partial(backward_kernel, lines, cuts, parts),
        out_shape=tuple(jax.ShapeDtypeStruct(s, f32) for s in outs),
        in_specs=[VMEM] * 4 + [ANY] * 12,
        out_specs=[VMEM] * len(outs),
        scratch_shapes=[pltpu.VMEM(*s) for s in scratch]
        + [
            dma((9, Scatter.sems(lines))),
            dma((9, Scatter.sems(lines))),
            dma((16,)),
            dma((2, 2)),
            dma((2 + lines,)),
            dma((2 + lines,)),
        ],
        compiler_params=pltpu.CompilerParams(
            collective_id=1, has_side_effects=True, vmem_limit_bytes=63 << 20
        ),
    )(*operands)


def plain_gather(own_a, own_d, pack, own_cd, own_g):
    axes = ("tower", "dp")
    tiles = lax.all_gather(own_g, axes, axis=0)
    return (
        lax.all_gather(own_a, "dp", axis=0, tiled=True),
        lax.all_gather(own_d, "dp", axis=0, tiled=True),
        lax.all_gather(pack.astype(jnp.bfloat16), axes, axis=1, tiled=True),
        lax.all_gather(own_cd, axes, axis=0, tiled=True),
        tiles.reshape((2, -1) + own_g.shape),
    )


def plain_scatter(g_a, g_d, g_ca, g_cd, vec, parts, cuts):
    axes = ("tower", "dp")

    def added(grad, over, axis):
        return lax.psum_scatter(
            grad.astype(jnp.float32), over, scatter_dimension=axis, tiled=True
        )

    a = added(g_a.reshape(-1, g_a.shape[-1]), "dp", 0)
    d = added(g_d.reshape(-1, g_d.shape[-1]), "dp", 0)
    ca = added(g_ca.reshape(2, -1, g_ca.shape[-1]), axes, 1)
    cd = added(g_cd.reshape(-1, g_cd.shape[-1]), axes, 0)
    at = [sum(cuts[:i]) for i in range(len(cuts) + 1)]
    cross = [
        jnp.concatenate([ca[0][:, i:j], ca[1][:, i:j]], axis=1) for i, j in zip(at[:-1], at[1:])
    ]
    first, second = parts[0], parts[0] + parts[1]
    self_parts = [a[:, :first], a[:, first:second], a[:, second:]]
    return (*self_parts, d, *cross, cd, lax.psum(vec, axes))


def layer_norm(value_matrix, norm_gain):
    center = value_matrix - jnp.mean(value_matrix, axis=-1, keepdims=True)
    spread = jnp.mean(center * center, axis=-1, keepdims=True)
    return center * lax.rsqrt(spread + EPSILON) * norm_gain


def norm_back(value_matrix, norm_gain, grad_out):
    result, puller = jax.vjp(layer_norm, value_matrix, norm_gain)
    return puller(grad_out)


def dot(a, b):
    return jnp.dot(a, b, preferred_element_type=jnp.float32)


def dot_tn(a, b):
    return jnp.einsum("rd,re->de", a, b, preferred_element_type=jnp.float32)


def dot_nt(a, b):
    return jnp.einsum("re,de->rd", a, b, preferred_element_type=jnp.float32)


def low(value_matrix):
    return value_matrix.astype(jnp.bfloat16)


def masks(counts, lengths, row_count, decoder):
    row_index = jnp.arange(row_count, dtype=jnp.int32)
    bounds = jnp.cumsum(counts)
    image_of = jnp.sum((row_index[:, None] >= bounds[None, :]).astype(jnp.int32), axis=1)
    caption_of = row_index // CAP_LEN
    in_place = row_index - caption_of * CAP_LEN
    caption_slots = jnp.arange(lengths.shape[0], dtype=jnp.int32)
    length_rows = jnp.sum(
        jnp.where(caption_of[:, None] == caption_slots[None, :], lengths[None, :], 0), axis=1
    )
    valid_rows = in_place < length_rows
    image_mask = image_of[:, None] == image_of[None, :]
    text_mask = (
        (caption_of[:, None] == caption_of[None, :])
        & (in_place[None, :] <= in_place[:, None])
        & valid_rows[None, :]
    )
    cross_mask = caption_of[:, None] == image_of[None, :]
    return jnp.where(decoder, text_mask, image_mask), cross_mask, valid_rows


def heads(value_matrix):
    return value_matrix.reshape(value_matrix.shape[0], -1, HD)


def attend(query, key, value, allowed):
    scores = jnp.einsum(
        "qhd,khd->hqk", heads(query), heads(key), preferred_element_type=jnp.float32
    ) * HD ** (-0.5)
    weight = jax.nn.softmax(jnp.where(allowed[None], scores, NEGATIVE), axis=-1)
    mixed = jnp.einsum("hqk,khd->qhd", low(weight), heads(value), preferred_element_type=jnp.float32)
    return low(mixed.reshape(query.shape)), weight


def attend_back(query, key, value, weight, grad_mixed):
    grad_mixed = heads(grad_mixed)
    grad_value = jnp.einsum("hqk,qhd->khd", low(weight), grad_mixed, preferred_element_type=jnp.float32)
    grad_weight = jnp.einsum("qhd,khd->hqk", grad_mixed, heads(value), preferred_element_type=jnp.float32)
    grad_score = low(
        weight * (grad_weight - jnp.sum(grad_weight * weight, axis=-1, keepdims=True))
    )
    grad_query = jnp.einsum(
        "hqk,khd->qhd", grad_score, heads(key), preferred_element_type=jnp.float32
    ) * HD ** (-0.5)
    grad_key = jnp.einsum(
        "hqk,qhd->khd", grad_score, heads(query), preferred_element_type=jnp.float32
    ) * HD ** (-0.5)
    return tuple(low(g.reshape(query.shape)) for g in (grad_query, grad_key, grad_value))


def mlp_forward(stream, gain, up, down):
    hidden = low(layer_norm(stream, gain))
    wide = dot(hidden, up)
    active = low(jax.nn.gelu(wide))
    return dot(active, down), (hidden, wide, active)


def mlp_back(stream, gain, up, down, stored, grad):
    hidden, wide, active = stored
    branch = low(grad)
    grad_down = dot_tn(active, branch)
    result, puller = jax.vjp(jax.nn.gelu, wide)
    grad_wide = low(puller(dot_nt(branch, down))[0])
    grad_up = dot_tn(hidden, grad_wide)
    grad_stream, grad_gain = norm_back(stream, gain, dot_nt(grad_wide, up))
    return grad + grad_stream, grad_gain, grad_up, grad_down


def squares(value_matrix, row_weight):
    return jnp.sum(row_weight[:, None] * value_matrix * value_matrix)


def plain_shards(
    tokens, cotangent, kept_counts, caption_lengths, attn_gain, qkv_weight, attn_out, mlp_gain,
    mlp_up, mlp_down, query_gain, image_gain, cross_gain, cross_query, cross_keyval, cross_out,
    cross_up, cross_down,
):
    f32 = jnp.float32
    dp_count = lax.axis_size("dp")
    lines = dp_count // 4
    tower, dp = lax.axis_index("tower"), lax.axis_index("dp")
    decoder = tower == 1
    row_count, width = tokens.shape[1:]
    rows = attn_gain.shape[1]
    few = query_gain.shape[0]

    def tile_row(value):
        return jnp.pad(value.astype(f32), (0, 128 - value.shape[0]))

    gain_tile = jnp.stack(
        [tile_row(attn_gain[0]), tile_row(mlp_gain[0])]
        + [tile_row(g) for g in (query_gain, image_gain, cross_gain)]
        + [jnp.zeros((128,), f32)] * 3
    )
    cross_shards = (cross_query, cross_keyval, cross_out, cross_up)
    cuts = tuple(w.shape[1] // 2 for w in cross_shards)
    pack = jnp.stack(
        [
            jnp.concatenate([w[:, h * n : (h + 1) * n] for w, n in zip(cross_shards, cuts)], axis=1)
            for h in range(2)
        ]
    ).astype(f32)
    self_parts = (qkv_weight.shape[2], attn_out.shape[2], mlp_up.shape[2])
    own_a = jnp.concatenate([qkv_weight[0], attn_out[0], mlp_up[0]], axis=1)
    full_a, full_d, full_ca, full_cd, full_g = plain_gather(
        own_a, mlp_down[0], pack, cross_down, gain_tile
    )
    qkv = full_a[:, : self_parts[0]]
    out = full_a[:, self_parts[0] : self_parts[0] + self_parts[1]]
    up = full_a[:, self_parts[0] + self_parts[1] :]
    down = full_d
    plane_gains = lax.dynamic_index_in_dim(full_g, tower, 0, keepdims=False)
    gain_1 = plane_gains[:, 0, :rows].reshape(-1)
    gain_2 = plane_gains[:, 1, :rows].reshape(-1)
    gain_q, gain_i, gain_c = (full_g[:, :, 2 + i, :few].reshape(-1) for i in range(3))

    stream = tokens[0].astype(f32)
    upstream = cotangent[0].astype(f32)
    allowed, cross_allowed, valid_rows = masks(kept_counts[0], caption_lengths, row_count, decoder)
    row_weight = jnp.where(decoder, valid_rows, True).astype(f32)

    normed = low(layer_norm(stream, gain_1))
    joined = low(dot(normed, qkv))
    query, key, value = jnp.split(joined, 3, axis=1)
    mixed, weight = attend(query, key, value, allowed)
    attn_branch = dot(mixed, out)
    middle = stream + attn_branch
    mlp_branch, mlp_stored = mlp_forward(middle, gain_2, up, down)
    layer_y = middle + mlp_branch
    image_rows = low(layer_y)
    arrived = lax.ppermute(image_rows, "tower", [(0, 1)])

    def run_cross(operands):
        text_y, image_in = operands
        at = [0]
        for n in cuts:
            at.append(at[-1] + n)
        cq, ckv, co, cu = (
            jnp.concatenate([full_ca[0][:, a:b], full_ca[1][:, a:b]], axis=1)
            for a, b in zip(at[:-1], at[1:])
        )
        image_in = image_in.astype(f32)
        image_normed = low(layer_norm(image_in, gain_i))
        keyval = low(dot(image_normed, ckv))
        c_key, c_value = jnp.split(keyval, 2, axis=1)
        c_normed = low(layer_norm(text_y, gain_q))
        c_query = low(dot(c_normed, cq))
        c_mixed, c_weight = attend(c_query, c_key, c_value, cross_allowed)
        c_branch = dot(c_mixed, co)
        c_middle = text_y + c_branch
        c_mlp, c_stored = mlp_forward(c_middle, gain_c, cu, full_cd)
        final_rows = c_middle + c_mlp
        grad_middle, grad_gain_c, grad_cu, grad_cd = mlp_back(
            c_middle, gain_c, cu, full_cd, c_stored, upstream
        )
        grad_branch = low(grad_middle)
        grad_co = dot_tn(c_mixed, grad_branch)
        grad_q, grad_k, grad_v = attend_back(
            c_query, c_key, c_value, c_weight, low(dot_nt(grad_branch, co))
        )
        grad_cq = dot_tn(c_normed, grad_q)
        grad_text, grad_gain_q = norm_back(text_y, gain_q, dot_nt(grad_q, cq))
        grad_keyval = jnp.concatenate([grad_k, grad_v], axis=1)
        grad_ckv = dot_tn(image_normed, grad_keyval)
        grad_image, grad_gain_i = norm_back(image_in, gain_i, dot_nt(grad_keyval, ckv))
        cross_sums = jnp.stack(
            [
                squares(c_branch, row_weight),
                squares(c_mlp, row_weight),
                squares(final_rows, row_weight),
            ]
        )
        grads = tuple(low(g) for g in (grad_cq, grad_ckv, grad_co, grad_cu))
        grad_ca = jnp.stack(
            [
                jnp.concatenate([g[:, h * n : (h + 1) * n] for g, n in zip(grads, cuts)], axis=1)
                for h in range(2)
            ]
        )
        return (
            low(final_rows),
            grad_middle + grad_text,
            low(grad_image),
            grad_ca,
            low(grad_cd),
            jnp.concatenate([grad_gain_q, grad_gain_i, grad_gain_c]),
            cross_sums,
        )

    def skip_cross(operands):
        shapes = jax.eval_shape(run_cross, operands)
        return tuple(jnp.zeros(s.shape, s.dtype) for s in shapes)

    final_rows, grad_text, grad_image, grad_ca, grad_cd, grad_cross_gains, cross_sums = lax.cond(
        decoder, run_cross, skip_cross, (layer_y, arrived)
    )
    returned = lax.ppermute(grad_image, "tower", [(1, 0)]).astype(f32)
    grad_top = jnp.where(decoder, grad_text, upstream + returned)

    grad_middle, grad_gain_2, grad_up, grad_down = mlp_back(
        middle, gain_2, up, down, mlp_stored, grad_top
    )
    grad_branch = low(grad_middle)
    grad_out = dot_tn(mixed, grad_branch)
    grad_joined = jnp.concatenate(
        attend_back(query, key, value, weight, low(dot_nt(grad_branch, out))), axis=1
    )
    grad_qkv = dot_tn(normed, grad_joined)
    grad_stream, grad_gain_1 = norm_back(stream, gain_1, dot_nt(grad_joined, qkv))
    grad_stream = grad_middle + grad_stream

    layer_sums = jnp.stack(
        [
            squares(stream, row_weight),
            squares(attn_branch, row_weight),
            squares(mlp_branch, row_weight),
            squares(layer_y, row_weight),
        ]
    )
    encoder_part = jnp.where(decoder, 0.0, layer_sums)
    decoder_part = jnp.where(decoder, jnp.concatenate([layer_sums[:3], cross_sums]), 0.0)
    counted = jnp.where(decoder, jnp.sum(valid_rows.astype(f32)), 0.0)
    line = tile_row(jnp.concatenate([encoder_part, decoder_part, counted[None]]))
    self_gains = jnp.concatenate([grad_gain_1, grad_gain_2])
    zero = jnp.zeros_like(self_gains)
    vec = jnp.concatenate(
        [
            jnp.where(decoder, zero, self_gains),
            jnp.where(decoder, self_gains, zero),
            grad_cross_gains,
            line,
        ]
    ).reshape(-1, 128)
    vec = jnp.pad(vec, ((0, -vec.shape[0] % 8), (0, 0)))
    grad_a = jnp.concatenate([low(grad_qkv), low(grad_out), low(grad_up)], axis=1)
    chips = 2 * lines
    results = plain_scatter(
        grad_a.reshape(chips, 2, rows, -1),
        low(grad_down).reshape(chips, 2, -1, width),
        grad_ca.reshape(2, 2, chips, 2 * few, -1),
        grad_cd.reshape(2, chips, 2, -1, width),
        vec,
        self_parts,
        cuts,
    )
    o_qkv, o_out, o_up, o_d, o_cq, o_ckv, o_co, o_cu, o_cd, o_vec = results
    flat = o_vec.reshape(-1)
    own_gains = lax.dynamic_slice(flat, (tower * 2 * width,), (2 * width,))
    g_1, g_2 = (lax.dynamic_slice(own_gains, (i * width + dp * rows,), (rows,)) for i in range(2))
    g_q, g_i, g_c = (
        lax.dynamic_slice(
            flat, ((4 + i) * width + (tower * dp_count + dp) * few,), (few,)
        )
        for i in range(3)
    )
    sums = flat[7 * width : 7 * width + 11]
    encoder_count = jnp.full((4,), float(row_count * dp_count), f32)
    divisor = jnp.concatenate([encoder_count, jnp.full((6,), 1.0, f32) * sums[10]]) * width
    rms_values = jnp.sqrt(sums[:10] / divisor)
    layer_out = jnp.where(decoder, final_rows, image_rows)
    return (
        layer_out[None], grad_stream[None], g_1[None], o_qkv[None], o_out[None], g_2[None],
        o_up[None], o_d[None], g_q, g_i, g_c, o_cq, o_ckv, o_co, o_cu, o_cd, rms_values,
    )


def fused_shards(
    tokens, cotangent, kept_counts, caption_lengths, attn_gain, qkv_weight, attn_out, mlp_gain,
    mlp_up, mlp_down, query_gain, image_gain, cross_gain, cross_query, cross_keyval, cross_out,
    cross_up, cross_down,
):
    f32 = jnp.float32
    dp_count = lax.axis_size("dp")
    lines = dp_count // 4
    tower, dp = lax.axis_index("tower"), lax.axis_index("dp")
    decoder = tower == 1
    row_count, width = tokens.shape[1:]
    rows = attn_gain.shape[1]
    few = query_gain.shape[0]
    lane = jnp.arange(width)

    def in_place(value, index):
        n = value.shape[0]
        return jnp.where(lane // n == index, jnp.tile(value.astype(f32), width // n), 0.0)

    first, second = in_place(attn_gain[0], dp), in_place(mlp_gain[0], dp)
    zero = jnp.zeros_like(first)
    gvec = jnp.stack(
        [
            jnp.where(decoder, zero, first),
            jnp.where(decoder, zero, second),
            jnp.where(decoder, first, zero),
            jnp.where(decoder, second, zero),
        ]
        + [in_place(g, tower * dp_count + dp) for g in (query_gain, image_gain, cross_gain)]
        + [zero]
    )
    cross_shards = (cross_query, cross_keyval, cross_out, cross_up)
    cuts = tuple(w.shape[1] // 2 for w in cross_shards)
    pack = jnp.stack(
        [
            jnp.concatenate([w[:, h * n : (h + 1) * n] for w, n in zip(cross_shards, cuts)], axis=1)
            for h in range(2)
        ]
    ).astype(f32)
    parts = (qkv_weight.shape[2], attn_out.shape[2], mlp_up.shape[2])
    own_a = jnp.concatenate([qkv_weight[0], attn_out[0], mlp_up[0]], axis=1)
    allowed, cross_allowed, valid_rows = masks(kept_counts[0], caption_lengths, row_count, decoder)
    row_weight = jnp.where(decoder, valid_rows, True).astype(f32)[:, None]
    (
        full_a, full_d, sum_ca, sum_cd, h1, qkv, mixed, weight, middle, h2, active, slope,
        gains, layer_out, top, vec,
    ) = forward(
        lines, cuts, parts, tokens[0], cotangent[0], allowed.astype(f32), cross_allowed.astype(f32),
        row_weight, gvec, own_a, mlp_down[0], pack, cross_down,
    )
    shard_shapes = [
        w.shape[-2:]
        for w in (
            qkv_weight, attn_out, mlp_up, mlp_down, cross_query, cross_keyval, cross_out, cross_up,
            cross_down,
        )
    ]
    o_qkv, o_out, o_up, o_d, o_cq, o_ckv, o_co, o_cu, o_cd, input_grad, o_vec = backward(
        lines, cuts, parts, shard_shapes, tokens[0], top, gains, vec, full_a, full_d, sum_ca,
        sum_cd, h1, qkv, mixed, weight, middle, h2, active, slope,
    )
    g_1, g_2 = (
        lax.dynamic_slice(o_vec, (2 * tower + i, dp * rows), (1, rows)) for i in range(2)
    )
    g_q, g_i, g_c = (
        lax.dynamic_slice(o_vec, (4 + i, (tower * dp_count + dp) * few), (1, few))[0]
        for i in range(3)
    )
    sums = o_vec[7]
    encoder_count = jnp.full((4,), float(row_count * dp_count), f32)
    divisor = jnp.concatenate([encoder_count, jnp.full((6,), 1.0, f32) * sums[10]]) * width
    rms_values = jnp.sqrt(sums[:10] / divisor)
    return (
        layer_out[None], input_grad[None], g_1, o_qkv[None], o_out[None], g_2, o_up[None],
        o_d[None], g_q, g_i, g_c, o_cq, o_ckv, o_co, o_cu, o_cd, rms_values,
    )


def shards(*arrays):
    dp_count = lax.axis_size("dp")
    cross_query, cross_down = arrays[13], arrays[17]
    fills = dp_count % 4 == 0 and dp_count > 4
    fills = fills and cross_query.shape[0] % 8 == 0 and cross_down.shape[0] % 16 == 0
    return fused_shards(*arrays) if fills else plain_shards(*arrays)


def solution(mesh):
    rows = P("tower", "dp", None)
    gain = P("tower", "dp")
    cross_gain = P(("tower", "dp"))
    cross = P(("tower", "dp"), None)
    weights = (gain, rows, rows, gain, rows, rows) + (cross_gain,) * 3 + (cross,) * 5
    return jax.shard_map(
        shards,
        mesh=mesh,
        in_specs=(rows, rows, P("dp", None), P("dp")) + weights,
        out_specs=(rows, rows) + weights + (P(),),
        check_vma=False,
    )
```

```python
import functools

import jax
import jax.numpy as jnp
from jax import lax
from jax.experimental import pallas as pl
from jax.experimental.pallas import tpu as pltpu
from jax.sharding import PartitionSpec as P

HD = 64
CAP_LEN = 64
EPSILON = 1e-06
NEGATIVE = -1000000000.0

MESH_ID = pl.DeviceIdType.MESH
ANY = pl.BlockSpec(memory_space=pl.ANY)
VMEM = pl.BlockSpec(memory_space=pltpu.VMEM)
SMEM = pl.BlockSpec(memory_space=pltpu.SMEM)


class Net:
    def __init__(self, lines):
        self.lines = lines
        self.tower = lax.axis_index("tower")
        self.dp = lax.axis_index("dp")
        self.core = self.dp % 2
        self.y = (self.dp // 2) % 2
        self.z = self.dp // 4
        self.chip = self.dp // 2
        self.text = self.tower == 1
        self.image = self.tower == 0
        self.low = self.z > 0
        self.high = self.z < lines - 1
        self.sends = []

    def target(self, way):
        if way == "core":
            return (self.tower, self.dp + 1 - 2 * self.core)
        if way == "y":
            return (self.tower, self.dp + 2 - 4 * self.y)
        if way == "x":
            return (1 - self.tower, self.dp)
        if way == "up":
            return (self.tower, jnp.minimum(self.dp + 4, 4 * self.lines - 1))
        return (self.tower, jnp.maximum(self.dp - 4, 0))

    def beyond(self, k):
        return (self.tower, 4 * lax.rem(self.z + k, self.lines) + self.dp % 4)

    def barrier(self):
        sem = pltpu.get_barrier_semaphore()
        partners = [self.target(way) for way in ("core", "y", "x")]
        partners += [self.beyond(k) for k in range(1, self.lines)]
        for partner in partners:
            pl.semaphore_signal(sem, inc=1, device_id=partner, device_id_type=MESH_ID)
        pl.semaphore_wait(sem, len(partners))

    def copy(self, way, src, dst, send_sem, recv_sem):
        return pltpu.make_async_remote_copy(
            src_ref=src,
            dst_ref=dst,
            send_sem=send_sem,
            recv_sem=recv_sem,
            device_id=self.target(way),
            device_id_type=MESH_ID,
        )

    def send(self, way, src, dst, send_sem, recv_sem, there=None):
        copy = self.copy(way, src, dst, send_sem, recv_sem)
        when(there, copy.start)
        self.sends.append((copy, there))

    def arrive(self, src, send_sem, recv_sem, there=None):
        copy = self.copy("core", src, src, send_sem, recv_sem)
        when(there, copy.wait_recv)

    def finish(self):
        for copy, there in self.sends:
            when(there, copy.wait_send)
        self.sends = []


def when(there, act):
    if there is None:
        act()
    else:
        pl.when(there)(act)


def both(*conditions):
    kept = [c for c in conditions if c is not None]
    if not kept:
        return None
    result = kept[0]
    for c in kept[1:]:
        result = jnp.logical_and(result, c)
    return result


class Gather:
    def __init__(self, net, own, place, crossing, send_sem, recv_sem, local_sem, everywhere=False):
        self.net, self.own, self.place, self.crossing = net, own, place, crossing
        self.send_sem, self.recv_sem, self.local_sem = send_sem, recv_sem, local_sem
        lines = net.lines
        self.at_z, self.at_y, self.at_x, self.at_core = 0, 2 * lines, 3 * lines, 5 * lines
        self.to_x = net.image if crossing else None
        self.to_core = net.text if crossing and not everywhere else None

    @staticmethod
    def sems(lines):
        return 11 * lines

    def piece(self, chip, tower=None, core=None):
        net = self.net
        return self.place(
            net.tower if tower is None else tower, chip, net.core if core is None else core
        )

    def pass_on(self, chip, src, there=None, tower=None):
        net = self.net
        dst = self.piece(chip, tower)
        plane = net.tower if tower is None else tower
        if self.crossing and tower is None:
            s = self.at_x + chip
            net.send("x", src, dst, self.send_sem.at[s], self.recv_sem.at[s], both(there, net.image))
        s = self.at_core + plane * 2 * net.lines + chip
        net.send("core", src, dst, self.send_sem.at[s], self.recv_sem.at[s], both(there, self.to_core))

    def start(self):
        net = self.net
        dst = self.piece(net.chip)
        self.local = None
        if self.own is None:
            self.own = dst
        else:
            self.local = pltpu.make_async_copy(self.own, dst, self.local_sem)
            self.local.start()
        for way, there, slot in (("up", net.high, 1), ("down", net.low, net.lines + 1)):
            s = self.at_z + slot
            net.send(way, self.own, dst, self.send_sem.at[s], self.recv_sem.at[s], there)
        s = self.at_y + net.z
        net.send("y", self.own, dst, self.send_sem.at[s], self.recv_sem.at[s])
        self.pass_on(net.chip, self.own)

    def hop(self, k):
        net = self.net
        for way, there, further, sign, base in (
            ("up", net.z >= k, net.high, -1, 0),
            ("down", net.z + k < net.lines, net.low, 1, net.lines),
        ):
            z = jnp.clip(net.z + sign * k, 0, net.lines - 1)
            chip = 2 * z + net.y
            src = self.piece(chip)
            s = self.at_z + base + k
            net.arrive(src, self.send_sem.at[s], self.recv_sem.at[s], there)
            if k + 1 < net.lines:
                s = s + 1
                net.send(way, src, src, self.send_sem.at[s], self.recv_sem.at[s], both(there, further))
            s = self.at_y + z
            net.send("y", src, src, self.send_sem.at[s], self.recv_sem.at[s], there)
            self.pass_on(chip, src, there)

    def beside(self, k):
        net = self.net
        ways = ((None, 0),) if k == 0 else ((net.z >= k, -k), (net.z + k < net.lines, k))
        for there, offset in ways:
            z = jnp.clip(net.z + offset, 0, net.lines - 1)
            chip = 2 * z + 1 - net.y
            src = self.piece(chip)
            s = self.at_y + z
            net.arrive(src, self.send_sem.at[s], self.recv_sem.at[s], there)
            self.pass_on(chip, src, there)

    def from_image(self, k):
        if not self.crossing:
            return
        net = self.net
        ways = ((None, 0),) if k == 0 else ((net.z >= k, -k), (net.z + k < net.lines, k))
        for there, offset in ways:
            z = jnp.clip(net.z + offset, 0, net.lines - 1)
            for y in (net.y, 1 - net.y):
                chip = 2 * z + y
                src = self.piece(chip, 0)
                s = self.at_x + chip
                net.arrive(src, self.send_sem.at[s], self.recv_sem.at[s], both(there, net.text))
                self.pass_on(chip, src, both(there, net.text), 0)

    def done(self):
        net = self.net
        if self.local is not None:
            self.local.wait()

        def all_of(tower, base):
            def one(chip, carry):
                s = self.at_core + base + chip
                src = self.piece(chip, tower, 1 - net.core)
                net.arrive(src, self.send_sem.at[s], self.recv_sem.at[s])
                return carry

            def run():
                lax.fori_loop(0, 2 * net.lines, one, 0)

            return run

        when(self.to_core, all_of(net.tower, net.tower * 2 * net.lines))
        if self.crossing:
            when(net.text, all_of(0, 0))


class GatherBeside(Gather):
    def start(self):
        net = self.net
        dst = self.piece(net.chip)
        self.local = None
        if self.own is None:
            self.own = dst
        else:
            self.local = pltpu.make_async_copy(self.own, dst, self.local_sem)
            self.local.start()
        s = self.at_y
        net.send("y", self.own, dst, self.send_sem.at[s], self.recv_sem.at[s])
        self.set_off(self.own, net.chip, 0)
        self.pass_on(net.chip, self.own)

    def set_off(self, src, chip, second):
        net = self.net
        dst = self.piece(chip)
        for way, there, slot in (("up", net.high, 1), ("down", net.low, net.lines + 1)):
            s = self.z_sem(second) + slot
            net.send(way, src, dst, self.send_sem.at[s], self.recv_sem.at[s], there)

    def z_sem(self, second):
        return 9 * self.net.lines if second else self.at_z

    def hop(self, k):
        net = self.net
        for way, there, further, sign, base in (
            ("up", net.z >= k, net.high, -1, 0),
            ("down", net.z + k < net.lines, net.low, 1, net.lines),
        ):
            z = jnp.clip(net.z + sign * k, 0, net.lines - 1)
            for second, y in ((0, net.y), (1, 1 - net.y)):
                chip = 2 * z + y
                src = self.piece(chip)
                s = self.z_sem(second) + base + k
                net.arrive(src, self.send_sem.at[s], self.recv_sem.at[s], there)
                if k + 1 < net.lines:
                    s = s + 1
                    net.send(
                        way, src, src, self.send_sem.at[s], self.recv_sem.at[s], both(there, further)
                    )
                self.pass_on(chip, src, there)

    def beside(self, k):
        if k > 0:
            return
        net = self.net
        chip = 2 * net.z + 1 - net.y
        src = self.piece(chip)
        s = self.at_y
        net.arrive(src, self.send_sem.at[s], self.recv_sem.at[s])
        self.set_off(src, chip, 1)
        self.pass_on(chip, src)


class Small:
    def __init__(self, net, mine, arrived, sums, wide, send_sem, recv_sem):
        self.net, self.mine, self.arrived, self.sums, self.wide = net, mine, arrived, sums, wide
        self.send_sem, self.recv_sem = send_sem, recv_sem

    def exchange(self, step):
        src = self.mine if step == 0 else self.sums.at[step - 1]
        self.net.send(
            ("core", "y", "x")[step],
            src,
            self.arrived.at[step],
            self.send_sem.at[step],
            self.recv_sem.at[step],
        )

    def collect(self, step):
        self.net.arrive(self.arrived.at[step], self.send_sem.at[step], self.recv_sem.at[step])
        src = self.mine if step == 0 else self.sums.at[step - 1]
        self.sums[step] = src[...] + self.arrived[step]

    def spread(self):
        net = self.net
        for k in range(1, net.lines):
            s = 2 + k
            copy = pltpu.make_async_remote_copy(
                src_ref=self.sums.at[2],
                dst_ref=self.wide.at[k - 1],
                send_sem=self.send_sem.at[s],
                recv_sem=self.recv_sem.at[s],
                device_id=net.beyond(k),
                device_id_type=MESH_ID,
            )
            copy.start()
            net.sends.append((copy, None))

    def total(self, out):
        total = self.sums[2]
        for k in range(1, self.net.lines):
            s = 2 + k
            self.net.arrive(self.wide.at[k - 1], self.send_sem.at[s], self.recv_sem.at[s])
            total = total + self.wide[k - 1]
        out[...] = total


def product(a, b, axis_a=1, axis_b=0):
    return lax.dot_general(
        a, b, (((axis_a,), (axis_b,)), ((), ())), preferred_element_type=jnp.float32
    )


def low(value):
    return value.astype(jnp.bfloat16)


def blocks(count, size, body):
    def one(i, carry):
        body(pl.ds(pl.multiple_of(i * size, size), size))
        return carry

    lax.fori_loop(0, count // size, one, 0)


def row_step(rows):
    return next(s for s in (96, 64, 48, 32, 16) if rows % s == 0)


def centred(value):
    center = value - jnp.mean(value, axis=-1, keepdims=True)
    spread = jnp.mean(center * center, axis=-1, keepdims=True)
    return center * lax.rsqrt(spread + EPSILON), lax.rsqrt(spread + EPSILON)


def norm_rows(src, gain, out, also=None):
    def body(rows):
        value = src[rows, :].astype(jnp.float32)
        if also is not None:
            also(rows, value)
        out[rows, :] = low(centred(value)[0] * gain)

    blocks(src.shape[0], row_step(src.shape[0]), body)


def norm_back_rows(src, gain, grad, done, gain_grad):
    gain_grad[...] = jnp.zeros_like(gain_grad)

    def body(rows):
        n, scale = centred(src[rows, :].astype(jnp.float32))
        out = grad[rows, :]
        dn = out * gain
        gain_grad[...] += jnp.sum(out * n, axis=0, keepdims=True)
        back = dn - jnp.mean(dn, axis=-1, keepdims=True)
        done(rows, (back - n * jnp.mean(dn * n, axis=-1, keepdims=True)) * scale)

    blocks(src.shape[0], row_step(src.shape[0]), body)


class Sums:
    def __init__(self, ref, weight):
        self.ref, self.weight = ref, weight
        ref[...] = jnp.zeros_like(ref)

    def add(self, slot, rows, value):
        kept = jnp.sum(value * value, axis=-1, keepdims=True) * self.weight[rows, :]
        total = jnp.sum(kept, axis=0, keepdims=True)
        at = pl.ds(slot, 1)
        self.ref[at, :] = self.ref[at, :] + jnp.broadcast_to(total, (1, self.ref.shape[1]))

    def line(self):
        shape = self.ref.shape
        row = lax.broadcasted_iota(jnp.int32, shape, 0)
        lane = lax.broadcasted_iota(jnp.int32, shape, 1)
        return jnp.sum(jnp.where(row == lane, self.ref[...], 0.0), axis=0, keepdims=True)


def pair_count(width):
    pairs = width // (2 * HD)
    return next(n for n in (3, 2, 1) if pairs % n == 0)


def attention(query, key, value, allowed, weight, mixed):
    count, width = mixed.shape
    group = pair_count(width)
    left = lax.broadcasted_iota(jnp.int32, (count, 2 * HD), 1) < HD

    def one(step, carry):
        kept, scores = [], []
        for i in range(group):
            pair = step * group + i
            q, k, v = query(pair), key(pair), value(pair)
            zero = jnp.zeros_like(q)
            kept.append((pair, v))
            for part in (jnp.where(left, q, zero), jnp.where(left, zero, q)):
                scores.append(product(part, k, 1, 1) * HD ** (-0.5))
        weights = []
        for s in scores:
            s = jnp.where(allowed[...] > 0, s, NEGATIVE)
            e = jnp.exp(s - jnp.max(s, axis=-1, keepdims=True))
            weights.append(low(e / jnp.sum(e, axis=-1, keepdims=True)))
        for i, (pair, v) in enumerate(kept):
            first, second = weights[2 * i : 2 * i + 2]
            weight[2 * pair] = first
            weight[2 * pair + 1] = second
            both_heads = jnp.where(left, product(first, v), product(second, v))
            mixed[:, pl.ds(pl.multiple_of(pair * 2 * HD, 2 * HD), 2 * HD)] = low(both_heads)
        return carry

    lax.fori_loop(0, width // (2 * HD) // group, one, 0)


def attention_back(query, key, value, grad_mixed, weight, width, done):
    count = weight.shape[1]
    group = pair_count(width)
    left = lax.broadcasted_iota(jnp.int32, (count, 2 * HD), 1) < HD

    def one(step, carry):
        kept, raw = [], []
        for i in range(group):
            pair = step * group + i
            q, k, v, d = query(pair), key(pair), value(pair), grad_mixed(pair)
            zero = jnp.zeros_like(q)
            kept.append((pair, q, k))
            for h, part in enumerate((jnp.where(left, d, zero), jnp.where(left, zero, d))):
                raw.append((part, product(part, v, 1, 1), weight[2 * pair + h]))
        grads = []
        for part, dp, p in raw:
            p32 = p.astype(jnp.float32)
            grads.append(low(p32 * (dp - jnp.sum(dp * p32, axis=-1, keepdims=True))))
        for i, (pair, q, k) in enumerate(kept):
            (d0, _, p0), (d1, _, p1) = raw[2 * i : 2 * i + 2]
            s0, s1 = grads[2 * i : 2 * i + 2]
            zero = jnp.zeros_like(q)
            dv = product(p0, d0, 0, 0) + product(p1, d1, 0, 0)
            dk = product(s0, jnp.where(left, q, zero), 0, 0)
            dk = dk + product(s1, jnp.where(left, zero, q), 0, 0)
            dq = jnp.where(left, product(s0, k), product(s1, k))
            done(pair, low(dq * HD ** (-0.5)), low(dk * HD ** (-0.5)), low(dv))
        return carry

    lax.fori_loop(0, width // (2 * HD) // group, one, 0)


def pairs_of(ref, base=0):
    return lambda pair: ref[:, pl.ds(pl.multiple_of(base + pair * 2 * HD, 2 * HD), 2 * HD)]


def gelu_both(value):
    scale = 0.7978845608028654
    cube = 0.044715
    square = value * value
    bend = jnp.tanh(scale * value * (1.0 + cube * square))
    half = 0.5 * (1.0 + bend)
    slope = half + 0.5 * value * (1.0 - bend * bend) * scale * (1.0 + 3.0 * cube * square)
    return value * half, slope


def activate(wide, active, slope, columns):
    def body(rows):
        a, s = gelu_both(wide[rows, :])
        active[rows, columns] = low(a)
        slope[rows, columns] = s.astype(slope.dtype)

    blocks(wide.shape[0], 16, body)


GATHER = ("qk", "vo", "ca", "u0", "u1", "cu", "d0", "d1", "cd")
GATHER_NAMES = ("qk", "vo", "u0", "u1", "d0", "d1", "ca", "cu", "cd")
LEAD = 2
GATHER_BESIDE = ("cu",)
GATHER_FOUR = (
    "start d0", "start u0", "start vo", "do block", "start cd", "hop d0 1", "start ca", "start u1",
    "beside cd 0", "start cu", "hop ca 1", "hop vo 1", "start qk", "beside u0 0", "hop u0 1",
    "hop ca 2", "hop qk 1", "beside ca 0", "beside vo 0", "hop vo 2", "do gains0", "hop cd 1",
    "hop qk 2", "beside d0 0", "hop ca 3", "hop u0 2", "from_image cu 0", "hop vo 3",
    "from_image ca 0", "beside cu 0", "from_image ca 1", "hop u1 1", "beside d0 1", "beside ca 1",
    "beside vo 1", "start d1", "beside vo 2", "hop cu 1", "beside cd 1", "beside u0 1", "hop d0 2",
    "hop qk 3", "hop d1 1", "beside u1 0", "hop u1 2", "beside qk 0", "beside qk 1", "beside ca 2",
    "beside u0 2", "hop cu 2", "beside qk 2", "from_image cd 0", "do gains1", "from_image cd 1",
    "beside u1 1", "beside vo 3", "beside qk 3", "from_image ca 2", "beside ca 3", "hop u0 3",
    "do gains2", "hop d1 2", "done qk", "do norm", "do qk", "done vo", "do v", "do attend",
    "do out", "beside d0 2", "hop u1 3", "hop cu 3", "from_image cu 1", "hop d0 3", "hop cd 2",
    "from_image ca 3", "beside d1 0", "beside u0 3", "beside u1 2", "done ca", "hop d1 3",
    "done u0", "do up0", "from_image cu 2", "beside d1 1", "from_image cu 3", "beside d0 3",
    "hop cd 3", "beside d1 2", "beside u1 3", "done u1", "do up1", "do keep", "done cu",
    "from_image cd 2", "done d0", "do down0", "from_image cd 3", "beside cd 2", "beside d1 3",
    "beside cd 3", "done d1", "do down1", "do end", "done cd", "do query", "do rows",
)
AFTER = {
    "qk": ("norm", "qk"),
    "vo": ("v", "attend", "out"),
    "u0": ("up0",),
    "u1": ("up1", "keep"),
    "d0": ("down0",),
    "d1": ("down1", "end"),
}


def parsed(lines):
    events = []
    for line in lines:
        kind, name, *k = line.split()
        events.append((kind, name, int(k[0]) if k else 0))
    return events


def gather_order(lines):
    if lines == 4 and GATHER_FOUR:
        return parsed(GATHER_FOUR)
    slots = {}

    def put(slot, kind, name, k=0):
        slots.setdefault(max(slot, 0), []).append((kind, name, k))

    for index, name in enumerate(GATHER):
        late = 1 if name in GATHER_BESIDE else 0
        if name in ("ca", "cu"):
            put(index - LEAD + 1, "do", "block")
        put(index - LEAD + 1, "start", name)
        if late:
            put(index + 1, "beside", name)
        for k in range(1, lines):
            put(index + k + late, "hop", name, k)
        for k in range(late, lines):
            put(index + k + 1, "beside", name, k)
        for k in range(lines):
            put(index + k + 2 + late, "from_image", name, k)
        put(index + lines + 1 + late, "done", name)
        for step in AFTER.get(name, ()):
            put(index + lines + 1 + late, "do", step)
    for index in range(3):
        put(index + 1, "do", "gains%d" % index)
    rank = {"start": 0, "beside": 2, "hop": 1, "from_image": 3, "done": 4, "do": 5}
    events = []
    for slot in sorted(slots):

        def place(event):
            kind, name, k = event
            if kind == "beside" and name in GATHER_BESIDE:
                return 0.5
            if kind == "do" and name == "block":
                return -1
            if kind == "do" and name.startswith("gains"):
                return 0.2
            return rank[kind]

        events += [e for e in sorted(slots[slot], key=place) if e not in events]
    return events + [("do", "query", 0), ("do", "rows", 0)]


def place_gains(net, own, cross, out):
    width = out.shape[1]

    def placed(gain, index):
        count = gain.shape[1]
        lane = lax.broadcasted_iota(jnp.int32, (count, width), 1)
        row = lax.broadcasted_iota(jnp.int32, (count, width), 0)
        pick = jnp.where(lane == index * count + row, 1.0, 0.0)
        many = jnp.broadcast_to(gain[...].astype(jnp.float32), (8, count))
        return product(low(many), low(pick))[0:1]

    out[...] = jnp.zeros_like(out)
    for i, gain in enumerate(own):
        row = placed(gain, net.dp)
        out[i : i + 1, :] = jnp.where(net.image, row, 0.0)
        out[i + 2 : i + 3, :] = jnp.where(net.text, row, 0.0)
    for i, gain in enumerate(cross):
        out[4 + i : 5 + i, :] = placed(gain, net.tower * 4 * net.lines + net.dp)


def fill_masks(net, counts, lengths, allowed, cross_allowed, row_weight):
    shape = allowed.shape

    def place(index):
        image_of, bound = jnp.zeros_like(index), jnp.int32(0)
        for i in range(counts.shape[1]):
            bound = bound + counts[0, i]
            image_of = image_of + jnp.where(index >= bound, 1, 0)
        caption_of = index // CAP_LEN
        within = index - caption_of * CAP_LEN
        length = jnp.zeros_like(index)
        for i in range(lengths.shape[0]):
            length = jnp.where(caption_of == i, lengths[i], length)
        return image_of, caption_of, within, within < length

    row = place(lax.broadcasted_iota(jnp.int32, shape, 0))
    key = place(lax.broadcasted_iota(jnp.int32, shape, 1))
    image_mask = row[0] == key[0]
    text_mask = (row[1] == key[1]) & (key[2] <= row[2]) & key[3]
    here = jnp.where(net.text, text_mask.astype(jnp.float32), image_mask.astype(jnp.float32))
    allowed[...] = here
    cross_allowed[...] = (row[1] == key[0]).astype(jnp.float32)
    valid = place(lax.broadcasted_iota(jnp.int32, row_weight.shape, 0))[3]
    row_weight[...] = jnp.where(net.text, valid.astype(jnp.float32), 1.0)


def forward_kernel(
    lines, cuts, parts,
    counts, lengths, g_attn, g_mlp, g_query, g_image, g_cross, tok, cot, cq, ckv, co, cu, own_qkv, own_out, own_up, own_d, own_cd,
    full_a, full_d, sum_ca, sum_cd, o_h1, o_qkv, o_mixed, o_weight, o_middle, o_h2, o_active, o_slope,
    gains, layer_out, top, vec,
    w_a, w_d, w_ca, w_cd, h1, qkv, mixed, weight, middle, h2, active, slope, out_y, wide, branch,
    passed, image_out, n_q, n_i, query, keyval, c_mixed, c_weight, c_middle, h3, grad_wide, g_small,
    allowed, cross_allowed, row_weight, gvec, pack, swap, block, rcv_a, rcv_d, arrived, totals, spread, sums_ref, gain_rows,
    send_sem, recv_sem, local_sem, swap_sem, s_send, s_recv, pass_sem, out_sem, d_send, d_recv, d_local, own_sem,
):
    net = Net(lines)
    text, image = net.text, net.image
    rows, depth = own_qkv.shape[0], own_d.shape[0]
    all_a = sum(parts)
    few, part = pack.shape[1], own_cd.shape[0]
    width = tok.shape[1]
    half = pack.shape[2]
    a_qkv, a_out = parts[0], parts[0] + parts[1]
    q_end, kv_end, o_end = cuts[0], cuts[0] + cuts[1], cuts[0] + cuts[1] + cuts[2]
    tile = width

    placing = []
    for index, (src, at) in enumerate(((own_qkv, 0), (own_out, a_qkv), (own_up, a_out))):
        here = pl.ds(pl.multiple_of(net.dp * rows, rows), rows)
        copy = pltpu.make_async_copy(
            src, w_a.at[here, at : at + src.shape[1]], own_sem.at[index]
        )
        copy.start()
        placing.append(copy)
    at = 0
    for src, n in zip((cq, ckv, co, cu), cuts):
        whole = src[...].astype(jnp.float32)
        for h in range(2):
            pack[h, :, at : at + n] = whole[:, h * n : (h + 1) * n]
        at += n
    place_gains(net, (g_attn, g_mlp), (g_query, g_image, g_cross), gvec)
    net.barrier()
    for copy in placing:
        copy.wait()

    def columns(first, last):
        return lambda tower, chip, core: w_a.at[
            pl.ds(pl.multiple_of((2 * chip + core) * rows, rows), rows), first:last
        ]

    def crossed(first, last):
        return lambda tower, chip, core: w_ca.at[
            core,
            pl.ds(pl.multiple_of((tower * 2 * lines + chip) * 2 * few, 2 * few), 2 * few),
            first:last,
        ]

    def plan(index, own, place, crossing):
        beside = GATHER_NAMES[index] in GATHER_BESIDE
        kind = GatherBeside if beside else Gather
        return kind(
            net, own, place, crossing, send_sem.at[index], recv_sem.at[index], local_sem.at[index]
        )

    def self_part(index, first, last):
        return plan(index, None, columns(first, last), False)

    def down_part(index, first, last):
        return plan(
            index,
            own_d.at[:, first:last],
            lambda tower, chip, core: w_d.at[
                pl.ds(pl.multiple_of((2 * chip + core) * depth, depth), depth), first:last
            ],
            False,
        )

    def cross_part(index, first, last):
        return plan(index, block.at[:, first:last], crossed(first, last), True)

    mid = a_qkv - width
    jobs = {
        "qk": self_part(0, 0, mid),
        "vo": self_part(1, mid, a_out),
        "u0": self_part(2, a_out, a_out + 2 * width),
        "u1": self_part(3, a_out + 2 * width, all_a),
        "d0": down_part(4, 0, width // 2),
        "d1": down_part(5, width // 2, width),
        "ca": cross_part(6, 0, o_end),
        "cu": cross_part(7, o_end, half),
        "cd": plan(
            8,
            own_cd,
            lambda tower, chip, core: w_cd.at[
                pl.ds(pl.multiple_of((tower * 4 * lines + 2 * chip + core) * part, part), part), :
            ],
            True,
        ),
    }
    kept = []

    def keep(src, dst):
        copy = pltpu.make_async_copy(src, dst, out_sem.at[len(kept)])
        copy.start()
        kept.append(copy)

    swapped = net.copy("core", pack.at[1 - net.core], swap, swap_sem.at[0], swap_sem.at[1])
    swapped.start()
    small = Small(net, gvec, arrived, totals, spread, s_send, s_recv)
    sums = Sums(sums_ref, row_weight)
    base = 4 * net.tower
    gain_rows[...] = jnp.zeros_like(gain_rows)
    first = net.core == 0

    def gain(at):
        return jnp.where(text, gains[at + 2 : at + 3, :], gains[at : at + 1, :])

    def build_block():
        swapped.wait()
        mine = pack[net.core]
        theirs = swap[...]
        block[0:few] = low(jnp.where(first, mine, theirs))
        block[few:] = low(jnp.where(first, theirs, mine))

    def gains_over(index):
        def run():
            small.collect(index)
            if index < 2:
                small.exchange(index + 1)
            else:
                small.spread()

        return run

    def first_norm():
        small.total(gains)
        norm_rows(tok, gain(0), h1, lambda r, v: sums.add(base, r, v))
        keep(h1, o_h1)

    def project(first_column, last_column):
        def run():
            def qkv_tile(i, carry):
                cols = pl.ds(pl.multiple_of(first_column + i * tile, tile), tile)
                qkv[:, cols] = low(product(h1[...], w_a[:, cols]))
                return carry

            lax.fori_loop(0, (last_column - first_column) // tile, qkv_tile, 0)

        return run

    def attend():
        keep(qkv, o_qkv)
        attention(
            pairs_of(qkv), pairs_of(qkv, width), pairs_of(qkv, 2 * width), allowed, weight, mixed
        )
        keep(weight, o_weight)
        keep(mixed, o_mixed)

    def attn_out():
        branch[...] = product(mixed[...], w_a[:, a_qkv:a_out])

        def add_branch(r):
            value = branch[r, :]
            sums.add(base + 1, r, value)
            middle[r, :] = tok[r, :].astype(jnp.float32) + value

        blocks(tok.shape[0], row_step(tok.shape[0]), add_branch)
        keep(middle, o_middle)
        norm_rows(middle, gain(1), h2)
        keep(h2, o_h2)

    def go_up(first_tile, last_tile):
        def run():
            def up_tile(i, carry):
                at = pl.multiple_of((first_tile + i) * tile, tile)
                wide[...] = product(h2[...], w_a[:, pl.ds(a_out + at, tile)])
                activate(wide, active, slope, pl.ds(at, tile))
                return carry

            lax.fori_loop(0, last_tile - first_tile, up_tile, 0)

        return run

    def keep_up():
        keep(active, o_active)
        keep(slope, o_slope)
        keep(w_a, full_a)

    def go_down(first_column, last_column):
        def run():
            branch[:, first_column:last_column] = product(
                active[...], w_d[:, first_column:last_column]
            )

        return run

    def self_end():
        keep(w_d, full_d)

        def add_mlp(r):
            value = branch[r, :]
            sums.add(base + 2, r, value)
            y = middle[r, :] + value
            out_y[r, :] = y
            image_out[r, :] = low(y)

            @pl.when(image)
            def _():
                sums.add(3, r, y)

        blocks(tok.shape[0], row_step(tok.shape[0]), add_mlp)
        net.send("x", image_out, passed, pass_sem.at[0], pass_sem.at[1], image)

    def cross_queries():
        @pl.when(text)
        def _():
            norm_rows(out_y, gains[4:5, :], n_q)
            for h in range(2):
                at = h * cuts[0]
                query[:, at : at + cuts[0]] = low(product(n_q[...], w_ca[h, :, 0:q_end]))

    tiles = active.shape[1] // tile
    steps = {
        "block": build_block,
        "gains0": gains_over(0),
        "gains1": gains_over(1),
        "gains2": gains_over(2),
        "norm": first_norm,
        "qk": project(0, mid),
        "v": project(mid, a_qkv),
        "attend": attend,
        "out": attn_out,
        "up0": go_up(0, tiles // 2),
        "up1": go_up(tiles // 2, tiles),
        "keep": keep_up,
        "down0": go_down(0, width // 2),
        "down1": go_down(width // 2, width),
        "end": self_end,
        "query": cross_queries,
        "rows": lambda: net.arrive(passed, pass_sem.at[0], pass_sem.at[1], text),
    }
    small.exchange(0)
    fill_masks(net, counts, lengths, allowed, cross_allowed, row_weight)
    for kind, name, k in gather_order(lines):
        if kind == "do":
            steps[name]()
        elif kind == "start":
            jobs[name].start()
        elif kind == "done":
            jobs[name].done()
        else:
            getattr(jobs[name], kind)(k)

    net.finish()
    for copy in kept:
        copy.wait()
    def hand(index, src, rcv, there=text):
        net.send("core", src, rcv, d_send.at[index], d_recv.at[index], there)

    def merge(index, own, rcv, out):
        net.arrive(rcv, d_send.at[index], d_recv.at[index], text)

        @pl.when(text)
        def _():
            def add(r):
                rcv[r, :] = low(own[r, :].astype(jnp.float32) + rcv[r, :].astype(jnp.float32))

            blocks(rcv.shape[0], 16, add)
            pltpu.make_async_copy(rcv, out, d_local.at[index]).start()

    @pl.when(text)
    def _():
        norm_rows(passed, gains[5:6, :], n_i)
        for h in range(2):
            at = h * width
            keyval[:, at : at + width] = low(product(n_i[...], w_ca[h, :, q_end:kv_end]))
        attention(
            pairs_of(query), pairs_of(keyval), pairs_of(keyval, width), cross_allowed, c_weight, c_mixed
        )
        for h in range(2):
            at = h * cuts[2]
            branch[:, at : at + cuts[2]] = product(c_mixed[...], w_ca[h, :, kv_end:o_end])

        def add_cross(r):
            value = branch[r, :]
            sums.add(7, r, value)
            c_middle[r, :] = out_y[r, :] + value

        blocks(tok.shape[0], row_step(tok.shape[0]), add_cross)
        norm_rows(c_middle, gains[6:7, :], h3)

        for h in range(2):

            def cross_up(i, carry):
                at = pl.multiple_of(i * tile, tile)
                wide[...] = product(h3[...], w_ca[h, :, pl.ds(o_end + at, tile)])
                activate(wide, active, slope, pl.ds(h * cuts[3] + at, tile))
                return carry

            lax.fori_loop(0, cuts[3] // tile, cross_up, 0)
        branch[...] = product(active[...], w_cd[...])

        def add_final(r):
            value = branch[r, :]
            sums.add(8, r, value)
            z = c_middle[r, :] + value
            sums.add(9, r, z)
            layer_out[r, :] = low(z)

        blocks(tok.shape[0], row_step(tok.shape[0]), add_final)

        def down_tile(i, carry):
            cols = pl.ds(pl.multiple_of(i * tile, tile), tile)
            found = low(product(active[:, cols], cot[...], 0, 0))
            for k in range(tile // part):
                at = (k % 2) * (w_d.shape[0] // 2) + (k // 2) * part + i * (tile // 2)
                w_d[pl.ds(pl.multiple_of(at, part), part), :] = found[k * part : (k + 1) * part]
            grad = product(cot[...], w_cd[cols, :], 1, 1)
            grad_wide[:, cols] = low(grad * slope[:, cols])
            return carry

        lax.fori_loop(0, active.shape[1] // tile, down_tile, 0)

    share = w_d.shape[0] // 2
    hand(0, w_d.at[pl.ds(pl.multiple_of((1 - net.core) * share, share), share), :], rcv_d)

    @pl.when(text)
    def _():
        for h in range(2):

            def up_grad(i, carry):
                at = pl.multiple_of(i * tile, tile)
                w_a[:, pl.ds(h * half + o_end + at, tile)] = low(
                    product(h3[...], grad_wide[:, pl.ds(h * cuts[3] + at, tile)], 0, 0)
                )
                return carry

            lax.fori_loop(0, cuts[3] // tile, up_grad, 0)

    theirs_at = pl.multiple_of((1 - net.core) * half, half)
    mine_at = pl.multiple_of(net.core * half, half)
    hand(1, w_a.at[:, pl.ds(theirs_at + o_end, half - o_end)], rcv_a.at[:, o_end:half])

    @pl.when(text)
    def _():
        branch[...] = product(grad_wide[:, 0 : cuts[3]], w_ca[0, :, o_end:half], 1, 1) + product(
            grad_wide[:, cuts[3] :], w_ca[1, :, o_end:half], 1, 1
        )

        def mid_done(r, back):
            total = cot[r, :].astype(jnp.float32) + back
            c_middle[r, :] = total
            h3[r, :] = low(total)

        norm_back_rows(c_middle, gains[6:7, :], branch, mid_done, g_small)
        gain_rows[6:7, :] = g_small[...]
        for h in range(2):
            at = h * cuts[2]
            w_a[:, h * half + kv_end : h * half + o_end] = low(
                product(c_mixed[...], h3[:, at : at + cuts[2]], 0, 0)
            )
        branch[...] = product(h3[:, 0 : cuts[2]], w_ca[0, :, kv_end:o_end], 1, 1) + product(
            h3[:, cuts[2] :], w_ca[1, :, kv_end:o_end], 1, 1
        )
        c_mixed[...] = low(branch[...])

        def att_done(pair, dq, dk, dv):
            at = pl.multiple_of(pair * 2 * HD, 2 * HD)
            query[:, pl.ds(at, 2 * HD)] = dq
            keyval[:, pl.ds(at, 2 * HD)] = dk
            keyval[:, pl.ds(width + at, 2 * HD)] = dv

        attention_back(
            pairs_of(query),
            pairs_of(keyval),
            pairs_of(keyval, width),
            pairs_of(c_mixed),
            c_weight,
            width,
            att_done,
        )
        branch[...] = product(keyval[:, 0:width], w_ca[0, :, q_end:kv_end], 1, 1) + product(
            keyval[:, width:], w_ca[1, :, q_end:kv_end], 1, 1
        )

        def image_done(r, back):
            image_out[r, :] = low(back)

        norm_back_rows(passed, gains[5:6, :], branch, image_done, g_small)
        gain_rows[5:6, :] = g_small[...]

    net.send("x", image_out, passed, pass_sem.at[0], pass_sem.at[1], text)

    @pl.when(text)
    def _():
        for h in range(2):
            at = h * width
            w_a[:, h * half + q_end : h * half + kv_end] = low(
                product(n_i[...], keyval[:, at : at + width], 0, 0)
            )
            at = h * cuts[0]
            w_a[:, h * half : h * half + q_end] = low(
                product(n_q[...], query[:, at : at + cuts[0]], 0, 0)
            )

    hand(2, w_a.at[:, pl.ds(theirs_at, o_end)], rcv_a.at[:, 0:o_end])
    mine_d = w_d.at[pl.ds(pl.multiple_of(net.core * share, share), share), :]
    merge(0, mine_d, rcv_d, sum_cd)
    merge(
        1,
        w_a.at[:, pl.ds(mine_at + o_end, half - o_end)],
        rcv_a.at[:, o_end:half],
        sum_ca.at[:, o_end:half],
    )

    @pl.when(text)
    def _():
        branch[...] = product(query[:, 0 : cuts[0]], w_ca[0, :, 0:q_end], 1, 1) + product(
            query[:, cuts[0] :], w_ca[1, :, 0:q_end], 1, 1
        )

        def text_done(r, back):
            top[r, :] = c_middle[r, :] + back

        norm_back_rows(out_y, gains[4:5, :], branch, text_done, g_small)
        gain_rows[4:5, :] = g_small[...]
        sums_ref[10:11, :] = jnp.broadcast_to(
            jnp.sum(row_weight[...], axis=0, keepdims=True), (1, sums_ref.shape[1])
        )
        vec[...] = gain_rows[...]

    merge(2, w_a.at[:, pl.ds(mine_at, o_end)], rcv_a.at[:, 0:o_end], sum_ca.at[:, 0:o_end])
    net.arrive(passed, pass_sem.at[0], pass_sem.at[1], image)

    @pl.when(image)
    def _():
        vec[...] = jnp.zeros_like(vec)

        def add_back(r):
            top[r, :] = cot[r, :].astype(jnp.float32) + passed[r, :].astype(jnp.float32)
            layer_out[r, :] = image_out[r, :]

        blocks(tok.shape[0], row_step(tok.shape[0]), add_back)

    vec[7:8, 0 : sums_ref.shape[1]] = sums.line()

    @pl.when(text)
    def _():
        for index, (src, out) in enumerate(
            (
                (rcv_d, sum_cd),
                (rcv_a.at[:, o_end:half], sum_ca.at[:, o_end:half]),
                (rcv_a.at[:, 0:o_end], sum_ca.at[:, 0:o_end]),
            )
        ):
            pltpu.make_async_copy(src, out, d_local.at[index]).wait()

    net.finish()


def forward(lines, cuts, parts, *operands):
    tok, own_qkv, own_d, own_cd = operands[7], operands[13], operands[16], operands[17]
    cross_shards = operands[9:13]
    bf16, f32 = jnp.bfloat16, jnp.float32
    count = 4 * lines
    rows, width = tok.shape
    few, half = cross_shards[0].shape[0], sum(cuts)
    hidden = count * own_d.shape[0]
    all_a = (count * own_qkv.shape[0], sum(parts))
    gains_shape = (8, width)
    heads_n = width // HD
    jobs = 9
    shape = jax.ShapeDtypeStruct
    wide_b, wide_f = (rows, width), (rows, hidden)
    stored = [
        (wide_b, bf16),
        ((rows, parts[0]), bf16),
        (wide_b, bf16),
        ((heads_n, rows, rows), bf16),
        (wide_b, f32),
        (wide_b, bf16),
        (wide_f, bf16),
        (wide_f, f32),
    ]
    outs = [
        (all_a, bf16),
        ((hidden, width), bf16),
        ((width, half), bf16),
        ((hidden // 2, width), bf16),
        *stored,
        (gains_shape, f32),
        (wide_b, bf16),
        (wide_b, f32),
        (gains_shape, f32),
    ]
    scratch = [
        (all_a, bf16),
        ((hidden, width), bf16),
        ((2, width, half), bf16),
        ((hidden, width), bf16),
        *stored,
        (wide_b, f32),
        (wide_b, f32),
        (wide_b, f32),
        (wide_b, bf16),
        (wide_b, bf16),
        (wide_b, bf16),
        (wide_b, bf16),
        (wide_b, bf16),
        ((rows, 2 * width), bf16),
        (wide_b, bf16),
        ((heads_n, rows, rows), bf16),
        (wide_b, f32),
        (wide_b, bf16),
        (wide_f, bf16),
        ((1, width), f32),
        ((rows, rows), f32),
        ((rows, rows), f32),
        ((rows, 1), f32),
        (gains_shape, f32),
        ((2, few, half), f32),
        ((few, half), f32),
        ((2 * few, half), bf16),
        ((width, half), bf16),
        ((hidden // 2, width), bf16),
        ((3,) + gains_shape, f32),
        ((3,) + gains_shape, f32),
        ((lines - 1,) + gains_shape, f32),
        ((16, 128), f32),
        (gains_shape, f32),
    ]
    dma = pltpu.SemaphoreType.DMA
    return pl.pallas_call(
        functools.partial(forward_kernel, lines, cuts, parts),
        out_shape=tuple(shape(*o) for o in outs),
        in_specs=[SMEM, SMEM] + [VMEM] * 11 + [ANY] * 5,
        out_specs=[ANY] * 12 + [VMEM] * 4,
        scratch_shapes=[pltpu.VMEM(*s) for s in scratch]
        + [
            dma((jobs, Gather.sems(lines))),
            dma((jobs, Gather.sems(lines))),
            dma((jobs,)),
            dma((2,)),
            dma((2 + lines,)),
            dma((2 + lines,)),
            dma((2,)),
            dma((12,)),
            dma((3,)),
            dma((3,)),
            dma((3,)),
            dma((3,)),
        ],
        compiler_params=pltpu.CompilerParams(
            collective_id=0, has_side_effects=True, vmem_limit_bytes=63 << 20
        ),
    )(*operands)


class Scatter:
    def __init__(self, net, own, near, far, rcv, sems):
        self.net, self.own, self.near, self.far, self.rcv = net, own, near, far, rcv
        self.send_sem, self.recv_sem = sems

    @staticmethod
    def sems(lines):
        return 1 + 7 * lines

    def sem(self, s):
        return self.send_sem.at[s], self.recv_sem.at[s]

    def add(self, pairs, out):
        def one(r):
            total = pairs[0][r, :].astype(jnp.float32)
            for other in pairs[1:]:
                total = total + other[r, :].astype(jnp.float32)
            out[r, :] = total.astype(out.dtype)

        blocks(out.shape[0], 16, one)

    def chips(self, k):
        net = self.net
        if k == 0:
            return ((None, net.z),)
        return (
            (net.z + k < net.lines, jnp.minimum(net.z + k, net.lines - 1)),
            (net.z >= k, jnp.maximum(net.z - k, 0)),
        )

    def order(self):
        return [pair for k in range(self.net.lines - 1, -1, -1) for pair in self.chips(k)]

    def swap(self, theirs, rcv):
        self.whole = rcv
        self.net.send("core", theirs, rcv, *self.sem(0))

    def swapped(self):
        self.net.arrive(self.whole, *self.sem(0))

    def over_x(self, part):
        net = self.net
        for there, z in self.order():
            for y in (1 - net.y, net.y):
                chip = 2 * z + y
                net.send("x", part(chip), self.own(chip), *self.sem(1 + chip), both(there, net.text))

    def from_x(self, chip, there):
        if self.rcv is None:
            net = self.net
            net.arrive(self.own(chip), *self.sem(1 + chip), both(there, net.image))

    def across(self, only=None):
        net = self.net
        for there, z in self.order():
            there = both(there, only)
            chip = 2 * z + 1 - net.y
            self.from_x(chip, there)
            own = self.own(chip)
            if self.rcv is not None:
                when(there, lambda: self.add([own, self.rcv(chip)], own))
            net.send("y", own, self.near(z), *self.sem(1 + 2 * net.lines + z), there)

    def here(self, chip, z):
        parts = [self.own(chip), self.near(z)]
        return parts if self.rcv is None else parts + [self.rcv(chip)]

    def along(self, k):
        net = self.net
        lines = net.lines
        for up, (there, z) in zip((True, False), self.chips(k)):
            chip = 2 * z + net.y
            base = (1 + 3 * lines) if up else (1 + 4 * lines)
            self.from_x(chip, there)
            net.arrive(self.near(z), *self.sem(1 + 2 * lines + z), there)
            more = net.low if up else net.high
            s = base + z
            net.arrive(self.far(z), *self.sem(s), both(there, more))
            own = self.own(chip)
            parts = self.here(chip, z)
            when(both(there, more), lambda: self.add(parts + [self.far(z)], own))
            when(both(there, jnp.logical_not(more)), lambda: self.add(parts, own))
            slot = z if up else jnp.where(z == net.z - 1, lines, z)
            net.send("up" if up else "down", own, self.far(slot), *self.sem(s), there)

    def turn(self):
        pass

    def total(self, out):
        net = self.net
        lines = net.lines
        self.from_x(net.chip, None)
        net.arrive(self.near(net.z), *self.sem(1 + 2 * lines + net.z))
        net.arrive(self.far(net.z), *self.sem(1 + 3 * lines + net.z), net.low)
        net.arrive(self.far(lines), *self.sem(1 + 4 * lines + net.z), net.high)
        parts = self.here(net.chip, net.z)
        low_part, high_part = self.far(net.z), self.far(lines)
        when(both(net.low, net.high), lambda: self.add(parts + [low_part, high_part], out))
        when(jnp.logical_not(net.low), lambda: self.add(parts + [high_part], out))
        when(jnp.logical_not(net.high), lambda: self.add(parts + [low_part], out))


class ScatterAlong(Scatter):
    def across(self, only=None):
        pass

    def spot(self, z, second):
        if not second:
            return self.far(z)
        if isinstance(z, int):
            return self.extra(0)
        return self.near(z)

    def line_sems(self, up, second):
        lines = self.net.lines
        return 1 + (3 + 2 * second + (0 if up else 1)) * lines

    def parts(self, chip):
        return [self.own(chip)] if self.rcv is None else [self.own(chip), self.rcv(chip)]

    def along(self, k):
        net = self.net
        for up, (there, z) in zip((True, False), self.chips(k)):
            for second, y in ((0, net.y), (1, 1 - net.y)):
                chip = 2 * z + y
                self.from_x(chip, there)
                more = net.low if up else net.high
                s = self.line_sems(up, second) + z
                net.arrive(self.spot(z, second), *self.sem(s), both(there, more))
                own = self.own(chip)
                parts = self.parts(chip)
                with_far = parts + [self.spot(z, second)]
                when(both(there, more), lambda: self.add(with_far, own))
                if len(parts) > 1:
                    when(both(there, jnp.logical_not(more)), lambda: self.add(parts, own))
                way = "up" if up else "down"
                if up:
                    net.send(way, own, self.spot(z, second), *self.sem(s), there)
                else:
                    last = z == net.z - 1
                    net.send(
                        way, own, self.spot(net.lines, second), *self.sem(s), both(there, last)
                    )
                    net.send(
                        way,
                        own,
                        self.spot(z, second),
                        *self.sem(s),
                        both(there, jnp.logical_not(last)),
                    )

    def gathered(self, second, more, out):
        net = self.net
        lines = net.lines
        chip = 2 * net.z + (1 - net.y if second else net.y)
        self.from_x(chip, None)
        s = self.line_sems(True, second) + net.z
        net.arrive(self.spot(net.z, second), *self.sem(s), net.low)
        s = self.line_sems(False, second) + net.z
        net.arrive(self.spot(lines, second), *self.sem(s), net.high)
        parts = self.parts(chip) + more
        low_part, high_part = self.spot(net.z, second), self.spot(lines, second)
        when(both(net.low, net.high), lambda: self.add(parts + [low_part, high_part], out))
        when(jnp.logical_not(net.low), lambda: self.add(parts + [high_part], out))
        when(jnp.logical_not(net.high), lambda: self.add(parts + [low_part], out))

    def turn(self):
        net = self.net
        own = self.own(2 * net.z + 1 - net.y)
        self.gathered(1, [], own)
        net.send("y", own, self.extra(1), *self.sem(1 + 2 * net.lines))

    def total(self, out):
        self.net.arrive(self.extra(1), *self.sem(1 + 2 * self.net.lines))
        self.gathered(0, [self.extra(1)], out)


def strip(ref, size, first, last):
    return lambda i: ref.at[pl.ds(pl.multiple_of(i * size, size), size), first:last]


def backward_kernel(
    lines, cuts, parts,
    tok, top_in, gains, vec_in, full_a, full_d, sum_ca, sum_cd,
    i_h1, i_qkv, i_mixed, i_weight, i_middle, i_h2, i_active, i_slope,
    o_qkv, o_out, o_up, o_d, o_cq, o_ckv, o_co, o_cu, o_cd, input_grad, o_vec,
    h1, qkv, mixed, weight, middle, h2, active, slope,
    g_a, g_d, rcv_a, rcv_d, near_a, near_d, far_a, far_d,
    own_ca, own_cd, near_ca, near_cd, far_ca, far_cd,
    w_d, w_up, top, branch, n_grad, g_small, vec, fin, fin_vo, extra_d, swap, arrived, totals, spread,
    send_sem, recv_sem, load_sem, swap_sem, s_send, s_recv,
):
    net = Net(lines)
    net.barrier()
    text, image = net.text, net.image
    width = tok.shape[1]
    tile = width
    rows, depth = o_qkv.shape[0], o_d.shape[0]
    few, part = 2 * o_cq.shape[0], o_cd.shape[0]
    half = own_ca.shape[1]
    a_out = parts[0] + parts[1]
    all_a = g_a.shape[2]
    o_end = cuts[0] + cuts[1] + cuts[2]
    theirs = 1 - net.core

    def load(index, src, dst):
        copy = pltpu.make_async_copy(src, dst, load_sem.at[index])
        copy.start()
        return copy

    l_active = load(0, i_active, active)
    l_wd = load(1, full_d, w_d)
    l_slope = load(2, i_slope, slope)
    l_h2 = load(3, i_h2, h2)
    l_up = load(4, full_a.at[:, a_out:], w_up)
    l_middle = load(5, i_middle, middle)
    l_mixed = load(6, i_mixed, mixed)
    l_qkv = load(7, i_qkv, qkv)
    l_weight = load(8, i_weight, weight)
    l_h1 = load(9, i_h1, h1)

    def job(index, own, near, far, rcv, extra=None):
        kind = ScatterAlong if SCATTER_NAMES[index] in SCATTER_ALONG else Scatter
        made = kind(net, own, near, far, rcv, (send_sem.at[index], recv_sem.at[index]))
        made.extra = extra
        return made

    def self_a(index, first, last):
        return job(
            index,
            strip(g_a.at[net.core], rows, first, last),
            strip(near_a, rows, first, last),
            strip(far_a, rows, first, last),
            strip(rcv_a, rows, first, last),
        )

    def cross_a(index, first, last):
        return job(
            index,
            strip(own_ca, few, first, last),
            strip(near_ca, few, first, last),
            strip(far_ca, few, first, last),
            None,
        )

    def self_d(index, first, last):
        return job(
            index,
            strip(g_d.at[net.core], depth, first, last),
            strip(near_d, depth, first, last),
            strip(far_d, depth, first, last),
            strip(rcv_d, depth, first, last),
            strip(extra_d, depth, first, last),
        )

    mid, middle_up, middle_d = parts[0] - width, a_out + 2 * width, width // 2
    jobs = {
        "d0": self_d(0, 0, middle_d),
        "d1": self_d(1, middle_d, width),
        "u0": self_a(2, a_out, middle_up),
        "u1": self_a(3, middle_up, all_a),
        "qk": self_a(4, 0, mid),
        "vo": self_a(5, mid, a_out),
        "cd": job(
            6,
            strip(own_cd, part, 0, width),
            strip(near_cd, part, 0, width),
            strip(far_cd, part, 0, width),
            None,
        ),
        "cu": cross_a(7, o_end, half),
        "ca": cross_a(8, 0, o_end),
    }

    def swap_a(name, first, last):
        jobs[name].swap(g_a.at[theirs, :, first:last], rcv_a.at[:, first:last])

    def swap_d(name, first, last):
        jobs[name].swap(g_d.at[theirs, :, first:last], rcv_d.at[:, first:last])

    def across(name, only=None):
        if jobs[name].rcv is not None:
            jobs[name].swapped()
        jobs[name].across(only)

    plane_a, plane_d = own_ca.shape[0], own_cd.shape[0]
    c_loads = (
        pltpu.make_async_copy(sum_cd.at[plane_d : 2 * plane_d, :], own_cd, load_sem.at[10]),
        pltpu.make_async_copy(sum_ca.at[plane_a : 2 * plane_a, :], own_ca, load_sem.at[11]),
    )

    @pl.when(text)
    def _():
        for copy in c_loads:
            copy.start()

    def start_x(name):
        at = {"cd": (sum_cd, part, 0, width), "cu": (sum_ca, few, o_end, half), "ca": (sum_ca, few, 0, o_end)}
        jobs[name].over_x(strip(*at[name]))

    def round_top():
        def body(r):
            n_grad[r, :] = low(top_in[r, :])

        blocks(tok.shape[0], row_step(tok.shape[0]), body)

        @pl.when(text)
        def _():
            for copy in c_loads:
                copy.wait()

    def down_grads():
        l_active.wait()
        l_wd.wait()
        l_slope.wait()

        def down_tile(i, carry):
            cols = pl.ds(pl.multiple_of(i * tile, tile), tile)
            found = low(product(active[:, cols], n_grad[...], 0, 0))
            each = tile // depth
            for k in range(each):
                at = pl.multiple_of(((i * each + k) // 2) * depth, depth)
                g_d[k % 2, pl.ds(at, depth), :] = found[k * depth : (k + 1) * depth]
            grad = product(n_grad[...], w_d[cols, :], 1, 1)
            active[:, cols] = low(grad * slope[:, cols])
            return carry

        lax.fori_loop(0, active.shape[1] // tile, down_tile, 0)
        for i in range(4):
            src = full_a.at[:, i * width : (i + 1) * width]
            l_four.append(load(12 + i, src, w_d.at[i * width : (i + 1) * width, :]))
        l_h2.wait()

    l_four = []

    def put_a(found, at):
        for k in range(width // rows):
            g_a[k % 2, (k // 2) * rows : (k // 2 + 1) * rows, pl.ds(at, found.shape[1])] = found[
                k * rows : (k + 1) * rows
            ]

    def up_grads(first_tile, last_tile):
        def run():
            def up_tile(i, carry):
                at = pl.multiple_of(i * tile, tile)
                found = low(product(h2[...], active[:, pl.ds(at, tile)], 0, 0))
                put_a(found, pl.multiple_of(a_out + at, tile))
                return carry

            lax.fori_loop(first_tile, last_tile, up_tile, 0)

        return run

    def own_gain(at):
        return jnp.where(text, gains[at + 2 : at + 3, :], gains[at : at + 1, :])

    at_vec = 2 * net.tower

    def mid_grads():
        l_up.wait()
        branch[...] = product(active[...], w_up[...], 1, 1)
        l_middle.wait()

        def mid_done(r, back):
            total = top_in[r, :] + back
            top[r, :] = total
            n_grad[r, :] = low(total)

        norm_back_rows(middle, own_gain(1), branch, mid_done, g_small)
        vec[...] = vec_in[...]
        vec[pl.ds(at_vec + 1, 1), :] = g_small[...]

    def out_grads():
        l_mixed.wait()
        for copy in l_four:
            copy.wait()
        put_a(low(product(mixed[...], n_grad[...], 0, 0)), parts[0])
        mixed[...] = low(product(n_grad[...], w_d[3 * width : 4 * width, :], 1, 1))

    def att_grads():
        l_qkv.wait()
        l_weight.wait()

        def att_done(pair, dq, dk, dv):
            at = pl.multiple_of(pair * 2 * HD, 2 * HD)
            for k, grad in enumerate((dq, dk, dv)):
                qkv[:, pl.ds(pl.multiple_of(k * width + at, 2 * HD), 2 * HD)] = grad

        attention_back(
            pairs_of(qkv),
            pairs_of(qkv, width),
            pairs_of(qkv, 2 * width),
            pairs_of(mixed),
            weight,
            width,
            att_done,
        )
        l_h1.wait()

    def qkv_grads(first_tile, last_tile):
        def run():
            def qkv_tile(i, carry):
                at = pl.multiple_of(i * tile, tile)
                put_a(low(product(h1[...], qkv[:, pl.ds(at, tile)], 0, 0)), at)
                return carry

            lax.fori_loop(first_tile, last_tile, qkv_tile, 0)

        return run

    small = Small(net, vec, arrived, totals, spread, s_send, s_recv)

    def first_grads():
        branch[...] = (
            product(qkv[:, 0:width], w_d[0:width, :], 1, 1)
            + product(qkv[:, width : 2 * width], w_d[width : 2 * width, :], 1, 1)
            + product(qkv[:, 2 * width :], w_d[2 * width : 3 * width, :], 1, 1)
        )

        def first_done(r, back):
            input_grad[r, :] = top[r, :] + back

        norm_back_rows(tok, own_gain(0), branch, first_done, g_small)
        vec[pl.ds(at_vec, 1), :] = g_small[...]
        small.exchange(0)

    def small_step(index):
        def run():
            small.collect(index)
            if index < 2:
                small.exchange(index + 1)
            else:
                small.spread()

        return run

    up_tiles = (all_a - a_out) // tile
    steps = {
        "top": round_top,
        "down": down_grads,
        "up0": up_grads(0, up_tiles // 2),
        "up1": up_grads(up_tiles // 2, up_tiles),
        "mid": mid_grads,
        "out": out_grads,
        "att": att_grads,
        "qk": qkv_grads(0, mid // tile),
        "v": qkv_grads(mid // tile, parts[0] // tile),
        "first": first_grads,
        "small0": small_step(0),
        "small1": small_step(1),
        "small2": small_step(2),
    }
    share = few // 2
    first = net.core == 0
    swaps = {}

    def start_swap(name, index, first_column, last_column):
        copy = net.copy(
            "core",
            fin.at[pl.ds(pl.multiple_of(theirs * share, share), share), first_column:last_column],
            swap.at[:, first_column:last_column],
            swap_sem.at[index, 0],
            swap_sem.at[index, 1],
        )
        copy.start()
        swaps[name] = copy

    def put_cross(out, at, n):
        mine = fin[pl.ds(pl.multiple_of(net.core * share, share), share), at : at + n]
        other = swap[:, at : at + n]
        out[:, 0:n] = jnp.where(first, mine, other)
        out[:, n:] = jnp.where(first, other, mine)

    def put_vo():
        o_qkv[:, mid:] = fin_vo[:, 0 : parts[0] - mid]
        o_out[...] = fin_vo[:, parts[0] - mid :]

    totals_to = {
        "d0": (o_d.at[:, 0:middle_d], None),
        "d1": (o_d.at[:, middle_d:], None),
        "u0": (o_up.at[:, 0 : middle_up - a_out], None),
        "u1": (o_up.at[:, middle_up - a_out :], None),
        "qk": (o_qkv.at[:, 0:mid], None),
        "vo": (fin_vo, put_vo),
        "cd": (o_cd, None),
        "cu": (fin.at[:, o_end:half], lambda: start_swap("cu", 0, o_end, half)),
        "ca": (fin.at[:, 0:o_end], lambda: start_swap("ca", 1, 0, o_end)),
    }
    spans = {
        "d0": (0, middle_d),
        "d1": (middle_d, width),
        "u0": (a_out, middle_up),
        "u1": (middle_up, all_a),
        "qk": (0, mid),
        "vo": (mid, a_out),
    }
    for kind, name, k in scatter_order(lines):
        if kind == "do":
            steps[name]()
        elif kind == "x":
            start_x(name)
        elif kind == "swap":
            (swap_d if name in ("d0", "d1") else swap_a)(name, *spans[name])
        elif kind == "across":
            across(name, (None, text, image)[k])
        elif kind == "along":
            jobs[name].along(k)
        elif kind == "turn":
            jobs[name].turn()
        else:
            out, then = totals_to[name]
            jobs[name].total(out)
            if then is not None:
                then()
    small.total(o_vec)
    swaps["cu"].wait()
    put_cross(o_cu, o_end, cuts[3])
    swaps["ca"].wait()
    at = 0
    for out, n in zip((o_cq, o_ckv, o_co), cuts):
        put_cross(out, at, n)
        at += n
    net.finish()


SCATTER = ("d0", "d1", "u0", "u1", "cd", "qk", "vo", "cu", "ca")
SCATTER_NAMES = ("d0", "d1", "u0", "u1", "qk", "vo", "cd", "cu", "ca")
SCATTER_ALONG = ("d0", "d1")
BEFORE = {0: ("qk", "vo", "cd"), 3: ("cu",), 5: ("ca",)}
SCATTER_HEAD = (
    "x cd", "x cu", "x ca", "do top", "across cd 1", "do down", "swap d0", "swap d1", "do up0", "swap u0",
    "across d0", "do up1", "swap u1", "across d1", "do mid", "across u0", "across u1", "do out", "do att",
    "do qk", "swap qk", "do v", "swap vo", "do first",
)


def scatter_order(lines):
    if lines == 4 and SCATTER_FOUR:
        return parsed(SCATTER_FOUR)
    events = parsed(SCATTER_HEAD)
    count = len(SCATTER)
    for slot in range(count + lines):
        for name in BEFORE.get(slot, ()):
            events.append(("across", name, 2 if name == "cd" else 0))
        if 1 <= slot <= 3:
            events.append(("do", "small%d" % (slot - 1), 0))
        for k in range(lines - 1, -2, -1):
            index = slot - (lines - 1 - k)
            if 0 <= index < count:
                kind = "along" if k > 0 else "turn" if k == 0 else "total"
                events.append((kind, SCATTER[index], k))
    return events


SCATTER_FOUR = (
    "do top", "do down", "swap d0", "swap d1", "do up0", "x cd", "x cu", "swap u0", "across d0",
    "along d0 3", "across d1", "do up1", "swap u1", "along d1 3", "across u0", "across cd 1",
    "do mid", "along u0 3", "across u1", "do out", "along d1 2", "do att", "x ca", "along d0 2",
    "across cd 2", "along u0 2", "do qk", "along d1 1", "along cd 3", "along u1 3", "swap qk",
    "along cd 2", "across cu", "along u0 1", "along cu 3", "do v", "along d0 1", "along cu 2",
    "along cd 1", "across qk", "along qk 3", "along cu 1", "swap vo", "do first", "along u1 2",
    "across ca", "across vo", "do small0", "along ca 3", "turn d0", "turn d1", "do small1",
    "along u1 1", "along qk 2", "along qk 1", "do small2", "along vo 3", "along ca 2", "along vo 2",
    "total u0", "along ca 1", "total u1", "along vo 1", "total d0", "total qk", "total cu",
    "total cd", "total d1", "total ca", "total vo",
)


def backward(lines, cuts, parts, own_shapes, *operands):
    bf16, f32 = jnp.bfloat16, jnp.float32
    tok, top, gains, vec, full_a, full_d, sum_ca, sum_cd = operands[:8]
    stored = [(o.shape, o.dtype) for o in operands[8:]]
    chips = 2 * lines
    row_count, width = tok.shape
    hidden, all_a = full_d.shape[0], full_a.shape[1]
    half = sum_ca.shape[1]
    rows, depth = width // (2 * chips), hidden // (2 * chips)
    few, part = width // (2 * chips), hidden // (4 * chips)
    outs = [*own_shapes, (row_count, width), vec.shape]
    rcv_a, rcv_d = (chips * rows, all_a), (chips * depth, width)
    own_ca, own_cd = (chips * few, half), (chips * part, width)

    def line(size, count):
        return (size * count, all_a), (depth * count, width)

    scratch = [
        *stored,
        ((2,) + rcv_a, bf16),
        ((2,) + rcv_d, bf16),
        (rcv_a, bf16),
        (rcv_d, bf16),
        ((lines * rows, all_a), bf16),
        ((lines * depth, width), bf16),
        (((lines + 1) * rows, all_a), bf16),
        (((lines + 1) * depth, width), bf16),
        (own_ca, bf16),
        (own_cd, bf16),
        ((lines * few, half), bf16),
        ((lines * part, width), bf16),
        (((lines + 1) * few, half), bf16),
        (((lines + 1) * part, width), bf16),
        ((hidden, width), bf16),
        ((width, hidden), bf16),
        ((row_count, width), f32),
        ((row_count, width), f32),
        ((row_count, width), bf16),
        ((1, width), f32),
        (vec.shape, f32),
        ((rows, half), f32),
        ((rows, 2 * width), f32),
        ((2 * depth, width), bf16),
        ((few // 2, half), f32),
        ((3,) + vec.shape, f32),
        ((3,) + vec.shape, f32),
        ((lines - 1,) + vec.shape, f32),
    ]
    dma = pltpu.SemaphoreType.DMA
    return pl.pallas_call(
        functools.partial(backward_kernel, lines, cuts, parts),
        out_shape=tuple(jax.ShapeDtypeStruct(s, f32) for s in outs),
        in_specs=[VMEM] * 4 + [ANY] * 12,
        out_specs=[VMEM] * len(outs),
        scratch_shapes=[pltpu.VMEM(*s) for s in scratch]
        + [
            dma((9, Scatter.sems(lines))),
            dma((9, Scatter.sems(lines))),
            dma((16,)),
            dma((2, 2)),
            dma((2 + lines,)),
            dma((2 + lines,)),
        ],
        compiler_params=pltpu.CompilerParams(
            collective_id=1, has_side_effects=True, vmem_limit_bytes=63 << 20
        ),
    )(*operands)


def final_kernel(lines, rows, few, vec, *refs):
    count = (len(refs) - 7) // 2
    ins, outs = refs[:count], refs[count : 2 * count]
    g_1, g_2, g_q, g_i, g_c, rms, sems = refs[2 * count :]
    copies = [pltpu.make_async_copy(a, b, sems.at[i]) for i, (a, b) in enumerate(zip(ins, outs))]
    for copy in copies:
        copy.start()
    tower, dp = lax.axis_index("tower"), lax.axis_index("dp")
    width = vec.shape[1]

    def cut(n, at):
        lane = lax.broadcasted_iota(jnp.int32, (width, n), 0)
        index = lax.broadcasted_iota(jnp.int32, (width, n), 1)
        pick = jnp.where(lane == at + index, 1.0, 0.0)
        return lax.dot_general(
            vec[...],
            pick,
            (((1,), (0,)), ((), ())),
            precision=lax.Precision.HIGHEST,
            preferred_element_type=jnp.float32,
        )

    own = cut(rows, dp * rows)
    cross = cut(few, (tower * 4 * lines + dp) * few)
    g_1[...] = jnp.where(tower == 1, own[2:3], own[0:1])
    g_2[...] = jnp.where(tower == 1, own[3:4], own[1:2])
    g_q[...] = cross[4:5]
    g_i[...] = cross[5:6]
    g_c[...] = cross[6:7]
    sums = vec[7:8, 0:128]
    lane = lax.broadcasted_iota(jnp.int32, sums.shape, 1)
    valid = jnp.sum(jnp.where(lane == 10, sums, 0.0), axis=1, keepdims=True)
    images = ins[0].shape[0] * 4.0 * lines
    divisor = jnp.where(lane < 4, images, valid) * width
    rms[...] = jnp.sqrt(sums / divisor)
    for copy in copies:
        copy.wait()


def final(lines, rows, few, vec, *results):
    f32 = jnp.float32
    small = [(1, rows)] * 2 + [(1, few)] * 3 + [(1, 128)]
    return pl.pallas_call(
        functools.partial(final_kernel, lines, rows, few),
        out_shape=tuple(jax.ShapeDtypeStruct(r.shape, r.dtype) for r in results)
        + tuple(jax.ShapeDtypeStruct(s, f32) for s in small),
        in_specs=[VMEM] + [ANY] * len(results),
        out_specs=[VMEM] * (len(results) + 6),
        scratch_shapes=[pltpu.SemaphoreType.DMA((len(results),))],
        compiler_params=pltpu.CompilerParams(vmem_limit_bytes=62 << 20),
    )(vec, *results)


def plain_gather(own_a, own_d, pack, own_cd, own_g):
    axes = ("tower", "dp")
    tiles = lax.all_gather(own_g, axes, axis=0)
    return (
        lax.all_gather(own_a, "dp", axis=0, tiled=True),
        lax.all_gather(own_d, "dp", axis=0, tiled=True),
        lax.all_gather(pack.astype(jnp.bfloat16), axes, axis=1, tiled=True),
        lax.all_gather(own_cd, axes, axis=0, tiled=True),
        tiles.reshape((2, -1) + own_g.shape),
    )


def plain_scatter(g_a, g_d, g_ca, g_cd, vec, parts, cuts):
    axes = ("tower", "dp")

    def added(grad, over, axis):
        return lax.psum_scatter(
            grad.astype(jnp.float32), over, scatter_dimension=axis, tiled=True
        )

    a = added(g_a.reshape(-1, g_a.shape[-1]), "dp", 0)
    d = added(g_d.reshape(-1, g_d.shape[-1]), "dp", 0)
    ca = added(g_ca.reshape(2, -1, g_ca.shape[-1]), axes, 1)
    cd = added(g_cd.reshape(-1, g_cd.shape[-1]), axes, 0)
    at = [sum(cuts[:i]) for i in range(len(cuts) + 1)]
    cross = [
        jnp.concatenate([ca[0][:, i:j], ca[1][:, i:j]], axis=1) for i, j in zip(at[:-1], at[1:])
    ]
    first, second = parts[0], parts[0] + parts[1]
    self_parts = [a[:, :first], a[:, first:second], a[:, second:]]
    return (*self_parts, d, *cross, cd, lax.psum(vec, axes))


def layer_norm(value_matrix, norm_gain):
    center = value_matrix - jnp.mean(value_matrix, axis=-1, keepdims=True)
    spread = jnp.mean(center * center, axis=-1, keepdims=True)
    return center * lax.rsqrt(spread + EPSILON) * norm_gain


def norm_back(value_matrix, norm_gain, grad_out):
    result, puller = jax.vjp(layer_norm, value_matrix, norm_gain)
    return puller(grad_out)


def dot(a, b):
    return jnp.dot(a, b, preferred_element_type=jnp.float32)


def dot_tn(a, b):
    return jnp.einsum("rd,re->de", a, b, preferred_element_type=jnp.float32)


def dot_nt(a, b):
    return jnp.einsum("re,de->rd", a, b, preferred_element_type=jnp.float32)


def low(value_matrix):
    return value_matrix.astype(jnp.bfloat16)


def masks(counts, lengths, row_count, decoder):
    row_index = jnp.arange(row_count, dtype=jnp.int32)
    bounds = jnp.cumsum(counts)
    image_of = jnp.sum((row_index[:, None] >= bounds[None, :]).astype(jnp.int32), axis=1)
    caption_of = row_index // CAP_LEN
    in_place = row_index - caption_of * CAP_LEN
    caption_slots = jnp.arange(lengths.shape[0], dtype=jnp.int32)
    length_rows = jnp.sum(
        jnp.where(caption_of[:, None] == caption_slots[None, :], lengths[None, :], 0), axis=1
    )
    valid_rows = in_place < length_rows
    image_mask = image_of[:, None] == image_of[None, :]
    text_mask = (
        (caption_of[:, None] == caption_of[None, :])
        & (in_place[None, :] <= in_place[:, None])
        & valid_rows[None, :]
    )
    cross_mask = caption_of[:, None] == image_of[None, :]
    return jnp.where(decoder, text_mask, image_mask), cross_mask, valid_rows


def heads(value_matrix):
    return value_matrix.reshape(value_matrix.shape[0], -1, HD)


def attend(query, key, value, allowed):
    scores = jnp.einsum(
        "qhd,khd->hqk", heads(query), heads(key), preferred_element_type=jnp.float32
    ) * HD ** (-0.5)
    weight = jax.nn.softmax(jnp.where(allowed[None], scores, NEGATIVE), axis=-1)
    mixed = jnp.einsum("hqk,khd->qhd", low(weight), heads(value), preferred_element_type=jnp.float32)
    return low(mixed.reshape(query.shape)), weight


def attend_back(query, key, value, weight, grad_mixed):
    grad_mixed = heads(grad_mixed)
    grad_value = jnp.einsum("hqk,qhd->khd", low(weight), grad_mixed, preferred_element_type=jnp.float32)
    grad_weight = jnp.einsum("qhd,khd->hqk", grad_mixed, heads(value), preferred_element_type=jnp.float32)
    grad_score = low(
        weight * (grad_weight - jnp.sum(grad_weight * weight, axis=-1, keepdims=True))
    )
    grad_query = jnp.einsum(
        "hqk,khd->qhd", grad_score, heads(key), preferred_element_type=jnp.float32
    ) * HD ** (-0.5)
    grad_key = jnp.einsum(
        "hqk,qhd->khd", grad_score, heads(query), preferred_element_type=jnp.float32
    ) * HD ** (-0.5)
    return tuple(low(g.reshape(query.shape)) for g in (grad_query, grad_key, grad_value))


def mlp_forward(stream, gain, up, down):
    hidden = low(layer_norm(stream, gain))
    wide = dot(hidden, up)
    active = low(jax.nn.gelu(wide))
    return dot(active, down), (hidden, wide, active)


def mlp_back(stream, gain, up, down, stored, grad):
    hidden, wide, active = stored
    branch = low(grad)
    grad_down = dot_tn(active, branch)
    result, puller = jax.vjp(jax.nn.gelu, wide)
    grad_wide = low(puller(dot_nt(branch, down))[0])
    grad_up = dot_tn(hidden, grad_wide)
    grad_stream, grad_gain = norm_back(stream, gain, dot_nt(grad_wide, up))
    return grad + grad_stream, grad_gain, grad_up, grad_down


def squares(value_matrix, row_weight):
    return jnp.sum(row_weight[:, None] * value_matrix * value_matrix)


def plain_shards(
    tokens, cotangent, kept_counts, caption_lengths, attn_gain, qkv_weight, attn_out, mlp_gain,
    mlp_up, mlp_down, query_gain, image_gain, cross_gain, cross_query, cross_keyval, cross_out,
    cross_up, cross_down,
):
    f32 = jnp.float32
    dp_count = lax.axis_size("dp")
    lines = dp_count // 4
    tower, dp = lax.axis_index("tower"), lax.axis_index("dp")
    decoder = tower == 1
    row_count, width = tokens.shape[1:]
    rows = attn_gain.shape[1]
    few = query_gain.shape[0]

    def tile_row(value):
        return jnp.pad(value.astype(f32), (0, 128 - value.shape[0]))

    gain_tile = jnp.stack(
        [tile_row(attn_gain[0]), tile_row(mlp_gain[0])]
        + [tile_row(g) for g in (query_gain, image_gain, cross_gain)]
        + [jnp.zeros((128,), f32)] * 3
    )
    cross_shards = (cross_query, cross_keyval, cross_out, cross_up)
    cuts = tuple(w.shape[1] // 2 for w in cross_shards)
    pack = jnp.stack(
        [
            jnp.concatenate([w[:, h * n : (h + 1) * n] for w, n in zip(cross_shards, cuts)], axis=1)
            for h in range(2)
        ]
    ).astype(f32)
    self_parts = (qkv_weight.shape[2], attn_out.shape[2], mlp_up.shape[2])
    own_a = jnp.concatenate([qkv_weight[0], attn_out[0], mlp_up[0]], axis=1)
    full_a, full_d, full_ca, full_cd, full_g = plain_gather(
        own_a, mlp_down[0], pack, cross_down, gain_tile
    )
    qkv = full_a[:, : self_parts[0]]
    out = full_a[:, self_parts[0] : self_parts[0] + self_parts[1]]
    up = full_a[:, self_parts[0] + self_parts[1] :]
    down = full_d
    plane_gains = lax.dynamic_index_in_dim(full_g, tower, 0, keepdims=False)
    gain_1 = plane_gains[:, 0, :rows].reshape(-1)
    gain_2 = plane_gains[:, 1, :rows].reshape(-1)
    gain_q, gain_i, gain_c = (full_g[:, :, 2 + i, :few].reshape(-1) for i in range(3))

    stream = tokens[0].astype(f32)
    upstream = cotangent[0].astype(f32)
    allowed, cross_allowed, valid_rows = masks(kept_counts[0], caption_lengths, row_count, decoder)
    row_weight = jnp.where(decoder, valid_rows, True).astype(f32)

    normed = low(layer_norm(stream, gain_1))
    joined = low(dot(normed, qkv))
    query, key, value = jnp.split(joined, 3, axis=1)
    mixed, weight = attend(query, key, value, allowed)
    attn_branch = dot(mixed, out)
    middle = stream + attn_branch
    mlp_branch, mlp_stored = mlp_forward(middle, gain_2, up, down)
    layer_y = middle + mlp_branch
    image_rows = low(layer_y)
    arrived = lax.ppermute(image_rows, "tower", [(0, 1)])

    def run_cross(operands):
        text_y, image_in = operands
        at = [0]
        for n in cuts:
            at.append(at[-1] + n)
        cq, ckv, co, cu = (
            jnp.concatenate([full_ca[0][:, a:b], full_ca[1][:, a:b]], axis=1)
            for a, b in zip(at[:-1], at[1:])
        )
        image_in = image_in.astype(f32)
        image_normed = low(layer_norm(image_in, gain_i))
        keyval = low(dot(image_normed, ckv))
        c_key, c_value = jnp.split(keyval, 2, axis=1)
        c_normed = low(layer_norm(text_y, gain_q))
        c_query = low(dot(c_normed, cq))
        c_mixed, c_weight = attend(c_query, c_key, c_value, cross_allowed)
        c_branch = dot(c_mixed, co)
        c_middle = text_y + c_branch
        c_mlp, c_stored = mlp_forward(c_middle, gain_c, cu, full_cd)
        final_rows = c_middle + c_mlp
        grad_middle, grad_gain_c, grad_cu, grad_cd = mlp_back(
            c_middle, gain_c, cu, full_cd, c_stored, upstream
        )
        grad_branch = low(grad_middle)
        grad_co = dot_tn(c_mixed, grad_branch)
        grad_q, grad_k, grad_v = attend_back(
            c_query, c_key, c_value, c_weight, low(dot_nt(grad_branch, co))
        )
        grad_cq = dot_tn(c_normed, grad_q)
        grad_text, grad_gain_q = norm_back(text_y, gain_q, dot_nt(grad_q, cq))
        grad_keyval = jnp.concatenate([grad_k, grad_v], axis=1)
        grad_ckv = dot_tn(image_normed, grad_keyval)
        grad_image, grad_gain_i = norm_back(image_in, gain_i, dot_nt(grad_keyval, ckv))
        cross_sums = jnp.stack(
            [
                squares(c_branch, row_weight),
                squares(c_mlp, row_weight),
                squares(final_rows, row_weight),
            ]
        )
        grads = tuple(low(g) for g in (grad_cq, grad_ckv, grad_co, grad_cu))
        grad_ca = jnp.stack(
            [
                jnp.concatenate([g[:, h * n : (h + 1) * n] for g, n in zip(grads, cuts)], axis=1)
                for h in range(2)
            ]
        )
        return (
            low(final_rows),
            grad_middle + grad_text,
            low(grad_image),
            grad_ca,
            low(grad_cd),
            jnp.concatenate([grad_gain_q, grad_gain_i, grad_gain_c]),
            cross_sums,
        )

    def skip_cross(operands):
        shapes = jax.eval_shape(run_cross, operands)
        return tuple(jnp.zeros(s.shape, s.dtype) for s in shapes)

    final_rows, grad_text, grad_image, grad_ca, grad_cd, grad_cross_gains, cross_sums = lax.cond(
        decoder, run_cross, skip_cross, (layer_y, arrived)
    )
    returned = lax.ppermute(grad_image, "tower", [(1, 0)]).astype(f32)
    grad_top = jnp.where(decoder, grad_text, upstream + returned)

    grad_middle, grad_gain_2, grad_up, grad_down = mlp_back(
        middle, gain_2, up, down, mlp_stored, grad_top
    )
    grad_branch = low(grad_middle)
    grad_out = dot_tn(mixed, grad_branch)
    grad_joined = jnp.concatenate(
        attend_back(query, key, value, weight, low(dot_nt(grad_branch, out))), axis=1
    )
    grad_qkv = dot_tn(normed, grad_joined)
    grad_stream, grad_gain_1 = norm_back(stream, gain_1, dot_nt(grad_joined, qkv))
    grad_stream = grad_middle + grad_stream

    layer_sums = jnp.stack(
        [
            squares(stream, row_weight),
            squares(attn_branch, row_weight),
            squares(mlp_branch, row_weight),
            squares(layer_y, row_weight),
        ]
    )
    encoder_part = jnp.where(decoder, 0.0, layer_sums)
    decoder_part = jnp.where(decoder, jnp.concatenate([layer_sums[:3], cross_sums]), 0.0)
    counted = jnp.where(decoder, jnp.sum(valid_rows.astype(f32)), 0.0)
    line = tile_row(jnp.concatenate([encoder_part, decoder_part, counted[None]]))
    self_gains = jnp.concatenate([grad_gain_1, grad_gain_2])
    zero = jnp.zeros_like(self_gains)
    vec = jnp.concatenate(
        [
            jnp.where(decoder, zero, self_gains),
            jnp.where(decoder, self_gains, zero),
            grad_cross_gains,
            line,
        ]
    ).reshape(-1, 128)
    vec = jnp.pad(vec, ((0, -vec.shape[0] % 8), (0, 0)))
    grad_a = jnp.concatenate([low(grad_qkv), low(grad_out), low(grad_up)], axis=1)
    chips = 2 * lines
    results = plain_scatter(
        grad_a.reshape(chips, 2, rows, -1),
        low(grad_down).reshape(chips, 2, -1, width),
        grad_ca.reshape(2, 2, chips, 2 * few, -1),
        grad_cd.reshape(2, chips, 2, -1, width),
        vec,
        self_parts,
        cuts,
    )
    o_qkv, o_out, o_up, o_d, o_cq, o_ckv, o_co, o_cu, o_cd, o_vec = results
    flat = o_vec.reshape(-1)
    own_gains = lax.dynamic_slice(flat, (tower * 2 * width,), (2 * width,))
    g_1, g_2 = (lax.dynamic_slice(own_gains, (i * width + dp * rows,), (rows,)) for i in range(2))
    g_q, g_i, g_c = (
        lax.dynamic_slice(
            flat, ((4 + i) * width + (tower * dp_count + dp) * few,), (few,)
        )
        for i in range(3)
    )
    sums = flat[7 * width : 7 * width + 11]
    encoder_count = jnp.full((4,), float(row_count * dp_count), f32)
    divisor = jnp.concatenate([encoder_count, jnp.full((6,), 1.0, f32) * sums[10]]) * width
    rms_values = jnp.sqrt(sums[:10] / divisor)
    layer_out = jnp.where(decoder, final_rows, image_rows)
    return (
        layer_out[None], grad_stream[None], g_1[None], o_qkv[None], o_out[None], g_2[None],
        o_up[None], o_d[None], g_q, g_i, g_c, o_cq, o_ckv, o_co, o_cu, o_cd, rms_values,
    )


def fused_shards(
    tokens, cotangent, kept_counts, caption_lengths, attn_gain, qkv_weight, attn_out, mlp_gain,
    mlp_up, mlp_down, query_gain, image_gain, cross_gain, cross_query, cross_keyval, cross_out,
    cross_up, cross_down,
):
    f32 = jnp.float32
    dp_count = lax.axis_size("dp")
    lines = dp_count // 4
    row_count, width = tokens.shape[1:]
    rows = attn_gain.shape[1]
    few = query_gain.shape[0]
    cross_shards = (cross_query, cross_keyval, cross_out, cross_up)
    cuts = tuple(w.shape[1] // 2 for w in cross_shards)
    parts = (qkv_weight.shape[2], attn_out.shape[2], mlp_up.shape[2])
    (
        full_a, full_d, sum_ca, sum_cd, h1, qkv, mixed, weight, middle, h2, active, slope,
        gains, layer_out, top, vec,
    ) = forward(
        lines, cuts, parts, kept_counts, caption_lengths, attn_gain, mlp_gain,
        query_gain[None], image_gain[None], cross_gain[None], tokens[0], cotangent[0],
        *cross_shards, qkv_weight[0], attn_out[0], mlp_up[0], mlp_down[0], cross_down,
    )
    shard_shapes = [
        w.shape[-2:]
        for w in (
            qkv_weight, attn_out, mlp_up, mlp_down, cross_query, cross_keyval, cross_out, cross_up,
            cross_down,
        )
    ]
    *weight_grads, input_grad, o_vec = backward(
        lines, cuts, parts, shard_shapes, tokens[0], top, gains, vec, full_a, full_d, sum_ca,
        sum_cd, h1, qkv, mixed, weight, middle, h2, active, slope,
    )
    (
        layer_out, input_grad, o_qkv, o_out, o_up, o_d, o_cq, o_ckv, o_co, o_cu, o_cd,
        g_1, g_2, g_q, g_i, g_c, rms,
    ) = final(lines, rows, few, o_vec, layer_out, input_grad, *weight_grads)
    return (
        layer_out[None], input_grad[None], g_1, o_qkv[None], o_out[None], g_2, o_up[None],
        o_d[None], g_q[0], g_i[0], g_c[0], o_cq, o_ckv, o_co, o_cu, o_cd, rms[0, :10],
    )


def shards(*arrays):
    dp_count = lax.axis_size("dp")
    cross_query, cross_down = arrays[13], arrays[17]
    fills = dp_count % 4 == 0 and dp_count > 4
    fills = fills and cross_query.shape[0] % 8 == 0 and cross_down.shape[0] % 16 == 0
    return fused_shards(*arrays) if fills else plain_shards(*arrays)


def solution(mesh):
    rows = P("tower", "dp", None)
    gain = P("tower", "dp")
    cross_gain = P(("tower", "dp"))
    cross = P(("tower", "dp"), None)
    weights = (gain, rows, rows, gain, rows, rows) + (cross_gain,) * 3 + (cross,) * 5
    return jax.shard_map(
        shards,
        mesh=mesh,
        in_specs=(rows, rows, P("dp", None), P("dp")) + weights,
        out_specs=(rows, rows) + weights + (P(),),
        check_vma=False,
    )
```

```python
import functools

import jax
import jax.numpy as jnp
from jax import lax
from jax.experimental import pallas as pl
from jax.experimental.pallas import tpu as pltpu
from jax.sharding import PartitionSpec as P

HD = 64
CAP_LEN = 64
EPSILON = 1e-06
NEGATIVE = -1000000000.0

MESH_ID = pl.DeviceIdType.MESH
ANY = pl.BlockSpec(memory_space=pl.ANY)
VMEM = pl.BlockSpec(memory_space=pltpu.VMEM)
SMEM = pl.BlockSpec(memory_space=pltpu.SMEM)


class Net:
    def __init__(self, lines):
        self.lines = lines
        self.tower = lax.axis_index("tower")
        self.dp = lax.axis_index("dp")
        self.core = self.dp % 2
        self.y = (self.dp // 2) % 2
        self.z = self.dp // 4
        self.chip = self.dp // 2
        self.text = self.tower == 1
        self.image = self.tower == 0
        self.low = self.z > 0
        self.high = self.z < lines - 1
        self.sends = []
        self.slow = []

    def target(self, way):
        if way == "core":
            return (self.tower, self.dp + 1 - 2 * self.core)
        if way == "y":
            return (self.tower, self.dp + 2 - 4 * self.y)
        if way == "x":
            return (1 - self.tower, self.dp)
        if way == "up":
            return (self.tower, jnp.minimum(self.dp + 4, 4 * self.lines - 1))
        return (self.tower, jnp.maximum(self.dp - 4, 0))

    def beyond(self, k):
        return (self.tower, 4 * lax.rem(self.z + k, self.lines) + self.dp % 4)

    def greet(self):
        sem = pltpu.get_barrier_semaphore()
        partners = [self.target(way) for way in ("core", "y", "x")]
        partners += [self.beyond(k) for k in range(1, self.lines)]
        for partner in partners:
            pl.semaphore_signal(sem, inc=1, device_id=partner, device_id_type=MESH_ID)
        self.partners = len(partners)

    def meet(self):
        pl.semaphore_wait(pltpu.get_barrier_semaphore(), self.partners)

    def copy(self, way, src, dst, send_sem, recv_sem):
        return pltpu.make_async_remote_copy(
            src_ref=src,
            dst_ref=dst,
            send_sem=send_sem,
            recv_sem=recv_sem,
            device_id=self.target(way),
            device_id_type=MESH_ID,
        )

    def send(self, way, src, dst, send_sem, recv_sem, there=None, slow=False):
        copy = self.copy(way, src, dst, send_sem, recv_sem)
        when(there, copy.start)
        (self.slow if slow else self.sends).append((copy, there))

    def arrive(self, src, send_sem, recv_sem, there=None):
        copy = self.copy("core", src, src, send_sem, recv_sem)
        when(there, copy.wait_recv)

    def drain(self, kept=0):
        while len(self.sends) > kept:
            copy, there = self.sends.pop(0)
            when(there, copy.wait_send)

    def finish(self):
        self.drain()
        self.sends, self.slow = self.slow, []
        self.drain()


def when(there, act):
    if there is None:
        act()
    else:
        pl.when(there)(act)


def both(*conditions):
    kept = [c for c in conditions if c is not None]
    if not kept:
        return None
    result = kept[0]
    for c in kept[1:]:
        result = jnp.logical_and(result, c)
    return result


class Gather:
    def __init__(self, net, own, place, crossing, send_sem, recv_sem, local_sem, everywhere=False):
        self.net, self.own, self.place, self.crossing = net, own, place, crossing
        self.send_sem, self.recv_sem, self.local_sem = send_sem, recv_sem, local_sem
        lines = net.lines
        self.at_z, self.at_y, self.at_x, self.at_core = 0, 2 * lines, 3 * lines, 5 * lines
        self.to_x = net.image if crossing else None
        self.to_core = net.text if crossing and not everywhere else None

    @staticmethod
    def sems(lines):
        return 11 * lines

    def piece(self, chip, tower=None, core=None):
        net = self.net
        return self.place(
            net.tower if tower is None else tower, chip, net.core if core is None else core
        )

    def pass_on(self, chip, src, there=None, tower=None):
        net = self.net
        dst = self.piece(chip, tower)
        plane = net.tower if tower is None else tower
        if self.crossing and tower is None:
            s = self.at_x + chip
            net.send("x", src, dst, self.send_sem.at[s], self.recv_sem.at[s], both(there, net.image))
        s = self.at_core + plane * 2 * net.lines + chip
        net.send("core", src, dst, self.send_sem.at[s], self.recv_sem.at[s], both(there, self.to_core))

    def start(self):
        net = self.net
        dst = self.piece(net.chip)
        self.local = None
        if self.own is None:
            self.own = dst
        else:
            self.local = pltpu.make_async_copy(self.own, dst, self.local_sem)
            self.local.start()
        for way, there, slot in (("up", net.high, 1), ("down", net.low, net.lines + 1)):
            s = self.at_z + slot
            net.send(way, self.own, dst, self.send_sem.at[s], self.recv_sem.at[s], there)
        s = self.at_y + net.z
        net.send("y", self.own, dst, self.send_sem.at[s], self.recv_sem.at[s])
        self.pass_on(net.chip, self.own)

    def hop(self, k):
        net = self.net
        for way, there, further, sign, base in (
            ("up", net.z >= k, net.high, -1, 0),
            ("down", net.z + k < net.lines, net.low, 1, net.lines),
        ):
            z = jnp.clip(net.z + sign * k, 0, net.lines - 1)
            chip = 2 * z + net.y
            src = self.piece(chip)
            s = self.at_z + base + k
            net.arrive(src, self.send_sem.at[s], self.recv_sem.at[s], there)
            if k + 1 < net.lines:
                s = s + 1
                net.send(way, src, src, self.send_sem.at[s], self.recv_sem.at[s], both(there, further))
            s = self.at_y + z
            net.send("y", src, src, self.send_sem.at[s], self.recv_sem.at[s], there)
            self.pass_on(chip, src, there)

    def beside(self, k):
        net = self.net
        ways = ((None, 0),) if k == 0 else ((net.z >= k, -k), (net.z + k < net.lines, k))
        for there, offset in ways:
            z = jnp.clip(net.z + offset, 0, net.lines - 1)
            chip = 2 * z + 1 - net.y
            src = self.piece(chip)
            s = self.at_y + z
            net.arrive(src, self.send_sem.at[s], self.recv_sem.at[s], there)
            self.pass_on(chip, src, there)

    def from_image(self, k):
        if not self.crossing:
            return
        net = self.net
        ways = ((None, 0),) if k == 0 else ((net.z >= k, -k), (net.z + k < net.lines, k))
        for there, offset in ways:
            z = jnp.clip(net.z + offset, 0, net.lines - 1)
            for y in (net.y, 1 - net.y):
                chip = 2 * z + y
                src = self.piece(chip, 0)
                s = self.at_x + chip
                net.arrive(src, self.send_sem.at[s], self.recv_sem.at[s], both(there, net.text))
                self.pass_on(chip, src, both(there, net.text), 0)

    def done(self):
        net = self.net
        if self.local is not None:
            self.local.wait()

        def all_of(tower, base):
            def one(chip, carry):
                s = self.at_core + base + chip
                src = self.piece(chip, tower, 1 - net.core)
                net.arrive(src, self.send_sem.at[s], self.recv_sem.at[s])
                return carry

            def run():
                lax.fori_loop(0, 2 * net.lines, one, 0)

            return run

        when(self.to_core, all_of(net.tower, net.tower * 2 * net.lines))
        if self.crossing:
            when(net.text, all_of(0, 0))


class GatherBeside(Gather):
    def start(self):
        net = self.net
        dst = self.piece(net.chip)
        self.local = None
        if self.own is None:
            self.own = dst
        else:
            self.local = pltpu.make_async_copy(self.own, dst, self.local_sem)
            self.local.start()
        s = self.at_y
        net.send("y", self.own, dst, self.send_sem.at[s], self.recv_sem.at[s])
        self.set_off(self.own, net.chip, 0)
        self.pass_on(net.chip, self.own)

    def set_off(self, src, chip, second):
        net = self.net
        dst = self.piece(chip)
        for way, there, slot in (("up", net.high, 1), ("down", net.low, net.lines + 1)):
            s = self.z_sem(second) + slot
            net.send(way, src, dst, self.send_sem.at[s], self.recv_sem.at[s], there)

    def z_sem(self, second):
        return 9 * self.net.lines if second else self.at_z

    def hop(self, k):
        net = self.net
        for way, there, further, sign, base in (
            ("up", net.z >= k, net.high, -1, 0),
            ("down", net.z + k < net.lines, net.low, 1, net.lines),
        ):
            z = jnp.clip(net.z + sign * k, 0, net.lines - 1)
            for second, y in ((0, net.y), (1, 1 - net.y)):
                chip = 2 * z + y
                src = self.piece(chip)
                s = self.z_sem(second) + base + k
                net.arrive(src, self.send_sem.at[s], self.recv_sem.at[s], there)
                if k + 1 < net.lines:
                    s = s + 1
                    net.send(
                        way, src, src, self.send_sem.at[s], self.recv_sem.at[s], both(there, further)
                    )
                self.pass_on(chip, src, there)

    def beside(self, k):
        if k > 0:
            return
        net = self.net
        chip = 2 * net.z + 1 - net.y
        src = self.piece(chip)
        s = self.at_y
        net.arrive(src, self.send_sem.at[s], self.recv_sem.at[s])
        self.set_off(src, chip, 1)
        self.pass_on(chip, src)


class Small:
    def __init__(self, net, mine, arrived, sums, wide, send_sem, recv_sem):
        self.net, self.mine, self.arrived, self.sums, self.wide = net, mine, arrived, sums, wide
        self.send_sem, self.recv_sem = send_sem, recv_sem

    def exchange(self, step):
        src = self.mine if step == 0 else self.sums.at[step - 1]
        self.net.send(
            ("core", "y", "x")[step],
            src,
            self.arrived.at[step],
            self.send_sem.at[step],
            self.recv_sem.at[step],
        )

    def collect(self, step):
        self.net.arrive(self.arrived.at[step], self.send_sem.at[step], self.recv_sem.at[step])
        src = self.mine if step == 0 else self.sums.at[step - 1]
        self.sums[step] = src[...] + self.arrived[step]

    def spread(self):
        net = self.net
        for k in range(1, net.lines):
            s = 2 + k
            copy = pltpu.make_async_remote_copy(
                src_ref=self.sums.at[2],
                dst_ref=self.wide.at[k - 1],
                send_sem=self.send_sem.at[s],
                recv_sem=self.recv_sem.at[s],
                device_id=net.beyond(k),
                device_id_type=MESH_ID,
            )
            copy.start()
            net.sends.append((copy, None))

    def total(self, out):
        total = self.sums[2]
        for k in range(1, self.net.lines):
            s = 2 + k
            self.net.arrive(self.wide.at[k - 1], self.send_sem.at[s], self.recv_sem.at[s])
            total = total + self.wide[k - 1]
        out[...] = total


def product(a, b, axis_a=1, axis_b=0):
    return lax.dot_general(
        a, b, (((axis_a,), (axis_b,)), ((), ())), preferred_element_type=jnp.float32
    )


def low(value):
    return value.astype(jnp.bfloat16)


def blocks(count, size, body):
    def one(i, carry):
        body(pl.ds(pl.multiple_of(i * size, size), size))
        return carry

    lax.fori_loop(0, count // size, one, 0)


def row_step(rows):
    return next(s for s in (96, 64, 48, 32, 16) if rows % s == 0)


def centred(value):
    center = value - jnp.mean(value, axis=-1, keepdims=True)
    spread = jnp.mean(center * center, axis=-1, keepdims=True)
    return center * lax.rsqrt(spread + EPSILON), lax.rsqrt(spread + EPSILON)


def norm_rows(src, gain, out, also=None):
    def body(rows):
        value = src[rows, :].astype(jnp.float32)
        if also is not None:
            also(rows, value)
        out[rows, :] = low(centred(value)[0] * gain)

    blocks(src.shape[0], row_step(src.shape[0]), body)


def norm_back_rows(src, gain, grad, done, gain_grad, fresh=True):
    if fresh:
        gain_grad[...] = jnp.zeros_like(gain_grad)

    def body(rows):
        n, scale = centred(src[rows, :].astype(jnp.float32))
        out = grad[rows, :]
        dn = out * gain
        gain_grad[...] += jnp.sum(out * n, axis=0, keepdims=True)
        back = dn - jnp.mean(dn, axis=-1, keepdims=True)
        done(rows, (back - n * jnp.mean(dn * n, axis=-1, keepdims=True)) * scale)

    blocks(src.shape[0], row_step(src.shape[0]), body)


class Sums:
    def __init__(self, ref, weight):
        self.ref, self.weight = ref, weight
        ref[...] = jnp.zeros_like(ref)

    def add(self, slot, rows, value):
        kept = jnp.sum(value * value, axis=-1, keepdims=True) * self.weight[rows, :]
        total = jnp.sum(kept, axis=0, keepdims=True)
        at = pl.ds(slot, 1)
        self.ref[at, :] = self.ref[at, :] + jnp.broadcast_to(total, (1, self.ref.shape[1]))

    def line(self):
        shape = self.ref.shape
        row = lax.broadcasted_iota(jnp.int32, shape, 0)
        lane = lax.broadcasted_iota(jnp.int32, shape, 1)
        return jnp.sum(jnp.where(row == lane, self.ref[...], 0.0), axis=0, keepdims=True)


def pair_count(width):
    pairs = width // (2 * HD)
    return next(n for n in (3, 2, 1) if pairs % n == 0)


def attention(query, key, value, allowed, weight, mixed):
    count, width = mixed.shape
    group = pair_count(width)
    left = lax.broadcasted_iota(jnp.int32, (count, 2 * HD), 1) < HD

    def one(step, carry):
        kept, scores = [], []
        for i in range(group):
            pair = step * group + i
            q, k, v = query(pair), key(pair), value(pair)
            zero = jnp.zeros_like(q)
            kept.append((pair, v))
            for part in (jnp.where(left, q, zero), jnp.where(left, zero, q)):
                scores.append(product(part, k, 1, 1) * HD ** (-0.5))
        weights = []
        for s in scores:
            s = jnp.where(allowed[...] > 0, s, NEGATIVE)
            e = jnp.exp(s - jnp.max(s, axis=-1, keepdims=True))
            weights.append(low(e / jnp.sum(e, axis=-1, keepdims=True)))
        for i, (pair, v) in enumerate(kept):
            first, second = weights[2 * i : 2 * i + 2]
            weight[2 * pair] = first
            weight[2 * pair + 1] = second
            both_heads = jnp.where(left, product(first, v), product(second, v))
            mixed[:, pl.ds(pl.multiple_of(pair * 2 * HD, 2 * HD), 2 * HD)] = low(both_heads)
        return carry

    lax.fori_loop(0, width // (2 * HD) // group, one, 0)


def attention_back(query, key, value, grad_mixed, weight, width, done):
    count = weight.shape[1]
    group = pair_count(width)
    left = lax.broadcasted_iota(jnp.int32, (count, 2 * HD), 1) < HD

    def one(step, carry):
        kept, raw = [], []
        for i in range(group):
            pair = step * group + i
            q, k, v, d = query(pair), key(pair), value(pair), grad_mixed(pair)
            zero = jnp.zeros_like(q)
            kept.append((pair, q, k))
            for h, part in enumerate((jnp.where(left, d, zero), jnp.where(left, zero, d))):
                raw.append((part, product(part, v, 1, 1), weight[2 * pair + h]))
        grads = []
        for part, dp, p in raw:
            p32 = p.astype(jnp.float32)
            grads.append(low(p32 * (dp - jnp.sum(dp * p32, axis=-1, keepdims=True))))
        for i, (pair, q, k) in enumerate(kept):
            (d0, _, p0), (d1, _, p1) = raw[2 * i : 2 * i + 2]
            s0, s1 = grads[2 * i : 2 * i + 2]
            zero = jnp.zeros_like(q)
            dv = product(p0, d0, 0, 0) + product(p1, d1, 0, 0)
            dk = product(s0, jnp.where(left, q, zero), 0, 0)
            dk = dk + product(s1, jnp.where(left, zero, q), 0, 0)
            dq = jnp.where(left, product(s0, k), product(s1, k))
            done(pair, low(dq * HD ** (-0.5)), low(dk * HD ** (-0.5)), low(dv))
        return carry

    lax.fori_loop(0, width // (2 * HD) // group, one, 0)


def pairs_of(ref, base=0):
    return lambda pair: ref[:, pl.ds(pl.multiple_of(base + pair * 2 * HD, 2 * HD), 2 * HD)]


def gelu_both(value):
    scale = 0.7978845608028654
    cube = 0.044715
    square = value * value
    bend = jnp.tanh(scale * value * (1.0 + cube * square))
    half = 0.5 * (1.0 + bend)
    slope = half + 0.5 * value * (1.0 - bend * bend) * scale * (1.0 + 3.0 * cube * square)
    return value * half, slope


def activate(wide, active, slope, columns):
    def body(rows):
        a, s = gelu_both(wide[rows, :])
        active[rows, columns] = low(a)
        slope[rows, columns] = s.astype(slope.dtype)

    blocks(wide.shape[0], 16, body)


GATHER = ("qk", "vo", "ca", "u0", "u1", "cu", "d0", "d1", "d2", "cd")
GATHER_NAMES = ("qk", "vo", "u0", "u1", "d0", "d1", "d2", "ca", "cu", "cd")
LEAD = 2
GATHER_BESIDE = ("d0", "d1")
GATHER_FOUR = (
    "start d0", "start d2", "start d1", "start qk", "start cd", "do block", "start cu", "start vo",
    "start ca", "hop cd 1", "hop ca 1", "beside cd 0", "start u0", "hop qk 1", "beside d1 0",
    "hop ca 2", "beside d0 0", "hop vo 1", "do gains0", "beside ca 0", "hop qk 2", "do gains1",
    "beside cd 1", "hop cd 2", "beside u0 0", "beside qk 0", "hop vo 2", "hop cu 1", "hop u0 1",
    "beside vo 0", "hop ca 3", "hop vo 3", "beside ca 1", "hop u0 2", "do gains2",
    "from_image ca 0", "beside cd 2", "hop cu 2", "from_image cd 0", "beside cu 0", "hop cd 3",
    "hop d1 1", "start u1", "beside cu 1", "beside qk 1", "hop qk 3", "beside ca 2", "hop u1 1",
    "beside vo 1", "beside ca 3", "hop u0 3", "hop u1 2", "beside qk 2", "from_image ca 1",
    "hop d0 1", "from_image cu 0", "beside qk 3", "beside d2 0", "hop u1 3", "beside vo 2",
    "from_image cu 1", "beside u0 1", "done qk", "do norm", "do qk", "hop d2 1", "beside u1 0",
    "beside vo 3", "hop d0 2", "from_image ca 2", "beside cd 3", "from_image cd 1", "hop cu 3",
    "hop d2 2", "done vo", "do v", "do attend", "do out", "beside u1 1", "beside cu 2",
    "from_image cd 2", "hop d1 2", "beside u0 2", "beside u1 2", "beside u1 3", "beside u0 3",
    "from_image cd 3", "hop d0 3", "hop d2 3", "from_image ca 3", "done u0", "do up0",
    "beside cu 3", "done u1", "do up1", "do keep", "hop d1 3", "done d0", "do down0",
    "from_image cu 2", "beside d2 1", "from_image cu 3", "beside d2 2", "beside d2 3", "done d1",
    "do down1", "done cd", "done ca", "done cu", "done d2", "do down2", "do end", "do query",
    "do rows", "do cross0", "do cross1", "do cross2", "do cross3", "do cross4",
)
AFTER = {
    "qk": ("norm", "qk"),
    "vo": ("v", "attend", "out"),
    "u0": ("up0",),
    "u1": ("up1", "keep"),
    "d0": ("down0",),
    "d1": ("down1",),
    "d2": ("down2", "end"),
}


def parsed(lines):
    events = []
    for line in lines:
        kind, name, *k = line.split()
        events.append((kind, name, int(k[0]) if k else 0))
    return events


def gather_order(lines):
    if lines == 4 and GATHER_FOUR:
        return parsed(GATHER_FOUR)
    slots = {}

    def put(slot, kind, name, k=0):
        slots.setdefault(max(slot, 0), []).append((kind, name, k))

    for index, name in enumerate(GATHER):
        late = 1 if name in GATHER_BESIDE else 0
        if name in ("ca", "cu"):
            put(index - LEAD + 1, "do", "block")
        put(index - LEAD + 1, "start", name)
        if late:
            put(index + 1, "beside", name)
        for k in range(1, lines):
            put(index + k + late, "hop", name, k)
        for k in range(late, lines):
            put(index + k + 1, "beside", name, k)
        for k in range(lines):
            put(index + k + 2 + late, "from_image", name, k)
        put(index + lines + 1 + late, "done", name)
        for step in AFTER.get(name, ()):
            put(index + lines + 1 + late, "do", step)
    for index in range(3):
        put(index + 1, "do", "gains%d" % index)
    rank = {"start": 0, "beside": 2, "hop": 1, "from_image": 3, "done": 4, "do": 5}
    events = []
    for slot in sorted(slots):

        def place(event):
            kind, name, k = event
            if kind == "beside" and name in GATHER_BESIDE:
                return 0.5
            if kind == "do" and name == "block":
                return -1
            if kind == "do" and name.startswith("gains"):
                return 0.2
            return rank[kind]

        events += [e for e in sorted(slots[slot], key=place) if e not in events]
    last = ["query", "rows"] + ["cross%d" % i for i in range(5)]
    return events + [("do", name, 0) for name in last]


def place_gains(net, own, cross, out):
    width = out.shape[1]

    def placed(gain, index):
        count = gain.shape[1]
        lane = lax.broadcasted_iota(jnp.int32, (count, width), 1)
        row = lax.broadcasted_iota(jnp.int32, (count, width), 0)
        pick = jnp.where(lane == index * count + row, 1.0, 0.0)
        many = jnp.broadcast_to(gain[...].astype(jnp.float32), (8, count))
        return product(low(many), low(pick))[0:1]

    out[...] = jnp.zeros_like(out)
    for i, gain in enumerate(own):
        row = placed(gain, net.dp)
        out[i : i + 1, :] = jnp.where(net.image, row, 0.0)
        out[i + 2 : i + 3, :] = jnp.where(net.text, row, 0.0)
    for i, gain in enumerate(cross):
        out[4 + i : 5 + i, :] = placed(gain, net.tower * 4 * net.lines + net.dp)


def fill_masks(net, counts, lengths, allowed, cross_allowed, row_weight):
    shape = allowed.shape

    def place(index):
        image_of, bound = jnp.zeros_like(index), jnp.int32(0)
        for i in range(counts.shape[1]):
            bound = bound + counts[0, i]
            image_of = image_of + jnp.where(index >= bound, 1, 0)
        caption_of = index // CAP_LEN
        within = index - caption_of * CAP_LEN
        length = jnp.zeros_like(index)
        for i in range(lengths.shape[0]):
            length = jnp.where(caption_of == i, lengths[i], length)
        return image_of, caption_of, within, within < length

    row = place(lax.broadcasted_iota(jnp.int32, shape, 0))
    key = place(lax.broadcasted_iota(jnp.int32, shape, 1))
    image_mask = row[0] == key[0]
    text_mask = (row[1] == key[1]) & (key[2] <= row[2]) & key[3]
    here = jnp.where(net.text, text_mask.astype(jnp.float32), image_mask.astype(jnp.float32))
    allowed[...] = here
    cross_allowed[...] = (row[1] == key[0]).astype(jnp.float32)
    valid = place(lax.broadcasted_iota(jnp.int32, row_weight.shape, 0))[3]
    row_weight[...] = jnp.where(net.text, valid.astype(jnp.float32), 1.0)


def forward_kernel(
    lines, cuts, parts,
    counts, lengths, g_attn, g_mlp, g_query, g_image, g_cross, tok, cot, cq, ckv, co, cu, own_qkv, own_out, own_up, own_d, own_cd,
    full_a, full_d, sum_ca, sum_cd, o_h1, o_qkv, o_mixed, o_weight, o_middle, o_h2, o_active, o_slope,
    gains, layer_out, top, vec,
    w_a, w_d, w_ca, w_cd, h1, qkv, mixed, weight, middle, h2, active, slope, out_y, wide, branch,
    passed, returned, image_out, n_x, g_mixed, n_q, n_i, query, keyval, c_mixed, c_weight, c_middle, h3, grad_wide, g_small,
    allowed, cross_allowed, row_weight, gvec, pack, swap, block, rcv_a, rcv_d, arrived, totals, spread, sums_ref, gain_rows,
    send_sem, recv_sem, local_sem, swap_sem, s_send, s_recv, pass_sem, out_sem, d_send, d_recv, d_local, own_sem,
):
    net = Net(lines)
    net.greet()
    text, image = net.text, net.image
    rows, depth = own_qkv.shape[0], own_d.shape[0]
    all_a = sum(parts)
    few, part = pack.shape[1], own_cd.shape[0]
    width = tok.shape[1]
    half = pack.shape[2]
    a_qkv, a_out = parts[0], parts[0] + parts[1]
    q_end, kv_end, o_end = cuts[0], cuts[0] + cuts[1], cuts[0] + cuts[1] + cuts[2]
    tile = width

    placing = []
    for index, (src, at) in enumerate(((own_qkv, 0), (own_out, a_qkv), (own_up, a_out))):
        here = pl.ds(pl.multiple_of(net.dp * rows, rows), rows)
        copy = pltpu.make_async_copy(
            src, w_a.at[here, at : at + src.shape[1]], own_sem.at[index]
        )
        copy.start()
        placing.append(copy)
    at = 0
    for src, n in zip((cq, ckv, co, cu), cuts):
        whole = src[...].astype(jnp.float32)
        for h in range(2):
            pack[h, :, at : at + n] = whole[:, h * n : (h + 1) * n]
        at += n
    place_gains(net, (g_attn, g_mlp), (g_query, g_image, g_cross), gvec)
    net.meet()
    for copy in placing:
        copy.wait()

    def columns(first, last):
        return lambda tower, chip, core: w_a.at[
            pl.ds(pl.multiple_of((2 * chip + core) * rows, rows), rows), first:last
        ]

    def crossed(first, last):
        return lambda tower, chip, core: w_ca.at[
            core,
            pl.ds(pl.multiple_of((tower * 2 * lines + chip) * 2 * few, 2 * few), 2 * few),
            first:last,
        ]

    def plan(index, own, place, crossing):
        beside = GATHER_NAMES[index] in GATHER_BESIDE
        kind = GatherBeside if beside else Gather
        return kind(
            net, own, place, crossing, send_sem.at[index], recv_sem.at[index], local_sem.at[index]
        )

    def self_part(index, first, last):
        return plan(index, None, columns(first, last), False)

    def down_part(index, first, last):
        return plan(
            index,
            own_d.at[:, first:last],
            lambda tower, chip, core: w_d.at[
                pl.ds(pl.multiple_of((2 * chip + core) * depth, depth), depth), first:last
            ],
            False,
        )

    def cross_part(index, first, last):
        return plan(index, block.at[:, first:last], crossed(first, last), True)

    mid, third = a_qkv - width, width // 3
    jobs = {
        "qk": self_part(0, 0, mid),
        "vo": self_part(1, mid, a_out),
        "u0": self_part(2, a_out, a_out + 2 * width),
        "u1": self_part(3, a_out + 2 * width, all_a),
        "d0": down_part(4, 0, third),
        "d1": down_part(5, third, 2 * third),
        "d2": down_part(6, 2 * third, width),
        "ca": cross_part(7, 0, o_end),
        "cu": cross_part(8, o_end, half),
        "cd": plan(
            9,
            own_cd,
            lambda tower, chip, core: w_cd.at[
                pl.ds(pl.multiple_of((tower * 4 * lines + 2 * chip + core) * part, part), part), :
            ],
            True,
        ),
    }
    kept = []

    def keep(src, dst):
        copy = pltpu.make_async_copy(src, dst, out_sem.at[len(kept)])
        copy.start()
        kept.append(copy)

    swapped = net.copy("core", pack.at[1 - net.core], swap, swap_sem.at[0], swap_sem.at[1])
    swapped.start()
    small = Small(net, gvec, arrived, totals, spread, s_send, s_recv)
    sums = Sums(sums_ref, row_weight)
    base = 4 * net.tower
    gain_rows[...] = jnp.zeros_like(gain_rows)
    first = net.core == 0

    def gain(at):
        return jnp.where(text, gains[at + 2 : at + 3, :], gains[at : at + 1, :])

    def build_block():
        swapped.wait()
        mine = pack[net.core]
        theirs = swap[...]
        block[0:few] = low(jnp.where(first, mine, theirs))
        block[few:] = low(jnp.where(first, theirs, mine))

    def gains_over(index):
        def run():
            small.collect(index)
            if index < 2:
                small.exchange(index + 1)
            else:
                small.spread()

        return run

    def first_norm():
        small.total(gains)
        fill_masks(net, counts, lengths, allowed, cross_allowed, row_weight)
        norm_rows(tok, gain(0), h1, lambda r, v: sums.add(base, r, v))
        keep(h1, o_h1)

    def project(first_column, last_column):
        def run():
            def qkv_tile(i, carry):
                cols = pl.ds(pl.multiple_of(first_column + i * tile, tile), tile)
                qkv[:, cols] = low(product(h1[...], w_a[:, cols]))
                return carry

            lax.fori_loop(0, (last_column - first_column) // tile, qkv_tile, 0)

        return run

    def attend():
        keep(qkv, o_qkv)
        attention(
            pairs_of(qkv), pairs_of(qkv, width), pairs_of(qkv, 2 * width), allowed, weight, mixed
        )
        keep(weight, o_weight)
        keep(mixed, o_mixed)

    def attn_out():
        branch[...] = product(mixed[...], w_a[:, a_qkv:a_out])

        def add_branch(r):
            value = branch[r, :]
            sums.add(base + 1, r, value)
            middle[r, :] = tok[r, :].astype(jnp.float32) + value

        blocks(tok.shape[0], row_step(tok.shape[0]), add_branch)
        keep(middle, o_middle)
        norm_rows(middle, gain(1), h2)
        keep(h2, o_h2)

    def go_up(first_tile, last_tile):
        def run():
            def up_tile(i, carry):
                at = pl.multiple_of((first_tile + i) * tile, tile)
                wide[...] = product(h2[...], w_a[:, pl.ds(a_out + at, tile)])
                activate(wide, active, slope, pl.ds(at, tile))
                return carry

            lax.fori_loop(0, last_tile - first_tile, up_tile, 0)

        return run

    def keep_up():
        keep(active, o_active)
        keep(slope, o_slope)
        keep(w_a, full_a)

    def go_down(index):
        first_column, last_column = index * third, (index + 1) * third

        def run():
            branch[:, first_column:last_column] = product(
                active[...], w_d[:, first_column:last_column]
            )

            def add_mlp(r):
                value = branch[r, first_column:last_column]
                sums.add(base + 2, r, value)
                y = middle[r, first_column:last_column] + value
                out_y[r, first_column:last_column] = y
                image_out[r, first_column:last_column] = low(y)

                @pl.when(image)
                def _():
                    sums.add(3, r, y)

            blocks(tok.shape[0], row_step(tok.shape[0]), add_mlp)
            net.send(
                "x",
                image_out.at[:, first_column:last_column],
                passed.at[:, first_column:last_column],
                pass_sem.at[0, index],
                pass_sem.at[1, index],
                image,
            )

        return run

    def self_end():
        keep(w_d, full_d)

    def rows_arrive():
        for index in range(3):
            part_of = passed.at[:, index * third : (index + 1) * third]
            net.arrive(part_of, pass_sem.at[0, index], pass_sem.at[1, index], text)

    def cross_queries():
        @pl.when(text)
        def _():
            norm_rows(out_y, gains[4:5, :], n_q)
            for h in range(2):
                at = h * cuts[0]
                query[:, at : at + cuts[0]] = low(product(n_q[...], w_ca[h, :, 0:q_end]))

    def cross_keys():
        @pl.when(text)
        def _():
            norm_rows(passed, gains[5:6, :], n_i)
            for h in range(2):
                at = h * width
                keyval[:, at : at + width] = low(product(n_i[...], w_ca[h, :, q_end:kv_end]))

    def cross_attend():
        @pl.when(text)
        def _():
            attention(
                pairs_of(query),
                pairs_of(keyval),
                pairs_of(keyval, width),
                cross_allowed,
                c_weight,
                c_mixed,
            )

    def cross_out():
        @pl.when(text)
        def _():
            for h in range(2):
                at = h * cuts[2]
                branch[:, at : at + cuts[2]] = product(c_mixed[...], w_ca[h, :, kv_end:o_end])

            def add_cross(r):
                value = branch[r, :]
                sums.add(7, r, value)
                c_middle[r, :] = out_y[r, :] + value

            blocks(tok.shape[0], row_step(tok.shape[0]), add_cross)
            norm_rows(c_middle, gains[6:7, :], h3)

    def cross_up():
        for copy in kept:
            copy.wait()

        @pl.when(text)
        def _():
            for h in range(2):

                def one(i, carry):
                    at = pl.multiple_of(i * tile, tile)
                    wide[...] = product(h3[...], w_ca[h, :, pl.ds(o_end + at, tile)])
                    activate(wide, active, slope, pl.ds(h * cuts[3] + at, tile))
                    return carry

                lax.fori_loop(0, cuts[3] // tile, one, 0)

    def cross_down():
        @pl.when(text)
        def _():
            branch[...] = product(active[...], w_cd[...])

            def add_final(r):
                value = branch[r, :]
                sums.add(8, r, value)
                z = c_middle[r, :] + value
                sums.add(9, r, z)
                layer_out[r, :] = low(z)

            blocks(tok.shape[0], row_step(tok.shape[0]), add_final)

    tiles = active.shape[1] // tile
    steps = {
        "block": build_block,
        "gains0": gains_over(0),
        "gains1": gains_over(1),
        "gains2": gains_over(2),
        "norm": first_norm,
        "qk": project(0, mid),
        "v": project(mid, a_qkv),
        "attend": attend,
        "out": attn_out,
        "up0": go_up(0, tiles // 2),
        "up1": go_up(tiles // 2, tiles),
        "keep": keep_up,
        "down0": go_down(0),
        "down1": go_down(1),
        "down2": go_down(2),
        "end": self_end,
        "query": cross_queries,
        "rows": rows_arrive,
        "cross0": cross_keys,
        "cross1": cross_attend,
        "cross2": cross_out,
        "cross3": cross_up,
        "cross4": cross_down,
    }
    small.exchange(0)
    for kind, name, k in gather_order(lines):
        if kind == "do":
            steps[name]()
        elif kind == "start":
            jobs[name].start()
        elif kind == "done":
            jobs[name].done()
        else:
            getattr(jobs[name], kind)(k)

    net.finish()
    def hand(index, src, rcv, there=text):
        net.send("core", src, rcv, d_send.at[index], d_recv.at[index], there)

    def merge(index, own, rcv, out):
        net.arrive(rcv, d_send.at[index], d_recv.at[index], text)

        @pl.when(text)
        def _():
            def add(r):
                rcv[r, :] = low(own[r, :].astype(jnp.float32) + rcv[r, :].astype(jnp.float32))

            blocks(rcv.shape[0], 16, add)
            pltpu.make_async_copy(rcv, out, d_local.at[index]).start()

    @pl.when(text)
    def _():
        def down_tile(i, carry):
            cols = pl.ds(pl.multiple_of(i * tile, tile), tile)
            found = low(product(active[:, cols], cot[...], 0, 0))
            for k in range(tile // part):
                at = (k % 2) * (w_d.shape[0] // 2) + (k // 2) * part + i * (tile // 2)
                w_d[pl.ds(pl.multiple_of(at, part), part), :] = found[k * part : (k + 1) * part]
            grad = product(cot[...], w_cd[cols, :], 1, 1)
            grad_wide[:, cols] = low(grad * slope[:, cols])
            return carry

        lax.fori_loop(0, active.shape[1] // tile, down_tile, 0)

    share = w_d.shape[0] // 2
    hand(0, w_d.at[pl.ds(pl.multiple_of((1 - net.core) * share, share), share), :], rcv_d)

    @pl.when(text)
    def _():
        for h in range(2):

            def up_grad(i, carry):
                at = pl.multiple_of(i * tile, tile)
                w_a[:, pl.ds(h * half + o_end + at, tile)] = low(
                    product(h3[...], grad_wide[:, pl.ds(h * cuts[3] + at, tile)], 0, 0)
                )
                return carry

            lax.fori_loop(0, cuts[3] // tile, up_grad, 0)

    theirs_at = pl.multiple_of((1 - net.core) * half, half)
    mine_at = pl.multiple_of(net.core * half, half)
    hand(1, w_a.at[:, pl.ds(theirs_at + o_end, half - o_end)], rcv_a.at[:, o_end:half])

    @pl.when(text)
    def _():
        branch[...] = product(grad_wide[:, 0 : cuts[3]], w_ca[0, :, o_end:half], 1, 1) + product(
            grad_wide[:, cuts[3] :], w_ca[1, :, o_end:half], 1, 1
        )

        def mid_done(r, back):
            total = cot[r, :].astype(jnp.float32) + back
            c_middle[r, :] = total
            n_x[r, :] = low(total)

        norm_back_rows(c_middle, gains[6:7, :], branch, mid_done, g_small)
        gain_rows[6:7, :] = g_small[...]
        branch[...] = product(n_x[:, 0 : cuts[2]], w_ca[0, :, kv_end:o_end], 1, 1) + product(
            n_x[:, cuts[2] :], w_ca[1, :, kv_end:o_end], 1, 1
        )
        g_mixed[...] = low(branch[...])

        def att_done(pair, dq, dk, dv):
            at = pl.multiple_of(pair * 2 * HD, 2 * HD)
            query[:, pl.ds(at, 2 * HD)] = dq
            keyval[:, pl.ds(at, 2 * HD)] = dk
            keyval[:, pl.ds(width + at, 2 * HD)] = dv

        attention_back(
            pairs_of(query),
            pairs_of(keyval),
            pairs_of(keyval, width),
            pairs_of(g_mixed),
            c_weight,
            width,
            att_done,
        )

    rows_half = tok.shape[0] // 2
    for index in range(2):
        at = index * rows_half
        here = slice(at, at + rows_half)

        @pl.when(text)
        def _():
            branch[here, :] = product(
                keyval[here, 0:width], w_ca[0, :, q_end:kv_end], 1, 1
            ) + product(keyval[here, width:], w_ca[1, :, q_end:kv_end], 1, 1)

            def image_done(r, back):
                image_out[pl.ds(at + r.start, r.size), :] = low(back)

            norm_back_rows(
                passed.at[here], gains[5:6, :], branch.at[here], image_done, g_small, index == 0
            )
            if index == 1:
                gain_rows[5:6, :] = g_small[...]

        net.send(
            "x",
            image_out.at[here],
            returned.at[here],
            pass_sem.at[2, index],
            pass_sem.at[3, index],
            text,
        )

    @pl.when(text)
    def _():
        for h in range(2):
            at = h * cuts[2]
            w_a[:, h * half + kv_end : h * half + o_end] = low(
                product(c_mixed[...], n_x[:, at : at + cuts[2]], 0, 0)
            )
        for h in range(2):
            at = h * width
            w_a[:, h * half + q_end : h * half + kv_end] = low(
                product(n_i[...], keyval[:, at : at + width], 0, 0)
            )
            at = h * cuts[0]
            w_a[:, h * half : h * half + q_end] = low(
                product(n_q[...], query[:, at : at + cuts[0]], 0, 0)
            )

    hand(2, w_a.at[:, pl.ds(theirs_at, o_end)], rcv_a.at[:, 0:o_end])
    mine_d = w_d.at[pl.ds(pl.multiple_of(net.core * share, share), share), :]
    merge(0, mine_d, rcv_d, sum_cd)
    merge(
        1,
        w_a.at[:, pl.ds(mine_at + o_end, half - o_end)],
        rcv_a.at[:, o_end:half],
        sum_ca.at[:, o_end:half],
    )

    @pl.when(text)
    def _():
        branch[...] = product(query[:, 0 : cuts[0]], w_ca[0, :, 0:q_end], 1, 1) + product(
            query[:, cuts[0] :], w_ca[1, :, 0:q_end], 1, 1
        )

        def text_done(r, back):
            top[r, :] = c_middle[r, :] + back

        norm_back_rows(out_y, gains[4:5, :], branch, text_done, g_small)
        gain_rows[4:5, :] = g_small[...]
        sums_ref[10:11, :] = jnp.broadcast_to(
            jnp.sum(row_weight[...], axis=0, keepdims=True), (1, sums_ref.shape[1])
        )
        vec[...] = gain_rows[...]

    merge(2, w_a.at[:, pl.ds(mine_at, o_end)], rcv_a.at[:, 0:o_end], sum_ca.at[:, 0:o_end])
    for index in range(2):
        net.arrive(
            returned.at[index * rows_half : (index + 1) * rows_half],
            pass_sem.at[2, index],
            pass_sem.at[3, index],
            image,
        )

    @pl.when(image)
    def _():
        vec[...] = jnp.zeros_like(vec)

        def add_back(r):
            top[r, :] = cot[r, :].astype(jnp.float32) + returned[r, :].astype(jnp.float32)
            layer_out[r, :] = image_out[r, :]

        blocks(tok.shape[0], row_step(tok.shape[0]), add_back)

    vec[7:8, 0 : sums_ref.shape[1]] = sums.line()

    @pl.when(text)
    def _():
        for index, (src, out) in enumerate(
            (
                (rcv_d, sum_cd),
                (rcv_a.at[:, o_end:half], sum_ca.at[:, o_end:half]),
                (rcv_a.at[:, 0:o_end], sum_ca.at[:, 0:o_end]),
            )
        ):
            pltpu.make_async_copy(src, out, d_local.at[index]).wait()

    net.finish()


def forward(lines, cuts, parts, *operands):
    tok, own_qkv, own_d, own_cd = operands[7], operands[13], operands[16], operands[17]
    cross_shards = operands[9:13]
    bf16, f32 = jnp.bfloat16, jnp.float32
    count = 4 * lines
    rows, width = tok.shape
    few, half = cross_shards[0].shape[0], sum(cuts)
    hidden = count * own_d.shape[0]
    all_a = (count * own_qkv.shape[0], sum(parts))
    gains_shape = (8, width)
    heads_n = width // HD
    jobs = 10
    shape = jax.ShapeDtypeStruct
    wide_b, wide_f = (rows, width), (rows, hidden)
    stored = [
        (wide_b, bf16),
        ((rows, parts[0]), bf16),
        (wide_b, bf16),
        ((heads_n, rows, rows), bf16),
        (wide_b, f32),
        (wide_b, bf16),
        (wide_f, bf16),
        (wide_f, f32),
    ]
    outs = [
        (all_a, bf16),
        ((hidden, width), bf16),
        ((width, half), bf16),
        ((hidden // 2, width), bf16),
        *stored,
        (gains_shape, f32),
        (wide_b, bf16),
        (wide_b, f32),
        (gains_shape, f32),
    ]
    scratch = [
        (all_a, bf16),
        ((hidden, width), bf16),
        ((2, width, half), bf16),
        ((hidden, width), bf16),
        *stored,
        (wide_b, f32),
        (wide_b, f32),
        (wide_b, f32),
        (wide_b, bf16),
        (wide_b, bf16),
        (wide_b, bf16),
        (wide_b, bf16),
        (wide_b, bf16),
        (wide_b, bf16),
        (wide_b, bf16),
        (wide_b, bf16),
        ((rows, 2 * width), bf16),
        (wide_b, bf16),
        ((heads_n, rows, rows), bf16),
        (wide_b, f32),
        (wide_b, bf16),
        (wide_f, bf16),
        ((1, width), f32),
        ((rows, rows), f32),
        ((rows, rows), f32),
        ((rows, 1), f32),
        (gains_shape, f32),
        ((2, few, half), f32),
        ((few, half), f32),
        ((2 * few, half), bf16),
        ((width, half), bf16),
        ((hidden // 2, width), bf16),
        ((3,) + gains_shape, f32),
        ((3,) + gains_shape, f32),
        ((lines - 1,) + gains_shape, f32),
        ((16, 128), f32),
        (gains_shape, f32),
    ]
    dma = pltpu.SemaphoreType.DMA
    return pl.pallas_call(
        functools.partial(forward_kernel, lines, cuts, parts),
        out_shape=tuple(shape(*o) for o in outs),
        in_specs=[SMEM, SMEM] + [VMEM] * 11 + [ANY] * 5,
        out_specs=[ANY] * 12 + [VMEM] * 4,
        scratch_shapes=[pltpu.VMEM(*s) for s in scratch]
        + [
            dma((jobs, Gather.sems(lines))),
            dma((jobs, Gather.sems(lines))),
            dma((jobs,)),
            dma((2,)),
            dma((2 + lines,)),
            dma((2 + lines,)),
            dma((4, 3)),
            dma((12,)),
            dma((3,)),
            dma((3,)),
            dma((3,)),
            dma((3,)),
        ],
        compiler_params=pltpu.CompilerParams(
            collective_id=0, has_side_effects=True, vmem_limit_bytes=63 << 20
        ),
    )(*operands)


class Scatter:
    def __init__(self, net, own, near, far, rcv, sems):
        self.net, self.own, self.near, self.far, self.rcv = net, own, near, far, rcv
        self.send_sem, self.recv_sem = sems

    @staticmethod
    def sems(lines):
        return 1 + 7 * lines

    def sem(self, s):
        return self.send_sem.at[s], self.recv_sem.at[s]

    def add(self, pairs, out):
        def one(r):
            total = pairs[0][r, :].astype(jnp.float32)
            for other in pairs[1:]:
                total = total + other[r, :].astype(jnp.float32)
            out[r, :] = total.astype(out.dtype)

        blocks(out.shape[0], 16, one)

    def chips(self, k):
        net = self.net
        if k == 0:
            return ((None, net.z),)
        return (
            (net.z + k < net.lines, jnp.minimum(net.z + k, net.lines - 1)),
            (net.z >= k, jnp.maximum(net.z - k, 0)),
        )

    def order(self):
        return [pair for k in range(self.net.lines - 1, -1, -1) for pair in self.chips(k)]

    def swap(self, theirs, rcv):
        self.whole = rcv
        self.net.send("core", theirs, rcv, *self.sem(0))

    def swapped(self):
        self.net.arrive(self.whole, *self.sem(0))

    def over_x(self, part):
        net = self.net
        for there, z in self.order():
            for y in (1 - net.y, net.y):
                chip = 2 * z + y
                net.send(
                    "x", part(chip), self.own(chip), *self.sem(1 + chip), both(there, net.text), True
                )

    def from_x(self, chip, there):
        if self.rcv is None:
            net = self.net
            net.arrive(self.own(chip), *self.sem(1 + chip), both(there, net.image))

    def across(self, only=None):
        net = self.net
        for there, z in self.order():
            there = both(there, only)
            chip = 2 * z + 1 - net.y
            self.from_x(chip, there)
            own = self.own(chip)
            if self.rcv is not None:
                when(there, lambda: self.add([own, self.rcv(chip)], own))
            net.send("y", own, self.near(z), *self.sem(1 + 2 * net.lines + z), there)

    def here(self, chip, z):
        parts = [self.own(chip), self.near(z)]
        return parts if self.rcv is None else parts + [self.rcv(chip)]

    def along(self, k):
        net = self.net
        lines = net.lines
        for up, (there, z) in zip((True, False), self.chips(k)):
            chip = 2 * z + net.y
            base = (1 + 3 * lines) if up else (1 + 4 * lines)
            self.from_x(chip, there)
            net.arrive(self.near(z), *self.sem(1 + 2 * lines + z), there)
            more = net.low if up else net.high
            s = base + z
            net.arrive(self.far(z), *self.sem(s), both(there, more))
            own = self.own(chip)
            parts = self.here(chip, z)
            when(both(there, more), lambda: self.add(parts + [self.far(z)], own))
            when(both(there, jnp.logical_not(more)), lambda: self.add(parts, own))
            slot = z if up else jnp.where(z == net.z - 1, lines, z)
            net.send("up" if up else "down", own, self.far(slot), *self.sem(s), there)

    def turn(self):
        pass

    def total(self, out):
        net = self.net
        lines = net.lines
        self.from_x(net.chip, None)
        net.arrive(self.near(net.z), *self.sem(1 + 2 * lines + net.z))
        net.arrive(self.far(net.z), *self.sem(1 + 3 * lines + net.z), net.low)
        net.arrive(self.far(lines), *self.sem(1 + 4 * lines + net.z), net.high)
        parts = self.here(net.chip, net.z)
        low_part, high_part = self.far(net.z), self.far(lines)
        when(both(net.low, net.high), lambda: self.add(parts + [low_part, high_part], out))
        when(jnp.logical_not(net.low), lambda: self.add(parts + [high_part], out))
        when(jnp.logical_not(net.high), lambda: self.add(parts + [low_part], out))


class ScatterAlong(Scatter):
    def across(self, only=None):
        pass

    def spot(self, z, second):
        if not second:
            return self.far(z)
        if isinstance(z, int):
            return self.extra(0)
        return self.near(z)

    def line_sems(self, up, second):
        lines = self.net.lines
        return 1 + (3 + 2 * second + (0 if up else 1)) * lines

    def parts(self, chip):
        return [self.own(chip)] if self.rcv is None else [self.own(chip), self.rcv(chip)]

    def along(self, k):
        net = self.net
        for up, (there, z) in zip((True, False), self.chips(k)):
            for second, y in ((0, net.y), (1, 1 - net.y)):
                chip = 2 * z + y
                self.from_x(chip, there)
                more = net.low if up else net.high
                s = self.line_sems(up, second) + z
                net.arrive(self.spot(z, second), *self.sem(s), both(there, more))
                own = self.own(chip)
                parts = self.parts(chip)
                with_far = parts + [self.spot(z, second)]
                when(both(there, more), lambda: self.add(with_far, own))
                if len(parts) > 1:
                    when(both(there, jnp.logical_not(more)), lambda: self.add(parts, own))
                way = "up" if up else "down"
                if up:
                    net.send(way, own, self.spot(z, second), *self.sem(s), there)
                else:
                    last = z == net.z - 1
                    net.send(
                        way, own, self.spot(net.lines, second), *self.sem(s), both(there, last)
                    )
                    net.send(
                        way,
                        own,
                        self.spot(z, second),
                        *self.sem(s),
                        both(there, jnp.logical_not(last)),
                    )

    def gathered(self, second, more, out):
        net = self.net
        lines = net.lines
        chip = 2 * net.z + (1 - net.y if second else net.y)
        self.from_x(chip, None)
        s = self.line_sems(True, second) + net.z
        net.arrive(self.spot(net.z, second), *self.sem(s), net.low)
        s = self.line_sems(False, second) + net.z
        net.arrive(self.spot(lines, second), *self.sem(s), net.high)
        parts = self.parts(chip) + more
        low_part, high_part = self.spot(net.z, second), self.spot(lines, second)
        when(both(net.low, net.high), lambda: self.add(parts + [low_part, high_part], out))
        when(jnp.logical_not(net.low), lambda: self.add(parts + [high_part], out))
        when(jnp.logical_not(net.high), lambda: self.add(parts + [low_part], out))

    def turn(self):
        net = self.net
        own = self.own(2 * net.z + 1 - net.y)
        self.gathered(1, [], own)
        net.send("y", own, self.extra(1), *self.sem(1 + 2 * net.lines))

    def total(self, out):
        self.net.arrive(self.extra(1), *self.sem(1 + 2 * self.net.lines))
        self.gathered(0, [self.extra(1)], out)


def strip(ref, size, first, last):
    return lambda i: ref.at[pl.ds(pl.multiple_of(i * size, size), size), first:last]


def backward_kernel(
    lines, cuts, parts,
    tok, top_in, gains, vec_in, full_a, full_d, sum_ca, sum_cd,
    i_h1, i_qkv, i_mixed, i_weight, i_middle, i_h2, i_active, i_slope,
    r_qkv, r_out, r_up, r_d, r_cq, r_ckv, r_co, r_cu, r_cd, r_grad, o_vec,
    o_qkv, o_out, o_up, o_d, o_cq, o_ckv, o_co, o_cu, o_cd, input_grad,
    h1, qkv, mixed, weight, middle, h2, active, slope,
    g_a, g_d, rcv_a, rcv_d, near_a, near_d, far_a, far_d,
    own_ca, own_cd, near_ca, near_cd, far_ca, far_cd,
    w_d, w_up, top, branch, n_grad, g_small, vec, fin, fin_vo, extra_a, extra_d, swap, arrived, totals, spread,
    send_sem, recv_sem, load_sem, swap_sem, s_send, s_recv, out_sem,
):
    net = Net(lines)
    net.greet()
    left = []

    def leave(src, out):
        copy = pltpu.make_async_copy(src, out, out_sem.at[len(left)])
        copy.start()
        left.append(copy)

    text, image = net.text, net.image
    width = tok.shape[1]
    tile = width
    rows, depth = o_qkv.shape[0], o_d.shape[0]
    few, part = 2 * o_cq.shape[0], o_cd.shape[0]
    half = own_ca.shape[1]
    a_out = parts[0] + parts[1]
    all_a = g_a.shape[2]
    o_end = cuts[0] + cuts[1] + cuts[2]
    theirs = 1 - net.core

    def load(index, src, dst):
        copy = pltpu.make_async_copy(src, dst, load_sem.at[index])
        copy.start()
        return copy

    l_active = load(0, i_active, active)
    l_wd = load(1, full_d, w_d)
    l_slope = load(2, i_slope, slope)
    l_h2 = load(3, i_h2, h2)
    l_up = load(4, full_a.at[:, a_out:], w_up)
    l_middle = load(5, i_middle, middle)
    l_mixed = load(6, i_mixed, mixed)
    l_qkv = load(7, i_qkv, qkv)
    l_weight = load(8, i_weight, weight)
    l_h1 = load(9, i_h1, h1)

    net.meet()

    def job(index, own, near, far, rcv, extra=None):
        kind = ScatterAlong if SCATTER_NAMES[index] in SCATTER_ALONG else Scatter
        made = kind(net, own, near, far, rcv, (send_sem.at[index], recv_sem.at[index]))
        made.extra = extra
        return made

    def self_a(index, first, last):
        return job(
            index,
            strip(g_a.at[net.core], rows, first, last),
            strip(near_a, rows, first, last),
            strip(far_a, rows, first, last),
            strip(rcv_a, rows, first, last),
            strip(extra_a, rows, first, last),
        )

    def cross_a(index, first, last):
        return job(
            index,
            strip(own_ca, few, first, last),
            strip(near_ca, few, first, last),
            strip(far_ca, few, first, last),
            None,
        )

    def self_d(index, first, last):
        return job(
            index,
            strip(g_d.at[net.core], depth, first, last),
            strip(near_d, depth, first, last),
            strip(far_d, depth, first, last),
            strip(rcv_d, depth, first, last),
            strip(extra_d, depth, first, last),
        )

    mid, middle_up, third = parts[0] - width, a_out + 2 * width, width // 3
    jobs = {
        "d0": self_d(0, 0, third),
        "d1": self_d(1, third, 2 * third),
        "d2": self_d(2, 2 * third, width),
        "u0": self_a(3, a_out, middle_up),
        "u1": self_a(4, middle_up, all_a),
        "qk": self_a(5, 0, mid),
        "vo": self_a(6, mid, a_out),
        "cd": job(
            7,
            strip(own_cd, part, 0, width),
            strip(near_cd, part, 0, width),
            strip(far_cd, part, 0, width),
            None,
        ),
        "cu": cross_a(8, o_end, half),
        "ca": cross_a(9, 0, o_end),
    }

    def swap_a(name, first, last):
        jobs[name].swap(g_a.at[theirs, :, first:last], rcv_a.at[:, first:last])

    def swap_d(name, first, last):
        jobs[name].swap(g_d.at[theirs, :, first:last], rcv_d.at[:, first:last])

    def across(name, only=None):
        if jobs[name].rcv is not None:
            jobs[name].swapped()
        jobs[name].across(only)

    plane_a, plane_d = own_ca.shape[0], own_cd.shape[0]
    c_loads = (
        pltpu.make_async_copy(sum_cd.at[plane_d : 2 * plane_d, :], own_cd, load_sem.at[10]),
        pltpu.make_async_copy(sum_ca.at[plane_a : 2 * plane_a, :], own_ca, load_sem.at[11]),
    )

    @pl.when(text)
    def _():
        for copy in c_loads:
            copy.start()

    def start_x(name):
        at = {"cd": (sum_cd, part, 0, width), "cu": (sum_ca, few, o_end, half), "ca": (sum_ca, few, 0, o_end)}
        jobs[name].over_x(strip(*at[name]))

    def round_top():
        def body(r):
            n_grad[r, :] = low(top_in[r, :])

        blocks(tok.shape[0], row_step(tok.shape[0]), body)

        @pl.when(text)
        def _():
            for copy in c_loads:
                copy.wait()

    def down_grads():
        l_active.wait()

        def down_tile(i, carry):
            cols = pl.ds(pl.multiple_of(i * tile, tile), tile)
            found = low(product(active[:, cols], n_grad[...], 0, 0))
            each = tile // depth
            for k in range(each):
                at = pl.multiple_of(((i * each + k) // 2) * depth, depth)
                g_d[k % 2, pl.ds(at, depth), :] = found[k * depth : (k + 1) * depth]
            return carry

        lax.fori_loop(0, active.shape[1] // tile, down_tile, 0)

    def wide_grads():
        l_wd.wait()
        l_slope.wait()

        def wide_tile(i, carry):
            cols = pl.ds(pl.multiple_of(i * tile, tile), tile)
            grad = product(n_grad[...], w_d[cols, :], 1, 1)
            active[:, cols] = low(grad * slope[:, cols])
            return carry

        lax.fori_loop(0, active.shape[1] // tile, wide_tile, 0)
        for i in range(4):
            src = full_a.at[:, i * width : (i + 1) * width]
            l_four.append(load(12 + i, src, w_d.at[i * width : (i + 1) * width, :]))
        l_h2.wait()

    l_four = []

    def put_a(found, at):
        for k in range(width // rows):
            g_a[k % 2, (k // 2) * rows : (k // 2 + 1) * rows, pl.ds(at, found.shape[1])] = found[
                k * rows : (k + 1) * rows
            ]

    def up_grads(first_tile, last_tile):
        def run():
            def up_tile(i, carry):
                at = pl.multiple_of(i * tile, tile)
                found = low(product(h2[...], active[:, pl.ds(at, tile)], 0, 0))
                put_a(found, pl.multiple_of(a_out + at, tile))
                return carry

            lax.fori_loop(first_tile, last_tile, up_tile, 0)

        return run

    def own_gain(at):
        return jnp.where(text, gains[at + 2 : at + 3, :], gains[at : at + 1, :])

    at_vec = 2 * net.tower

    def mid_grads():
        l_up.wait()
        branch[...] = product(active[...], w_up[...], 1, 1)
        l_middle.wait()

        def mid_done(r, back):
            total = top_in[r, :] + back
            top[r, :] = total
            n_grad[r, :] = low(total)

        norm_back_rows(middle, own_gain(1), branch, mid_done, g_small)
        vec[...] = vec_in[...]
        vec[pl.ds(at_vec + 1, 1), :] = g_small[...]

    def out_grads():
        l_mixed.wait()
        for copy in l_four:
            copy.wait()
        put_a(low(product(mixed[...], n_grad[...], 0, 0)), parts[0])
        mixed[...] = low(product(n_grad[...], w_d[3 * width : 4 * width, :], 1, 1))

    def att_grads():
        l_qkv.wait()
        l_weight.wait()

        def att_done(pair, dq, dk, dv):
            at = pl.multiple_of(pair * 2 * HD, 2 * HD)
            for k, grad in enumerate((dq, dk, dv)):
                qkv[:, pl.ds(pl.multiple_of(k * width + at, 2 * HD), 2 * HD)] = grad

        attention_back(
            pairs_of(qkv),
            pairs_of(qkv, width),
            pairs_of(qkv, 2 * width),
            pairs_of(mixed),
            weight,
            width,
            att_done,
        )
        l_h1.wait()

    def qkv_grads(first_tile, last_tile):
        def run():
            def qkv_tile(i, carry):
                at = pl.multiple_of(i * tile, tile)
                put_a(low(product(h1[...], qkv[:, pl.ds(at, tile)], 0, 0)), at)
                return carry

            lax.fori_loop(first_tile, last_tile, qkv_tile, 0)

        return run

    small = Small(net, vec, arrived, totals, spread, s_send, s_recv)

    def first_grads():
        branch[...] = (
            product(qkv[:, 0:width], w_d[0:width, :], 1, 1)
            + product(qkv[:, width : 2 * width], w_d[width : 2 * width, :], 1, 1)
            + product(qkv[:, 2 * width :], w_d[2 * width : 3 * width, :], 1, 1)
        )

        def first_done(r, back):
            input_grad[r, :] = top[r, :] + back

        norm_back_rows(tok, own_gain(0), branch, first_done, g_small)
        leave(input_grad, r_grad)
        vec[pl.ds(at_vec, 1), :] = g_small[...]
        small.exchange(0)

    def small_step(index):
        def run():
            small.collect(index)
            if index < 2:
                small.exchange(index + 1)
            else:
                small.spread()

        return run

    up_tiles = (all_a - a_out) // tile
    steps = {
        "top": round_top,
        "down": down_grads,
        "wide": wide_grads,
        "up0": up_grads(0, up_tiles // 2),
        "up1": up_grads(up_tiles // 2, up_tiles),
        "mid": mid_grads,
        "out": out_grads,
        "att": att_grads,
        "qk": qkv_grads(0, mid // tile),
        "v": qkv_grads(mid // tile, parts[0] // tile),
        "first": first_grads,
        "small0": small_step(0),
        "small1": small_step(1),
        "small2": small_step(2),
    }
    share = few // 2
    first = net.core == 0
    swaps = {}

    def start_swap(name, index, first_column, last_column):
        copy = net.copy(
            "core",
            fin.at[pl.ds(pl.multiple_of(theirs * share, share), share), first_column:last_column],
            swap.at[:, first_column:last_column],
            swap_sem.at[index, 0],
            swap_sem.at[index, 1],
        )
        copy.start()
        swaps[name] = copy

    def put_cross(out, at, n):
        mine = fin[pl.ds(pl.multiple_of(net.core * share, share), share), at : at + n]
        other = swap[:, at : at + n]
        out[:, 0:n] = jnp.where(first, mine, other)
        out[:, n:] = jnp.where(first, other, mine)

    def put_vo():
        o_qkv[:, mid:] = fin_vo[:, 0 : parts[0] - mid]
        o_out[...] = fin_vo[:, parts[0] - mid :]
        leave(o_qkv.at[:, mid:], r_qkv.at[:, mid:])
        leave(o_out, r_out)

    def going(ref, out, first_column, last_column):
        src = ref.at[:, first_column:last_column]
        return src, lambda: leave(src, out.at[:, first_column:last_column])

    totals_to = {
        "d0": going(o_d, r_d, 0, third),
        "d1": going(o_d, r_d, third, 2 * third),
        "d2": going(o_d, r_d, 2 * third, width),
        "u0": going(o_up, r_up, 0, middle_up - a_out),
        "u1": going(o_up, r_up, middle_up - a_out, all_a - a_out),
        "qk": going(o_qkv, r_qkv, 0, mid),
        "vo": (fin_vo, put_vo),
        "cd": going(o_cd, r_cd, 0, width),
        "cu": (fin.at[:, o_end:half], lambda: start_swap("cu", 0, o_end, half)),
        "ca": (fin.at[:, 0:o_end], lambda: start_swap("ca", 1, 0, o_end)),
    }
    spans = {
        "d0": (0, third),
        "d1": (third, 2 * third),
        "d2": (2 * third, width),
        "u0": (a_out, middle_up),
        "u1": (middle_up, all_a),
        "qk": (0, mid),
        "vo": (mid, a_out),
    }
    for kind, name, k in scatter_order(lines):
        if kind == "do":
            steps[name]()
        elif kind == "x":
            start_x(name)
        elif kind == "swap":
            (swap_d if name in ("d0", "d1", "d2") else swap_a)(name, *spans[name])
        elif kind == "across":
            across(name, (None, text, image)[k])
        elif kind == "along":
            jobs[name].along(k)
        elif kind == "turn":
            jobs[name].turn()
        else:
            out, then = totals_to[name]
            jobs[name].total(out)
            if then is not None:
                then()
    swaps["cu"].wait()
    put_cross(o_cu, o_end, cuts[3])
    leave(o_cu, r_cu)
    small.total(o_vec)
    swaps["ca"].wait()
    at = 0
    for out, result, n in zip((o_cq, o_ckv, o_co), (r_cq, r_ckv, r_co), cuts):
        put_cross(out, at, n)
        leave(out, result)
        at += n
    net.finish()
    for copy in left:
        copy.wait()


SCATTER = ("d0", "d1", "d2", "u0", "u1", "cd", "qk", "vo", "cu", "ca")
SCATTER_NAMES = ("d0", "d1", "d2", "u0", "u1", "qk", "vo", "cd", "cu", "ca")
SCATTER_ALONG = ("d0", "u0")
BEFORE = {0: ("qk", "vo", "cd"), 3: ("cu",), 5: ("ca",)}
SCATTER_HEAD = (
    "x cd", "x cu", "x ca", "do top", "do down", "swap d0", "swap d1", "swap d2", "across cd 1",
    "do wide", "across d0", "across d1", "across d2", "do up0", "swap u0", "do up1", "swap u1",
    "do mid", "across u0", "across u1", "do out", "do att", "do qk", "swap qk", "do v", "swap vo",
    "do first",
)


def scatter_order(lines):
    if lines == 4 and SCATTER_FOUR:
        return parsed(SCATTER_FOUR)
    events = parsed(SCATTER_HEAD)
    count = len(SCATTER)
    for slot in range(count + lines):
        for name in BEFORE.get(slot, ()):
            events.append(("across", name, 2 if name == "cd" else 0))
        if 1 <= slot <= 3:
            events.append(("do", "small%d" % (slot - 1), 0))
        for k in range(lines - 1, -2, -1):
            index = slot - (lines - 1 - k)
            if 0 <= index < count:
                kind = "along" if k > 0 else "turn" if k == 0 else "total"
                events.append((kind, SCATTER[index], k))
    return events


SCATTER_FOUR = (
    "do top", "do down", "swap d0", "swap d1", "swap d2", "x cd", "do wide", "across d0",
    "along d0 3", "across cd 1", "across d1", "do up0", "swap u0", "along d0 2", "do up1",
    "across d2", "swap u1", "across u0", "along u0 3", "along d0 1", "do mid", "along u0 2",
    "across cd 2", "x ca", "x cu", "across u1", "do out", "along d1 3", "along d2 3", "along d2 2",
    "do att", "along cd 3", "do qk", "along cd 2", "swap qk", "along d1 2", "across qk",
    "along u1 3", "do v", "swap vo", "along u0 1", "along u1 2", "do first", "across vo",
    "along qk 3", "along u1 1", "do small0", "along qk 2", "along d2 1", "along vo 3", "do small1",
    "along cd 1", "along vo 2", "across cu", "do small2", "along cu 3", "total d2", "along vo 1",
    "across ca", "along cu 2", "total u1", "along qk 1", "along ca 3", "turn u0", "along d1 1",
    "along ca 2", "along cu 1", "total qk", "total cd", "turn d0", "along ca 1", "total vo",
    "total cu", "total d1", "total d0", "total u0", "total ca",
)


def backward(lines, cuts, parts, own_shapes, *operands):
    bf16, f32 = jnp.bfloat16, jnp.float32
    tok, top, gains, vec, full_a, full_d, sum_ca, sum_cd = operands[:8]
    stored = [(o.shape, o.dtype) for o in operands[8:]]
    chips = 2 * lines
    row_count, width = tok.shape
    hidden, all_a = full_d.shape[0], full_a.shape[1]
    half = sum_ca.shape[1]
    rows, depth = width // (2 * chips), hidden // (2 * chips)
    few, part = width // (2 * chips), hidden // (4 * chips)
    results = [*own_shapes, (row_count, width)]
    outs = [*results, vec.shape]
    rcv_a, rcv_d = (chips * rows, all_a), (chips * depth, width)
    own_ca, own_cd = (chips * few, half), (chips * part, width)

    def line(size, count):
        return (size * count, all_a), (depth * count, width)

    scratch = [
        *((shape, f32) for shape in results),
        *stored,
        ((2,) + rcv_a, bf16),
        ((2,) + rcv_d, bf16),
        (rcv_a, bf16),
        (rcv_d, bf16),
        ((lines * rows, all_a), bf16),
        ((lines * depth, width), bf16),
        (((lines + 1) * rows, all_a), bf16),
        (((lines + 1) * depth, width), bf16),
        (own_ca, bf16),
        (own_cd, bf16),
        ((lines * few, half), bf16),
        ((lines * part, width), bf16),
        (((lines + 1) * few, half), bf16),
        (((lines + 1) * part, width), bf16),
        ((hidden, width), bf16),
        ((width, hidden), bf16),
        ((row_count, width), f32),
        ((row_count, width), f32),
        ((row_count, width), bf16),
        ((1, width), f32),
        (vec.shape, f32),
        ((rows, half), f32),
        ((rows, 2 * width), f32),
        ((2 * rows, all_a), bf16),
        ((2 * depth, width), bf16),
        ((few // 2, half), f32),
        ((3,) + vec.shape, f32),
        ((3,) + vec.shape, f32),
        ((lines - 1,) + vec.shape, f32),
    ]
    dma = pltpu.SemaphoreType.DMA
    return pl.pallas_call(
        functools.partial(backward_kernel, lines, cuts, parts),
        out_shape=tuple(jax.ShapeDtypeStruct(s, f32) for s in outs),
        in_specs=[VMEM] * 4 + [ANY] * 12,
        out_specs=[ANY] * len(results) + [VMEM],
        scratch_shapes=[pltpu.VMEM(*s) for s in scratch]
        + [
            dma((10, Scatter.sems(lines))),
            dma((10, Scatter.sems(lines))),
            dma((16,)),
            dma((2, 2)),
            dma((2 + lines,)),
            dma((2 + lines,)),
            dma((16,)),
        ],
        compiler_params=pltpu.CompilerParams(
            collective_id=1, has_side_effects=True, vmem_limit_bytes=63 << 20
        ),
    )(*operands)


def final_kernel(lines, rows, few, vec, *refs):
    count = (len(refs) - 7) // 3
    ins, outs = refs[:count], refs[count : 2 * count]
    g_1, g_2, g_q, g_i, g_c, rms, *held, sems = refs[2 * count :]
    come = [pltpu.make_async_copy(a, b, sems.at[0, i]) for i, (a, b) in enumerate(zip(ins, held))]
    go = [pltpu.make_async_copy(a, b, sems.at[1, i]) for i, (a, b) in enumerate(zip(held, outs))]
    for copy in come:
        copy.start()
    tower, dp = lax.axis_index("tower"), lax.axis_index("dp")
    width = vec.shape[1]

    def cut(n, at):
        lane = lax.broadcasted_iota(jnp.int32, (width, n), 0)
        index = lax.broadcasted_iota(jnp.int32, (width, n), 1)
        pick = jnp.where(lane == at + index, 1.0, 0.0)
        return lax.dot_general(
            vec[...],
            pick,
            (((1,), (0,)), ((), ())),
            precision=lax.Precision.HIGHEST,
            preferred_element_type=jnp.float32,
        )

    own = cut(rows, dp * rows)
    cross = cut(few, (tower * 4 * lines + dp) * few)
    g_1[...] = jnp.where(tower == 1, own[2:3], own[0:1])
    g_2[...] = jnp.where(tower == 1, own[3:4], own[1:2])
    g_q[...] = cross[4:5]
    g_i[...] = cross[5:6]
    g_c[...] = cross[6:7]
    sums = vec[7:8, 0:128]
    lane = lax.broadcasted_iota(jnp.int32, sums.shape, 1)
    valid = jnp.sum(jnp.where(lane == 10, sums, 0.0), axis=1, keepdims=True)
    images = ins[0].shape[0] * 4.0 * lines
    divisor = jnp.where(lane < 4, images, valid) * width
    rms[...] = jnp.sqrt(sums / divisor)[0, : rms.shape[0]]
    for here, there in zip(come, go):
        here.wait()
        there.start()
    for copy in go:
        copy.wait()


def final(lines, rows, few, vec, *results):
    f32 = jnp.float32
    small = [(1, rows)] * 2 + [(1, few)] * 3 + [(10,)]
    return pl.pallas_call(
        functools.partial(final_kernel, lines, rows, few),
        out_shape=tuple(jax.ShapeDtypeStruct(r.shape, r.dtype) for r in results)
        + tuple(jax.ShapeDtypeStruct(s, f32) for s in small),
        in_specs=[VMEM] + [ANY] * len(results),
        out_specs=[ANY] * len(results) + [VMEM] * 6,
        scratch_shapes=[pltpu.VMEM(r.shape, r.dtype) for r in results]
        + [pltpu.SemaphoreType.DMA((2, len(results)))],
        compiler_params=pltpu.CompilerParams(vmem_limit_bytes=62 << 20),
    )(vec, *results)


def plain_gather(own_a, own_d, pack, own_cd, own_g):
    axes = ("tower", "dp")
    tiles = lax.all_gather(own_g, axes, axis=0)
    return (
        lax.all_gather(own_a, "dp", axis=0, tiled=True),
        lax.all_gather(own_d, "dp", axis=0, tiled=True),
        lax.all_gather(pack.astype(jnp.bfloat16), axes, axis=1, tiled=True),
        lax.all_gather(own_cd, axes, axis=0, tiled=True),
        tiles.reshape((2, -1) + own_g.shape),
    )


def plain_scatter(g_a, g_d, g_ca, g_cd, vec, parts, cuts):
    axes = ("tower", "dp")

    def added(grad, over, axis):
        return lax.psum_scatter(
            grad.astype(jnp.float32), over, scatter_dimension=axis, tiled=True
        )

    a = added(g_a.reshape(-1, g_a.shape[-1]), "dp", 0)
    d = added(g_d.reshape(-1, g_d.shape[-1]), "dp", 0)
    ca = added(g_ca.reshape(2, -1, g_ca.shape[-1]), axes, 1)
    cd = added(g_cd.reshape(-1, g_cd.shape[-1]), axes, 0)
    at = [sum(cuts[:i]) for i in range(len(cuts) + 1)]
    cross = [
        jnp.concatenate([ca[0][:, i:j], ca[1][:, i:j]], axis=1) for i, j in zip(at[:-1], at[1:])
    ]
    first, second = parts[0], parts[0] + parts[1]
    self_parts = [a[:, :first], a[:, first:second], a[:, second:]]
    return (*self_parts, d, *cross, cd, lax.psum(vec, axes))


def layer_norm(value_matrix, norm_gain):
    center = value_matrix - jnp.mean(value_matrix, axis=-1, keepdims=True)
    spread = jnp.mean(center * center, axis=-1, keepdims=True)
    return center * lax.rsqrt(spread + EPSILON) * norm_gain


def norm_back(value_matrix, norm_gain, grad_out):
    result, puller = jax.vjp(layer_norm, value_matrix, norm_gain)
    return puller(grad_out)


def dot(a, b):
    return jnp.dot(a, b, preferred_element_type=jnp.float32)


def dot_tn(a, b):
    return jnp.einsum("rd,re->de", a, b, preferred_element_type=jnp.float32)


def dot_nt(a, b):
    return jnp.einsum("re,de->rd", a, b, preferred_element_type=jnp.float32)


def low(value_matrix):
    return value_matrix.astype(jnp.bfloat16)


def masks(counts, lengths, row_count, decoder):
    row_index = jnp.arange(row_count, dtype=jnp.int32)
    bounds = jnp.cumsum(counts)
    image_of = jnp.sum((row_index[:, None] >= bounds[None, :]).astype(jnp.int32), axis=1)
    caption_of = row_index // CAP_LEN
    in_place = row_index - caption_of * CAP_LEN
    caption_slots = jnp.arange(lengths.shape[0], dtype=jnp.int32)
    length_rows = jnp.sum(
        jnp.where(caption_of[:, None] == caption_slots[None, :], lengths[None, :], 0), axis=1
    )
    valid_rows = in_place < length_rows
    image_mask = image_of[:, None] == image_of[None, :]
    text_mask = (
        (caption_of[:, None] == caption_of[None, :])
        & (in_place[None, :] <= in_place[:, None])
        & valid_rows[None, :]
    )
    cross_mask = caption_of[:, None] == image_of[None, :]
    return jnp.where(decoder, text_mask, image_mask), cross_mask, valid_rows


def heads(value_matrix):
    return value_matrix.reshape(value_matrix.shape[0], -1, HD)


def attend(query, key, value, allowed):
    scores = jnp.einsum(
        "qhd,khd->hqk", heads(query), heads(key), preferred_element_type=jnp.float32
    ) * HD ** (-0.5)
    weight = jax.nn.softmax(jnp.where(allowed[None], scores, NEGATIVE), axis=-1)
    mixed = jnp.einsum("hqk,khd->qhd", low(weight), heads(value), preferred_element_type=jnp.float32)
    return low(mixed.reshape(query.shape)), weight


def attend_back(query, key, value, weight, grad_mixed):
    grad_mixed = heads(grad_mixed)
    grad_value = jnp.einsum("hqk,qhd->khd", low(weight), grad_mixed, preferred_element_type=jnp.float32)
    grad_weight = jnp.einsum("qhd,khd->hqk", grad_mixed, heads(value), preferred_element_type=jnp.float32)
    grad_score = low(
        weight * (grad_weight - jnp.sum(grad_weight * weight, axis=-1, keepdims=True))
    )
    grad_query = jnp.einsum(
        "hqk,khd->qhd", grad_score, heads(key), preferred_element_type=jnp.float32
    ) * HD ** (-0.5)
    grad_key = jnp.einsum(
        "hqk,qhd->khd", grad_score, heads(query), preferred_element_type=jnp.float32
    ) * HD ** (-0.5)
    return tuple(low(g.reshape(query.shape)) for g in (grad_query, grad_key, grad_value))


def mlp_forward(stream, gain, up, down):
    hidden = low(layer_norm(stream, gain))
    wide = dot(hidden, up)
    active = low(jax.nn.gelu(wide))
    return dot(active, down), (hidden, wide, active)


def mlp_back(stream, gain, up, down, stored, grad):
    hidden, wide, active = stored
    branch = low(grad)
    grad_down = dot_tn(active, branch)
    result, puller = jax.vjp(jax.nn.gelu, wide)
    grad_wide = low(puller(dot_nt(branch, down))[0])
    grad_up = dot_tn(hidden, grad_wide)
    grad_stream, grad_gain = norm_back(stream, gain, dot_nt(grad_wide, up))
    return grad + grad_stream, grad_gain, grad_up, grad_down


def squares(value_matrix, row_weight):
    return jnp.sum(row_weight[:, None] * value_matrix * value_matrix)


def plain_shards(
    tokens, cotangent, kept_counts, caption_lengths, attn_gain, qkv_weight, attn_out, mlp_gain,
    mlp_up, mlp_down, query_gain, image_gain, cross_gain, cross_query, cross_keyval, cross_out,
    cross_up, cross_down,
):
    f32 = jnp.float32
    dp_count = lax.axis_size("dp")
    lines = dp_count // 4
    tower, dp = lax.axis_index("tower"), lax.axis_index("dp")
    decoder = tower == 1
    row_count, width = tokens.shape[1:]
    rows = attn_gain.shape[1]
    few = query_gain.shape[0]

    def tile_row(value):
        return jnp.pad(value.astype(f32), (0, 128 - value.shape[0]))

    gain_tile = jnp.stack(
        [tile_row(attn_gain[0]), tile_row(mlp_gain[0])]
        + [tile_row(g) for g in (query_gain, image_gain, cross_gain)]
        + [jnp.zeros((128,), f32)] * 3
    )
    cross_shards = (cross_query, cross_keyval, cross_out, cross_up)
    cuts = tuple(w.shape[1] // 2 for w in cross_shards)
    pack = jnp.stack(
        [
            jnp.concatenate([w[:, h * n : (h + 1) * n] for w, n in zip(cross_shards, cuts)], axis=1)
            for h in range(2)
        ]
    ).astype(f32)
    self_parts = (qkv_weight.shape[2], attn_out.shape[2], mlp_up.shape[2])
    own_a = jnp.concatenate([qkv_weight[0], attn_out[0], mlp_up[0]], axis=1)
    full_a, full_d, full_ca, full_cd, full_g = plain_gather(
        own_a, mlp_down[0], pack, cross_down, gain_tile
    )
    qkv = full_a[:, : self_parts[0]]
    out = full_a[:, self_parts[0] : self_parts[0] + self_parts[1]]
    up = full_a[:, self_parts[0] + self_parts[1] :]
    down = full_d
    plane_gains = lax.dynamic_index_in_dim(full_g, tower, 0, keepdims=False)
    gain_1 = plane_gains[:, 0, :rows].reshape(-1)
    gain_2 = plane_gains[:, 1, :rows].reshape(-1)
    gain_q, gain_i, gain_c = (full_g[:, :, 2 + i, :few].reshape(-1) for i in range(3))

    stream = tokens[0].astype(f32)
    upstream = cotangent[0].astype(f32)
    allowed, cross_allowed, valid_rows = masks(kept_counts[0], caption_lengths, row_count, decoder)
    row_weight = jnp.where(decoder, valid_rows, True).astype(f32)

    normed = low(layer_norm(stream, gain_1))
    joined = low(dot(normed, qkv))
    query, key, value = jnp.split(joined, 3, axis=1)
    mixed, weight = attend(query, key, value, allowed)
    attn_branch = dot(mixed, out)
    middle = stream + attn_branch
    mlp_branch, mlp_stored = mlp_forward(middle, gain_2, up, down)
    layer_y = middle + mlp_branch
    image_rows = low(layer_y)
    arrived = lax.ppermute(image_rows, "tower", [(0, 1)])

    def run_cross(operands):
        text_y, image_in = operands
        at = [0]
        for n in cuts:
            at.append(at[-1] + n)
        cq, ckv, co, cu = (
            jnp.concatenate([full_ca[0][:, a:b], full_ca[1][:, a:b]], axis=1)
            for a, b in zip(at[:-1], at[1:])
        )
        image_in = image_in.astype(f32)
        image_normed = low(layer_norm(image_in, gain_i))
        keyval = low(dot(image_normed, ckv))
        c_key, c_value = jnp.split(keyval, 2, axis=1)
        c_normed = low(layer_norm(text_y, gain_q))
        c_query = low(dot(c_normed, cq))
        c_mixed, c_weight = attend(c_query, c_key, c_value, cross_allowed)
        c_branch = dot(c_mixed, co)
        c_middle = text_y + c_branch
        c_mlp, c_stored = mlp_forward(c_middle, gain_c, cu, full_cd)
        final_rows = c_middle + c_mlp
        grad_middle, grad_gain_c, grad_cu, grad_cd = mlp_back(
            c_middle, gain_c, cu, full_cd, c_stored, upstream
        )
        grad_branch = low(grad_middle)
        grad_co = dot_tn(c_mixed, grad_branch)
        grad_q, grad_k, grad_v = attend_back(
            c_query, c_key, c_value, c_weight, low(dot_nt(grad_branch, co))
        )
        grad_cq = dot_tn(c_normed, grad_q)
        grad_text, grad_gain_q = norm_back(text_y, gain_q, dot_nt(grad_q, cq))
        grad_keyval = jnp.concatenate([grad_k, grad_v], axis=1)
        grad_ckv = dot_tn(image_normed, grad_keyval)
        grad_image, grad_gain_i = norm_back(image_in, gain_i, dot_nt(grad_keyval, ckv))
        cross_sums = jnp.stack(
            [
                squares(c_branch, row_weight),
                squares(c_mlp, row_weight),
                squares(final_rows, row_weight),
            ]
        )
        grads = tuple(low(g) for g in (grad_cq, grad_ckv, grad_co, grad_cu))
        grad_ca = jnp.stack(
            [
                jnp.concatenate([g[:, h * n : (h + 1) * n] for g, n in zip(grads, cuts)], axis=1)
                for h in range(2)
            ]
        )
        return (
            low(final_rows),
            grad_middle + grad_text,
            low(grad_image),
            grad_ca,
            low(grad_cd),
            jnp.concatenate([grad_gain_q, grad_gain_i, grad_gain_c]),
            cross_sums,
        )

    def skip_cross(operands):
        shapes = jax.eval_shape(run_cross, operands)
        return tuple(jnp.zeros(s.shape, s.dtype) for s in shapes)

    final_rows, grad_text, grad_image, grad_ca, grad_cd, grad_cross_gains, cross_sums = lax.cond(
        decoder, run_cross, skip_cross, (layer_y, arrived)
    )
    returned = lax.ppermute(grad_image, "tower", [(1, 0)]).astype(f32)
    grad_top = jnp.where(decoder, grad_text, upstream + returned)

    grad_middle, grad_gain_2, grad_up, grad_down = mlp_back(
        middle, gain_2, up, down, mlp_stored, grad_top
    )
    grad_branch = low(grad_middle)
    grad_out = dot_tn(mixed, grad_branch)
    grad_joined = jnp.concatenate(
        attend_back(query, key, value, weight, low(dot_nt(grad_branch, out))), axis=1
    )
    grad_qkv = dot_tn(normed, grad_joined)
    grad_stream, grad_gain_1 = norm_back(stream, gain_1, dot_nt(grad_joined, qkv))
    grad_stream = grad_middle + grad_stream

    layer_sums = jnp.stack(
        [
            squares(stream, row_weight),
            squares(attn_branch, row_weight),
            squares(mlp_branch, row_weight),
            squares(layer_y, row_weight),
        ]
    )
    encoder_part = jnp.where(decoder, 0.0, layer_sums)
    decoder_part = jnp.where(decoder, jnp.concatenate([layer_sums[:3], cross_sums]), 0.0)
    counted = jnp.where(decoder, jnp.sum(valid_rows.astype(f32)), 0.0)
    line = tile_row(jnp.concatenate([encoder_part, decoder_part, counted[None]]))
    self_gains = jnp.concatenate([grad_gain_1, grad_gain_2])
    zero = jnp.zeros_like(self_gains)
    vec = jnp.concatenate(
        [
            jnp.where(decoder, zero, self_gains),
            jnp.where(decoder, self_gains, zero),
            grad_cross_gains,
            line,
        ]
    ).reshape(-1, 128)
    vec = jnp.pad(vec, ((0, -vec.shape[0] % 8), (0, 0)))
    grad_a = jnp.concatenate([low(grad_qkv), low(grad_out), low(grad_up)], axis=1)
    chips = 2 * lines
    results = plain_scatter(
        grad_a.reshape(chips, 2, rows, -1),
        low(grad_down).reshape(chips, 2, -1, width),
        grad_ca.reshape(2, 2, chips, 2 * few, -1),
        grad_cd.reshape(2, chips, 2, -1, width),
        vec,
        self_parts,
        cuts,
    )
    o_qkv, o_out, o_up, o_d, o_cq, o_ckv, o_co, o_cu, o_cd, o_vec = results
    flat = o_vec.reshape(-1)
    own_gains = lax.dynamic_slice(flat, (tower * 2 * width,), (2 * width,))
    g_1, g_2 = (lax.dynamic_slice(own_gains, (i * width + dp * rows,), (rows,)) for i in range(2))
    g_q, g_i, g_c = (
        lax.dynamic_slice(
            flat, ((4 + i) * width + (tower * dp_count + dp) * few,), (few,)
        )
        for i in range(3)
    )
    sums = flat[7 * width : 7 * width + 11]
    encoder_count = jnp.full((4,), float(row_count * dp_count), f32)
    divisor = jnp.concatenate([encoder_count, jnp.full((6,), 1.0, f32) * sums[10]]) * width
    rms_values = jnp.sqrt(sums[:10] / divisor)
    layer_out = jnp.where(decoder, final_rows, image_rows)
    return (
        layer_out[None], grad_stream[None], g_1[None], o_qkv[None], o_out[None], g_2[None],
        o_up[None], o_d[None], g_q, g_i, g_c, o_cq, o_ckv, o_co, o_cu, o_cd, rms_values,
    )


def fused_shards(
    tokens, cotangent, kept_counts, caption_lengths, attn_gain, qkv_weight, attn_out, mlp_gain,
    mlp_up, mlp_down, query_gain, image_gain, cross_gain, cross_query, cross_keyval, cross_out,
    cross_up, cross_down,
):
    f32 = jnp.float32
    dp_count = lax.axis_size("dp")
    lines = dp_count // 4
    row_count, width = tokens.shape[1:]
    rows = attn_gain.shape[1]
    few = query_gain.shape[0]
    cross_shards = (cross_query, cross_keyval, cross_out, cross_up)
    cuts = tuple(w.shape[1] // 2 for w in cross_shards)
    parts = (qkv_weight.shape[2], attn_out.shape[2], mlp_up.shape[2])
    (
        full_a, full_d, sum_ca, sum_cd, h1, qkv, mixed, weight, middle, h2, active, slope,
        gains, layer_out, top, vec,
    ) = forward(
        lines, cuts, parts, kept_counts, caption_lengths, attn_gain, mlp_gain,
        query_gain[None], image_gain[None], cross_gain[None], tokens[0], cotangent[0],
        *cross_shards, qkv_weight[0], attn_out[0], mlp_up[0], mlp_down[0], cross_down,
    )
    shard_shapes = [
        w.shape[-2:]
        for w in (
            qkv_weight, attn_out, mlp_up, mlp_down, cross_query, cross_keyval, cross_out, cross_up,
            cross_down,
        )
    ]
    *weight_grads, input_grad, o_vec = backward(
        lines, cuts, parts, shard_shapes, tokens[0], top, gains, vec, full_a, full_d, sum_ca,
        sum_cd, h1, qkv, mixed, weight, middle, h2, active, slope,
    )
    (
        layer_out, input_grad, o_qkv, o_out, o_up, o_d, o_cq, o_ckv, o_co, o_cu, o_cd,
        g_1, g_2, g_q, g_i, g_c, rms,
    ) = final(lines, rows, few, o_vec, layer_out, input_grad, *weight_grads)
    return (
        layer_out[None], input_grad[None], g_1, o_qkv[None], o_out[None], g_2, o_up[None],
        o_d[None], g_q[0], g_i[0], g_c[0], o_cq, o_ckv, o_co, o_cu, o_cd, rms,
    )


def shards(*arrays):
    dp_count = lax.axis_size("dp")
    cross_query, cross_down = arrays[13], arrays[17]
    fills = dp_count % 4 == 0 and dp_count > 4
    fills = fills and cross_query.shape[0] % 8 == 0 and cross_down.shape[0] % 16 == 0
    return fused_shards(*arrays) if fills else plain_shards(*arrays)


def solution(mesh):
    rows = P("tower", "dp", None)
    gain = P("tower", "dp")
    cross_gain = P(("tower", "dp"))
    cross = P(("tower", "dp"), None)
    weights = (gain, rows, rows, gain, rows, rows) + (cross_gain,) * 3 + (cross,) * 5
    return jax.shard_map(
        shards,
        mesh=mesh,
        in_specs=(rows, rows, P("dp", None), P("dp")) + weights,
        out_specs=(rows, rows) + weights + (P(),),
        check_vma=False,
    )
```

```python
import functools

import jax
import jax.numpy as jnp
from jax import lax
from jax.experimental import pallas as pl
from jax.experimental.pallas import tpu as pltpu
from jax.sharding import PartitionSpec as P

HD = 64
CAP_LEN = 64
EPSILON = 1e-06
NEGATIVE = -1000000000.0

MESH_ID = pl.DeviceIdType.MESH
ANY = pl.BlockSpec(memory_space=pl.ANY)
VMEM = pl.BlockSpec(memory_space=pltpu.VMEM)
SMEM = pl.BlockSpec(memory_space=pltpu.SMEM)


class Net:
    def __init__(self, lines):
        self.lines = lines
        self.tower = lax.axis_index("tower")
        self.dp = lax.axis_index("dp")
        self.core = self.dp % 2
        self.y = (self.dp // 2) % 2
        self.z = self.dp // 4
        self.chip = self.dp // 2
        self.text = self.tower == 1
        self.image = self.tower == 0
        self.low = self.z > 0
        self.high = self.z < lines - 1
        self.sends = []
        self.slow = []

    def target(self, way):
        if way == "core":
            return (self.tower, self.dp + 1 - 2 * self.core)
        if way == "y":
            return (self.tower, self.dp + 2 - 4 * self.y)
        if way == "x":
            return (1 - self.tower, self.dp)
        if way == "up":
            return (self.tower, jnp.minimum(self.dp + 4, 4 * self.lines - 1))
        return (self.tower, jnp.maximum(self.dp - 4, 0))

    def beyond(self, k):
        return (self.tower, 4 * lax.rem(self.z + k, self.lines) + self.dp % 4)

    def greet(self):
        sem = pltpu.get_barrier_semaphore()
        partners = [self.target(way) for way in ("core", "y", "x")]
        partners += [self.beyond(k) for k in range(1, self.lines)]
        for partner in partners:
            pl.semaphore_signal(sem, inc=1, device_id=partner, device_id_type=MESH_ID)
        self.partners = len(partners)

    def meet(self):
        pl.semaphore_wait(pltpu.get_barrier_semaphore(), self.partners)

    def copy(self, way, src, dst, send_sem, recv_sem):
        return pltpu.make_async_remote_copy(
            src_ref=src,
            dst_ref=dst,
            send_sem=send_sem,
            recv_sem=recv_sem,
            device_id=self.target(way),
            device_id_type=MESH_ID,
        )

    def send(self, way, src, dst, send_sem, recv_sem, there=None, slow=False):
        copy = self.copy(way, src, dst, send_sem, recv_sem)
        when(there, copy.start)
        (self.slow if slow else self.sends).append((copy, there))

    def arrive(self, src, send_sem, recv_sem, there=None):
        copy = self.copy("core", src, src, send_sem, recv_sem)
        when(there, copy.wait_recv)

    def drain(self, kept=0):
        while len(self.sends) > kept:
            copy, there = self.sends.pop(0)
            when(there, copy.wait_send)

    def finish(self):
        self.drain()
        self.sends, self.slow = self.slow, []
        self.drain()


def when(there, act):
    if there is None:
        act()
    else:
        pl.when(there)(act)


def both(*conditions):
    kept = [c for c in conditions if c is not None]
    if not kept:
        return None
    result = kept[0]
    for c in kept[1:]:
        result = jnp.logical_and(result, c)
    return result


class Gather:
    def __init__(self, net, own, place, crossing, send_sem, recv_sem, local_sem, everywhere=False):
        self.net, self.own, self.place, self.crossing = net, own, place, crossing
        self.send_sem, self.recv_sem, self.local_sem = send_sem, recv_sem, local_sem
        lines = net.lines
        self.at_z, self.at_y, self.at_x, self.at_core = 0, 2 * lines, 3 * lines, 5 * lines
        self.to_x = net.image if crossing else None
        self.to_core = net.text if crossing and not everywhere else None

    @staticmethod
    def sems(lines):
        return 11 * lines

    def piece(self, chip, tower=None, core=None):
        net = self.net
        return self.place(
            net.tower if tower is None else tower, chip, net.core if core is None else core
        )

    def pass_on(self, chip, src, there=None, tower=None):
        net = self.net
        dst = self.piece(chip, tower)
        plane = net.tower if tower is None else tower
        if self.crossing and tower is None:
            s = self.at_x + chip
            net.send("x", src, dst, self.send_sem.at[s], self.recv_sem.at[s], both(there, net.image))
        s = self.at_core + plane * 2 * net.lines + chip
        net.send("core", src, dst, self.send_sem.at[s], self.recv_sem.at[s], both(there, self.to_core))

    def start(self):
        net = self.net
        dst = self.piece(net.chip)
        self.local = None
        if self.own is None:
            self.own = dst
        else:
            self.local = pltpu.make_async_copy(self.own, dst, self.local_sem)
            self.local.start()
        for way, there, slot in (("up", net.high, 1), ("down", net.low, net.lines + 1)):
            s = self.at_z + slot
            net.send(way, self.own, dst, self.send_sem.at[s], self.recv_sem.at[s], there)
        s = self.at_y + net.z
        net.send("y", self.own, dst, self.send_sem.at[s], self.recv_sem.at[s])
        self.pass_on(net.chip, self.own)

    def hop(self, k):
        net = self.net
        for way, there, further, sign, base in (
            ("up", net.z >= k, net.high, -1, 0),
            ("down", net.z + k < net.lines, net.low, 1, net.lines),
        ):
            z = jnp.clip(net.z + sign * k, 0, net.lines - 1)
            chip = 2 * z + net.y
            src = self.piece(chip)
            s = self.at_z + base + k
            net.arrive(src, self.send_sem.at[s], self.recv_sem.at[s], there)
            if k + 1 < net.lines:
                s = s + 1
                net.send(way, src, src, self.send_sem.at[s], self.recv_sem.at[s], both(there, further))
            s = self.at_y + z
            net.send("y", src, src, self.send_sem.at[s], self.recv_sem.at[s], there)
            self.pass_on(chip, src, there)

    def beside(self, k):
        net = self.net
        ways = ((None, 0),) if k == 0 else ((net.z >= k, -k), (net.z + k < net.lines, k))
        for there, offset in ways:
            z = jnp.clip(net.z + offset, 0, net.lines - 1)
            chip = 2 * z + 1 - net.y
            src = self.piece(chip)
            s = self.at_y + z
            net.arrive(src, self.send_sem.at[s], self.recv_sem.at[s], there)
            self.pass_on(chip, src, there)

    def from_image(self, k):
        if not self.crossing:
            return
        net = self.net
        ways = ((None, 0),) if k == 0 else ((net.z >= k, -k), (net.z + k < net.lines, k))
        for there, offset in ways:
            z = jnp.clip(net.z + offset, 0, net.lines - 1)
            for y in (net.y, 1 - net.y):
                chip = 2 * z + y
                src = self.piece(chip, 0)
                s = self.at_x + chip
                net.arrive(src, self.send_sem.at[s], self.recv_sem.at[s], both(there, net.text))
                self.pass_on(chip, src, both(there, net.text), 0)

    def done(self):
        net = self.net
        if self.local is not None:
            self.local.wait()

        def all_of(tower, base):
            def one(chip, carry):
                s = self.at_core + base + chip
                src = self.piece(chip, tower, 1 - net.core)
                net.arrive(src, self.send_sem.at[s], self.recv_sem.at[s])
                return carry

            def run():
                lax.fori_loop(0, 2 * net.lines, one, 0)

            return run

        when(self.to_core, all_of(net.tower, net.tower * 2 * net.lines))
        if self.crossing:
            when(net.text, all_of(0, 0))


class GatherBeside(Gather):
    def start(self):
        net = self.net
        dst = self.piece(net.chip)
        self.local = None
        if self.own is None:
            self.own = dst
        else:
            self.local = pltpu.make_async_copy(self.own, dst, self.local_sem)
            self.local.start()
        s = self.at_y
        net.send("y", self.own, dst, self.send_sem.at[s], self.recv_sem.at[s])
        self.set_off(self.own, net.chip, 0)
        self.pass_on(net.chip, self.own)

    def set_off(self, src, chip, second):
        net = self.net
        dst = self.piece(chip)
        for way, there, slot in (("up", net.high, 1), ("down", net.low, net.lines + 1)):
            s = self.z_sem(second) + slot
            net.send(way, src, dst, self.send_sem.at[s], self.recv_sem.at[s], there)

    def z_sem(self, second):
        return 9 * self.net.lines if second else self.at_z

    def hop(self, k):
        net = self.net
        for way, there, further, sign, base in (
            ("up", net.z >= k, net.high, -1, 0),
            ("down", net.z + k < net.lines, net.low, 1, net.lines),
        ):
            z = jnp.clip(net.z + sign * k, 0, net.lines - 1)
            for second, y in ((0, net.y), (1, 1 - net.y)):
                chip = 2 * z + y
                src = self.piece(chip)
                s = self.z_sem(second) + base + k
                net.arrive(src, self.send_sem.at[s], self.recv_sem.at[s], there)
                if k + 1 < net.lines:
                    s = s + 1
                    net.send(
                        way, src, src, self.send_sem.at[s], self.recv_sem.at[s], both(there, further)
                    )
                self.pass_on(chip, src, there)

    def beside(self, k):
        if k > 0:
            return
        net = self.net
        chip = 2 * net.z + 1 - net.y
        src = self.piece(chip)
        s = self.at_y
        net.arrive(src, self.send_sem.at[s], self.recv_sem.at[s])
        self.set_off(src, chip, 1)
        self.pass_on(chip, src)


class Small:
    def __init__(self, net, mine, arrived, sums, wide, send_sem, recv_sem):
        self.net, self.mine, self.arrived, self.sums, self.wide = net, mine, arrived, sums, wide
        self.send_sem, self.recv_sem = send_sem, recv_sem

    def exchange(self, step):
        src = self.mine if step == 0 else self.sums.at[step - 1]
        self.net.send(
            ("core", "y", "x")[step],
            src,
            self.arrived.at[step],
            self.send_sem.at[step],
            self.recv_sem.at[step],
        )

    def collect(self, step):
        self.net.arrive(self.arrived.at[step], self.send_sem.at[step], self.recv_sem.at[step])
        src = self.mine if step == 0 else self.sums.at[step - 1]
        self.sums[step] = src[...] + self.arrived[step]

    def spread(self):
        net = self.net
        for k in range(1, net.lines):
            s = 2 + k
            copy = pltpu.make_async_remote_copy(
                src_ref=self.sums.at[2],
                dst_ref=self.wide.at[k - 1],
                send_sem=self.send_sem.at[s],
                recv_sem=self.recv_sem.at[s],
                device_id=net.beyond(k),
                device_id_type=MESH_ID,
            )
            copy.start()
            net.sends.append((copy, None))

    def total(self, out):
        total = self.sums[2]
        for k in range(1, self.net.lines):
            s = 2 + k
            self.net.arrive(self.wide.at[k - 1], self.send_sem.at[s], self.recv_sem.at[s])
            total = total + self.wide[k - 1]
        out[...] = total


def product(a, b, axis_a=1, axis_b=0):
    return lax.dot_general(
        a, b, (((axis_a,), (axis_b,)), ((), ())), preferred_element_type=jnp.float32
    )


def low(value):
    return value.astype(jnp.bfloat16)


def blocks(count, size, body):
    def one(i, carry):
        body(pl.ds(pl.multiple_of(i * size, size), size))
        return carry

    lax.fori_loop(0, count // size, one, 0)


def row_step(rows):
    return next(s for s in (96, 64, 48, 32, 16) if rows % s == 0)


def centred(value):
    center = value - jnp.mean(value, axis=-1, keepdims=True)
    spread = jnp.mean(center * center, axis=-1, keepdims=True)
    return center * lax.rsqrt(spread + EPSILON), lax.rsqrt(spread + EPSILON)


def norm_rows(src, gain, out, also=None):
    def body(rows):
        value = src[rows, :].astype(jnp.float32)
        if also is not None:
            also(rows, value)
        out[rows, :] = low(centred(value)[0] * gain)

    blocks(src.shape[0], row_step(src.shape[0]), body)


def norm_back_rows(src, gain, grad, done, gain_grad, fresh=True):
    if fresh:
        gain_grad[...] = jnp.zeros_like(gain_grad)

    def body(rows):
        n, scale = centred(src[rows, :].astype(jnp.float32))
        out = grad[rows, :]
        dn = out * gain
        gain_grad[...] += jnp.sum(out * n, axis=0, keepdims=True)
        back = dn - jnp.mean(dn, axis=-1, keepdims=True)
        done(rows, (back - n * jnp.mean(dn * n, axis=-1, keepdims=True)) * scale)

    blocks(src.shape[0], row_step(src.shape[0]), body)


class Sums:
    def __init__(self, ref, weight):
        self.ref, self.weight = ref, weight
        ref[...] = jnp.zeros_like(ref)

    def add(self, slot, rows, value):
        kept = jnp.sum(value * value, axis=-1, keepdims=True) * self.weight[rows, :]
        total = jnp.sum(kept, axis=0, keepdims=True)
        at = pl.ds(slot, 1)
        self.ref[at, :] = self.ref[at, :] + jnp.broadcast_to(total, (1, self.ref.shape[1]))

    def line(self):
        shape = self.ref.shape
        row = lax.broadcasted_iota(jnp.int32, shape, 0)
        lane = lax.broadcasted_iota(jnp.int32, shape, 1)
        return jnp.sum(jnp.where(row == lane, self.ref[...], 0.0), axis=0, keepdims=True)


def pair_count(width):
    pairs = width // (2 * HD)
    return next(n for n in (3, 2, 1) if pairs % n == 0)


def attention(query, key, value, allowed, weight, mixed):
    count, width = mixed.shape
    group = pair_count(width)
    left = lax.broadcasted_iota(jnp.int32, (count, 2 * HD), 1) < HD

    def one(step, carry):
        kept, scores = [], []
        for i in range(group):
            pair = step * group + i
            q, k, v = query(pair), key(pair), value(pair)
            zero = jnp.zeros_like(q)
            kept.append((pair, v))
            for part in (jnp.where(left, q, zero), jnp.where(left, zero, q)):
                scores.append(product(part, k, 1, 1) * HD ** (-0.5))
        weights = []
        for s in scores:
            s = jnp.where(allowed[...] > 0, s, NEGATIVE)
            e = jnp.exp(s - jnp.max(s, axis=-1, keepdims=True))
            weights.append(low(e / jnp.sum(e, axis=-1, keepdims=True)))
        for i, (pair, v) in enumerate(kept):
            first, second = weights[2 * i : 2 * i + 2]
            weight[2 * pair] = first
            weight[2 * pair + 1] = second
            both_heads = jnp.where(left, product(first, v), product(second, v))
            mixed[:, pl.ds(pl.multiple_of(pair * 2 * HD, 2 * HD), 2 * HD)] = low(both_heads)
        return carry

    lax.fori_loop(0, width // (2 * HD) // group, one, 0, unroll=True)


def attention_back(query, key, value, grad_mixed, weight, width, done):
    count = weight.shape[1]
    group = pair_count(width)
    left = lax.broadcasted_iota(jnp.int32, (count, 2 * HD), 1) < HD

    def one(step, carry):
        kept, raw = [], []
        for i in range(group):
            pair = step * group + i
            q, k, v, d = query(pair), key(pair), value(pair), grad_mixed(pair)
            zero = jnp.zeros_like(q)
            kept.append((pair, q, k))
            for h, part in enumerate((jnp.where(left, d, zero), jnp.where(left, zero, d))):
                raw.append((part, product(part, v, 1, 1), weight[2 * pair + h]))
        grads = []
        for part, dp, p in raw:
            p32 = p.astype(jnp.float32)
            grads.append(low(p32 * (dp - jnp.sum(dp * p32, axis=-1, keepdims=True))))
        for i, (pair, q, k) in enumerate(kept):
            (d0, _, p0), (d1, _, p1) = raw[2 * i : 2 * i + 2]
            s0, s1 = grads[2 * i : 2 * i + 2]
            zero = jnp.zeros_like(q)
            dv = product(p0, d0, 0, 0) + product(p1, d1, 0, 0)
            dk = product(s0, jnp.where(left, q, zero), 0, 0)
            dk = dk + product(s1, jnp.where(left, zero, q), 0, 0)
            dq = jnp.where(left, product(s0, k), product(s1, k))
            done(pair, low(dq * HD ** (-0.5)), low(dk * HD ** (-0.5)), low(dv))
        return carry

    lax.fori_loop(0, width // (2 * HD) // group, one, 0, unroll=True)


def pairs_of(ref, base=0):
    return lambda pair: ref[:, pl.ds(pl.multiple_of(base + pair * 2 * HD, 2 * HD), 2 * HD)]


def gelu_both(value):
    scale = 0.7978845608028654
    cube = 0.044715
    square = value * value
    bend = jnp.tanh(scale * value * (1.0 + cube * square))
    half = 0.5 * (1.0 + bend)
    slope = half + 0.5 * value * (1.0 - bend * bend) * scale * (1.0 + 3.0 * cube * square)
    return value * half, slope


def activate(wide, active, slope, columns):
    def body(rows):
        a, s = gelu_both(wide[rows, :])
        active[rows, columns] = low(a)
        slope[rows, columns] = s.astype(slope.dtype)

    blocks(wide.shape[0], 16, body)


GATHER = ("qk", "vo", "ca", "u0", "u1", "cu", "d0", "d1", "d2", "cd")
GATHER_NAMES = ("qk", "vo", "u0", "u1", "d0", "d1", "d2", "ca", "cu", "cd")
LEAD = 2
GATHER_BESIDE = ("d0", "d1")
GATHER_FOUR = (
    "start d0", "start d2", "start d1", "start qk", "start cd", "do block", "start cu", "start vo",
    "start ca", "hop cd 1", "hop ca 1", "beside cd 0", "start u0", "hop qk 1", "beside d1 0",
    "hop ca 2", "beside d0 0", "hop vo 1", "do gains0", "beside ca 0", "hop qk 2", "do gains1",
    "beside cd 1", "hop cd 2", "beside u0 0", "beside qk 0", "hop vo 2", "hop cu 1", "hop u0 1",
    "beside vo 0", "hop ca 3", "hop vo 3", "beside ca 1", "hop u0 2", "do gains2",
    "from_image ca 0", "beside cd 2", "hop cu 2", "from_image cd 0", "beside cu 0", "hop cd 3",
    "hop d1 1", "start u1", "beside cu 1", "beside qk 1", "hop qk 3", "beside ca 2", "hop u1 1",
    "beside vo 1", "beside ca 3", "hop u0 3", "hop u1 2", "beside qk 2", "from_image ca 1",
    "hop d0 1", "from_image cu 0", "beside qk 3", "beside d2 0", "hop u1 3", "beside vo 2",
    "from_image cu 1", "beside u0 1", "done qk", "do norm", "do qk", "hop d2 1", "beside u1 0",
    "beside vo 3", "hop d0 2", "from_image ca 2", "beside cd 3", "from_image cd 1", "hop cu 3",
    "hop d2 2", "done vo", "do v", "do attend", "do out", "beside u1 1", "beside cu 2",
    "from_image cd 2", "hop d1 2", "beside u0 2", "beside u1 2", "beside u1 3", "beside u0 3",
    "from_image cd 3", "hop d0 3", "hop d2 3", "from_image ca 3", "done u0", "do up0",
    "beside cu 3", "done u1", "do up1", "do keep", "hop d1 3", "done d0", "do down0",
    "from_image cu 2", "beside d2 1", "from_image cu 3", "beside d2 2", "beside d2 3", "done d1",
    "do down1", "done cd", "done ca", "done cu", "done d2", "do down2", "do end", "do query",
    "do rows", "do cross0", "do cross1", "do cross2", "do cross3", "do cross4",
)
AFTER = {
    "qk": ("norm", "qk"),
    "vo": ("v", "attend", "out"),
    "u0": ("up0",),
    "u1": ("up1", "keep"),
    "d0": ("down0",),
    "d1": ("down1",),
    "d2": ("down2", "end"),
}


def parsed(lines):
    events = []
    for line in lines:
        kind, name, *k = line.split()
        events.append((kind, name, int(k[0]) if k else 0))
    return events


def gather_order(lines):
    if lines == 4 and GATHER_FOUR:
        return parsed(GATHER_FOUR)
    slots = {}

    def put(slot, kind, name, k=0):
        slots.setdefault(max(slot, 0), []).append((kind, name, k))

    for index, name in enumerate(GATHER):
        late = 1 if name in GATHER_BESIDE else 0
        if name in ("ca", "cu"):
            put(index - LEAD + 1, "do", "block")
        put(index - LEAD + 1, "start", name)
        if late:
            put(index + 1, "beside", name)
        for k in range(1, lines):
            put(index + k + late, "hop", name, k)
        for k in range(late, lines):
            put(index + k + 1, "beside", name, k)
        for k in range(lines):
            put(index + k + 2 + late, "from_image", name, k)
        put(index + lines + 1 + late, "done", name)
        for step in AFTER.get(name, ()):
            put(index + lines + 1 + late, "do", step)
    for index in range(3):
        put(index + 1, "do", "gains%d" % index)
    rank = {"start": 0, "beside": 2, "hop": 1, "from_image": 3, "done": 4, "do": 5}
    events = []
    for slot in sorted(slots):

        def place(event):
            kind, name, k = event
            if kind == "beside" and name in GATHER_BESIDE:
                return 0.5
            if kind == "do" and name == "block":
                return -1
            if kind == "do" and name.startswith("gains"):
                return 0.2
            return rank[kind]

        events += [e for e in sorted(slots[slot], key=place) if e not in events]
    last = ["query", "rows"] + ["cross%d" % i for i in range(5)]
    return events + [("do", name, 0) for name in last]


def place_gains(net, own, cross, out):
    width = out.shape[1]

    def placed(gain, index):
        count = gain.shape[1]
        lane = lax.broadcasted_iota(jnp.int32, (count, width), 1)
        row = lax.broadcasted_iota(jnp.int32, (count, width), 0)
        pick = jnp.where(lane == index * count + row, 1.0, 0.0)
        many = jnp.broadcast_to(gain[...].astype(jnp.float32), (8, count))
        return product(low(many), low(pick))[0:1]

    out[...] = jnp.zeros_like(out)
    for i, gain in enumerate(own):
        row = placed(gain, net.dp)
        out[i : i + 1, :] = jnp.where(net.image, row, 0.0)
        out[i + 2 : i + 3, :] = jnp.where(net.text, row, 0.0)
    for i, gain in enumerate(cross):
        out[4 + i : 5 + i, :] = placed(gain, net.tower * 4 * net.lines + net.dp)


def fill_masks(net, counts, lengths, allowed, cross_allowed, row_weight):
    shape = allowed.shape

    def place(index):
        image_of, bound = jnp.zeros_like(index), jnp.int32(0)
        for i in range(counts.shape[1]):
            bound = bound + counts[0, i]
            image_of = image_of + jnp.where(index >= bound, 1, 0)
        caption_of = index // CAP_LEN
        within = index - caption_of * CAP_LEN
        length = jnp.zeros_like(index)
        for i in range(lengths.shape[0]):
            length = jnp.where(caption_of == i, lengths[i], length)
        return image_of, caption_of, within, within < length

    row = place(lax.broadcasted_iota(jnp.int32, shape, 0))
    key = place(lax.broadcasted_iota(jnp.int32, shape, 1))
    image_mask = row[0] == key[0]
    text_mask = (row[1] == key[1]) & (key[2] <= row[2]) & key[3]
    here = jnp.where(net.text, text_mask.astype(jnp.float32), image_mask.astype(jnp.float32))
    allowed[...] = here
    cross_allowed[...] = (row[1] == key[0]).astype(jnp.float32)
    valid = place(lax.broadcasted_iota(jnp.int32, row_weight.shape, 0))[3]
    row_weight[...] = jnp.where(net.text, valid.astype(jnp.float32), 1.0)


def forward_kernel(
    lines, cuts, parts,
    counts, lengths, g_attn, g_mlp, g_query, g_image, g_cross,
    i_tok, i_cot, i_cq, i_ckv, i_co, i_cu, own_qkv, own_out, own_up, own_d, own_cd,
    full_a, full_d, sum_ca, sum_cd, o_h1, o_qkv, o_mixed, o_weight, o_middle, o_h2, o_active, o_slope,
    gains, layer_out, top, vec,
    tok, cot, cq, ckv, co, cu, w_a, w_d, w_ca, w_cd, h1, qkv, mixed, weight, middle, h2, active, slope, out_y, wide, branch,
    passed, returned, image_out, n_x, g_mixed, n_q, n_i, query, keyval, c_mixed, c_weight, c_middle, h3, grad_wide, g_small,
    allowed, cross_allowed, row_weight, gvec, pack, swap, block, rcv_d, sib_q, sib_i, sib_m, sib_h, sib_du, sib_dx, sib_dq, sib_dkv, arrived, totals, spread, sums_ref, gain_rows,
    send_sem, recv_sem, local_sem, swap_sem, s_send, s_recv, pass_sem, out_sem, d_send, d_recv, d_local, own_sem, in_sem, e_send, e_recv,
):
    net = Net(lines)
    net.greet()
    text, image = net.text, net.image
    rows, depth = own_qkv.shape[0], own_d.shape[0]
    all_a = sum(parts)
    few, part = pack.shape[1], own_cd.shape[0]
    width = tok.shape[1]
    half = pack.shape[2]
    a_qkv, a_out = parts[0], parts[0] + parts[1]
    q_end, kv_end, o_end = cuts[0], cuts[0] + cuts[1], cuts[0] + cuts[1] + cuts[2]
    tile = width

    placing = []
    for index, (src, at) in enumerate(((own_qkv, 0), (own_out, a_qkv), (own_up, a_out))):
        here = pl.ds(pl.multiple_of(net.dp * rows, rows), rows)
        copy = pltpu.make_async_copy(
            src, w_a.at[here, at : at + src.shape[1]], own_sem.at[index]
        )
        copy.start()
        placing.append(copy)
    loads = []
    for src, held in ((i_cq, cq), (i_ckv, ckv), (i_co, co), (i_cu, cu), (i_tok, tok), (i_cot, cot)):
        copy = pltpu.make_async_copy(src, held, in_sem.at[len(loads)])
        copy.start()
        loads.append(copy)
    place_gains(net, (g_attn, g_mlp), (g_query, g_image, g_cross), gvec)
    for copy in loads:
        copy.wait()
    at = 0
    for src, n in zip((cq, ckv, co, cu), cuts):
        whole = src[...].astype(jnp.float32)
        for h in range(2):
            pack[h, :, at : at + n] = whole[:, h * n : (h + 1) * n]
        at += n
    net.meet()
    for copy in placing:
        copy.wait()

    def columns(first, last):
        return lambda tower, chip, core: w_a.at[
            pl.ds(pl.multiple_of((2 * chip + core) * rows, rows), rows), first:last
        ]

    def crossed(first, last):
        return lambda tower, chip, core: w_ca.at[
            core,
            pl.ds(pl.multiple_of((tower * 2 * lines + chip) * 2 * few, 2 * few), 2 * few),
            first:last,
        ]

    def plan(index, own, place, crossing):
        beside = GATHER_NAMES[index] in GATHER_BESIDE
        kind = GatherBeside if beside else Gather
        return kind(
            net, own, place, crossing, send_sem.at[index], recv_sem.at[index], local_sem.at[index]
        )

    def self_part(index, first, last):
        return plan(index, None, columns(first, last), False)

    def down_part(index, first, last):
        return plan(
            index,
            own_d.at[:, first:last],
            lambda tower, chip, core: w_d.at[
                pl.ds(pl.multiple_of((2 * chip + core) * depth, depth), depth), first:last
            ],
            False,
        )

    def cross_part(index, first, last):
        return plan(index, block.at[:, first:last], crossed(first, last), True)

    mid, third = a_qkv - width, width // 3
    jobs = {
        "qk": self_part(0, 0, mid),
        "vo": self_part(1, mid, a_out),
        "u0": self_part(2, a_out, a_out + 2 * width),
        "u1": self_part(3, a_out + 2 * width, all_a),
        "d0": down_part(4, 0, third),
        "d1": down_part(5, third, 2 * third),
        "d2": down_part(6, 2 * third, width),
        "ca": cross_part(7, 0, o_end),
        "cu": cross_part(8, o_end, half),
        "cd": plan(
            9,
            own_cd,
            lambda tower, chip, core: w_cd.at[
                pl.ds(pl.multiple_of((tower * 4 * lines + 2 * chip + core) * part, part), part), :
            ],
            True,
        ),
    }
    kept = []

    def keep(src, dst):
        copy = pltpu.make_async_copy(src, dst, out_sem.at[len(kept)])
        copy.start()
        kept.append(copy)

    theirs = 1 - net.core

    def share_rows(index, src, dst):
        net.send("core", src, dst, e_send.at[index], e_recv.at[index], text)

    def shared(index, dst):
        net.arrive(dst, e_send.at[index], e_recv.at[index], text)

    def half_of(core, n):
        return pl.ds(pl.multiple_of(core * n, n), n)

    swapped = net.copy("core", pack.at[1 - net.core], swap, swap_sem.at[0], swap_sem.at[1])
    swapped.start()
    small = Small(net, gvec, arrived, totals, spread, s_send, s_recv)
    sums = Sums(sums_ref, row_weight)
    base = 4 * net.tower
    gain_rows[...] = jnp.zeros_like(gain_rows)
    first = net.core == 0

    def gain(at):
        return jnp.where(text, gains[at + 2 : at + 3, :], gains[at : at + 1, :])

    def build_block():
        swapped.wait()
        mine = pack[net.core]
        theirs = swap[...]
        block[0:few] = low(jnp.where(first, mine, theirs))
        block[few:] = low(jnp.where(first, theirs, mine))

    def gains_over(index):
        def run():
            small.collect(index)
            if index < 2:
                small.exchange(index + 1)
            else:
                small.spread()

        return run

    def first_norm():
        small.total(gains)
        fill_masks(net, counts, lengths, allowed, cross_allowed, row_weight)
        norm_rows(tok, gain(0), h1, lambda r, v: sums.add(base, r, v))
        keep(h1, o_h1)

    def project(first_column, last_column):
        def run():
            def qkv_tile(i, carry):
                cols = pl.ds(pl.multiple_of(first_column + i * tile, tile), tile)
                qkv[:, cols] = low(product(h1[...], w_a[:, cols]))
                return carry

            lax.fori_loop(0, (last_column - first_column) // tile, qkv_tile, 0)

        return run

    def attend():
        keep(qkv, o_qkv)
        attention(
            pairs_of(qkv), pairs_of(qkv, width), pairs_of(qkv, 2 * width), allowed, weight, mixed
        )
        keep(weight, o_weight)
        keep(mixed, o_mixed)

    def attn_out():
        branch[...] = product(mixed[...], w_a[:, a_qkv:a_out])

        def add_branch(r):
            value = branch[r, :]
            sums.add(base + 1, r, value)
            middle[r, :] = tok[r, :].astype(jnp.float32) + value

        blocks(tok.shape[0], row_step(tok.shape[0]), add_branch)
        keep(middle, o_middle)
        norm_rows(middle, gain(1), h2)
        keep(h2, o_h2)

    def go_up(first_tile, last_tile):
        def run():
            def up_tile(i, carry):
                at = pl.multiple_of((first_tile + i) * tile, tile)
                wide[...] = product(h2[...], w_a[:, pl.ds(a_out + at, tile)])
                activate(wide, active, slope, pl.ds(at, tile))
                return carry

            lax.fori_loop(0, last_tile - first_tile, up_tile, 0)

        return run

    def keep_up():
        keep(active, o_active)
        keep(slope, o_slope)
        keep(w_a, full_a)

    def go_down(index):
        first_column, last_column = index * third, (index + 1) * third

        def run():
            branch[:, first_column:last_column] = product(
                active[...], w_d[:, first_column:last_column]
            )

            def add_mlp(r):
                value = branch[r, first_column:last_column]
                sums.add(base + 2, r, value)
                y = middle[r, first_column:last_column] + value
                out_y[r, first_column:last_column] = y
                image_out[r, first_column:last_column] = low(y)

                @pl.when(image)
                def _():
                    sums.add(3, r, y)

            blocks(tok.shape[0], row_step(tok.shape[0]), add_mlp)
            net.send(
                "x",
                image_out.at[:, first_column:last_column],
                passed.at[:, first_column:last_column],
                pass_sem.at[0, index],
                pass_sem.at[1, index],
                image,
            )

        return run

    def self_end():
        keep(w_d, full_d)

    def rows_arrive():
        for index in range(3):
            part_of = passed.at[:, index * third : (index + 1) * third]
            net.arrive(part_of, pass_sem.at[0, index], pass_sem.at[1, index], text)

    def cross_queries():
        @pl.when(text)
        def _():
            norm_rows(out_y, gains[4:5, :], n_q)
            for h in range(2):
                at = h * cuts[0]
                query[:, at : at + cuts[0]] = low(product(n_q[...], w_ca[h, :, 0:q_end]))

        share_rows(0, n_q, sib_q)

    def cross_keys():
        @pl.when(text)
        def _():
            norm_rows(passed, gains[5:6, :], n_i)
            for h in range(2):
                at = h * width
                keyval[:, at : at + width] = low(product(n_i[...], w_ca[h, :, q_end:kv_end]))

        share_rows(1, n_i, sib_i)

    def cross_attend():
        @pl.when(text)
        def _():
            attention(
                pairs_of(query),
                pairs_of(keyval),
                pairs_of(keyval, width),
                cross_allowed,
                c_weight,
                c_mixed,
            )

        share_rows(2, c_mixed, sib_m)

    def cross_out():
        @pl.when(text)
        def _():
            for h in range(2):
                at = h * cuts[2]
                branch[:, at : at + cuts[2]] = product(c_mixed[...], w_ca[h, :, kv_end:o_end])

            def add_cross(r):
                value = branch[r, :]
                sums.add(7, r, value)
                c_middle[r, :] = out_y[r, :] + value

            blocks(tok.shape[0], row_step(tok.shape[0]), add_cross)
            norm_rows(c_middle, gains[6:7, :], h3)

        share_rows(3, h3, sib_h)

    def cross_up():
        for copy in kept:
            copy.wait()

        @pl.when(text)
        def _():
            for h in range(2):

                def one(i, carry):
                    at = pl.multiple_of(i * tile, tile)
                    wide[...] = product(h3[...], w_ca[h, :, pl.ds(o_end + at, tile)])
                    activate(wide, active, slope, pl.ds(h * cuts[3] + at, tile))
                    return carry

                lax.fori_loop(0, cuts[3] // tile, one, 0, unroll=True)

    def cross_down():
        @pl.when(text)
        def _():
            branch[...] = product(active[...], w_cd[...])

            def add_final(r):
                value = branch[r, :]
                sums.add(8, r, value)
                z = c_middle[r, :] + value
                sums.add(9, r, z)
                layer_out[r, :] = low(z)

            blocks(tok.shape[0], row_step(tok.shape[0]), add_final)

    tiles = active.shape[1] // tile
    steps = {
        "block": build_block,
        "gains0": gains_over(0),
        "gains1": gains_over(1),
        "gains2": gains_over(2),
        "norm": first_norm,
        "qk": project(0, mid),
        "v": project(mid, a_qkv),
        "attend": attend,
        "out": attn_out,
        "up0": go_up(0, tiles // 2),
        "up1": go_up(tiles // 2, tiles),
        "keep": keep_up,
        "down0": go_down(0),
        "down1": go_down(1),
        "down2": go_down(2),
        "end": self_end,
        "query": cross_queries,
        "rows": rows_arrive,
        "cross0": cross_keys,
        "cross1": cross_attend,
        "cross2": cross_out,
        "cross3": cross_up,
        "cross4": cross_down,
    }
    small.exchange(0)
    for kind, name, k in gather_order(lines):
        if kind == "do":
            steps[name]()
        elif kind == "start":
            jobs[name].start()
        elif kind == "done":
            jobs[name].done()
        else:
            getattr(jobs[name], kind)(k)

    net.finish()
    def hand(index, src, rcv, there=text):
        net.send("core", src, rcv, d_send.at[index], d_recv.at[index], there)

    def merge(index, own, rcv, out):
        net.arrive(rcv, d_send.at[index], d_recv.at[index], text)

        @pl.when(text)
        def _():
            def add(r):
                rcv[r, :] = low(own[r, :].astype(jnp.float32) + rcv[r, :].astype(jnp.float32))

            blocks(rcv.shape[0], 16, add)
            pltpu.make_async_copy(rcv, out, d_local.at[index]).start()

    @pl.when(text)
    def _():
        def down_tile(i, carry):
            cols = pl.ds(pl.multiple_of(i * tile, tile), tile)
            found = low(product(active[:, cols], cot[...], 0, 0))
            for k in range(tile // part):
                at = (k % 2) * (w_d.shape[0] // 2) + (k // 2) * part + i * (tile // 2)
                w_d[pl.ds(pl.multiple_of(at, part), part), :] = found[k * part : (k + 1) * part]
            grad = product(cot[...], w_cd[cols, :], 1, 1)
            grad_wide[:, cols] = low(grad * slope[:, cols])
            return carry

        lax.fori_loop(0, active.shape[1] // tile, down_tile, 0, unroll=True)

    share = w_d.shape[0] // 2
    hand(0, w_d.at[pl.ds(pl.multiple_of((1 - net.core) * share, share), share), :], rcv_d)
    share_rows(4, grad_wide.at[:, half_of(theirs, cuts[3])], sib_du)

    @pl.when(text)
    def _():
        branch[...] = product(grad_wide[:, 0 : cuts[3]], w_ca[0, :, o_end:half], 1, 1) + product(
            grad_wide[:, cuts[3] :], w_ca[1, :, o_end:half], 1, 1
        )

        def mid_done(r, back):
            total = cot[r, :].astype(jnp.float32) + back
            c_middle[r, :] = total
            n_x[r, :] = low(total)

        norm_back_rows(c_middle, gains[6:7, :], branch, mid_done, g_small)
        gain_rows[6:7, :] = g_small[...]

    share_rows(5, n_x.at[:, half_of(theirs, cuts[2])], sib_dx)

    @pl.when(text)
    def _():
        branch[...] = product(n_x[:, 0 : cuts[2]], w_ca[0, :, kv_end:o_end], 1, 1) + product(
            n_x[:, cuts[2] :], w_ca[1, :, kv_end:o_end], 1, 1
        )
        g_mixed[...] = low(branch[...])

        def att_done(pair, dq, dk, dv):
            at = pl.multiple_of(pair * 2 * HD, 2 * HD)
            query[:, pl.ds(at, 2 * HD)] = dq
            keyval[:, pl.ds(at, 2 * HD)] = dk
            keyval[:, pl.ds(width + at, 2 * HD)] = dv

        attention_back(
            pairs_of(query),
            pairs_of(keyval),
            pairs_of(keyval, width),
            pairs_of(g_mixed),
            c_weight,
            width,
            att_done,
        )

    share_rows(6, query.at[:, half_of(theirs, cuts[0])], sib_dq)
    share_rows(7, keyval.at[:, half_of(theirs, cuts[1])], sib_dkv)
    rows_half = tok.shape[0] // 2
    for index in range(2):
        at = index * rows_half
        here = slice(at, at + rows_half)

        @pl.when(text)
        def _():
            branch[here, :] = product(
                keyval[here, 0:width], w_ca[0, :, q_end:kv_end], 1, 1
            ) + product(keyval[here, width:], w_ca[1, :, q_end:kv_end], 1, 1)

            def image_done(r, back):
                image_out[pl.ds(at + r.start, r.size), :] = low(back)

            norm_back_rows(
                passed.at[here], gains[5:6, :], branch.at[here], image_done, g_small, index == 0
            )
            if index == 1:
                gain_rows[5:6, :] = g_small[...]

        net.send(
            "x",
            image_out.at[here],
            returned.at[here],
            pass_sem.at[2, index],
            pass_sem.at[3, index],
            text,
        )

    for index, dst in enumerate((sib_q, sib_i, sib_m, sib_h, sib_du, sib_dx, sib_dq, sib_dkv)):
        shared(index, dst)

    def cross_out_to(index, first, last):
        return pltpu.make_async_copy(w_a.at[:, first:last], sum_ca.at[:, first:last], d_local.at[index])

    @pl.when(text)
    def _():
        def both_rows(x, dy, sib_x, sib_dy):
            return low(product(x, dy, 0, 0) + product(sib_x, sib_dy, 0, 0))

        def up_grad(i, carry):
            at = pl.multiple_of(i * tile, tile)
            mine = pl.ds(pl.multiple_of(net.core * cuts[3] + at, tile), tile)
            w_a[:, pl.ds(o_end + at, tile)] = both_rows(
                h3[...], grad_wide[:, mine], sib_h[...], sib_du[:, pl.ds(at, tile)]
            )
            return carry

        lax.fori_loop(0, cuts[3] // tile, up_grad, 0, unroll=True)
        cross_out_to(1, o_end, half).start()
        mine = half_of(net.core, cuts[0])
        w_a[:, 0:q_end] = both_rows(n_q[...], query[:, mine], sib_q[...], sib_dq[...])
        mine = half_of(net.core, cuts[1])
        w_a[:, q_end:kv_end] = both_rows(n_i[...], keyval[:, mine], sib_i[...], sib_dkv[...])
        mine = half_of(net.core, cuts[2])
        w_a[:, kv_end:o_end] = both_rows(c_mixed[...], n_x[:, mine], sib_m[...], sib_dx[...])
        cross_out_to(2, 0, o_end).start()

    mine_d = w_d.at[pl.ds(pl.multiple_of(net.core * share, share), share), :]
    merge(0, mine_d, rcv_d, sum_cd)
    @pl.when(text)
    def _():
        branch[...] = product(query[:, 0 : cuts[0]], w_ca[0, :, 0:q_end], 1, 1) + product(
            query[:, cuts[0] :], w_ca[1, :, 0:q_end], 1, 1
        )

        def text_done(r, back):
            top[r, :] = c_middle[r, :] + back

        norm_back_rows(out_y, gains[4:5, :], branch, text_done, g_small)
        gain_rows[4:5, :] = g_small[...]
        sums_ref[10:11, :] = jnp.broadcast_to(
            jnp.sum(row_weight[...], axis=0, keepdims=True), (1, sums_ref.shape[1])
        )
        vec[...] = gain_rows[...]

    for index in range(2):
        net.arrive(
            returned.at[index * rows_half : (index + 1) * rows_half],
            pass_sem.at[2, index],
            pass_sem.at[3, index],
            image,
        )

    @pl.when(image)
    def _():
        vec[...] = jnp.zeros_like(vec)

        def add_back(r):
            top[r, :] = cot[r, :].astype(jnp.float32) + returned[r, :].astype(jnp.float32)
            layer_out[r, :] = image_out[r, :]

        blocks(tok.shape[0], row_step(tok.shape[0]), add_back)

    vec[7:8, 0 : sums_ref.shape[1]] = sums.line()

    @pl.when(text)
    def _():
        pltpu.make_async_copy(rcv_d, sum_cd, d_local.at[0]).wait()
        cross_out_to(1, o_end, half).wait()
        cross_out_to(2, 0, o_end).wait()

    net.finish()


def forward(lines, cuts, parts, *operands):
    tok, own_qkv, own_d, own_cd = operands[7], operands[13], operands[16], operands[17]
    cross_shards = operands[9:13]
    bf16, f32 = jnp.bfloat16, jnp.float32
    count = 4 * lines
    rows, width = tok.shape
    few, half = cross_shards[0].shape[0], sum(cuts)
    hidden = count * own_d.shape[0]
    all_a = (count * own_qkv.shape[0], sum(parts))
    gains_shape = (8, width)
    heads_n = width // HD
    jobs = 10
    shape = jax.ShapeDtypeStruct
    wide_b, wide_f = (rows, width), (rows, hidden)
    stored = [
        (wide_b, bf16),
        ((rows, parts[0]), bf16),
        (wide_b, bf16),
        ((heads_n, rows, rows), bf16),
        (wide_b, f32),
        (wide_b, bf16),
        (wide_f, bf16),
        (wide_f, f32),
    ]
    outs = [
        (all_a, bf16),
        ((hidden, width), bf16),
        ((width, half), bf16),
        ((hidden // 2, width), bf16),
        *stored,
        (gains_shape, f32),
        (wide_b, bf16),
        (wide_b, f32),
        (gains_shape, f32),
    ]
    scratch = [
        (wide_b, bf16),
        (wide_b, bf16),
        *((w.shape, bf16) for w in cross_shards),
        (all_a, bf16),
        ((hidden, width), bf16),
        ((2, width, half), bf16),
        ((hidden, width), bf16),
        *stored,
        (wide_b, f32),
        (wide_b, f32),
        (wide_b, f32),
        (wide_b, bf16),
        (wide_b, bf16),
        (wide_b, bf16),
        (wide_b, bf16),
        (wide_b, bf16),
        (wide_b, bf16),
        (wide_b, bf16),
        (wide_b, bf16),
        ((rows, 2 * width), bf16),
        (wide_b, bf16),
        ((heads_n, rows, rows), bf16),
        (wide_b, f32),
        (wide_b, bf16),
        (wide_f, bf16),
        ((1, width), f32),
        ((rows, rows), f32),
        ((rows, rows), f32),
        ((rows, 1), f32),
        (gains_shape, f32),
        ((2, few, half), f32),
        ((few, half), f32),
        ((2 * few, half), bf16),
        ((hidden // 2, width), bf16),
        *[(wide_b, bf16)] * 4,
        *(((rows, cuts[i]), bf16) for i in (3, 2, 0, 1)),
        ((3,) + gains_shape, f32),
        ((3,) + gains_shape, f32),
        ((lines - 1,) + gains_shape, f32),
        ((16, 128), f32),
        (gains_shape, f32),
    ]
    dma = pltpu.SemaphoreType.DMA
    return pl.pallas_call(
        functools.partial(forward_kernel, lines, cuts, parts),
        out_shape=tuple(shape(*o) for o in outs),
        in_specs=[SMEM, SMEM] + [VMEM] * 5 + [ANY] * 11,
        out_specs=[ANY] * 12 + [VMEM] * 4,
        scratch_shapes=[pltpu.VMEM(*s) for s in scratch]
        + [
            dma((jobs, Gather.sems(lines))),
            dma((jobs, Gather.sems(lines))),
            dma((jobs,)),
            dma((2,)),
            dma((2 + lines,)),
            dma((2 + lines,)),
            dma((4, 3)),
            dma((12,)),
            dma((3,)),
            dma((3,)),
            dma((3,)),
            dma((3,)),
            dma((6,)),
            dma((8,)),
            dma((8,)),
        ],
        compiler_params=pltpu.CompilerParams(
            collective_id=0, has_side_effects=True, vmem_limit_bytes=63 << 20
        ),
    )(*operands)


class Scatter:
    def __init__(self, net, own, near, far, rcv, sems):
        self.net, self.own, self.near, self.far, self.rcv = net, own, near, far, rcv
        self.send_sem, self.recv_sem = sems

    @staticmethod
    def sems(lines):
        return 1 + 7 * lines

    def sem(self, s):
        return self.send_sem.at[s], self.recv_sem.at[s]

    def add(self, pairs, out):
        def one(r):
            total = pairs[0][r, :].astype(jnp.float32)
            for other in pairs[1:]:
                total = total + other[r, :].astype(jnp.float32)
            out[r, :] = total.astype(out.dtype)

        blocks(out.shape[0], 16, one)

    def chips(self, k):
        net = self.net
        if k == 0:
            return ((None, net.z),)
        return (
            (net.z + k < net.lines, jnp.minimum(net.z + k, net.lines - 1)),
            (net.z >= k, jnp.maximum(net.z - k, 0)),
        )

    def order(self):
        return [pair for k in range(self.net.lines - 1, -1, -1) for pair in self.chips(k)]

    def swap(self, theirs, rcv):
        self.whole = rcv
        self.net.send("core", theirs, rcv, *self.sem(0))

    def swapped(self):
        self.net.arrive(self.whole, *self.sem(0))

    def over_x(self, part):
        net = self.net
        for there, z in self.order():
            for y in (1 - net.y, net.y):
                chip = 2 * z + y
                net.send(
                    "x", part(chip), self.own(chip), *self.sem(1 + chip), both(there, net.text), True
                )

    def from_x(self, chip, there):
        if self.rcv is None:
            net = self.net
            net.arrive(self.own(chip), *self.sem(1 + chip), both(there, net.image))

    def across(self, only=None):
        net = self.net
        for there, z in self.order():
            there = both(there, only)
            chip = 2 * z + 1 - net.y
            self.from_x(chip, there)
            own = self.own(chip)
            if self.rcv is not None:
                when(there, lambda: self.add([own, self.rcv(chip)], own))
            net.send("y", own, self.near(z), *self.sem(1 + 2 * net.lines + z), there)

    def here(self, chip, z):
        parts = [self.own(chip), self.near(z)]
        return parts if self.rcv is None else parts + [self.rcv(chip)]

    def along(self, k):
        net = self.net
        lines = net.lines
        for up, (there, z) in zip((True, False), self.chips(k)):
            chip = 2 * z + net.y
            base = (1 + 3 * lines) if up else (1 + 4 * lines)
            self.from_x(chip, there)
            net.arrive(self.near(z), *self.sem(1 + 2 * lines + z), there)
            more = net.low if up else net.high
            s = base + z
            net.arrive(self.far(z), *self.sem(s), both(there, more))
            own = self.own(chip)
            parts = self.here(chip, z)
            when(both(there, more), lambda: self.add(parts + [self.far(z)], own))
            when(both(there, jnp.logical_not(more)), lambda: self.add(parts, own))
            slot = z if up else jnp.where(z == net.z - 1, lines, z)
            net.send("up" if up else "down", own, self.far(slot), *self.sem(s), there)

    def turn(self):
        pass

    def total(self, out):
        net = self.net
        lines = net.lines
        self.from_x(net.chip, None)
        net.arrive(self.near(net.z), *self.sem(1 + 2 * lines + net.z))
        net.arrive(self.far(net.z), *self.sem(1 + 3 * lines + net.z), net.low)
        net.arrive(self.far(lines), *self.sem(1 + 4 * lines + net.z), net.high)
        parts = self.here(net.chip, net.z)
        low_part, high_part = self.far(net.z), self.far(lines)
        when(both(net.low, net.high), lambda: self.add(parts + [low_part, high_part], out))
        when(jnp.logical_not(net.low), lambda: self.add(parts + [high_part], out))
        when(jnp.logical_not(net.high), lambda: self.add(parts + [low_part], out))


class ScatterAlong(Scatter):
    def across(self, only=None):
        pass

    def spot(self, z, second):
        if not second:
            return self.far(z)
        if isinstance(z, int):
            return self.extra(0)
        return self.near(z)

    def line_sems(self, up, second):
        lines = self.net.lines
        return 1 + (3 + 2 * second + (0 if up else 1)) * lines

    def parts(self, chip):
        return [self.own(chip)] if self.rcv is None else [self.own(chip), self.rcv(chip)]

    def along(self, k):
        net = self.net
        for up, (there, z) in zip((True, False), self.chips(k)):
            for second, y in ((0, net.y), (1, 1 - net.y)):
                chip = 2 * z + y
                self.from_x(chip, there)
                more = net.low if up else net.high
                s = self.line_sems(up, second) + z
                net.arrive(self.spot(z, second), *self.sem(s), both(there, more))
                own = self.own(chip)
                parts = self.parts(chip)
                with_far = parts + [self.spot(z, second)]
                when(both(there, more), lambda: self.add(with_far, own))
                if len(parts) > 1:
                    when(both(there, jnp.logical_not(more)), lambda: self.add(parts, own))
                way = "up" if up else "down"
                if up:
                    net.send(way, own, self.spot(z, second), *self.sem(s), there)
                else:
                    last = z == net.z - 1
                    net.send(
                        way, own, self.spot(net.lines, second), *self.sem(s), both(there, last)
                    )
                    net.send(
                        way,
                        own,
                        self.spot(z, second),
                        *self.sem(s),
                        both(there, jnp.logical_not(last)),
                    )

    def gathered(self, second, more, out):
        net = self.net
        lines = net.lines
        chip = 2 * net.z + (1 - net.y if second else net.y)
        self.from_x(chip, None)
        s = self.line_sems(True, second) + net.z
        net.arrive(self.spot(net.z, second), *self.sem(s), net.low)
        s = self.line_sems(False, second) + net.z
        net.arrive(self.spot(lines, second), *self.sem(s), net.high)
        parts = self.parts(chip) + more
        low_part, high_part = self.spot(net.z, second), self.spot(lines, second)
        when(both(net.low, net.high), lambda: self.add(parts + [low_part, high_part], out))
        when(jnp.logical_not(net.low), lambda: self.add(parts + [high_part], out))
        when(jnp.logical_not(net.high), lambda: self.add(parts + [low_part], out))

    def turn(self):
        net = self.net
        own = self.own(2 * net.z + 1 - net.y)
        self.gathered(1, [], own)
        net.send("y", own, self.extra(1), *self.sem(1 + 2 * net.lines))

    def total(self, out):
        self.net.arrive(self.extra(1), *self.sem(1 + 2 * self.net.lines))
        self.gathered(0, [self.extra(1)], out)


def strip(ref, size, first, last):
    return lambda i: ref.at[pl.ds(pl.multiple_of(i * size, size), size), first:last]


def backward_kernel(
    lines, cuts, parts,
    i_tok, i_top, gains, vec_in, full_a, full_d, sum_ca, sum_cd,
    i_h1, i_qkv, i_mixed, i_weight, i_middle, i_h2, i_active, i_slope,
    r_qkv, r_out, r_up, r_d, r_cq, r_ckv, r_co, r_cu, r_cd, r_grad, o_vec,
    o_qkv, o_out, o_up, o_d, o_cq, o_ckv, o_co, o_cu, o_cd, input_grad,
    tok, top_in, h1, qkv, mixed, weight, middle, h2, active, slope,
    g_a, g_d, rcv_a, rcv_d, near_a, near_d, far_a, far_d,
    own_ca, own_cd, near_ca, near_cd, far_ca, far_cd,
    w_d, w_up, top, branch, n_grad, g_small, vec, fin, fin_vo, extra_a, extra_d, swap, arrived, totals, spread,
    send_sem, recv_sem, load_sem, swap_sem, s_send, s_recv, out_sem,
):
    net = Net(lines)
    net.greet()
    left = []

    def leave(src, out):
        copy = pltpu.make_async_copy(src, out, out_sem.at[len(left)])
        copy.start()
        left.append(copy)

    text, image = net.text, net.image
    width = tok.shape[1]
    tile = width
    rows, depth = o_qkv.shape[0], o_d.shape[0]
    few, part = 2 * o_cq.shape[0], o_cd.shape[0]
    half = own_ca.shape[1]
    a_out = parts[0] + parts[1]
    all_a = g_a.shape[2]
    o_end = cuts[0] + cuts[1] + cuts[2]
    theirs = 1 - net.core

    def load(index, src, dst):
        copy = pltpu.make_async_copy(src, dst, load_sem.at[index])
        copy.start()
        return copy

    l_top = load(16, i_top, top_in)
    l_active = load(0, i_active, active)
    l_wd = load(1, full_d, w_d)
    l_slope = load(2, i_slope, slope)
    l_h2 = load(3, i_h2, h2)
    l_up = load(4, full_a.at[:, a_out:], w_up)
    l_middle = load(5, i_middle, middle)
    l_mixed = load(6, i_mixed, mixed)
    l_qkv = load(7, i_qkv, qkv)
    l_weight = load(8, i_weight, weight)
    l_h1 = load(9, i_h1, h1)
    l_tok = load(17, i_tok, tok)

    def job(index, own, near, far, rcv, extra=None):
        kind = ScatterAlong if SCATTER_NAMES[index] in SCATTER_ALONG else Scatter
        made = kind(net, own, near, far, rcv, (send_sem.at[index], recv_sem.at[index]))
        made.extra = extra
        return made

    def self_a(index, first, last):
        return job(
            index,
            strip(g_a.at[net.core], rows, first, last),
            strip(near_a, rows, first, last),
            strip(far_a, rows, first, last),
            strip(rcv_a, rows, first, last),
            strip(extra_a, rows, first, last),
        )

    def cross_a(index, first, last):
        return job(
            index,
            strip(own_ca, few, first, last),
            strip(near_ca, few, first, last),
            strip(far_ca, few, first, last),
            None,
        )

    def self_d(index, first, last):
        return job(
            index,
            strip(g_d.at[net.core], depth, first, last),
            strip(near_d, depth, first, last),
            strip(far_d, depth, first, last),
            strip(rcv_d, depth, first, last),
            strip(extra_d, depth, first, last),
        )

    mid, middle_up, third = parts[0] - width, a_out + 2 * width, width // 3
    jobs = {
        "d0": self_d(0, 0, third),
        "d1": self_d(1, third, 2 * third),
        "d2": self_d(2, 2 * third, width),
        "u0": self_a(3, a_out, middle_up),
        "u1": self_a(4, middle_up, all_a),
        "qk": self_a(5, 0, mid),
        "vo": self_a(6, mid, a_out),
        "cd": job(
            7,
            strip(own_cd, part, 0, width),
            strip(near_cd, part, 0, width),
            strip(far_cd, part, 0, width),
            None,
        ),
        "cu": cross_a(8, o_end, half),
        "ca": cross_a(9, 0, o_end),
    }

    def swap_a(name, first, last):
        jobs[name].swap(g_a.at[theirs, :, first:last], rcv_a.at[:, first:last])

    def swap_d(name, first, last):
        jobs[name].swap(g_d.at[theirs, :, first:last], rcv_d.at[:, first:last])

    def across(name, only=None):
        if jobs[name].rcv is not None:
            jobs[name].swapped()
        jobs[name].across(only)

    plane_a, plane_d = own_ca.shape[0], own_cd.shape[0]
    c_loads = (
        pltpu.make_async_copy(sum_cd.at[plane_d : 2 * plane_d, :], own_cd, load_sem.at[10]),
        pltpu.make_async_copy(sum_ca.at[plane_a : 2 * plane_a, :], own_ca, load_sem.at[11]),
    )

    @pl.when(text)
    def _():
        for copy in c_loads:
            copy.start()

    def start_x(name):
        at = {"cd": (sum_cd, part, 0, width), "cu": (sum_ca, few, o_end, half), "ca": (sum_ca, few, 0, o_end)}
        jobs[name].over_x(strip(*at[name]))

    def round_top():
        l_top.wait()

        def body(r):
            n_grad[r, :] = low(top_in[r, :])

        blocks(tok.shape[0], row_step(tok.shape[0]), body)

        @pl.when(text)
        def _():
            for copy in c_loads:
                copy.wait()

    def down_grads():
        l_active.wait()

        def down_tile(i, carry):
            cols = pl.ds(pl.multiple_of(i * tile, tile), tile)
            found = low(product(active[:, cols], n_grad[...], 0, 0))
            each = tile // depth
            for k in range(each):
                at = pl.multiple_of(((i * each + k) // 2) * depth, depth)
                g_d[k % 2, pl.ds(at, depth), :] = found[k * depth : (k + 1) * depth]
            return carry

        lax.fori_loop(0, active.shape[1] // tile, down_tile, 0)

    def wide_grads():
        l_wd.wait()
        l_slope.wait()

        def wide_tile(i, carry):
            cols = pl.ds(pl.multiple_of(i * tile, tile), tile)
            grad = product(n_grad[...], w_d[cols, :], 1, 1)
            active[:, cols] = low(grad * slope[:, cols])
            return carry

        lax.fori_loop(0, active.shape[1] // tile, wide_tile, 0)
        for i in range(4):
            src = full_a.at[:, i * width : (i + 1) * width]
            l_four.append(load(12 + i, src, w_d.at[i * width : (i + 1) * width, :]))
        l_h2.wait()

    l_four = []

    def put_a(found, at):
        for k in range(width // rows):
            g_a[k % 2, (k // 2) * rows : (k // 2 + 1) * rows, pl.ds(at, found.shape[1])] = found[
                k * rows : (k + 1) * rows
            ]

    def up_grads(first_tile, last_tile):
        def run():
            def up_tile(i, carry):
                at = pl.multiple_of(i * tile, tile)
                found = low(product(h2[...], active[:, pl.ds(at, tile)], 0, 0))
                put_a(found, pl.multiple_of(a_out + at, tile))
                return carry

            lax.fori_loop(first_tile, last_tile, up_tile, 0)

        return run

    def own_gain(at):
        return jnp.where(text, gains[at + 2 : at + 3, :], gains[at : at + 1, :])

    at_vec = 2 * net.tower

    def mid_grads():
        l_up.wait()
        branch[...] = product(active[...], w_up[...], 1, 1)
        l_middle.wait()

        def mid_done(r, back):
            total = top_in[r, :] + back
            top[r, :] = total
            n_grad[r, :] = low(total)

        norm_back_rows(middle, own_gain(1), branch, mid_done, g_small)
        vec[...] = vec_in[...]
        vec[pl.ds(at_vec + 1, 1), :] = g_small[...]

    def out_grads():
        l_mixed.wait()
        for copy in l_four:
            copy.wait()
        put_a(low(product(mixed[...], n_grad[...], 0, 0)), parts[0])
        mixed[...] = low(product(n_grad[...], w_d[3 * width : 4 * width, :], 1, 1))

    def att_grads():
        l_qkv.wait()
        l_weight.wait()

        def att_done(pair, dq, dk, dv):
            at = pl.multiple_of(pair * 2 * HD, 2 * HD)
            for k, grad in enumerate((dq, dk, dv)):
                qkv[:, pl.ds(pl.multiple_of(k * width + at, 2 * HD), 2 * HD)] = grad

        attention_back(
            pairs_of(qkv),
            pairs_of(qkv, width),
            pairs_of(qkv, 2 * width),
            pairs_of(mixed),
            weight,
            width,
            att_done,
        )
        l_h1.wait()

    def qkv_grads(first_tile, last_tile):
        def run():
            def qkv_tile(i, carry):
                at = pl.multiple_of(i * tile, tile)
                put_a(low(product(h1[...], qkv[:, pl.ds(at, tile)], 0, 0)), at)
                return carry

            lax.fori_loop(first_tile, last_tile, qkv_tile, 0)

        return run

    small = Small(net, vec, arrived, totals, spread, s_send, s_recv)

    def first_grads():
        l_tok.wait()
        branch[...] = (
            product(qkv[:, 0:width], w_d[0:width, :], 1, 1)
            + product(qkv[:, width : 2 * width], w_d[width : 2 * width, :], 1, 1)
            + product(qkv[:, 2 * width :], w_d[2 * width : 3 * width, :], 1, 1)
        )

        def first_done(r, back):
            input_grad[r, :] = top[r, :] + back

        norm_back_rows(tok, own_gain(0), branch, first_done, g_small)
        leave(input_grad, r_grad)
        vec[pl.ds(at_vec, 1), :] = g_small[...]
        small.exchange(0)

    def small_step(index):
        def run():
            small.collect(index)
            if index < 2:
                small.exchange(index + 1)
            else:
                small.spread()

        return run

    up_tiles = (all_a - a_out) // tile
    steps = {
        "top": round_top,
        "down": down_grads,
        "wide": wide_grads,
        "up0": up_grads(0, up_tiles // 2),
        "up1": up_grads(up_tiles // 2, up_tiles),
        "mid": mid_grads,
        "out": out_grads,
        "att": att_grads,
        "qk": qkv_grads(0, mid // tile),
        "v": qkv_grads(mid // tile, parts[0] // tile),
        "first": first_grads,
        "small0": small_step(0),
        "small1": small_step(1),
        "small2": small_step(2),
    }
    share = few // 2
    first = net.core == 0
    swaps = {}

    def start_swap(name, index, first_column, last_column):
        copy = net.copy(
            "core",
            fin.at[pl.ds(pl.multiple_of(theirs * share, share), share), first_column:last_column],
            swap.at[:, first_column:last_column],
            swap_sem.at[index, 0],
            swap_sem.at[index, 1],
        )
        copy.start()
        swaps[name] = copy

    def put_cross(out, at, n):
        mine = fin[pl.ds(pl.multiple_of(net.core * share, share), share), at : at + n]
        other = swap[:, at : at + n]
        out[:, 0:n] = jnp.where(first, mine, other)
        out[:, n:] = jnp.where(first, other, mine)

    def put_vo():
        o_qkv[:, mid:] = fin_vo[:, 0 : parts[0] - mid]
        o_out[...] = fin_vo[:, parts[0] - mid :]
        leave(o_qkv.at[:, mid:], r_qkv.at[:, mid:])
        leave(o_out, r_out)

    def going(ref, out, first_column, last_column):
        src = ref.at[:, first_column:last_column]
        return src, lambda: leave(src, out.at[:, first_column:last_column])

    totals_to = {
        "d0": going(o_d, r_d, 0, third),
        "d1": going(o_d, r_d, third, 2 * third),
        "d2": going(o_d, r_d, 2 * third, width),
        "u0": going(o_up, r_up, 0, middle_up - a_out),
        "u1": going(o_up, r_up, middle_up - a_out, all_a - a_out),
        "qk": going(o_qkv, r_qkv, 0, mid),
        "vo": (fin_vo, put_vo),
        "cd": going(o_cd, r_cd, 0, width),
        "cu": (fin.at[:, o_end:half], lambda: start_swap("cu", 0, o_end, half)),
        "ca": (fin.at[:, 0:o_end], lambda: start_swap("ca", 1, 0, o_end)),
    }
    spans = {
        "d0": (0, third),
        "d1": (third, 2 * third),
        "d2": (2 * third, width),
        "u0": (a_out, middle_up),
        "u1": (middle_up, all_a),
        "qk": (0, mid),
        "vo": (mid, a_out),
    }
    events = scatter_order(lines)
    for kind, name, k in events[:2]:
        steps[name]()
    net.meet()
    for kind, name, k in events[2:]:
        if kind == "do":
            steps[name]()
        elif kind == "x":
            start_x(name)
        elif kind == "swap":
            (swap_d if name in ("d0", "d1", "d2") else swap_a)(name, *spans[name])
        elif kind == "across":
            across(name, (None, text, image)[k])
        elif kind == "along":
            jobs[name].along(k)
        elif kind == "turn":
            jobs[name].turn()
        else:
            out, then = totals_to[name]
            jobs[name].total(out)
            if then is not None:
                then()
    swaps["cu"].wait()
    put_cross(o_cu, o_end, cuts[3])
    leave(o_cu, r_cu)
    small.total(o_vec)
    swaps["ca"].wait()
    at = 0
    for out, result, n in zip((o_cq, o_ckv, o_co), (r_cq, r_ckv, r_co), cuts):
        put_cross(out, at, n)
        leave(out, result)
        at += n
    net.finish()
    for copy in left:
        copy.wait()


SCATTER = ("d0", "d1", "d2", "u0", "u1", "cd", "qk", "vo", "cu", "ca")
SCATTER_NAMES = ("d0", "d1", "d2", "u0", "u1", "qk", "vo", "cd", "cu", "ca")
SCATTER_ALONG = ("d0", "u0")
BEFORE = {0: ("qk", "vo", "cd"), 3: ("cu",), 5: ("ca",)}
SCATTER_HEAD = (
    "do top", "do down", "x cd", "x cu", "x ca", "swap d0", "swap d1", "swap d2", "across cd 1",
    "do wide", "across d0", "across d1", "across d2", "do up0", "swap u0", "do up1", "swap u1",
    "do mid", "across u0", "across u1", "do out", "do att", "do qk", "swap qk", "do v", "swap vo",
    "do first",
)


def scatter_order(lines):
    if lines == 4 and SCATTER_FOUR:
        return parsed(SCATTER_FOUR)
    events = parsed(SCATTER_HEAD)
    count = len(SCATTER)
    for slot in range(count + lines):
        for name in BEFORE.get(slot, ()):
            events.append(("across", name, 2 if name == "cd" else 0))
        if 1 <= slot <= 3:
            events.append(("do", "small%d" % (slot - 1), 0))
        for k in range(lines - 1, -2, -1):
            index = slot - (lines - 1 - k)
            if 0 <= index < count:
                kind = "along" if k > 0 else "turn" if k == 0 else "total"
                events.append((kind, SCATTER[index], k))
    return events


SCATTER_FOUR = (
    "do top", "do down", "swap d0", "swap d1", "swap d2", "x cd", "do wide", "across d0",
    "along d0 3", "across cd 1", "across d1", "do up0", "swap u0", "along d0 2", "do up1",
    "across d2", "swap u1", "across u0", "along u0 3", "along d0 1", "do mid", "along u0 2",
    "across cd 2", "x ca", "x cu", "across u1", "do out", "along d1 3", "along d2 3", "along d2 2",
    "do att", "along cd 3", "do qk", "along cd 2", "swap qk", "along d1 2", "across qk",
    "along u1 3", "do v", "swap vo", "along u0 1", "along u1 2", "do first", "across vo",
    "along qk 3", "along u1 1", "do small0", "along qk 2", "along d2 1", "along vo 3", "do small1",
    "along cd 1", "along vo 2", "across cu", "do small2", "along cu 3", "total d2", "along vo 1",
    "across ca", "along cu 2", "total u1", "along qk 1", "along ca 3", "turn u0", "along d1 1",
    "along ca 2", "along cu 1", "total qk", "total cd", "turn d0", "along ca 1", "total vo",
    "total cu", "total d1", "total d0", "total u0", "total ca",
)


def backward(lines, cuts, parts, own_shapes, *operands):
    bf16, f32 = jnp.bfloat16, jnp.float32
    tok, top, gains, vec, full_a, full_d, sum_ca, sum_cd = operands[:8]
    stored = [(o.shape, o.dtype) for o in operands[8:]]
    chips = 2 * lines
    row_count, width = tok.shape
    hidden, all_a = full_d.shape[0], full_a.shape[1]
    half = sum_ca.shape[1]
    rows, depth = width // (2 * chips), hidden // (2 * chips)
    few, part = width // (2 * chips), hidden // (4 * chips)
    results = [*own_shapes, (row_count, width)]
    outs = [*results, vec.shape]
    rcv_a, rcv_d = (chips * rows, all_a), (chips * depth, width)
    own_ca, own_cd = (chips * few, half), (chips * part, width)

    def line(size, count):
        return (size * count, all_a), (depth * count, width)

    scratch = [
        *((shape, f32) for shape in results),
        (tok.shape, tok.dtype),
        (top.shape, top.dtype),
        *stored,
        ((2,) + rcv_a, bf16),
        ((2,) + rcv_d, bf16),
        (rcv_a, bf16),
        (rcv_d, bf16),
        ((lines * rows, all_a), bf16),
        ((lines * depth, width), bf16),
        (((lines + 1) * rows, all_a), bf16),
        (((lines + 1) * depth, width), bf16),
        (own_ca, bf16),
        (own_cd, bf16),
        ((lines * few, half), bf16),
        ((lines * part, width), bf16),
        (((lines + 1) * few, half), bf16),
        (((lines + 1) * part, width), bf16),
        ((hidden, width), bf16),
        ((width, hidden), bf16),
        ((row_count, width), f32),
        ((row_count, width), f32),
        ((row_count, width), bf16),
        ((1, width), f32),
        (vec.shape, f32),
        ((rows, half), f32),
        ((rows, 2 * width), f32),
        ((2 * rows, all_a), bf16),
        ((2 * depth, width), bf16),
        ((few // 2, half), f32),
        ((3,) + vec.shape, f32),
        ((3,) + vec.shape, f32),
        ((lines - 1,) + vec.shape, f32),
    ]
    dma = pltpu.SemaphoreType.DMA
    return pl.pallas_call(
        functools.partial(backward_kernel, lines, cuts, parts),
        out_shape=tuple(jax.ShapeDtypeStruct(s, f32) for s in outs),
        in_specs=[ANY] * 2 + [VMEM] * 2 + [ANY] * 12,
        out_specs=[ANY] * len(results) + [VMEM],
        scratch_shapes=[pltpu.VMEM(*s) for s in scratch]
        + [
            dma((10, Scatter.sems(lines))),
            dma((10, Scatter.sems(lines))),
            dma((18,)),
            dma((2, 2)),
            dma((2 + lines,)),
            dma((2 + lines,)),
            dma((16,)),
        ],
        compiler_params=pltpu.CompilerParams(
            collective_id=1, has_side_effects=True, vmem_limit_bytes=63 << 20
        ),
    )(*operands)


def final_kernel(lines, rows, few, vec, *refs):
    count = (len(refs) - 7) // 3
    ins, outs = refs[:count], refs[count : 2 * count]
    g_1, g_2, g_q, g_i, g_c, rms, *held, sems = refs[2 * count :]
    come = [pltpu.make_async_copy(a, b, sems.at[0, i]) for i, (a, b) in enumerate(zip(ins, held))]
    go = [pltpu.make_async_copy(a, b, sems.at[1, i]) for i, (a, b) in enumerate(zip(held, outs))]
    for copy in come:
        copy.start()
    tower, dp = lax.axis_index("tower"), lax.axis_index("dp")
    width = vec.shape[1]

    def cut(n, at):
        lane = lax.broadcasted_iota(jnp.int32, (width, n), 0)
        index = lax.broadcasted_iota(jnp.int32, (width, n), 1)
        pick = jnp.where(lane == at + index, 1.0, 0.0)
        return lax.dot_general(
            vec[...],
            pick,
            (((1,), (0,)), ((), ())),
            precision=lax.Precision.HIGHEST,
            preferred_element_type=jnp.float32,
        )

    own = cut(rows, dp * rows)
    cross = cut(few, (tower * 4 * lines + dp) * few)
    g_1[...] = jnp.where(tower == 1, own[2:3], own[0:1])
    g_2[...] = jnp.where(tower == 1, own[3:4], own[1:2])
    g_q[...] = cross[4:5]
    g_i[...] = cross[5:6]
    g_c[...] = cross[6:7]
    sums = vec[7:8, 0:128]
    lane = lax.broadcasted_iota(jnp.int32, sums.shape, 1)
    valid = jnp.sum(jnp.where(lane == 10, sums, 0.0), axis=1, keepdims=True)
    images = ins[0].shape[0] * 4.0 * lines
    divisor = jnp.where(lane < 4, images, valid) * width
    rms[...] = jnp.sqrt(sums / divisor)[0, : rms.shape[0]]
    for here, there in zip(come, go):
        here.wait()
        there.start()
    for copy in go:
        copy.wait()


def final(lines, rows, few, vec, *results):
    f32 = jnp.float32
    small = [(1, rows)] * 2 + [(1, few)] * 3 + [(10,)]
    return pl.pallas_call(
        functools.partial(final_kernel, lines, rows, few),
        out_shape=tuple(jax.ShapeDtypeStruct(r.shape, r.dtype) for r in results)
        + tuple(jax.ShapeDtypeStruct(s, f32) for s in small),
        in_specs=[VMEM] + [ANY] * len(results),
        out_specs=[ANY] * len(results) + [VMEM] * 6,
        scratch_shapes=[pltpu.VMEM(r.shape, r.dtype) for r in results]
        + [pltpu.SemaphoreType.DMA((2, len(results)))],
        compiler_params=pltpu.CompilerParams(vmem_limit_bytes=62 << 20),
    )(vec, *results)


def plain_gather(own_a, own_d, pack, own_cd, own_g):
    axes = ("tower", "dp")
    tiles = lax.all_gather(own_g, axes, axis=0)
    return (
        lax.all_gather(own_a, "dp", axis=0, tiled=True),
        lax.all_gather(own_d, "dp", axis=0, tiled=True),
        lax.all_gather(pack.astype(jnp.bfloat16), axes, axis=1, tiled=True),
        lax.all_gather(own_cd, axes, axis=0, tiled=True),
        tiles.reshape((2, -1) + own_g.shape),
    )


def plain_scatter(g_a, g_d, g_ca, g_cd, vec, parts, cuts):
    axes = ("tower", "dp")

    def added(grad, over, axis):
        return lax.psum_scatter(
            grad.astype(jnp.float32), over, scatter_dimension=axis, tiled=True
        )

    a = added(g_a.reshape(-1, g_a.shape[-1]), "dp", 0)
    d = added(g_d.reshape(-1, g_d.shape[-1]), "dp", 0)
    ca = added(g_ca.reshape(2, -1, g_ca.shape[-1]), axes, 1)
    cd = added(g_cd.reshape(-1, g_cd.shape[-1]), axes, 0)
    at = [sum(cuts[:i]) for i in range(len(cuts) + 1)]
    cross = [
        jnp.concatenate([ca[0][:, i:j], ca[1][:, i:j]], axis=1) for i, j in zip(at[:-1], at[1:])
    ]
    first, second = parts[0], parts[0] + parts[1]
    self_parts = [a[:, :first], a[:, first:second], a[:, second:]]
    return (*self_parts, d, *cross, cd, lax.psum(vec, axes))


def layer_norm(value_matrix, norm_gain):
    center = value_matrix - jnp.mean(value_matrix, axis=-1, keepdims=True)
    spread = jnp.mean(center * center, axis=-1, keepdims=True)
    return center * lax.rsqrt(spread + EPSILON) * norm_gain


def norm_back(value_matrix, norm_gain, grad_out):
    result, puller = jax.vjp(layer_norm, value_matrix, norm_gain)
    return puller(grad_out)


def dot(a, b):
    return jnp.dot(a, b, preferred_element_type=jnp.float32)


def dot_tn(a, b):
    return jnp.einsum("rd,re->de", a, b, preferred_element_type=jnp.float32)


def dot_nt(a, b):
    return jnp.einsum("re,de->rd", a, b, preferred_element_type=jnp.float32)


def low(value_matrix):
    return value_matrix.astype(jnp.bfloat16)


def masks(counts, lengths, row_count, decoder):
    row_index = jnp.arange(row_count, dtype=jnp.int32)
    bounds = jnp.cumsum(counts)
    image_of = jnp.sum((row_index[:, None] >= bounds[None, :]).astype(jnp.int32), axis=1)
    caption_of = row_index // CAP_LEN
    in_place = row_index - caption_of * CAP_LEN
    caption_slots = jnp.arange(lengths.shape[0], dtype=jnp.int32)
    length_rows = jnp.sum(
        jnp.where(caption_of[:, None] == caption_slots[None, :], lengths[None, :], 0), axis=1
    )
    valid_rows = in_place < length_rows
    image_mask = image_of[:, None] == image_of[None, :]
    text_mask = (
        (caption_of[:, None] == caption_of[None, :])
        & (in_place[None, :] <= in_place[:, None])
        & valid_rows[None, :]
    )
    cross_mask = caption_of[:, None] == image_of[None, :]
    return jnp.where(decoder, text_mask, image_mask), cross_mask, valid_rows


def heads(value_matrix):
    return value_matrix.reshape(value_matrix.shape[0], -1, HD)


def attend(query, key, value, allowed):
    scores = jnp.einsum(
        "qhd,khd->hqk", heads(query), heads(key), preferred_element_type=jnp.float32
    ) * HD ** (-0.5)
    weight = jax.nn.softmax(jnp.where(allowed[None], scores, NEGATIVE), axis=-1)
    mixed = jnp.einsum("hqk,khd->qhd", low(weight), heads(value), preferred_element_type=jnp.float32)
    return low(mixed.reshape(query.shape)), weight


def attend_back(query, key, value, weight, grad_mixed):
    grad_mixed = heads(grad_mixed)
    grad_value = jnp.einsum("hqk,qhd->khd", low(weight), grad_mixed, preferred_element_type=jnp.float32)
    grad_weight = jnp.einsum("qhd,khd->hqk", grad_mixed, heads(value), preferred_element_type=jnp.float32)
    grad_score = low(
        weight * (grad_weight - jnp.sum(grad_weight * weight, axis=-1, keepdims=True))
    )
    grad_query = jnp.einsum(
        "hqk,khd->qhd", grad_score, heads(key), preferred_element_type=jnp.float32
    ) * HD ** (-0.5)
    grad_key = jnp.einsum(
        "hqk,qhd->khd", grad_score, heads(query), preferred_element_type=jnp.float32
    ) * HD ** (-0.5)
    return tuple(low(g.reshape(query.shape)) for g in (grad_query, grad_key, grad_value))


def mlp_forward(stream, gain, up, down):
    hidden = low(layer_norm(stream, gain))
    wide = dot(hidden, up)
    active = low(jax.nn.gelu(wide))
    return dot(active, down), (hidden, wide, active)


def mlp_back(stream, gain, up, down, stored, grad):
    hidden, wide, active = stored
    branch = low(grad)
    grad_down = dot_tn(active, branch)
    result, puller = jax.vjp(jax.nn.gelu, wide)
    grad_wide = low(puller(dot_nt(branch, down))[0])
    grad_up = dot_tn(hidden, grad_wide)
    grad_stream, grad_gain = norm_back(stream, gain, dot_nt(grad_wide, up))
    return grad + grad_stream, grad_gain, grad_up, grad_down


def squares(value_matrix, row_weight):
    return jnp.sum(row_weight[:, None] * value_matrix * value_matrix)


def plain_shards(
    tokens, cotangent, kept_counts, caption_lengths, attn_gain, qkv_weight, attn_out, mlp_gain,
    mlp_up, mlp_down, query_gain, image_gain, cross_gain, cross_query, cross_keyval, cross_out,
    cross_up, cross_down,
):
    f32 = jnp.float32
    dp_count = lax.axis_size("dp")
    lines = dp_count // 4
    tower, dp = lax.axis_index("tower"), lax.axis_index("dp")
    decoder = tower == 1
    row_count, width = tokens.shape[1:]
    rows = attn_gain.shape[1]
    few = query_gain.shape[0]

    def tile_row(value):
        return jnp.pad(value.astype(f32), (0, 128 - value.shape[0]))

    gain_tile = jnp.stack(
        [tile_row(attn_gain[0]), tile_row(mlp_gain[0])]
        + [tile_row(g) for g in (query_gain, image_gain, cross_gain)]
        + [jnp.zeros((128,), f32)] * 3
    )
    cross_shards = (cross_query, cross_keyval, cross_out, cross_up)
    cuts = tuple(w.shape[1] // 2 for w in cross_shards)
    pack = jnp.stack(
        [
            jnp.concatenate([w[:, h * n : (h + 1) * n] for w, n in zip(cross_shards, cuts)], axis=1)
            for h in range(2)
        ]
    ).astype(f32)
    self_parts = (qkv_weight.shape[2], attn_out.shape[2], mlp_up.shape[2])
    own_a = jnp.concatenate([qkv_weight[0], attn_out[0], mlp_up[0]], axis=1)
    full_a, full_d, full_ca, full_cd, full_g = plain_gather(
        own_a, mlp_down[0], pack, cross_down, gain_tile
    )
    qkv = full_a[:, : self_parts[0]]
    out = full_a[:, self_parts[0] : self_parts[0] + self_parts[1]]
    up = full_a[:, self_parts[0] + self_parts[1] :]
    down = full_d
    plane_gains = lax.dynamic_index_in_dim(full_g, tower, 0, keepdims=False)
    gain_1 = plane_gains[:, 0, :rows].reshape(-1)
    gain_2 = plane_gains[:, 1, :rows].reshape(-1)
    gain_q, gain_i, gain_c = (full_g[:, :, 2 + i, :few].reshape(-1) for i in range(3))

    stream = tokens[0].astype(f32)
    upstream = cotangent[0].astype(f32)
    allowed, cross_allowed, valid_rows = masks(kept_counts[0], caption_lengths, row_count, decoder)
    row_weight = jnp.where(decoder, valid_rows, True).astype(f32)

    normed = low(layer_norm(stream, gain_1))
    joined = low(dot(normed, qkv))
    query, key, value = jnp.split(joined, 3, axis=1)
    mixed, weight = attend(query, key, value, allowed)
    attn_branch = dot(mixed, out)
    middle = stream + attn_branch
    mlp_branch, mlp_stored = mlp_forward(middle, gain_2, up, down)
    layer_y = middle + mlp_branch
    image_rows = low(layer_y)
    arrived = lax.ppermute(image_rows, "tower", [(0, 1)])

    def run_cross(operands):
        text_y, image_in = operands
        at = [0]
        for n in cuts:
            at.append(at[-1] + n)
        cq, ckv, co, cu = (
            jnp.concatenate([full_ca[0][:, a:b], full_ca[1][:, a:b]], axis=1)
            for a, b in zip(at[:-1], at[1:])
        )
        image_in = image_in.astype(f32)
        image_normed = low(layer_norm(image_in, gain_i))
        keyval = low(dot(image_normed, ckv))
        c_key, c_value = jnp.split(keyval, 2, axis=1)
        c_normed = low(layer_norm(text_y, gain_q))
        c_query = low(dot(c_normed, cq))
        c_mixed, c_weight = attend(c_query, c_key, c_value, cross_allowed)
        c_branch = dot(c_mixed, co)
        c_middle = text_y + c_branch
        c_mlp, c_stored = mlp_forward(c_middle, gain_c, cu, full_cd)
        final_rows = c_middle + c_mlp
        grad_middle, grad_gain_c, grad_cu, grad_cd = mlp_back(
            c_middle, gain_c, cu, full_cd, c_stored, upstream
        )
        grad_branch = low(grad_middle)
        grad_co = dot_tn(c_mixed, grad_branch)
        grad_q, grad_k, grad_v = attend_back(
            c_query, c_key, c_value, c_weight, low(dot_nt(grad_branch, co))
        )
        grad_cq = dot_tn(c_normed, grad_q)
        grad_text, grad_gain_q = norm_back(text_y, gain_q, dot_nt(grad_q, cq))
        grad_keyval = jnp.concatenate([grad_k, grad_v], axis=1)
        grad_ckv = dot_tn(image_normed, grad_keyval)
        grad_image, grad_gain_i = norm_back(image_in, gain_i, dot_nt(grad_keyval, ckv))
        cross_sums = jnp.stack(
            [
                squares(c_branch, row_weight),
                squares(c_mlp, row_weight),
                squares(final_rows, row_weight),
            ]
        )
        grads = tuple(low(g) for g in (grad_cq, grad_ckv, grad_co, grad_cu))
        grad_ca = jnp.stack(
            [
                jnp.concatenate([g[:, h * n : (h + 1) * n] for g, n in zip(grads, cuts)], axis=1)
                for h in range(2)
            ]
        )
        return (
            low(final_rows),
            grad_middle + grad_text,
            low(grad_image),
            grad_ca,
            low(grad_cd),
            jnp.concatenate([grad_gain_q, grad_gain_i, grad_gain_c]),
            cross_sums,
        )

    def skip_cross(operands):
        shapes = jax.eval_shape(run_cross, operands)
        return tuple(jnp.zeros(s.shape, s.dtype) for s in shapes)

    final_rows, grad_text, grad_image, grad_ca, grad_cd, grad_cross_gains, cross_sums = lax.cond(
        decoder, run_cross, skip_cross, (layer_y, arrived)
    )
    returned = lax.ppermute(grad_image, "tower", [(1, 0)]).astype(f32)
    grad_top = jnp.where(decoder, grad_text, upstream + returned)

    grad_middle, grad_gain_2, grad_up, grad_down = mlp_back(
        middle, gain_2, up, down, mlp_stored, grad_top
    )
    grad_branch = low(grad_middle)
    grad_out = dot_tn(mixed, grad_branch)
    grad_joined = jnp.concatenate(
        attend_back(query, key, value, weight, low(dot_nt(grad_branch, out))), axis=1
    )
    grad_qkv = dot_tn(normed, grad_joined)
    grad_stream, grad_gain_1 = norm_back(stream, gain_1, dot_nt(grad_joined, qkv))
    grad_stream = grad_middle + grad_stream

    layer_sums = jnp.stack(
        [
            squares(stream, row_weight),
            squares(attn_branch, row_weight),
            squares(mlp_branch, row_weight),
            squares(layer_y, row_weight),
        ]
    )
    encoder_part = jnp.where(decoder, 0.0, layer_sums)
    decoder_part = jnp.where(decoder, jnp.concatenate([layer_sums[:3], cross_sums]), 0.0)
    counted = jnp.where(decoder, jnp.sum(valid_rows.astype(f32)), 0.0)
    line = tile_row(jnp.concatenate([encoder_part, decoder_part, counted[None]]))
    self_gains = jnp.concatenate([grad_gain_1, grad_gain_2])
    zero = jnp.zeros_like(self_gains)
    vec = jnp.concatenate(
        [
            jnp.where(decoder, zero, self_gains),
            jnp.where(decoder, self_gains, zero),
            grad_cross_gains,
            line,
        ]
    ).reshape(-1, 128)
    vec = jnp.pad(vec, ((0, -vec.shape[0] % 8), (0, 0)))
    grad_a = jnp.concatenate([low(grad_qkv), low(grad_out), low(grad_up)], axis=1)
    chips = 2 * lines
    results = plain_scatter(
        grad_a.reshape(chips, 2, rows, -1),
        low(grad_down).reshape(chips, 2, -1, width),
        grad_ca.reshape(2, 2, chips, 2 * few, -1),
        grad_cd.reshape(2, chips, 2, -1, width),
        vec,
        self_parts,
        cuts,
    )
    o_qkv, o_out, o_up, o_d, o_cq, o_ckv, o_co, o_cu, o_cd, o_vec = results
    flat = o_vec.reshape(-1)
    own_gains = lax.dynamic_slice(flat, (tower * 2 * width,), (2 * width,))
    g_1, g_2 = (lax.dynamic_slice(own_gains, (i * width + dp * rows,), (rows,)) for i in range(2))
    g_q, g_i, g_c = (
        lax.dynamic_slice(
            flat, ((4 + i) * width + (tower * dp_count + dp) * few,), (few,)
        )
        for i in range(3)
    )
    sums = flat[7 * width : 7 * width + 11]
    encoder_count = jnp.full((4,), float(row_count * dp_count), f32)
    divisor = jnp.concatenate([encoder_count, jnp.full((6,), 1.0, f32) * sums[10]]) * width
    rms_values = jnp.sqrt(sums[:10] / divisor)
    layer_out = jnp.where(decoder, final_rows, image_rows)
    return (
        layer_out[None], grad_stream[None], g_1[None], o_qkv[None], o_out[None], g_2[None],
        o_up[None], o_d[None], g_q, g_i, g_c, o_cq, o_ckv, o_co, o_cu, o_cd, rms_values,
    )


def fused_shards(
    tokens, cotangent, kept_counts, caption_lengths, attn_gain, qkv_weight, attn_out, mlp_gain,
    mlp_up, mlp_down, query_gain, image_gain, cross_gain, cross_query, cross_keyval, cross_out,
    cross_up, cross_down,
):
    f32 = jnp.float32
    dp_count = lax.axis_size("dp")
    lines = dp_count // 4
    row_count, width = tokens.shape[1:]
    rows = attn_gain.shape[1]
    few = query_gain.shape[0]
    cross_shards = (cross_query, cross_keyval, cross_out, cross_up)
    cuts = tuple(w.shape[1] // 2 for w in cross_shards)
    parts = (qkv_weight.shape[2], attn_out.shape[2], mlp_up.shape[2])
    (
        full_a, full_d, sum_ca, sum_cd, h1, qkv, mixed, weight, middle, h2, active, slope,
        gains, layer_out, top, vec,
    ) = forward(
        lines, cuts, parts, kept_counts, caption_lengths, attn_gain, mlp_gain,
        query_gain[None], image_gain[None], cross_gain[None], tokens[0], cotangent[0],
        *cross_shards, qkv_weight[0], attn_out[0], mlp_up[0], mlp_down[0], cross_down,
    )
    shard_shapes = [
        w.shape[-2:]
        for w in (
            qkv_weight, attn_out, mlp_up, mlp_down, cross_query, cross_keyval, cross_out, cross_up,
            cross_down,
        )
    ]
    *weight_grads, input_grad, o_vec = backward(
        lines, cuts, parts, shard_shapes, tokens[0], top, gains, vec, full_a, full_d, sum_ca,
        sum_cd, h1, qkv, mixed, weight, middle, h2, active, slope,
    )
    (
        layer_out, input_grad, o_qkv, o_out, o_up, o_d, o_cq, o_ckv, o_co, o_cu, o_cd,
        g_1, g_2, g_q, g_i, g_c, rms,
    ) = final(lines, rows, few, o_vec, layer_out, input_grad, *weight_grads)
    return (
        layer_out[None], input_grad[None], g_1, o_qkv[None], o_out[None], g_2, o_up[None],
        o_d[None], g_q[0], g_i[0], g_c[0], o_cq, o_ckv, o_co, o_cu, o_cd, rms,
    )


def shards(*arrays):
    dp_count = lax.axis_size("dp")
    cross_query, cross_down = arrays[13], arrays[17]
    fills = dp_count % 4 == 0 and dp_count > 4
    fills = fills and cross_query.shape[0] % 8 == 0 and cross_down.shape[0] % 16 == 0
    return fused_shards(*arrays) if fills else plain_shards(*arrays)


def solution(mesh):
    rows = P("tower", "dp", None)
    gain = P("tower", "dp")
    cross_gain = P(("tower", "dp"))
    cross = P(("tower", "dp"), None)
    weights = (gain, rows, rows, gain, rows, rows) + (cross_gain,) * 3 + (cross,) * 5
    return jax.shard_map(
        shards,
        mesh=mesh,
        in_specs=(rows, rows, P("dp", None), P("dp")) + weights,
        out_specs=(rows, rows) + weights + (P(),),
        check_vma=False,
    )
```

```python
import functools

import jax
import jax.numpy as jnp
from jax import lax
from jax.experimental import pallas as pl
from jax.experimental.pallas import tpu as pltpu
from jax.sharding import PartitionSpec as P

HD = 64
CAP_LEN = 64
EPSILON = 1e-06
NEGATIVE = -1000000000.0

MESH_ID = pl.DeviceIdType.MESH
ANY = pl.BlockSpec(memory_space=pl.ANY)
VMEM = pl.BlockSpec(memory_space=pltpu.VMEM)
SMEM = pl.BlockSpec(memory_space=pltpu.SMEM)


class Net:
    def __init__(self, lines):
        self.lines = lines
        self.tower = lax.axis_index("tower")
        self.dp = lax.axis_index("dp")
        self.core = self.dp % 2
        self.y = (self.dp // 2) % 2
        self.z = self.dp // 4
        self.chip = self.dp // 2
        self.text = self.tower == 1
        self.image = self.tower == 0
        self.low = self.z > 0
        self.high = self.z < lines - 1
        self.sends = []
        self.slow = []

    def target(self, way):
        if way == "core":
            return (self.tower, self.dp + 1 - 2 * self.core)
        if way == "y":
            return (self.tower, self.dp + 2 - 4 * self.y)
        if way == "x":
            return (1 - self.tower, self.dp)
        if way == "up":
            return (self.tower, jnp.minimum(self.dp + 4, 4 * self.lines - 1))
        return (self.tower, jnp.maximum(self.dp - 4, 0))

    def beyond(self, k):
        return (self.tower, 4 * lax.rem(self.z + k, self.lines) + self.dp % 4)

    def greet(self):
        sem = pltpu.get_barrier_semaphore()
        partners = [self.target(way) for way in ("core", "y", "x")]
        partners += [self.beyond(k) for k in range(1, self.lines)]
        for partner in partners:
            pl.semaphore_signal(sem, inc=1, device_id=partner, device_id_type=MESH_ID)
        self.partners = len(partners)

    def meet(self):
        pl.semaphore_wait(pltpu.get_barrier_semaphore(), self.partners)

    def copy(self, way, src, dst, send_sem, recv_sem):
        return pltpu.make_async_remote_copy(
            src_ref=src,
            dst_ref=dst,
            send_sem=send_sem,
            recv_sem=recv_sem,
            device_id=self.target(way),
            device_id_type=MESH_ID,
        )

    def send(self, way, src, dst, send_sem, recv_sem, there=None, slow=False):
        copy = self.copy(way, src, dst, send_sem, recv_sem)
        when(there, copy.start)
        (self.slow if slow else self.sends).append((copy, there))

    def arrive(self, src, send_sem, recv_sem, there=None):
        copy = self.copy("core", src, src, send_sem, recv_sem)
        when(there, copy.wait_recv)

    def drain(self, kept=0):
        while len(self.sends) > kept:
            copy, there = self.sends.pop(0)
            when(there, copy.wait_send)

    def finish(self):
        self.drain()
        self.sends, self.slow = self.slow, []
        self.drain()


def when(there, act):
    if there is None:
        act()
    else:
        pl.when(there)(act)


def both(*conditions):
    kept = [c for c in conditions if c is not None]
    if not kept:
        return None
    result = kept[0]
    for c in kept[1:]:
        result = jnp.logical_and(result, c)
    return result


class Gather:
    def __init__(self, net, own, place, crossing, send_sem, recv_sem, local_sem, everywhere=False):
        self.net, self.own, self.place, self.crossing = net, own, place, crossing
        self.send_sem, self.recv_sem, self.local_sem = send_sem, recv_sem, local_sem
        lines = net.lines
        self.at_z, self.at_y, self.at_x, self.at_core = 0, 2 * lines, 3 * lines, 5 * lines
        self.to_x = net.image if crossing else None
        self.to_core = net.text if crossing and not everywhere else None

    @staticmethod
    def sems(lines):
        return 11 * lines

    def piece(self, chip, tower=None, core=None):
        net = self.net
        return self.place(
            net.tower if tower is None else tower, chip, net.core if core is None else core
        )

    def pass_on(self, chip, src, there=None, tower=None):
        net = self.net
        dst = self.piece(chip, tower)
        plane = net.tower if tower is None else tower
        if self.crossing and tower is None:
            s = self.at_x + chip
            net.send("x", src, dst, self.send_sem.at[s], self.recv_sem.at[s], both(there, net.image))
        s = self.at_core + plane * 2 * net.lines + chip
        net.send("core", src, dst, self.send_sem.at[s], self.recv_sem.at[s], both(there, self.to_core))

    def start(self):
        net = self.net
        dst = self.piece(net.chip)
        self.local = None
        if self.own is None:
            self.own = dst
        else:
            self.local = pltpu.make_async_copy(self.own, dst, self.local_sem)
            self.local.start()
        for way, there, slot in (("up", net.high, 1), ("down", net.low, net.lines + 1)):
            s = self.at_z + slot
            net.send(way, self.own, dst, self.send_sem.at[s], self.recv_sem.at[s], there)
        s = self.at_y + net.z
        net.send("y", self.own, dst, self.send_sem.at[s], self.recv_sem.at[s])
        self.pass_on(net.chip, self.own)

    def hop(self, k):
        net = self.net
        for way, there, further, sign, base in (
            ("up", net.z >= k, net.high, -1, 0),
            ("down", net.z + k < net.lines, net.low, 1, net.lines),
        ):
            z = jnp.clip(net.z + sign * k, 0, net.lines - 1)
            chip = 2 * z + net.y
            src = self.piece(chip)
            s = self.at_z + base + k
            net.arrive(src, self.send_sem.at[s], self.recv_sem.at[s], there)
            if k + 1 < net.lines:
                s = s + 1
                net.send(way, src, src, self.send_sem.at[s], self.recv_sem.at[s], both(there, further))
            s = self.at_y + z
            net.send("y", src, src, self.send_sem.at[s], self.recv_sem.at[s], there)
            self.pass_on(chip, src, there)

    def beside(self, k):
        net = self.net
        ways = ((None, 0),) if k == 0 else ((net.z >= k, -k), (net.z + k < net.lines, k))
        for there, offset in ways:
            z = jnp.clip(net.z + offset, 0, net.lines - 1)
            chip = 2 * z + 1 - net.y
            src = self.piece(chip)
            s = self.at_y + z
            net.arrive(src, self.send_sem.at[s], self.recv_sem.at[s], there)
            self.pass_on(chip, src, there)

    def from_image(self, k):
        if not self.crossing:
            return
        net = self.net
        ways = ((None, 0),) if k == 0 else ((net.z >= k, -k), (net.z + k < net.lines, k))
        for there, offset in ways:
            z = jnp.clip(net.z + offset, 0, net.lines - 1)
            for y in (net.y, 1 - net.y):
                chip = 2 * z + y
                src = self.piece(chip, 0)
                s = self.at_x + chip
                net.arrive(src, self.send_sem.at[s], self.recv_sem.at[s], both(there, net.text))
                self.pass_on(chip, src, both(there, net.text), 0)

    def done(self):
        net = self.net
        if self.local is not None:
            self.local.wait()

        def all_of(tower, base):
            def one(chip, carry):
                s = self.at_core + base + chip
                src = self.piece(chip, tower, 1 - net.core)
                net.arrive(src, self.send_sem.at[s], self.recv_sem.at[s])
                return carry

            def run():
                lax.fori_loop(0, 2 * net.lines, one, 0)

            return run

        when(self.to_core, all_of(net.tower, net.tower * 2 * net.lines))
        if self.crossing:
            when(net.text, all_of(0, 0))


class GatherBeside(Gather):
    def start(self):
        net = self.net
        dst = self.piece(net.chip)
        self.local = None
        if self.own is None:
            self.own = dst
        else:
            self.local = pltpu.make_async_copy(self.own, dst, self.local_sem)
            self.local.start()
        s = self.at_y
        net.send("y", self.own, dst, self.send_sem.at[s], self.recv_sem.at[s])
        self.set_off(self.own, net.chip, 0)
        self.pass_on(net.chip, self.own)

    def set_off(self, src, chip, second):
        net = self.net
        dst = self.piece(chip)
        for way, there, slot in (("up", net.high, 1), ("down", net.low, net.lines + 1)):
            s = self.z_sem(second) + slot
            net.send(way, src, dst, self.send_sem.at[s], self.recv_sem.at[s], there)

    def z_sem(self, second):
        return 9 * self.net.lines if second else self.at_z

    def hop(self, k):
        net = self.net
        for way, there, further, sign, base in (
            ("up", net.z >= k, net.high, -1, 0),
            ("down", net.z + k < net.lines, net.low, 1, net.lines),
        ):
            z = jnp.clip(net.z + sign * k, 0, net.lines - 1)
            for second, y in ((0, net.y), (1, 1 - net.y)):
                chip = 2 * z + y
                src = self.piece(chip)
                s = self.z_sem(second) + base + k
                net.arrive(src, self.send_sem.at[s], self.recv_sem.at[s], there)
                if k + 1 < net.lines:
                    s = s + 1
                    net.send(
                        way, src, src, self.send_sem.at[s], self.recv_sem.at[s], both(there, further)
                    )
                self.pass_on(chip, src, there)

    def beside(self, k):
        if k > 0:
            return
        net = self.net
        chip = 2 * net.z + 1 - net.y
        src = self.piece(chip)
        s = self.at_y
        net.arrive(src, self.send_sem.at[s], self.recv_sem.at[s])
        self.set_off(src, chip, 1)
        self.pass_on(chip, src)


class Small:
    def __init__(self, net, mine, arrived, sums, wide, send_sem, recv_sem):
        self.net, self.mine, self.arrived, self.sums, self.wide = net, mine, arrived, sums, wide
        self.send_sem, self.recv_sem = send_sem, recv_sem

    def exchange(self, step):
        src = self.mine if step == 0 else self.sums.at[step - 1]
        self.net.send(
            ("core", "y", "x")[step],
            src,
            self.arrived.at[step],
            self.send_sem.at[step],
            self.recv_sem.at[step],
        )

    def collect(self, step):
        self.net.arrive(self.arrived.at[step], self.send_sem.at[step], self.recv_sem.at[step])
        src = self.mine if step == 0 else self.sums.at[step - 1]
        self.sums[step] = src[...] + self.arrived[step]

    def spread(self):
        net = self.net
        for k in range(1, net.lines):
            s = 2 + k
            copy = pltpu.make_async_remote_copy(
                src_ref=self.sums.at[2],
                dst_ref=self.wide.at[k - 1],
                send_sem=self.send_sem.at[s],
                recv_sem=self.recv_sem.at[s],
                device_id=net.beyond(k),
                device_id_type=MESH_ID,
            )
            copy.start()
            net.sends.append((copy, None))

    def total(self, out):
        total = self.sums[2]
        for k in range(1, self.net.lines):
            s = 2 + k
            self.net.arrive(self.wide.at[k - 1], self.send_sem.at[s], self.recv_sem.at[s])
            total = total + self.wide[k - 1]
        out[...] = total


def product(a, b, axis_a=1, axis_b=0):
    return lax.dot_general(
        a, b, (((axis_a,), (axis_b,)), ((), ())), preferred_element_type=jnp.float32
    )


def low(value):
    return value.astype(jnp.bfloat16)


def blocks(count, size, body):
    def one(i, carry):
        body(pl.ds(pl.multiple_of(i * size, size), size))
        return carry

    lax.fori_loop(0, count // size, one, 0)


def row_step(rows):
    return next(s for s in (96, 64, 48, 32, 16) if rows % s == 0)


def centred(value):
    center = value - jnp.mean(value, axis=-1, keepdims=True)
    spread = jnp.mean(center * center, axis=-1, keepdims=True)
    return center * lax.rsqrt(spread + EPSILON), lax.rsqrt(spread + EPSILON)


def norm_rows(src, gain, out, also=None):
    def body(rows):
        value = src[rows, :].astype(jnp.float32)
        if also is not None:
            also(rows, value)
        out[rows, :] = low(centred(value)[0] * gain)

    blocks(src.shape[0], row_step(src.shape[0]), body)


def norm_back_rows(src, gain, grad, done, gain_grad, fresh=True):
    if fresh:
        gain_grad[...] = jnp.zeros_like(gain_grad)

    def body(rows):
        n, scale = centred(src[rows, :].astype(jnp.float32))
        out = grad[rows, :]
        dn = out * gain
        gain_grad[...] += jnp.sum(out * n, axis=0, keepdims=True)
        back = dn - jnp.mean(dn, axis=-1, keepdims=True)
        done(rows, (back - n * jnp.mean(dn * n, axis=-1, keepdims=True)) * scale)

    blocks(src.shape[0], row_step(src.shape[0]), body)


class Sums:
    def __init__(self, ref, weight):
        self.ref, self.weight = ref, weight
        ref[...] = jnp.zeros_like(ref)

    def add(self, slot, rows, value):
        kept = jnp.sum(value * value, axis=-1, keepdims=True) * self.weight[rows, :]
        total = jnp.sum(kept, axis=0, keepdims=True)
        at = pl.ds(slot, 1)
        self.ref[at, :] = self.ref[at, :] + jnp.broadcast_to(total, (1, self.ref.shape[1]))

    def line(self):
        shape = self.ref.shape
        row = lax.broadcasted_iota(jnp.int32, shape, 0)
        lane = lax.broadcasted_iota(jnp.int32, shape, 1)
        return jnp.sum(jnp.where(row == lane, self.ref[...], 0.0), axis=0, keepdims=True)


def pair_count(width):
    pairs = width // (2 * HD)
    return next(n for n in (3, 2, 1) if pairs % n == 0)


def attention(query, key, value, allowed, weight, mixed):
    count, width = mixed.shape
    group = pair_count(width)
    left = lax.broadcasted_iota(jnp.int32, (count, 2 * HD), 1) < HD

    def one(step, carry):
        kept, scores = [], []
        for i in range(group):
            pair = step * group + i
            q, k, v = query(pair), key(pair), value(pair)
            zero = jnp.zeros_like(q)
            kept.append((pair, v))
            for part in (jnp.where(left, q, zero), jnp.where(left, zero, q)):
                scores.append(product(part, k, 1, 1) * HD ** (-0.5))
        weights = []
        for s in scores:
            s = jnp.where(allowed[...] > 0, s, NEGATIVE)
            e = jnp.exp(s - jnp.max(s, axis=-1, keepdims=True))
            weights.append(low(e / jnp.sum(e, axis=-1, keepdims=True)))
        for i, (pair, v) in enumerate(kept):
            first, second = weights[2 * i : 2 * i + 2]
            weight[2 * pair] = first
            weight[2 * pair + 1] = second
            both_heads = jnp.where(left, product(first, v), product(second, v))
            mixed[:, pl.ds(pl.multiple_of(pair * 2 * HD, 2 * HD), 2 * HD)] = low(both_heads)
        return carry

    lax.fori_loop(0, width // (2 * HD) // group, one, 0, unroll=True)


def attention_back(query, key, value, grad_mixed, weight, width, done):
    count = weight.shape[1]
    group = pair_count(width)
    left = lax.broadcasted_iota(jnp.int32, (count, 2 * HD), 1) < HD

    def one(step, carry):
        kept, raw = [], []
        for i in range(group):
            pair = step * group + i
            q, k, v, d = query(pair), key(pair), value(pair), grad_mixed(pair)
            zero = jnp.zeros_like(q)
            kept.append((pair, q, k))
            for h, part in enumerate((jnp.where(left, d, zero), jnp.where(left, zero, d))):
                raw.append((part, product(part, v, 1, 1), weight[2 * pair + h]))
        grads = []
        for part, dp, p in raw:
            p32 = p.astype(jnp.float32)
            grads.append(low(p32 * (dp - jnp.sum(dp * p32, axis=-1, keepdims=True))))
        for i, (pair, q, k) in enumerate(kept):
            (d0, _, p0), (d1, _, p1) = raw[2 * i : 2 * i + 2]
            s0, s1 = grads[2 * i : 2 * i + 2]
            zero = jnp.zeros_like(q)
            dv = product(p0, d0, 0, 0) + product(p1, d1, 0, 0)
            dk = product(s0, jnp.where(left, q, zero), 0, 0)
            dk = dk + product(s1, jnp.where(left, zero, q), 0, 0)
            dq = jnp.where(left, product(s0, k), product(s1, k))
            done(pair, low(dq * HD ** (-0.5)), low(dk * HD ** (-0.5)), low(dv))
        return carry

    lax.fori_loop(0, width // (2 * HD) // group, one, 0, unroll=True)


def pairs_of(ref, base=0):
    return lambda pair: ref[:, pl.ds(pl.multiple_of(base + pair * 2 * HD, 2 * HD), 2 * HD)]


def gelu_both(value):
    scale = 0.7978845608028654
    cube = 0.044715
    square = value * value
    bend = jnp.tanh(scale * value * (1.0 + cube * square))
    half = 0.5 * (1.0 + bend)
    slope = half + 0.5 * value * (1.0 - bend * bend) * scale * (1.0 + 3.0 * cube * square)
    return value * half, slope


def activate(wide, active, slope, columns):
    def body(rows):
        a, s = gelu_both(wide[rows, :])
        active[rows, columns] = low(a)
        slope[rows, columns] = s.astype(slope.dtype)

    blocks(wide.shape[0], 16, body)


GATHER = ("qk", "vo", "ca", "u0", "u1", "cu", "d0", "d1", "d2", "cd")
GATHER_NAMES = ("qk", "vo", "u0", "u1", "d0", "d1", "d2", "ca", "cu", "cd")
LEAD = 2
GATHER_BESIDE = ("d0", "d1")
GATHER_FOUR = (
    "start d0", "start cd", "start u0", "start d2", "start vo", "beside u0 0", "hop cd 1",
    "do block", "beside cd 0", "start qk", "start ca", "hop u0 1", "hop qk 1", "beside cd 1",
    "hop vo 1", "beside d0 0", "hop ca 1", "hop cd 2", "hop vo 2", "hop qk 2", "beside vo 0",
    "from_image cd 0", "start d1", "beside vo 1", "beside qk 0", "do gains0", "hop cd 3",
    "hop qk 3", "hop vo 3", "from_image ca 0", "hop u0 2", "beside ca 0", "hop ca 2", "start cu",
    "beside ca 1", "beside d2 0", "beside u0 1", "beside qk 1", "start u1", "beside cd 2",
    "hop ca 3", "hop d0 1", "from_image ca 1", "do gains1", "hop cu 1", "hop u1 1", "beside vo 2",
    "do gains2", "hop cu 2", "beside vo 3", "beside ca 2", "beside d1 0", "hop u0 3", "hop u1 2",
    "beside qk 2", "hop d2 1", "hop d0 2", "beside cu 0", "beside ca 3", "hop u1 3", "hop cu 3",
    "from_image cd 1", "beside u0 2", "beside qk 3", "beside cu 1", "from_image cd 2",
    "from_image ca 2", "beside cd 3", "done qk", "do norm", "do qk", "hop d1 1", "done vo", "do v",
    "do attend", "do out", "hop d2 2", "from_image ca 3", "from_image cu 0", "from_image cd 3",
    "beside cu 2", "beside u0 3", "hop d1 2", "beside u1 0", "from_image cu 1", "hop d0 3",
    "hop d2 3", "beside u1 1", "beside u1 2", "beside u1 3", "done u0", "do up0", "beside cu 3",
    "done u1", "do up1", "do keep", "hop d1 3", "from_image cu 2", "beside d2 1", "done cd",
    "done ca", "from_image cu 3", "done d0", "do down0", "beside d2 2", "beside d2 3", "done d1",
    "do down1", "done cu", "done d2", "do down2", "do end", "do query", "do rows", "do cross0",
    "do cross1", "do cross2", "do cross3", "do cross4",
)
AFTER = {
    "qk": ("norm", "qk"),
    "vo": ("v", "attend", "out"),
    "u0": ("up0",),
    "u1": ("up1", "keep"),
    "d0": ("down0",),
    "d1": ("down1",),
    "d2": ("down2", "end"),
}


def parsed(lines):
    events = []
    for line in lines:
        kind, name, *k = line.split()
        events.append((kind, name, int(k[0]) if k else 0))
    return events


def gather_order(lines):
    if lines == 4 and GATHER_FOUR:
        return parsed(GATHER_FOUR)
    slots = {}

    def put(slot, kind, name, k=0):
        slots.setdefault(max(slot, 0), []).append((kind, name, k))

    for index, name in enumerate(GATHER):
        late = 1 if name in GATHER_BESIDE else 0
        if name in ("ca", "cu"):
            put(index - LEAD + 1, "do", "block")
        put(index - LEAD + 1, "start", name)
        if late:
            put(index + 1, "beside", name)
        for k in range(1, lines):
            put(index + k + late, "hop", name, k)
        for k in range(late, lines):
            put(index + k + 1, "beside", name, k)
        for k in range(lines):
            put(index + k + 2 + late, "from_image", name, k)
        put(index + lines + 1 + late, "done", name)
        for step in AFTER.get(name, ()):
            put(index + lines + 1 + late, "do", step)
    for index in range(3):
        put(index + 1, "do", "gains%d" % index)
    rank = {"start": 0, "beside": 2, "hop": 1, "from_image": 3, "done": 4, "do": 5}
    events = []
    for slot in sorted(slots):

        def place(event):
            kind, name, k = event
            if kind == "beside" and name in GATHER_BESIDE:
                return 0.5
            if kind == "do" and name == "block":
                return -1
            if kind == "do" and name.startswith("gains"):
                return 0.2
            return rank[kind]

        events += [e for e in sorted(slots[slot], key=place) if e not in events]
    last = ["query", "rows"] + ["cross%d" % i for i in range(5)]
    return events + [("do", name, 0) for name in last]


def place_gains(net, own, cross, out):
    width = out.shape[1]

    def placed(gain, index):
        count = gain.shape[1]
        lane = lax.broadcasted_iota(jnp.int32, (count, width), 1)
        row = lax.broadcasted_iota(jnp.int32, (count, width), 0)
        pick = jnp.where(lane == index * count + row, 1.0, 0.0)
        many = jnp.broadcast_to(gain[...].astype(jnp.float32), (8, count))
        return product(low(many), low(pick))[0:1]

    out[...] = jnp.zeros_like(out)
    for i, gain in enumerate(own):
        row = placed(gain, net.dp)
        out[i : i + 1, :] = jnp.where(net.image, row, 0.0)
        out[i + 2 : i + 3, :] = jnp.where(net.text, row, 0.0)
    for i, gain in enumerate(cross):
        out[4 + i : 5 + i, :] = placed(gain, net.tower * 4 * net.lines + net.dp)


def fill_masks(net, counts, lengths, allowed, cross_allowed, row_weight):
    shape = allowed.shape

    def place(index):
        image_of, bound = jnp.zeros_like(index), jnp.int32(0)
        for i in range(counts.shape[1]):
            bound = bound + counts[0, i]
            image_of = image_of + jnp.where(index >= bound, 1, 0)
        caption_of = index // CAP_LEN
        within = index - caption_of * CAP_LEN
        length = jnp.zeros_like(index)
        for i in range(lengths.shape[0]):
            length = jnp.where(caption_of == i, lengths[i], length)
        return image_of, caption_of, within, within < length

    row = place(lax.broadcasted_iota(jnp.int32, shape, 0))
    key = place(lax.broadcasted_iota(jnp.int32, shape, 1))
    image_mask = row[0] == key[0]
    text_mask = (row[1] == key[1]) & (key[2] <= row[2]) & key[3]
    here = jnp.where(net.text, text_mask.astype(jnp.float32), image_mask.astype(jnp.float32))
    allowed[...] = here
    cross_allowed[...] = (row[1] == key[0]).astype(jnp.float32)
    valid = place(lax.broadcasted_iota(jnp.int32, row_weight.shape, 0))[3]
    row_weight[...] = jnp.where(net.text, valid.astype(jnp.float32), 1.0)


def forward_kernel(
    lines, cuts, parts,
    counts, lengths, g_attn, g_mlp, g_query, g_image, g_cross,
    i_tok, i_cot, i_cq, i_ckv, i_co, i_cu, own_qkv, own_out, own_up, own_d, own_cd,
    full_a, full_d, sum_ca, sum_cd, o_h1, o_qkv, o_mixed, o_weight, o_middle, o_h2, o_active, o_slope,
    gains, layer_out, top, vec,
    tok, cot, cq, ckv, co, cu, w_a, w_d, w_ca, w_cd, h1, qkv, mixed, weight, middle, h2, active, slope, out_y, wide, branch,
    passed, returned, image_out, n_x, g_mixed, n_q, n_i, query, keyval, c_mixed, c_weight, c_middle, h3, grad_wide, g_small,
    allowed, cross_allowed, row_weight, gvec, pack, swap, block, rcv_d, sib_q, sib_i, sib_m, sib_h, sib_du, sib_dx, sib_dq, sib_dkv, arrived, totals, spread, sums_ref, gain_rows,
    send_sem, recv_sem, local_sem, swap_sem, s_send, s_recv, pass_sem, out_sem, d_send, d_recv, d_local, own_sem, in_sem, e_send, e_recv,
):
    net = Net(lines)
    net.greet()
    text, image = net.text, net.image
    rows, depth = own_qkv.shape[0], own_d.shape[0]
    all_a = sum(parts)
    few, part = pack.shape[1], own_cd.shape[0]
    width = tok.shape[1]
    half = pack.shape[2]
    a_qkv, a_out = parts[0], parts[0] + parts[1]
    q_end, kv_end, o_end = cuts[0], cuts[0] + cuts[1], cuts[0] + cuts[1] + cuts[2]
    tile = width

    placing = []
    for index, (src, at) in enumerate(((own_qkv, 0), (own_out, a_qkv), (own_up, a_out))):
        here = pl.ds(pl.multiple_of(net.dp * rows, rows), rows)
        copy = pltpu.make_async_copy(
            src, w_a.at[here, at : at + src.shape[1]], own_sem.at[index]
        )
        copy.start()
        placing.append(copy)
    loads = []
    for src, held in ((i_cq, cq), (i_ckv, ckv), (i_co, co), (i_cu, cu), (i_tok, tok), (i_cot, cot)):
        copy = pltpu.make_async_copy(src, held, in_sem.at[len(loads)])
        copy.start()
        loads.append(copy)
    place_gains(net, (g_attn, g_mlp), (g_query, g_image, g_cross), gvec)
    for copy in loads:
        copy.wait()
    at = 0
    for src, n in zip((cq, ckv, co, cu), cuts):
        whole = src[...].astype(jnp.float32)
        for h in range(2):
            pack[h, :, at : at + n] = whole[:, h * n : (h + 1) * n]
        at += n
    net.meet()
    for copy in placing:
        copy.wait()

    def columns(first, last):
        return lambda tower, chip, core: w_a.at[
            pl.ds(pl.multiple_of((2 * chip + core) * rows, rows), rows), first:last
        ]

    def crossed(first, last):
        return lambda tower, chip, core: w_ca.at[
            core,
            pl.ds(pl.multiple_of((tower * 2 * lines + chip) * 2 * few, 2 * few), 2 * few),
            first:last,
        ]

    def plan(index, own, place, crossing):
        beside = GATHER_NAMES[index] in GATHER_BESIDE
        kind = GatherBeside if beside else Gather
        return kind(
            net, own, place, crossing, send_sem.at[index], recv_sem.at[index], local_sem.at[index]
        )

    def self_part(index, first, last):
        return plan(index, None, columns(first, last), False)

    def down_part(index, first, last):
        return plan(
            index,
            own_d.at[:, first:last],
            lambda tower, chip, core: w_d.at[
                pl.ds(pl.multiple_of((2 * chip + core) * depth, depth), depth), first:last
            ],
            False,
        )

    def cross_part(index, first, last):
        return plan(index, block.at[:, first:last], crossed(first, last), True)

    mid, third = a_qkv - width, width // 3
    jobs = {
        "qk": self_part(0, 0, mid),
        "vo": self_part(1, mid, a_out),
        "u0": self_part(2, a_out, a_out + 2 * width),
        "u1": self_part(3, a_out + 2 * width, all_a),
        "d0": down_part(4, 0, third),
        "d1": down_part(5, third, 2 * third),
        "d2": down_part(6, 2 * third, width),
        "ca": cross_part(7, 0, o_end),
        "cu": cross_part(8, o_end, half),
        "cd": plan(
            9,
            own_cd,
            lambda tower, chip, core: w_cd.at[
                pl.ds(pl.multiple_of((tower * 4 * lines + 2 * chip + core) * part, part), part), :
            ],
            True,
        ),
    }
    kept = []

    def keep(src, dst):
        copy = pltpu.make_async_copy(src, dst, out_sem.at[len(kept)])
        copy.start()
        kept.append(copy)

    theirs = 1 - net.core

    def share_rows(index, src, dst):
        net.send("core", src, dst, e_send.at[index], e_recv.at[index], text)

    def shared(index, dst):
        net.arrive(dst, e_send.at[index], e_recv.at[index], text)

    def half_of(core, n):
        return pl.ds(pl.multiple_of(core * n, n), n)

    swapped = net.copy("core", pack.at[1 - net.core], swap, swap_sem.at[0], swap_sem.at[1])
    swapped.start()
    small = Small(net, gvec, arrived, totals, spread, s_send, s_recv)
    sums = Sums(sums_ref, row_weight)
    base = 4 * net.tower
    gain_rows[...] = jnp.zeros_like(gain_rows)
    first = net.core == 0

    def gain(at):
        return jnp.where(text, gains[at + 2 : at + 3, :], gains[at : at + 1, :])

    def build_block():
        swapped.wait()
        mine = pack[net.core]
        theirs = swap[...]
        block[0:few] = low(jnp.where(first, mine, theirs))
        block[few:] = low(jnp.where(first, theirs, mine))

    def gains_over(index):
        def run():
            small.collect(index)
            if index < 2:
                small.exchange(index + 1)
            else:
                small.spread()

        return run

    def first_norm():
        small.total(gains)
        fill_masks(net, counts, lengths, allowed, cross_allowed, row_weight)
        norm_rows(tok, gain(0), h1, lambda r, v: sums.add(base, r, v))
        keep(h1, o_h1)

    def project(first_column, last_column):
        def run():
            def qkv_tile(i, carry):
                cols = pl.ds(pl.multiple_of(first_column + i * tile, tile), tile)
                qkv[:, cols] = low(product(h1[...], w_a[:, cols]))
                return carry

            lax.fori_loop(0, (last_column - first_column) // tile, qkv_tile, 0)

        return run

    def attend():
        keep(qkv, o_qkv)
        attention(
            pairs_of(qkv), pairs_of(qkv, width), pairs_of(qkv, 2 * width), allowed, weight, mixed
        )
        keep(weight, o_weight)
        keep(mixed, o_mixed)

    def attn_out():
        branch[...] = product(mixed[...], w_a[:, a_qkv:a_out])

        def add_branch(r):
            value = branch[r, :]
            sums.add(base + 1, r, value)
            middle[r, :] = tok[r, :].astype(jnp.float32) + value

        blocks(tok.shape[0], row_step(tok.shape[0]), add_branch)
        keep(middle, o_middle)
        norm_rows(middle, gain(1), h2)
        keep(h2, o_h2)

    def go_up(first_tile, last_tile):
        def run():
            def up_tile(i, carry):
                at = pl.multiple_of((first_tile + i) * tile, tile)
                wide[...] = product(h2[...], w_a[:, pl.ds(a_out + at, tile)])
                activate(wide, active, slope, pl.ds(at, tile))
                return carry

            lax.fori_loop(0, last_tile - first_tile, up_tile, 0)

        return run

    def keep_up():
        keep(active, o_active)
        keep(slope, o_slope)
        keep(w_a, full_a)

    def go_down(index):
        first_column, last_column = index * third, (index + 1) * third

        def run():
            branch[:, first_column:last_column] = product(
                active[...], w_d[:, first_column:last_column]
            )

            def add_mlp(r):
                value = branch[r, first_column:last_column]
                sums.add(base + 2, r, value)
                y = middle[r, first_column:last_column] + value
                out_y[r, first_column:last_column] = y
                image_out[r, first_column:last_column] = low(y)

                @pl.when(image)
                def _():
                    sums.add(3, r, y)

            blocks(tok.shape[0], row_step(tok.shape[0]), add_mlp)
            net.send(
                "x",
                image_out.at[:, first_column:last_column],
                passed.at[:, first_column:last_column],
                pass_sem.at[0, index],
                pass_sem.at[1, index],
                image,
            )

        return run

    def self_end():
        keep(w_d, full_d)

    def rows_arrive():
        for index in range(3):
            part_of = passed.at[:, index * third : (index + 1) * third]
            net.arrive(part_of, pass_sem.at[0, index], pass_sem.at[1, index], text)

    def cross_queries():
        @pl.when(text)
        def _():
            norm_rows(out_y, gains[4:5, :], n_q)
            for h in range(2):
                at = h * cuts[0]
                query[:, at : at + cuts[0]] = low(product(n_q[...], w_ca[h, :, 0:q_end]))

        share_rows(0, n_q, sib_q)

    def cross_keys():
        @pl.when(text)
        def _():
            norm_rows(passed, gains[5:6, :], n_i)
            for h in range(2):
                at = h * width
                keyval[:, at : at + width] = low(product(n_i[...], w_ca[h, :, q_end:kv_end]))

        share_rows(1, n_i, sib_i)

    def cross_attend():
        @pl.when(text)
        def _():
            attention(
                pairs_of(query),
                pairs_of(keyval),
                pairs_of(keyval, width),
                cross_allowed,
                c_weight,
                c_mixed,
            )

        share_rows(2, c_mixed, sib_m)

    def cross_out():
        @pl.when(text)
        def _():
            for h in range(2):
                at = h * cuts[2]
                branch[:, at : at + cuts[2]] = product(c_mixed[...], w_ca[h, :, kv_end:o_end])

            def add_cross(r):
                value = branch[r, :]
                sums.add(7, r, value)
                c_middle[r, :] = out_y[r, :] + value

            blocks(tok.shape[0], row_step(tok.shape[0]), add_cross)
            norm_rows(c_middle, gains[6:7, :], h3)

        share_rows(3, h3, sib_h)

    def cross_up():
        for copy in kept:
            copy.wait()

        @pl.when(text)
        def _():
            for h in range(2):

                def one(i, carry):
                    at = pl.multiple_of(i * tile, tile)
                    wide[...] = product(h3[...], w_ca[h, :, pl.ds(o_end + at, tile)])
                    activate(wide, active, slope, pl.ds(h * cuts[3] + at, tile))
                    return carry

                lax.fori_loop(0, cuts[3] // tile, one, 0, unroll=True)

    def cross_down():
        @pl.when(text)
        def _():
            branch[...] = product(active[...], w_cd[...])

            def add_final(r):
                value = branch[r, :]
                sums.add(8, r, value)
                z = c_middle[r, :] + value
                sums.add(9, r, z)
                layer_out[r, :] = low(z)

            blocks(tok.shape[0], row_step(tok.shape[0]), add_final)

    tiles = active.shape[1] // tile
    steps = {
        "block": build_block,
        "gains0": gains_over(0),
        "gains1": gains_over(1),
        "gains2": gains_over(2),
        "norm": first_norm,
        "qk": project(0, mid),
        "v": project(mid, a_qkv),
        "attend": attend,
        "out": attn_out,
        "up0": go_up(0, tiles // 2),
        "up1": go_up(tiles // 2, tiles),
        "keep": keep_up,
        "down0": go_down(0),
        "down1": go_down(1),
        "down2": go_down(2),
        "end": self_end,
        "query": cross_queries,
        "rows": rows_arrive,
        "cross0": cross_keys,
        "cross1": cross_attend,
        "cross2": cross_out,
        "cross3": cross_up,
        "cross4": cross_down,
    }
    small.exchange(0)
    for kind, name, k in gather_order(lines):
        if kind == "do":
            steps[name]()
        elif kind == "start":
            jobs[name].start()
        elif kind == "done":
            jobs[name].done()
        else:
            getattr(jobs[name], kind)(k)

    net.finish()
    def hand(index, src, rcv, there=text):
        net.send("core", src, rcv, d_send.at[index], d_recv.at[index], there)

    def merge(index, own, rcv, out):
        net.arrive(rcv, d_send.at[index], d_recv.at[index], text)

        @pl.when(text)
        def _():
            def add(r):
                rcv[r, :] = low(own[r, :].astype(jnp.float32) + rcv[r, :].astype(jnp.float32))

            blocks(rcv.shape[0], 16, add)
            pltpu.make_async_copy(rcv, out, d_local.at[index]).start()

    @pl.when(text)
    def _():
        def down_tile(i, carry):
            cols = pl.ds(pl.multiple_of(i * tile, tile), tile)
            found = low(product(active[:, cols], cot[...], 0, 0))
            for k in range(tile // part):
                at = (k % 2) * (w_d.shape[0] // 2) + (k // 2) * part + i * (tile // 2)
                w_d[pl.ds(pl.multiple_of(at, part), part), :] = found[k * part : (k + 1) * part]
            grad = product(cot[...], w_cd[cols, :], 1, 1)
            grad_wide[:, cols] = low(grad * slope[:, cols])
            return carry

        lax.fori_loop(0, active.shape[1] // tile, down_tile, 0, unroll=True)

    share = w_d.shape[0] // 2
    hand(0, w_d.at[pl.ds(pl.multiple_of((1 - net.core) * share, share), share), :], rcv_d)
    share_rows(4, grad_wide.at[:, half_of(theirs, cuts[3])], sib_du)

    @pl.when(text)
    def _():
        branch[...] = product(grad_wide[:, 0 : cuts[3]], w_ca[0, :, o_end:half], 1, 1) + product(
            grad_wide[:, cuts[3] :], w_ca[1, :, o_end:half], 1, 1
        )

        def mid_done(r, back):
            total = cot[r, :].astype(jnp.float32) + back
            c_middle[r, :] = total
            n_x[r, :] = low(total)

        norm_back_rows(c_middle, gains[6:7, :], branch, mid_done, g_small)
        gain_rows[6:7, :] = g_small[...]

    share_rows(5, n_x.at[:, half_of(theirs, cuts[2])], sib_dx)

    @pl.when(text)
    def _():
        branch[...] = product(n_x[:, 0 : cuts[2]], w_ca[0, :, kv_end:o_end], 1, 1) + product(
            n_x[:, cuts[2] :], w_ca[1, :, kv_end:o_end], 1, 1
        )
        g_mixed[...] = low(branch[...])

        def att_done(pair, dq, dk, dv):
            at = pl.multiple_of(pair * 2 * HD, 2 * HD)
            query[:, pl.ds(at, 2 * HD)] = dq
            keyval[:, pl.ds(at, 2 * HD)] = dk
            keyval[:, pl.ds(width + at, 2 * HD)] = dv

        attention_back(
            pairs_of(query),
            pairs_of(keyval),
            pairs_of(keyval, width),
            pairs_of(g_mixed),
            c_weight,
            width,
            att_done,
        )

    share_rows(6, query.at[:, half_of(theirs, cuts[0])], sib_dq)
    share_rows(7, keyval.at[:, half_of(theirs, cuts[1])], sib_dkv)
    rows_half = tok.shape[0] // 2
    for index in range(2):
        at = index * rows_half
        here = slice(at, at + rows_half)

        @pl.when(text)
        def _():
            branch[here, :] = product(
                keyval[here, 0:width], w_ca[0, :, q_end:kv_end], 1, 1
            ) + product(keyval[here, width:], w_ca[1, :, q_end:kv_end], 1, 1)

            def image_done(r, back):
                image_out[pl.ds(at + r.start, r.size), :] = low(back)

            norm_back_rows(
                passed.at[here], gains[5:6, :], branch.at[here], image_done, g_small, index == 0
            )
            if index == 1:
                gain_rows[5:6, :] = g_small[...]

        net.send(
            "x",
            image_out.at[here],
            returned.at[here],
            pass_sem.at[2, index],
            pass_sem.at[3, index],
            text,
        )

    for index, dst in enumerate((sib_q, sib_i, sib_m, sib_h, sib_du, sib_dx, sib_dq, sib_dkv)):
        shared(index, dst)

    def cross_out_to(index, first, last):
        return pltpu.make_async_copy(w_a.at[:, first:last], sum_ca.at[:, first:last], d_local.at[index])

    @pl.when(text)
    def _():
        def both_rows(x, dy, sib_x, sib_dy):
            return low(product(x, dy, 0, 0) + product(sib_x, sib_dy, 0, 0))

        def up_grad(i, carry):
            at = pl.multiple_of(i * tile, tile)
            mine = pl.ds(pl.multiple_of(net.core * cuts[3] + at, tile), tile)
            w_a[:, pl.ds(o_end + at, tile)] = both_rows(
                h3[...], grad_wide[:, mine], sib_h[...], sib_du[:, pl.ds(at, tile)]
            )
            return carry

        lax.fori_loop(0, cuts[3] // tile, up_grad, 0, unroll=True)
        cross_out_to(1, o_end, half).start()
        mine = half_of(net.core, cuts[0])
        w_a[:, 0:q_end] = both_rows(n_q[...], query[:, mine], sib_q[...], sib_dq[...])
        mine = half_of(net.core, cuts[1])
        w_a[:, q_end:kv_end] = both_rows(n_i[...], keyval[:, mine], sib_i[...], sib_dkv[...])
        mine = half_of(net.core, cuts[2])
        w_a[:, kv_end:o_end] = both_rows(c_mixed[...], n_x[:, mine], sib_m[...], sib_dx[...])
        cross_out_to(2, 0, o_end).start()

    mine_d = w_d.at[pl.ds(pl.multiple_of(net.core * share, share), share), :]
    merge(0, mine_d, rcv_d, sum_cd)
    @pl.when(text)
    def _():
        branch[...] = product(query[:, 0 : cuts[0]], w_ca[0, :, 0:q_end], 1, 1) + product(
            query[:, cuts[0] :], w_ca[1, :, 0:q_end], 1, 1
        )

        def text_done(r, back):
            top[r, :] = c_middle[r, :] + back

        norm_back_rows(out_y, gains[4:5, :], branch, text_done, g_small)
        gain_rows[4:5, :] = g_small[...]
        sums_ref[10:11, :] = jnp.broadcast_to(
            jnp.sum(row_weight[...], axis=0, keepdims=True), (1, sums_ref.shape[1])
        )
        vec[...] = gain_rows[...]

    for index in range(2):
        net.arrive(
            returned.at[index * rows_half : (index + 1) * rows_half],
            pass_sem.at[2, index],
            pass_sem.at[3, index],
            image,
        )

    @pl.when(image)
    def _():
        vec[...] = jnp.zeros_like(vec)

        def add_back(r):
            top[r, :] = cot[r, :].astype(jnp.float32) + returned[r, :].astype(jnp.float32)
            layer_out[r, :] = image_out[r, :]

        blocks(tok.shape[0], row_step(tok.shape[0]), add_back)

    vec[7:8, 0 : sums_ref.shape[1]] = sums.line()

    @pl.when(text)
    def _():
        pltpu.make_async_copy(rcv_d, sum_cd, d_local.at[0]).wait()
        cross_out_to(1, o_end, half).wait()
        cross_out_to(2, 0, o_end).wait()

    net.finish()


def forward(lines, cuts, parts, *operands):
    tok, own_qkv, own_d, own_cd = operands[7], operands[13], operands[16], operands[17]
    cross_shards = operands[9:13]
    bf16, f32 = jnp.bfloat16, jnp.float32
    count = 4 * lines
    rows, width = tok.shape
    few, half = cross_shards[0].shape[0], sum(cuts)
    hidden = count * own_d.shape[0]
    all_a = (count * own_qkv.shape[0], sum(parts))
    gains_shape = (8, width)
    heads_n = width // HD
    jobs = 10
    shape = jax.ShapeDtypeStruct
    wide_b, wide_f = (rows, width), (rows, hidden)
    stored = [
        (wide_b, bf16),
        ((rows, parts[0]), bf16),
        (wide_b, bf16),
        ((heads_n, rows, rows), bf16),
        (wide_b, f32),
        (wide_b, bf16),
        (wide_f, bf16),
        (wide_f, f32),
    ]
    outs = [
        (all_a, bf16),
        ((hidden, width), bf16),
        ((width, half), bf16),
        ((hidden // 2, width), bf16),
        *stored,
        (gains_shape, f32),
        (wide_b, bf16),
        (wide_b, f32),
        (gains_shape, f32),
    ]
    scratch = [
        (wide_b, bf16),
        (wide_b, bf16),
        *((w.shape, bf16) for w in cross_shards),
        (all_a, bf16),
        ((hidden, width), bf16),
        ((2, width, half), bf16),
        ((hidden, width), bf16),
        *stored,
        (wide_b, f32),
        (wide_b, f32),
        (wide_b, f32),
        (wide_b, bf16),
        (wide_b, bf16),
        (wide_b, bf16),
        (wide_b, bf16),
        (wide_b, bf16),
        (wide_b, bf16),
        (wide_b, bf16),
        (wide_b, bf16),
        ((rows, 2 * width), bf16),
        (wide_b, bf16),
        ((heads_n, rows, rows), bf16),
        (wide_b, f32),
        (wide_b, bf16),
        (wide_f, bf16),
        ((1, width), f32),
        ((rows, rows), f32),
        ((rows, rows), f32),
        ((rows, 1), f32),
        (gains_shape, f32),
        ((2, few, half), f32),
        ((few, half), f32),
        ((2 * few, half), bf16),
        ((hidden // 2, width), bf16),
        *[(wide_b, bf16)] * 4,
        *(((rows, cuts[i]), bf16) for i in (3, 2, 0, 1)),
        ((3,) + gains_shape, f32),
        ((3,) + gains_shape, f32),
        ((lines - 1,) + gains_shape, f32),
        ((16, 128), f32),
        (gains_shape, f32),
    ]
    dma = pltpu.SemaphoreType.DMA
    return pl.pallas_call(
        functools.partial(forward_kernel, lines, cuts, parts),
        out_shape=tuple(shape(*o) for o in outs),
        in_specs=[SMEM, SMEM] + [VMEM] * 5 + [ANY] * 11,
        out_specs=[ANY] * 12 + [VMEM] * 4,
        scratch_shapes=[pltpu.VMEM(*s) for s in scratch]
        + [
            dma((jobs, Gather.sems(lines))),
            dma((jobs, Gather.sems(lines))),
            dma((jobs,)),
            dma((2,)),
            dma((2 + lines,)),
            dma((2 + lines,)),
            dma((4, 3)),
            dma((12,)),
            dma((3,)),
            dma((3,)),
            dma((3,)),
            dma((3,)),
            dma((6,)),
            dma((8,)),
            dma((8,)),
        ],
        compiler_params=pltpu.CompilerParams(
            collective_id=0, has_side_effects=True, vmem_limit_bytes=63 << 20
        ),
    )(*operands)


class Scatter:
    def __init__(self, net, own, near, far, rcv, sems):
        self.net, self.own, self.near, self.far, self.rcv = net, own, near, far, rcv
        self.send_sem, self.recv_sem = sems

    @staticmethod
    def sems(lines):
        return 1 + 7 * lines

    def sem(self, s):
        return self.send_sem.at[s], self.recv_sem.at[s]

    def add(self, pairs, out):
        def one(r):
            total = pairs[0][r, :].astype(jnp.float32)
            for other in pairs[1:]:
                total = total + other[r, :].astype(jnp.float32)
            out[r, :] = total.astype(out.dtype)

        blocks(out.shape[0], 16, one)

    def chips(self, k):
        net = self.net
        if k == 0:
            return ((None, net.z),)
        return (
            (net.z + k < net.lines, jnp.minimum(net.z + k, net.lines - 1)),
            (net.z >= k, jnp.maximum(net.z - k, 0)),
        )

    def order(self):
        return [pair for k in range(self.net.lines - 1, -1, -1) for pair in self.chips(k)]

    def swap(self, theirs, rcv):
        self.whole = rcv
        self.net.send("core", theirs, rcv, *self.sem(0))

    def swapped(self):
        self.net.arrive(self.whole, *self.sem(0))

    def over_x(self, part):
        net = self.net
        for there, z in self.order():
            for y in (1 - net.y, net.y):
                chip = 2 * z + y
                net.send(
                    "x", part(chip), self.own(chip), *self.sem(1 + chip), both(there, net.text), True
                )

    def from_x(self, chip, there):
        if self.rcv is None:
            net = self.net
            net.arrive(self.own(chip), *self.sem(1 + chip), both(there, net.image))

    def across(self, only=None):
        net = self.net
        for there, z in self.order():
            there = both(there, only)
            chip = 2 * z + 1 - net.y
            self.from_x(chip, there)
            own = self.own(chip)
            if self.rcv is not None:
                when(there, lambda: self.add([own, self.rcv(chip)], own))
            net.send("y", own, self.near(z), *self.sem(1 + 2 * net.lines + z), there)

    def here(self, chip, z):
        parts = [self.own(chip), self.near(z)]
        return parts if self.rcv is None else parts + [self.rcv(chip)]

    def along(self, k):
        net = self.net
        lines = net.lines
        for up, (there, z) in zip((True, False), self.chips(k)):
            chip = 2 * z + net.y
            base = (1 + 3 * lines) if up else (1 + 4 * lines)
            self.from_x(chip, there)
            net.arrive(self.near(z), *self.sem(1 + 2 * lines + z), there)
            more = net.low if up else net.high
            s = base + z
            net.arrive(self.far(z), *self.sem(s), both(there, more))
            own = self.own(chip)
            parts = self.here(chip, z)
            when(both(there, more), lambda: self.add(parts + [self.far(z)], own))
            when(both(there, jnp.logical_not(more)), lambda: self.add(parts, own))
            slot = z if up else jnp.where(z == net.z - 1, lines, z)
            net.send("up" if up else "down", own, self.far(slot), *self.sem(s), there)

    def turn(self):
        pass

    def total(self, out):
        net = self.net
        lines = net.lines
        self.from_x(net.chip, None)
        net.arrive(self.near(net.z), *self.sem(1 + 2 * lines + net.z))
        net.arrive(self.far(net.z), *self.sem(1 + 3 * lines + net.z), net.low)
        net.arrive(self.far(lines), *self.sem(1 + 4 * lines + net.z), net.high)
        parts = self.here(net.chip, net.z)
        low_part, high_part = self.far(net.z), self.far(lines)
        when(both(net.low, net.high), lambda: self.add(parts + [low_part, high_part], out))
        when(jnp.logical_not(net.low), lambda: self.add(parts + [high_part], out))
        when(jnp.logical_not(net.high), lambda: self.add(parts + [low_part], out))


class ScatterAlong(Scatter):
    def across(self, only=None):
        pass

    def spot(self, z, second):
        if not second:
            return self.far(z)
        if isinstance(z, int):
            return self.extra(0)
        return self.near(z)

    def line_sems(self, up, second):
        lines = self.net.lines
        return 1 + (3 + 2 * second + (0 if up else 1)) * lines

    def parts(self, chip):
        return [self.own(chip)] if self.rcv is None else [self.own(chip), self.rcv(chip)]

    def along(self, k):
        net = self.net
        for up, (there, z) in zip((True, False), self.chips(k)):
            for second, y in ((0, net.y), (1, 1 - net.y)):
                chip = 2 * z + y
                self.from_x(chip, there)
                more = net.low if up else net.high
                s = self.line_sems(up, second) + z
                net.arrive(self.spot(z, second), *self.sem(s), both(there, more))
                own = self.own(chip)
                parts = self.parts(chip)
                with_far = parts + [self.spot(z, second)]
                when(both(there, more), lambda: self.add(with_far, own))
                if len(parts) > 1:
                    when(both(there, jnp.logical_not(more)), lambda: self.add(parts, own))
                way = "up" if up else "down"
                if up:
                    net.send(way, own, self.spot(z, second), *self.sem(s), there)
                else:
                    last = z == net.z - 1
                    net.send(
                        way, own, self.spot(net.lines, second), *self.sem(s), both(there, last)
                    )
                    net.send(
                        way,
                        own,
                        self.spot(z, second),
                        *self.sem(s),
                        both(there, jnp.logical_not(last)),
                    )

    def gathered(self, second, more, out):
        net = self.net
        lines = net.lines
        chip = 2 * net.z + (1 - net.y if second else net.y)
        self.from_x(chip, None)
        s = self.line_sems(True, second) + net.z
        net.arrive(self.spot(net.z, second), *self.sem(s), net.low)
        s = self.line_sems(False, second) + net.z
        net.arrive(self.spot(lines, second), *self.sem(s), net.high)
        parts = self.parts(chip) + more
        low_part, high_part = self.spot(net.z, second), self.spot(lines, second)
        when(both(net.low, net.high), lambda: self.add(parts + [low_part, high_part], out))
        when(jnp.logical_not(net.low), lambda: self.add(parts + [high_part], out))
        when(jnp.logical_not(net.high), lambda: self.add(parts + [low_part], out))

    def turn(self):
        net = self.net
        own = self.own(2 * net.z + 1 - net.y)
        self.gathered(1, [], own)
        net.send("y", own, self.extra(1), *self.sem(1 + 2 * net.lines))

    def total(self, out):
        self.net.arrive(self.extra(1), *self.sem(1 + 2 * self.net.lines))
        self.gathered(0, [self.extra(1)], out)


def strip(ref, size, first, last):
    return lambda i: ref.at[pl.ds(pl.multiple_of(i * size, size), size), first:last]


def backward_kernel(
    lines, cuts, parts,
    i_tok, i_top, gains, vec_in, full_a, full_d, sum_ca, sum_cd,
    i_h1, i_qkv, i_mixed, i_weight, i_middle, i_h2, i_active, i_slope,
    r_qkv, r_out, r_up, r_d, r_cq, r_ckv, r_co, r_cu, r_cd, r_grad, o_vec,
    o_qkv, o_out, o_up, o_d, o_cq, o_ckv, o_co, o_cu, o_cd, input_grad,
    tok, top_in, h1, qkv, mixed, weight, middle, h2, active, slope,
    g_a, g_d, rcv_a, rcv_d, near_a, near_d, far_a, far_d,
    own_ca, own_cd, near_ca, near_cd, far_ca, far_cd,
    w_d, w_up, top, branch, n_grad, g_small, vec, fin, fin_vo, extra_a, extra_d, swap, arrived, totals, spread,
    send_sem, recv_sem, load_sem, swap_sem, s_send, s_recv, out_sem,
):
    net = Net(lines)
    net.greet()
    left = []

    def leave(src, out):
        copy = pltpu.make_async_copy(src, out, out_sem.at[len(left)])
        copy.start()
        left.append(copy)

    text, image = net.text, net.image
    width = tok.shape[1]
    tile = width
    rows, depth = o_qkv.shape[0], o_d.shape[0]
    few, part = 2 * o_cq.shape[0], o_cd.shape[0]
    half = own_ca.shape[1]
    a_out = parts[0] + parts[1]
    all_a = g_a.shape[2]
    o_end = cuts[0] + cuts[1] + cuts[2]
    theirs = 1 - net.core

    def load(index, src, dst):
        copy = pltpu.make_async_copy(src, dst, load_sem.at[index])
        copy.start()
        return copy

    l_top = load(16, i_top, top_in)
    l_active = load(0, i_active, active)
    l_wd = load(1, full_d, w_d)
    l_slope = load(2, i_slope, slope)
    l_h2 = load(3, i_h2, h2)
    l_up = load(4, full_a.at[:, a_out:], w_up)
    l_middle = load(5, i_middle, middle)
    l_mixed = load(6, i_mixed, mixed)
    l_qkv = load(7, i_qkv, qkv)
    l_weight = load(8, i_weight, weight)
    l_h1 = load(9, i_h1, h1)
    l_tok = load(17, i_tok, tok)

    def job(index, own, near, far, rcv, extra=None):
        kind = ScatterAlong if SCATTER_NAMES[index] in SCATTER_ALONG else Scatter
        made = kind(net, own, near, far, rcv, (send_sem.at[index], recv_sem.at[index]))
        made.extra = extra
        return made

    def self_a(index, first, last):
        return job(
            index,
            strip(g_a.at[net.core], rows, first, last),
            strip(near_a, rows, first, last),
            strip(far_a, rows, first, last),
            strip(rcv_a, rows, first, last),
            strip(extra_a, rows, first, last),
        )

    def cross_a(index, first, last):
        return job(
            index,
            strip(own_ca, few, first, last),
            strip(near_ca, few, first, last),
            strip(far_ca, few, first, last),
            None,
        )

    def self_d(index, first, last):
        return job(
            index,
            strip(g_d.at[net.core], depth, first, last),
            strip(near_d, depth, first, last),
            strip(far_d, depth, first, last),
            strip(rcv_d, depth, first, last),
            strip(extra_d, depth, first, last),
        )

    mid, middle_up, third = parts[0] - width, a_out + 2 * width, width // 3
    jobs = {
        "d0": self_d(0, 0, third),
        "d1": self_d(1, third, 2 * third),
        "d2": self_d(2, 2 * third, width),
        "u0": self_a(3, a_out, middle_up),
        "u1": self_a(4, middle_up, all_a),
        "qk": self_a(5, 0, mid),
        "vo": self_a(6, mid, a_out),
        "cd": job(
            7,
            strip(own_cd, part, 0, width),
            strip(near_cd, part, 0, width),
            strip(far_cd, part, 0, width),
            None,
        ),
        "cu": cross_a(8, o_end, half),
        "ca": cross_a(9, 0, o_end),
    }

    def swap_a(name, first, last):
        jobs[name].swap(g_a.at[theirs, :, first:last], rcv_a.at[:, first:last])

    def swap_d(name, first, last):
        jobs[name].swap(g_d.at[theirs, :, first:last], rcv_d.at[:, first:last])

    def across(name, only=None):
        if jobs[name].rcv is not None:
            jobs[name].swapped()
        jobs[name].across(only)

    plane_a, plane_d = own_ca.shape[0], own_cd.shape[0]
    c_loads = (
        pltpu.make_async_copy(sum_cd.at[plane_d : 2 * plane_d, :], own_cd, load_sem.at[10]),
        pltpu.make_async_copy(sum_ca.at[plane_a : 2 * plane_a, :], own_ca, load_sem.at[11]),
    )

    @pl.when(text)
    def _():
        for copy in c_loads:
            copy.start()

    def start_x(name):
        at = {"cd": (sum_cd, part, 0, width), "cu": (sum_ca, few, o_end, half), "ca": (sum_ca, few, 0, o_end)}
        jobs[name].over_x(strip(*at[name]))

    def round_top():
        l_top.wait()

        def body(r):
            n_grad[r, :] = low(top_in[r, :])

        blocks(tok.shape[0], row_step(tok.shape[0]), body)

        @pl.when(text)
        def _():
            for copy in c_loads:
                copy.wait()

    def down_grads():
        l_active.wait()

        def down_tile(i, carry):
            cols = pl.ds(pl.multiple_of(i * tile, tile), tile)
            found = low(product(active[:, cols], n_grad[...], 0, 0))
            each = tile // depth
            for k in range(each):
                at = pl.multiple_of(((i * each + k) // 2) * depth, depth)
                g_d[k % 2, pl.ds(at, depth), :] = found[k * depth : (k + 1) * depth]
            return carry

        lax.fori_loop(0, active.shape[1] // tile, down_tile, 0)

    def wide_grads():
        l_wd.wait()
        l_slope.wait()

        def wide_tile(i, carry):
            cols = pl.ds(pl.multiple_of(i * tile, tile), tile)
            grad = product(n_grad[...], w_d[cols, :], 1, 1)
            active[:, cols] = low(grad * slope[:, cols])
            return carry

        lax.fori_loop(0, active.shape[1] // tile, wide_tile, 0)
        for i in range(4):
            src = full_a.at[:, i * width : (i + 1) * width]
            l_four.append(load(12 + i, src, w_d.at[i * width : (i + 1) * width, :]))
        l_h2.wait()

    l_four = []

    def put_a(found, at):
        for k in range(width // rows):
            g_a[k % 2, (k // 2) * rows : (k // 2 + 1) * rows, pl.ds(at, found.shape[1])] = found[
                k * rows : (k + 1) * rows
            ]

    def up_grads(first_tile, last_tile):
        def run():
            def up_tile(i, carry):
                at = pl.multiple_of(i * tile, tile)
                found = low(product(h2[...], active[:, pl.ds(at, tile)], 0, 0))
                put_a(found, pl.multiple_of(a_out + at, tile))
                return carry

            lax.fori_loop(first_tile, last_tile, up_tile, 0)

        return run

    def own_gain(at):
        return jnp.where(text, gains[at + 2 : at + 3, :], gains[at : at + 1, :])

    at_vec = 2 * net.tower

    def mid_grads():
        l_up.wait()
        branch[...] = product(active[...], w_up[...], 1, 1)
        l_middle.wait()

        def mid_done(r, back):
            total = top_in[r, :] + back
            top[r, :] = total
            n_grad[r, :] = low(total)

        norm_back_rows(middle, own_gain(1), branch, mid_done, g_small)
        vec[...] = vec_in[...]
        vec[pl.ds(at_vec + 1, 1), :] = g_small[...]

    def out_grads():
        l_mixed.wait()
        for copy in l_four:
            copy.wait()
        put_a(low(product(mixed[...], n_grad[...], 0, 0)), parts[0])
        mixed[...] = low(product(n_grad[...], w_d[3 * width : 4 * width, :], 1, 1))

    def att_grads():
        l_qkv.wait()
        l_weight.wait()

        def att_done(pair, dq, dk, dv):
            at = pl.multiple_of(pair * 2 * HD, 2 * HD)
            for k, grad in enumerate((dq, dk, dv)):
                qkv[:, pl.ds(pl.multiple_of(k * width + at, 2 * HD), 2 * HD)] = grad

        attention_back(
            pairs_of(qkv),
            pairs_of(qkv, width),
            pairs_of(qkv, 2 * width),
            pairs_of(mixed),
            weight,
            width,
            att_done,
        )
        l_h1.wait()

    def qkv_grads(first_tile, last_tile):
        def run():
            def qkv_tile(i, carry):
                at = pl.multiple_of(i * tile, tile)
                put_a(low(product(h1[...], qkv[:, pl.ds(at, tile)], 0, 0)), at)
                return carry

            lax.fori_loop(first_tile, last_tile, qkv_tile, 0)

        return run

    small = Small(net, vec, arrived, totals, spread, s_send, s_recv)

    def first_grads():
        l_tok.wait()
        branch[...] = (
            product(qkv[:, 0:width], w_d[0:width, :], 1, 1)
            + product(qkv[:, width : 2 * width], w_d[width : 2 * width, :], 1, 1)
            + product(qkv[:, 2 * width :], w_d[2 * width : 3 * width, :], 1, 1)
        )

        def first_done(r, back):
            input_grad[r, :] = top[r, :] + back

        norm_back_rows(tok, own_gain(0), branch, first_done, g_small)
        leave(input_grad, r_grad)
        vec[pl.ds(at_vec, 1), :] = g_small[...]
        small.exchange(0)

    def small_step(index):
        def run():
            small.collect(index)
            if index < 2:
                small.exchange(index + 1)
            else:
                small.spread()

        return run

    up_tiles = (all_a - a_out) // tile
    steps = {
        "top": round_top,
        "down": down_grads,
        "wide": wide_grads,
        "up0": up_grads(0, up_tiles // 2),
        "up1": up_grads(up_tiles // 2, up_tiles),
        "mid": mid_grads,
        "out": out_grads,
        "att": att_grads,
        "qk": qkv_grads(0, mid // tile),
        "v": qkv_grads(mid // tile, parts[0] // tile),
        "first": first_grads,
        "small0": small_step(0),
        "small1": small_step(1),
        "small2": small_step(2),
    }
    share = few // 2
    first = net.core == 0
    swaps = {}

    def start_swap(name, index, first_column, last_column):
        copy = net.copy(
            "core",
            fin.at[pl.ds(pl.multiple_of(theirs * share, share), share), first_column:last_column],
            swap.at[:, first_column:last_column],
            swap_sem.at[index, 0],
            swap_sem.at[index, 1],
        )
        copy.start()
        swaps[name] = copy

    def put_cross(out, at, n):
        mine = fin[pl.ds(pl.multiple_of(net.core * share, share), share), at : at + n]
        other = swap[:, at : at + n]
        out[:, 0:n] = jnp.where(first, mine, other)
        out[:, n:] = jnp.where(first, other, mine)

    def put_vo():
        o_qkv[:, mid:] = fin_vo[:, 0 : parts[0] - mid]
        o_out[...] = fin_vo[:, parts[0] - mid :]
        leave(o_qkv.at[:, mid:], r_qkv.at[:, mid:])
        leave(o_out, r_out)

    def going(ref, out, first_column, last_column):
        src = ref.at[:, first_column:last_column]
        return src, lambda: leave(src, out.at[:, first_column:last_column])

    totals_to = {
        "d0": going(o_d, r_d, 0, third),
        "d1": going(o_d, r_d, third, 2 * third),
        "d2": going(o_d, r_d, 2 * third, width),
        "u0": going(o_up, r_up, 0, middle_up - a_out),
        "u1": going(o_up, r_up, middle_up - a_out, all_a - a_out),
        "qk": going(o_qkv, r_qkv, 0, mid),
        "vo": (fin_vo, put_vo),
        "cd": going(o_cd, r_cd, 0, width),
        "cu": (fin.at[:, o_end:half], lambda: start_swap("cu", 0, o_end, half)),
        "ca": (fin.at[:, 0:o_end], lambda: start_swap("ca", 1, 0, o_end)),
    }
    spans = {
        "d0": (0, third),
        "d1": (third, 2 * third),
        "d2": (2 * third, width),
        "u0": (a_out, middle_up),
        "u1": (middle_up, all_a),
        "qk": (0, mid),
        "vo": (mid, a_out),
    }
    events = scatter_order(lines)
    for kind, name, k in events[:2]:
        steps[name]()
    net.meet()
    for kind, name, k in events[2:]:
        if kind == "do":
            steps[name]()
        elif kind == "x":
            start_x(name)
        elif kind == "swap":
            (swap_d if name in ("d0", "d1", "d2") else swap_a)(name, *spans[name])
        elif kind == "across":
            across(name, (None, text, image)[k])
        elif kind == "along":
            jobs[name].along(k)
        elif kind == "turn":
            jobs[name].turn()
        else:
            out, then = totals_to[name]
            jobs[name].total(out)
            if then is not None:
                then()
    swaps["cu"].wait()
    put_cross(o_cu, o_end, cuts[3])
    leave(o_cu, r_cu)
    small.total(o_vec)
    swaps["ca"].wait()
    at = 0
    for out, result, n in zip((o_cq, o_ckv, o_co), (r_cq, r_ckv, r_co), cuts):
        put_cross(out, at, n)
        leave(out, result)
        at += n
    net.finish()
    for copy in left:
        copy.wait()


SCATTER = ("d0", "d1", "d2", "u0", "u1", "cd", "qk", "vo", "cu", "ca")
SCATTER_NAMES = ("d0", "d1", "d2", "u0", "u1", "qk", "vo", "cd", "cu", "ca")
SCATTER_ALONG = ("d1", "u0")
BEFORE = {0: ("qk", "vo", "cd"), 3: ("cu",), 5: ("ca",)}
SCATTER_HEAD = (
    "do top", "do down", "x cd", "x cu", "x ca", "swap d0", "swap d1", "swap d2", "across cd 1",
    "do wide", "across d0", "across d1", "across d2", "do up0", "swap u0", "do up1", "swap u1",
    "do mid", "across u0", "across u1", "do out", "do att", "do qk", "swap qk", "do v", "swap vo",
    "do first",
)


def scatter_order(lines):
    if lines == 4 and SCATTER_FOUR:
        return parsed(SCATTER_FOUR)
    events = parsed(SCATTER_HEAD)
    count = len(SCATTER)
    for slot in range(count + lines):
        for name in BEFORE.get(slot, ()):
            events.append(("across", name, 2 if name == "cd" else 0))
        if 1 <= slot <= 3:
            events.append(("do", "small%d" % (slot - 1), 0))
        for k in range(lines - 1, -2, -1):
            index = slot - (lines - 1 - k)
            if 0 <= index < count:
                kind = "along" if k > 0 else "turn" if k == 0 else "total"
                events.append((kind, SCATTER[index], k))
    return events


SCATTER_FOUR = (
    "do top", "do down", "swap d0", "swap d1", "swap d2", "x cd", "do wide", "do up0", "across d1",
    "along d1 3", "across d0", "across d2", "x cu", "along d1 2", "swap u0", "across cd 1",
    "along d1 1", "along d0 3", "do up1", "across u0", "swap u1", "along d2 3", "along u0 3",
    "do mid", "across cd 2", "along d0 2", "along d0 1", "do out", "do att", "across u1",
    "along cd 3", "along u0 2", "along u1 3", "do qk", "x ca", "along cd 2", "along u1 2",
    "across cu", "along cd 1", "along cu 3", "swap qk", "along d2 2", "along cu 2", "along u0 1",
    "across qk", "along qk 3", "do v", "along u1 1", "swap vo", "along qk 2", "across ca",
    "total cd", "do first", "along qk 1", "along ca 3", "along cu 1", "do small0", "across vo",
    "along ca 2", "total u1", "do small1", "along vo 3", "turn u0", "total qk", "do small2",
    "along d2 1", "along vo 2", "total cu", "along ca 1", "turn d1", "along vo 1", "total ca",
    "total u0", "total d2", "total d1", "total d0", "total vo",
)


def backward(lines, cuts, parts, own_shapes, *operands):
    bf16, f32 = jnp.bfloat16, jnp.float32
    tok, top, gains, vec, full_a, full_d, sum_ca, sum_cd = operands[:8]
    stored = [(o.shape, o.dtype) for o in operands[8:]]
    chips = 2 * lines
    row_count, width = tok.shape
    hidden, all_a = full_d.shape[0], full_a.shape[1]
    half = sum_ca.shape[1]
    rows, depth = width // (2 * chips), hidden // (2 * chips)
    few, part = width // (2 * chips), hidden // (4 * chips)
    results = [*own_shapes, (row_count, width)]
    outs = [*results, vec.shape]
    rcv_a, rcv_d = (chips * rows, all_a), (chips * depth, width)
    own_ca, own_cd = (chips * few, half), (chips * part, width)

    def line(size, count):
        return (size * count, all_a), (depth * count, width)

    scratch = [
        *((shape, f32) for shape in results),
        (tok.shape, tok.dtype),
        (top.shape, top.dtype),
        *stored,
        ((2,) + rcv_a, bf16),
        ((2,) + rcv_d, bf16),
        (rcv_a, bf16),
        (rcv_d, bf16),
        ((lines * rows, all_a), bf16),
        ((lines * depth, width), bf16),
        (((lines + 1) * rows, all_a), bf16),
        (((lines + 1) * depth, width), bf16),
        (own_ca, bf16),
        (own_cd, bf16),
        ((lines * few, half), bf16),
        ((lines * part, width), bf16),
        (((lines + 1) * few, half), bf16),
        (((lines + 1) * part, width), bf16),
        ((hidden, width), bf16),
        ((width, hidden), bf16),
        ((row_count, width), f32),
        ((row_count, width), f32),
        ((row_count, width), bf16),
        ((1, width), f32),
        (vec.shape, f32),
        ((rows, half), f32),
        ((rows, 2 * width), f32),
        ((2 * rows, all_a), bf16),
        ((2 * depth, width), bf16),
        ((few // 2, half), f32),
        ((3,) + vec.shape, f32),
        ((3,) + vec.shape, f32),
        ((lines - 1,) + vec.shape, f32),
    ]
    dma = pltpu.SemaphoreType.DMA
    return pl.pallas_call(
        functools.partial(backward_kernel, lines, cuts, parts),
        out_shape=tuple(jax.ShapeDtypeStruct(s, f32) for s in outs),
        in_specs=[ANY] * 2 + [VMEM] * 2 + [ANY] * 12,
        out_specs=[ANY] * len(results) + [VMEM],
        scratch_shapes=[pltpu.VMEM(*s) for s in scratch]
        + [
            dma((10, Scatter.sems(lines))),
            dma((10, Scatter.sems(lines))),
            dma((18,)),
            dma((2, 2)),
            dma((2 + lines,)),
            dma((2 + lines,)),
            dma((16,)),
        ],
        compiler_params=pltpu.CompilerParams(
            collective_id=1, has_side_effects=True, vmem_limit_bytes=63 << 20
        ),
    )(*operands)


def final_kernel(lines, rows, few, vec, *refs):
    count = (len(refs) - 7) // 3
    ins, outs = refs[:count], refs[count : 2 * count]
    g_1, g_2, g_q, g_i, g_c, rms, *held, sems = refs[2 * count :]
    come = [pltpu.make_async_copy(a, b, sems.at[0, i]) for i, (a, b) in enumerate(zip(ins, held))]
    go = [pltpu.make_async_copy(a, b, sems.at[1, i]) for i, (a, b) in enumerate(zip(held, outs))]
    for copy in come:
        copy.start()
    tower, dp = lax.axis_index("tower"), lax.axis_index("dp")
    width = vec.shape[1]

    def cut(n, at):
        lane = lax.broadcasted_iota(jnp.int32, (width, n), 0)
        index = lax.broadcasted_iota(jnp.int32, (width, n), 1)
        pick = jnp.where(lane == at + index, 1.0, 0.0)
        return lax.dot_general(
            vec[...],
            pick,
            (((1,), (0,)), ((), ())),
            precision=lax.Precision.HIGHEST,
            preferred_element_type=jnp.float32,
        )

    own = cut(rows, dp * rows)
    cross = cut(few, (tower * 4 * lines + dp) * few)
    g_1[...] = jnp.where(tower == 1, own[2:3], own[0:1])
    g_2[...] = jnp.where(tower == 1, own[3:4], own[1:2])
    g_q[...] = cross[4:5]
    g_i[...] = cross[5:6]
    g_c[...] = cross[6:7]
    sums = vec[7:8, 0:128]
    lane = lax.broadcasted_iota(jnp.int32, sums.shape, 1)
    valid = jnp.sum(jnp.where(lane == 10, sums, 0.0), axis=1, keepdims=True)
    images = ins[0].shape[0] * 4.0 * lines
    divisor = jnp.where(lane < 4, images, valid) * width
    rms[...] = jnp.sqrt(sums / divisor)[0, : rms.shape[0]]
    for here, there in zip(come, go):
        here.wait()
        there.start()
    for copy in go:
        copy.wait()


def final(lines, rows, few, vec, *results):
    f32 = jnp.float32
    small = [(1, rows)] * 2 + [(1, few)] * 3 + [(10,)]
    return pl.pallas_call(
        functools.partial(final_kernel, lines, rows, few),
        out_shape=tuple(jax.ShapeDtypeStruct(r.shape, r.dtype) for r in results)
        + tuple(jax.ShapeDtypeStruct(s, f32) for s in small),
        in_specs=[VMEM] + [ANY] * len(results),
        out_specs=[ANY] * len(results) + [VMEM] * 6,
        scratch_shapes=[pltpu.VMEM(r.shape, r.dtype) for r in results]
        + [pltpu.SemaphoreType.DMA((2, len(results)))],
        compiler_params=pltpu.CompilerParams(vmem_limit_bytes=62 << 20),
    )(vec, *results)


def plain_gather(own_a, own_d, pack, own_cd, own_g):
    axes = ("tower", "dp")
    tiles = lax.all_gather(own_g, axes, axis=0)
    return (
        lax.all_gather(own_a, "dp", axis=0, tiled=True),
        lax.all_gather(own_d, "dp", axis=0, tiled=True),
        lax.all_gather(pack.astype(jnp.bfloat16), axes, axis=1, tiled=True),
        lax.all_gather(own_cd, axes, axis=0, tiled=True),
        tiles.reshape((2, -1) + own_g.shape),
    )


def plain_scatter(g_a, g_d, g_ca, g_cd, vec, parts, cuts):
    axes = ("tower", "dp")

    def added(grad, over, axis):
        return lax.psum_scatter(
            grad.astype(jnp.float32), over, scatter_dimension=axis, tiled=True
        )

    a = added(g_a.reshape(-1, g_a.shape[-1]), "dp", 0)
    d = added(g_d.reshape(-1, g_d.shape[-1]), "dp", 0)
    ca = added(g_ca.reshape(2, -1, g_ca.shape[-1]), axes, 1)
    cd = added(g_cd.reshape(-1, g_cd.shape[-1]), axes, 0)
    at = [sum(cuts[:i]) for i in range(len(cuts) + 1)]
    cross = [
        jnp.concatenate([ca[0][:, i:j], ca[1][:, i:j]], axis=1) for i, j in zip(at[:-1], at[1:])
    ]
    first, second = parts[0], parts[0] + parts[1]
    self_parts = [a[:, :first], a[:, first:second], a[:, second:]]
    return (*self_parts, d, *cross, cd, lax.psum(vec, axes))


def layer_norm(value_matrix, norm_gain):
    center = value_matrix - jnp.mean(value_matrix, axis=-1, keepdims=True)
    spread = jnp.mean(center * center, axis=-1, keepdims=True)
    return center * lax.rsqrt(spread + EPSILON) * norm_gain


def norm_back(value_matrix, norm_gain, grad_out):
    result, puller = jax.vjp(layer_norm, value_matrix, norm_gain)
    return puller(grad_out)


def dot(a, b):
    return jnp.dot(a, b, preferred_element_type=jnp.float32)


def dot_tn(a, b):
    return jnp.einsum("rd,re->de", a, b, preferred_element_type=jnp.float32)


def dot_nt(a, b):
    return jnp.einsum("re,de->rd", a, b, preferred_element_type=jnp.float32)


def low(value_matrix):
    return value_matrix.astype(jnp.bfloat16)


def masks(counts, lengths, row_count, decoder):
    row_index = jnp.arange(row_count, dtype=jnp.int32)
    bounds = jnp.cumsum(counts)
    image_of = jnp.sum((row_index[:, None] >= bounds[None, :]).astype(jnp.int32), axis=1)
    caption_of = row_index // CAP_LEN
    in_place = row_index - caption_of * CAP_LEN
    caption_slots = jnp.arange(lengths.shape[0], dtype=jnp.int32)
    length_rows = jnp.sum(
        jnp.where(caption_of[:, None] == caption_slots[None, :], lengths[None, :], 0), axis=1
    )
    valid_rows = in_place < length_rows
    image_mask = image_of[:, None] == image_of[None, :]
    text_mask = (
        (caption_of[:, None] == caption_of[None, :])
        & (in_place[None, :] <= in_place[:, None])
        & valid_rows[None, :]
    )
    cross_mask = caption_of[:, None] == image_of[None, :]
    return jnp.where(decoder, text_mask, image_mask), cross_mask, valid_rows


def heads(value_matrix):
    return value_matrix.reshape(value_matrix.shape[0], -1, HD)


def attend(query, key, value, allowed):
    scores = jnp.einsum(
        "qhd,khd->hqk", heads(query), heads(key), preferred_element_type=jnp.float32
    ) * HD ** (-0.5)
    weight = jax.nn.softmax(jnp.where(allowed[None], scores, NEGATIVE), axis=-1)
    mixed = jnp.einsum("hqk,khd->qhd", low(weight), heads(value), preferred_element_type=jnp.float32)
    return low(mixed.reshape(query.shape)), weight


def attend_back(query, key, value, weight, grad_mixed):
    grad_mixed = heads(grad_mixed)
    grad_value = jnp.einsum("hqk,qhd->khd", low(weight), grad_mixed, preferred_element_type=jnp.float32)
    grad_weight = jnp.einsum("qhd,khd->hqk", grad_mixed, heads(value), preferred_element_type=jnp.float32)
    grad_score = low(
        weight * (grad_weight - jnp.sum(grad_weight * weight, axis=-1, keepdims=True))
    )
    grad_query = jnp.einsum(
        "hqk,khd->qhd", grad_score, heads(key), preferred_element_type=jnp.float32
    ) * HD ** (-0.5)
    grad_key = jnp.einsum(
        "hqk,qhd->khd", grad_score, heads(query), preferred_element_type=jnp.float32
    ) * HD ** (-0.5)
    return tuple(low(g.reshape(query.shape)) for g in (grad_query, grad_key, grad_value))


def mlp_forward(stream, gain, up, down):
    hidden = low(layer_norm(stream, gain))
    wide = dot(hidden, up)
    active = low(jax.nn.gelu(wide))
    return dot(active, down), (hidden, wide, active)


def mlp_back(stream, gain, up, down, stored, grad):
    hidden, wide, active = stored
    branch = low(grad)
    grad_down = dot_tn(active, branch)
    result, puller = jax.vjp(jax.nn.gelu, wide)
    grad_wide = low(puller(dot_nt(branch, down))[0])
    grad_up = dot_tn(hidden, grad_wide)
    grad_stream, grad_gain = norm_back(stream, gain, dot_nt(grad_wide, up))
    return grad + grad_stream, grad_gain, grad_up, grad_down


def squares(value_matrix, row_weight):
    return jnp.sum(row_weight[:, None] * value_matrix * value_matrix)


def plain_shards(
    tokens, cotangent, kept_counts, caption_lengths, attn_gain, qkv_weight, attn_out, mlp_gain,
    mlp_up, mlp_down, query_gain, image_gain, cross_gain, cross_query, cross_keyval, cross_out,
    cross_up, cross_down,
):
    f32 = jnp.float32
    dp_count = lax.axis_size("dp")
    lines = dp_count // 4
    tower, dp = lax.axis_index("tower"), lax.axis_index("dp")
    decoder = tower == 1
    row_count, width = tokens.shape[1:]
    rows = attn_gain.shape[1]
    few = query_gain.shape[0]

    def tile_row(value):
        return jnp.pad(value.astype(f32), (0, 128 - value.shape[0]))

    gain_tile = jnp.stack(
        [tile_row(attn_gain[0]), tile_row(mlp_gain[0])]
        + [tile_row(g) for g in (query_gain, image_gain, cross_gain)]
        + [jnp.zeros((128,), f32)] * 3
    )
    cross_shards = (cross_query, cross_keyval, cross_out, cross_up)
    cuts = tuple(w.shape[1] // 2 for w in cross_shards)
    pack = jnp.stack(
        [
            jnp.concatenate([w[:, h * n : (h + 1) * n] for w, n in zip(cross_shards, cuts)], axis=1)
            for h in range(2)
        ]
    ).astype(f32)
    self_parts = (qkv_weight.shape[2], attn_out.shape[2], mlp_up.shape[2])
    own_a = jnp.concatenate([qkv_weight[0], attn_out[0], mlp_up[0]], axis=1)
    full_a, full_d, full_ca, full_cd, full_g = plain_gather(
        own_a, mlp_down[0], pack, cross_down, gain_tile
    )
    qkv = full_a[:, : self_parts[0]]
    out = full_a[:, self_parts[0] : self_parts[0] + self_parts[1]]
    up = full_a[:, self_parts[0] + self_parts[1] :]
    down = full_d
    plane_gains = lax.dynamic_index_in_dim(full_g, tower, 0, keepdims=False)
    gain_1 = plane_gains[:, 0, :rows].reshape(-1)
    gain_2 = plane_gains[:, 1, :rows].reshape(-1)
    gain_q, gain_i, gain_c = (full_g[:, :, 2 + i, :few].reshape(-1) for i in range(3))

    stream = tokens[0].astype(f32)
    upstream = cotangent[0].astype(f32)
    allowed, cross_allowed, valid_rows = masks(kept_counts[0], caption_lengths, row_count, decoder)
    row_weight = jnp.where(decoder, valid_rows, True).astype(f32)

    normed = low(layer_norm(stream, gain_1))
    joined = low(dot(normed, qkv))
    query, key, value = jnp.split(joined, 3, axis=1)
    mixed, weight = attend(query, key, value, allowed)
    attn_branch = dot(mixed, out)
    middle = stream + attn_branch
    mlp_branch, mlp_stored = mlp_forward(middle, gain_2, up, down)
    layer_y = middle + mlp_branch
    image_rows = low(layer_y)
    arrived = lax.ppermute(image_rows, "tower", [(0, 1)])

    def run_cross(operands):
        text_y, image_in = operands
        at = [0]
        for n in cuts:
            at.append(at[-1] + n)
        cq, ckv, co, cu = (
            jnp.concatenate([full_ca[0][:, a:b], full_ca[1][:, a:b]], axis=1)
            for a, b in zip(at[:-1], at[1:])
        )
        image_in = image_in.astype(f32)
        image_normed = low(layer_norm(image_in, gain_i))
        keyval = low(dot(image_normed, ckv))
        c_key, c_value = jnp.split(keyval, 2, axis=1)
        c_normed = low(layer_norm(text_y, gain_q))
        c_query = low(dot(c_normed, cq))
        c_mixed, c_weight = attend(c_query, c_key, c_value, cross_allowed)
        c_branch = dot(c_mixed, co)
        c_middle = text_y + c_branch
        c_mlp, c_stored = mlp_forward(c_middle, gain_c, cu, full_cd)
        final_rows = c_middle + c_mlp
        grad_middle, grad_gain_c, grad_cu, grad_cd = mlp_back(
            c_middle, gain_c, cu, full_cd, c_stored, upstream
        )
        grad_branch = low(grad_middle)
        grad_co = dot_tn(c_mixed, grad_branch)
        grad_q, grad_k, grad_v = attend_back(
            c_query, c_key, c_value, c_weight, low(dot_nt(grad_branch, co))
        )
        grad_cq = dot_tn(c_normed, grad_q)
        grad_text, grad_gain_q = norm_back(text_y, gain_q, dot_nt(grad_q, cq))
        grad_keyval = jnp.concatenate([grad_k, grad_v], axis=1)
        grad_ckv = dot_tn(image_normed, grad_keyval)
        grad_image, grad_gain_i = norm_back(image_in, gain_i, dot_nt(grad_keyval, ckv))
        cross_sums = jnp.stack(
            [
                squares(c_branch, row_weight),
                squares(c_mlp, row_weight),
                squares(final_rows, row_weight),
            ]
        )
        grads = tuple(low(g) for g in (grad_cq, grad_ckv, grad_co, grad_cu))
        grad_ca = jnp.stack(
            [
                jnp.concatenate([g[:, h * n : (h + 1) * n] for g, n in zip(grads, cuts)], axis=1)
                for h in range(2)
            ]
        )
        return (
            low(final_rows),
            grad_middle + grad_text,
            low(grad_image),
            grad_ca,
            low(grad_cd),
            jnp.concatenate([grad_gain_q, grad_gain_i, grad_gain_c]),
            cross_sums,
        )

    def skip_cross(operands):
        shapes = jax.eval_shape(run_cross, operands)
        return tuple(jnp.zeros(s.shape, s.dtype) for s in shapes)

    final_rows, grad_text, grad_image, grad_ca, grad_cd, grad_cross_gains, cross_sums = lax.cond(
        decoder, run_cross, skip_cross, (layer_y, arrived)
    )
    returned = lax.ppermute(grad_image, "tower", [(1, 0)]).astype(f32)
    grad_top = jnp.where(decoder, grad_text, upstream + returned)

    grad_middle, grad_gain_2, grad_up, grad_down = mlp_back(
        middle, gain_2, up, down, mlp_stored, grad_top
    )
    grad_branch = low(grad_middle)
    grad_out = dot_tn(mixed, grad_branch)
    grad_joined = jnp.concatenate(
        attend_back(query, key, value, weight, low(dot_nt(grad_branch, out))), axis=1
    )
    grad_qkv = dot_tn(normed, grad_joined)
    grad_stream, grad_gain_1 = norm_back(stream, gain_1, dot_nt(grad_joined, qkv))
    grad_stream = grad_middle + grad_stream

    layer_sums = jnp.stack(
        [
            squares(stream, row_weight),
            squares(attn_branch, row_weight),
            squares(mlp_branch, row_weight),
            squares(layer_y, row_weight),
        ]
    )
    encoder_part = jnp.where(decoder, 0.0, layer_sums)
    decoder_part = jnp.where(decoder, jnp.concatenate([layer_sums[:3], cross_sums]), 0.0)
    counted = jnp.where(decoder, jnp.sum(valid_rows.astype(f32)), 0.0)
    line = tile_row(jnp.concatenate([encoder_part, decoder_part, counted[None]]))
    self_gains = jnp.concatenate([grad_gain_1, grad_gain_2])
    zero = jnp.zeros_like(self_gains)
    vec = jnp.concatenate(
        [
            jnp.where(decoder, zero, self_gains),
            jnp.where(decoder, self_gains, zero),
            grad_cross_gains,
            line,
        ]
    ).reshape(-1, 128)
    vec = jnp.pad(vec, ((0, -vec.shape[0] % 8), (0, 0)))
    grad_a = jnp.concatenate([low(grad_qkv), low(grad_out), low(grad_up)], axis=1)
    chips = 2 * lines
    results = plain_scatter(
        grad_a.reshape(chips, 2, rows, -1),
        low(grad_down).reshape(chips, 2, -1, width),
        grad_ca.reshape(2, 2, chips, 2 * few, -1),
        grad_cd.reshape(2, chips, 2, -1, width),
        vec,
        self_parts,
        cuts,
    )
    o_qkv, o_out, o_up, o_d, o_cq, o_ckv, o_co, o_cu, o_cd, o_vec = results
    flat = o_vec.reshape(-1)
    own_gains = lax.dynamic_slice(flat, (tower * 2 * width,), (2 * width,))
    g_1, g_2 = (lax.dynamic_slice(own_gains, (i * width + dp * rows,), (rows,)) for i in range(2))
    g_q, g_i, g_c = (
        lax.dynamic_slice(
            flat, ((4 + i) * width + (tower * dp_count + dp) * few,), (few,)
        )
        for i in range(3)
    )
    sums = flat[7 * width : 7 * width + 11]
    encoder_count = jnp.full((4,), float(row_count * dp_count), f32)
    divisor = jnp.concatenate([encoder_count, jnp.full((6,), 1.0, f32) * sums[10]]) * width
    rms_values = jnp.sqrt(sums[:10] / divisor)
    layer_out = jnp.where(decoder, final_rows, image_rows)
    return (
        layer_out[None], grad_stream[None], g_1[None], o_qkv[None], o_out[None], g_2[None],
        o_up[None], o_d[None], g_q, g_i, g_c, o_cq, o_ckv, o_co, o_cu, o_cd, rms_values,
    )


def fused_shards(
    tokens, cotangent, kept_counts, caption_lengths, attn_gain, qkv_weight, attn_out, mlp_gain,
    mlp_up, mlp_down, query_gain, image_gain, cross_gain, cross_query, cross_keyval, cross_out,
    cross_up, cross_down,
):
    f32 = jnp.float32
    dp_count = lax.axis_size("dp")
    lines = dp_count // 4
    row_count, width = tokens.shape[1:]
    rows = attn_gain.shape[1]
    few = query_gain.shape[0]
    cross_shards = (cross_query, cross_keyval, cross_out, cross_up)
    cuts = tuple(w.shape[1] // 2 for w in cross_shards)
    parts = (qkv_weight.shape[2], attn_out.shape[2], mlp_up.shape[2])
    (
        full_a, full_d, sum_ca, sum_cd, h1, qkv, mixed, weight, middle, h2, active, slope,
        gains, layer_out, top, vec,
    ) = forward(
        lines, cuts, parts, kept_counts, caption_lengths, attn_gain, mlp_gain,
        query_gain[None], image_gain[None], cross_gain[None], tokens[0], cotangent[0],
        *cross_shards, qkv_weight[0], attn_out[0], mlp_up[0], mlp_down[0], cross_down,
    )
    shard_shapes = [
        w.shape[-2:]
        for w in (
            qkv_weight, attn_out, mlp_up, mlp_down, cross_query, cross_keyval, cross_out, cross_up,
            cross_down,
        )
    ]
    *weight_grads, input_grad, o_vec = backward(
        lines, cuts, parts, shard_shapes, tokens[0], top, gains, vec, full_a, full_d, sum_ca,
        sum_cd, h1, qkv, mixed, weight, middle, h2, active, slope,
    )
    (
        layer_out, input_grad, o_qkv, o_out, o_up, o_d, o_cq, o_ckv, o_co, o_cu, o_cd,
        g_1, g_2, g_q, g_i, g_c, rms,
    ) = final(lines, rows, few, o_vec, layer_out, input_grad, *weight_grads)
    return (
        layer_out[None], input_grad[None], g_1, o_qkv[None], o_out[None], g_2, o_up[None],
        o_d[None], g_q[0], g_i[0], g_c[0], o_cq, o_ckv, o_co, o_cu, o_cd, rms,
    )


def shards(*arrays):
    dp_count = lax.axis_size("dp")
    cross_query, cross_down = arrays[13], arrays[17]
    fills = dp_count % 4 == 0 and dp_count > 4
    fills = fills and cross_query.shape[0] % 8 == 0 and cross_down.shape[0] % 16 == 0
    return fused_shards(*arrays) if fills else plain_shards(*arrays)


def solution(mesh):
    rows = P("tower", "dp", None)
    gain = P("tower", "dp")
    cross_gain = P(("tower", "dp"))
    cross = P(("tower", "dp"), None)
    weights = (gain, rows, rows, gain, rows, rows) + (cross_gain,) * 3 + (cross,) * 5
    return jax.shard_map(
        shards,
        mesh=mesh,
        in_specs=(rows, rows, P("dp", None), P("dp")) + weights,
        out_specs=(rows, rows) + weights + (P(),),
        check_vma=False,
    )
```
